32 devices in a mesh: cells: 8 (over y, x, core), chrom: 4 (over z).
Axes of the slice: x: 2, y: 2, z: 4, core: 2. Of those that a mesh axis runs over, the one named last changes fastest.
Arguments:
- inputs: bfloat16 [16, 1024, 1280], P('cells', 'chrom'), may hold values from -6 to 6
- lengths: int32 [16], P('cells'), may hold values from 204 to 1024, as said below
- offsets: int32 [16, 24], P('cells'), may hold values from 1 to 1023, as said below
- cotangent: bfloat16 [16, 1024, 1280], P('cells', 'chrom'), may hold values from -6 to 6
- norm_gain: bfloat16 [1280], P('chrom'), may hold values from 0.5 to 1.5
- norm_shift: bfloat16 [1280], P('chrom'), may hold values from -1.75 to 1.75
- query_proj: bfloat16 [1280, 1280], P('chrom'), may hold values from -0.15625 to 0.15625
- query_bias: bfloat16 [1280], P('chrom'), may hold values from -1.75 to 1.75
- key_proj: bfloat16 [1280, 1280], P('chrom'), may hold values from -0.15625 to 0.15625
- value_proj: bfloat16 [1280, 1280], P('chrom'), may hold values from -0.15625 to 0.15625
- value_bias: bfloat16 [1280], P('chrom'), may hold values from -1.75 to 1.75
- output_proj: bfloat16 [1280, 1280], P('chrom'), may hold values from -1.25 to 1.25
- output_bias: bfloat16 [1280], P('chrom'), may hold values from -1.75 to 1.75
- second_gain: bfloat16 [1280], P('chrom'), may hold values from 0.5 to 1.5
- second_shift: bfloat16 [1280], P('chrom'), may hold values from -1.75 to 1.75
- inner_proj: bfloat16 [1280, 5120], P('chrom'), may hold values from -0.15625 to 0.15625
- inner_bias: bfloat16 [5120], P('chrom'), may hold values from -1.75 to 1.75
- outer_proj: bfloat16 [5120, 1280], P('chrom'), may hold values from -0.078125 to 0.078125
- outer_bias: bfloat16 [1280], P('chrom'), may hold values from -1.75 to 1.75
Outputs:
- block_out: bfloat16 [16, 1024, 1280], P('cells', 'chrom')
- input_grad: bfloat16 [16, 1024, 1280], P('cells', 'chrom')
- norm_gain_grad: float32 [1280], P('chrom')
- norm_shift_grad: float32 [1280], P('chrom')
- query_proj_grad: float32 [1280, 1280], P('chrom')
- query_bias_grad: float32 [1280], P('chrom')
- key_proj_grad: float32 [1280, 1280], P('chrom')
- value_proj_grad: float32 [1280, 1280], P('chrom')
- value_bias_grad: float32 [1280], P('chrom')
- output_proj_grad: float32 [1280, 1280], P('chrom')
- output_bias_grad: float32 [1280], P('chrom')
- second_gain_grad: float32 [1280], P('chrom')
- second_shift_grad: float32 [1280], P('chrom')
- inner_proj_grad: float32 [1280, 5120], P('chrom')
- inner_bias_grad: float32 [5120], P('chrom')
- outer_proj_grad: float32 [5120, 1280], P('chrom')
- outer_bias_grad: float32 [1280], P('chrom')
The draws below stay inside these ranges and needn't reach their ends.
Inputs may be any that keep to these rules, and one draw needn't show every extreme that they name: `lengths`: among the 2 cells of each index of cells one cell has exactly 1024 tokens. `offsets`: each cell's row is non-decreasing, its first entry is 1 and its last is the cell's length minus 1.
All inputs are finite; a program needn't handle non-finite values.
Results may differ from the reference program's by a relative error of at most 0.02.
Values may be sent and summed in bfloat16 or wider, within the bound.
A program may use at most 384 MiB of HBM per device.

```python
import jax
import jax.numpy as jnp
from jax import lax

D = 1280
HEADS = 20
HEAD_DIM = 64
FF = 5120
CELL_DEV = 2
GROUPS = 24
LEN = 1024
ALL_CELLS = 16


def cell_lengths(key):
    group_count = ALL_CELLS // CELL_DEV
    base_lengths = jax.random.randint(key, (ALL_CELLS,), LEN // 5, LEN + 1)
    chosen = jax.random.randint(jax.random.fold_in(key, 11), (group_count,), 0, CELL_DEV)
    within = jnp.arange(ALL_CELLS, dtype=jnp.int32) % CELL_DEV
    longest = within == jnp.repeat(chosen, CELL_DEV)
    return jnp.where(longest, LEN, base_lengths).astype(jnp.int32)


def draw_lengths(key, part):
    return cell_lengths(key)


def draw_offsets(key, part):
    cell_len = cell_lengths(key)
    key = jax.random.fold_in(key, 7)
    raw_draw = jax.random.randint(key, (ALL_CELLS, GROUPS), 0, 2 ** 20)
    starts = 1 + raw_draw * (cell_len[:, None] - 1) // 2 ** 20
    starts = jnp.sort(starts, axis=1)
    column = jnp.arange(GROUPS, dtype=jnp.int32)[None, :]
    starts = jnp.where(column == 0, 1, starts)
    starts = jnp.where(column == GROUPS - 1, cell_len[:, None] - 1, starts)
    return starts.astype(jnp.int32)


def levels(own_key, dims, split, smallest, largest):
    level, own = 1.0, jax.random.fold_in(own_key, 6)
    for position, shards_of in split:
        draws = jnp.exp(jax.random.uniform(jax.random.fold_in(own, position), (shards_of,), jnp.float32, smallest / len(split), largest / len(split)))
        level = level * jnp.repeat(draws, dims[position] // shards_of).reshape([-1 if axis == position else 1 for axis in range(len(dims))])
    return level


def bell_draw(rng, dims, deviation, most, shards=(), held_as=jnp.bfloat16):
    drawn = deviation * jax.random.normal(rng, dims, jnp.float32)
    if shards:
        drawn = drawn * levels(rng, dims, shards, -0.22, 0.18)
    return jnp.clip(drawn, -most, most).astype(held_as)


def setup_inputs(seed: int = 0) -> dict:
    splits = jax.random.split(jax.random.key(seed), 20)
    return {
        "inputs": bell_draw(splits[0], (ALL_CELLS, LEN, D), 1.0, 6.0, ((0, 8), (1, 4))),
        "lengths": draw_lengths(jax.random.fold_in(splits[19], 71), 0),
        "offsets": draw_offsets(jax.random.fold_in(splits[19], 71), 0),
        "cotangent": bell_draw(splits[3], (ALL_CELLS, LEN, D), 1.0, 6.0, ((0, 8), (1, 4))),
        "norm_gain": jnp.clip(1.0 + 0.1 * jax.random.normal(splits[4], (D,), jnp.float32), 0.5, 1.5).astype(jnp.bfloat16),
        "norm_shift": bell_draw(splits[5], (D,), 0.3, 1.75, ((0, 4),)),
        "query_proj": bell_draw(splits[6], (D, D), D ** -0.5, 0.15625, ((0, 4),)),
        "query_bias": bell_draw(splits[7], (D,), 0.3, 1.75, ((0, 4),)),
        "key_proj": bell_draw(splits[8], (D, D), D ** -0.5, 0.15625, ((0, 4),)),
        "value_proj": bell_draw(splits[9], (D, D), D ** -0.5, 0.15625, ((0, 4),)),
        "value_bias": bell_draw(splits[10], (D,), 0.3, 1.75, ((0, 4),)),
        "output_proj": bell_draw(splits[11], (D, D), (D // 64) ** -0.5, 1.25, ((0, 4),)),
        "output_bias": bell_draw(splits[12], (D,), 0.3, 1.75, ((0, 4),)),
        "second_gain": jnp.clip(1.0 + 0.1 * jax.random.normal(splits[13], (D,), jnp.float32), 0.5, 1.5).astype(jnp.bfloat16),
        "second_shift": bell_draw(splits[14], (D,), 0.3, 1.75, ((0, 4),)),
        "inner_proj": bell_draw(splits[15], (D, FF), D ** -0.5, 0.15625, ((0, 4),)),
        "inner_bias": bell_draw(splits[16], (FF,), 0.3, 1.75, ((0, 4),)),
        "outer_proj": bell_draw(splits[17], (FF, D), FF ** -0.5, 0.078125, ((0, 4),)),
        "outer_bias": bell_draw(splits[18], (D,), 0.3, 1.75, ((0, 4),)),
    }


eps_norm = 1e-05
group_bias = 1.0

@jax.custom_vjp
def low(v):
    return lax.optimization_barrier(v.astype(jnp.bfloat16)).astype(jnp.float32)

@jax.custom_vjp
def low_back(v):
    return v

def low_keep(v):
    return (low(v), None)

def low_pass(kept, grad):
    return (grad,)

def back_keep(v):
    return (v, None)

def back_low(kept, grad):
    return (low(grad),)
low.defvjp(low_keep, low_pass)
low_back.defvjp(back_keep, back_low)

def layer_norm(values, gain, shift):
    center = values - lax.optimization_barrier(jnp.mean(values, axis=-1, keepdims=True))
    spread = lax.optimization_barrier(jnp.mean(center * center, axis=-1, keepdims=True))
    return center * lax.rsqrt(spread + eps_norm) * gain + shift

def matmul(left, right):
    return jnp.dot(left, right, precision=lax.Precision.HIGHEST)

def cell_forward(params, states, length, starts):
    norm_gain, norm_shift, query_proj, query_bias, key_proj, value_proj, value_bias, output_proj, output_bias, second_gain, second_shift, inner_proj, inner_bias, outer_proj, outer_bias = params
    places = jnp.arange(LEN, dtype=jnp.int32)
    live = places < length
    groups = lax.optimization_barrier(jnp.sum((places[:, None] >= starts[None, :]).astype(jnp.int32), axis=1))
    same = (groups[:, None] == groups[None, :]).astype(jnp.float32)
    normed = low(layer_norm(states, norm_gain, norm_shift))
    queries = low_back(low(matmul(normed, query_proj) + query_bias)).reshape(LEN, HEADS, HEAD_DIM)
    key_rows = low_back(low(matmul(normed, key_proj))).reshape(LEN, HEADS, HEAD_DIM)
    vals = low_back(low(matmul(normed, value_proj) + value_bias)).reshape(LEN, HEADS, HEAD_DIM)
    raw = low_back(jnp.einsum('qhd,khd->hqk', queries, key_rows, precision=lax.Precision.HIGHEST) * HEAD_DIM ** (-0.5))
    masked = jnp.where(live[None, None, :], raw + group_bias * same[None], -jnp.inf)
    row_max = lax.optimization_barrier(jnp.max(masked, axis=-1, keepdims=True))
    exp_scores = jnp.exp(masked - row_max)
    attn_probs = exp_scores / lax.optimization_barrier(jnp.sum(exp_scores, axis=-1, keepdims=True))
    mixed_out = jnp.einsum('hqk,khd->qhd', low(attn_probs), vals, precision=lax.Precision.HIGHEST)
    mixed_out = low_back(low(mixed_out)).reshape(LEN, D)
    attended = low_back(matmul(mixed_out, output_proj) + output_bias)
    middle = states + attended
    second = low(layer_norm(middle, second_gain, second_shift))
    inner_pre = low_back(matmul(second, inner_proj) + inner_bias)
    active = low(jax.nn.gelu(inner_pre, approximate=False))
    result = middle + matmul(active, outer_proj) + outer_bias
    return jnp.where(live[:, None], result, 0.0)

def reference(inputs, lengths, offsets, cotangent, norm_gain, norm_shift, query_proj, query_bias, key_proj, value_proj, value_bias, output_proj, output_bias, second_gain, second_shift, inner_proj, inner_bias, outer_proj, outer_bias):
    params = tuple((member.astype(jnp.float32) for member in (norm_gain, norm_shift, query_proj, query_bias, key_proj, value_proj, value_bias, output_proj, output_bias, second_gain, second_shift, inner_proj, inner_bias, outer_proj, outer_bias)))
    states = inputs.astype(jnp.float32)

    def forward(weights, cell_states):

        def one_cell(packed):
            return cell_forward(weights, packed[0], packed[1], packed[2])
        return lax.map(jax.checkpoint(one_cell), (cell_states, lengths, offsets))
    outputs, pullback = jax.vjp(forward, params, states)
    weight_grads, state_grad = pullback(cotangent.astype(jnp.float32))
    return (outputs.astype(jnp.bfloat16), state_grad.astype(jnp.bfloat16), weight_grads[0], weight_grads[1], weight_grads[2], weight_grads[3], weight_grads[4], weight_grads[5], weight_grads[6], weight_grads[7], weight_grads[8], weight_grads[9], weight_grads[10], weight_grads[11], weight_grads[12], weight_grads[13], weight_grads[14])
```

```python
import functools

import jax
import jax.numpy as jnp
from jax import lax
from jax.experimental import pallas as pl
from jax.experimental.pallas import tpu as pltpu
from jax.sharding import PartitionSpec as P

HEADS = 20
HEAD_DIM = 64


eps_norm = 1e-05
group_bias = 1.0


def layer_norm(values, gain, shift):
    center = values - jnp.mean(values, axis=-1, keepdims=True)
    spread = jnp.mean(center * center, axis=-1, keepdims=True)
    return center * lax.rsqrt(spread + eps_norm) * gain + shift


def gelu_exact(values):
    return jax.nn.gelu(values, approximate=False)


def product(left, right):
    return jnp.dot(left, right, preferred_element_type=jnp.float32)


def left_product(left, right):
    return jnp.einsum("ra,rb->ab", left, right, preferred_element_type=jnp.float32)


def right_back(left, right):
    return jnp.einsum("rb,ab->ra", left, right, preferred_element_type=jnp.float32)


def column_sum(values):
    return jnp.sum(values, axis=0, dtype=jnp.float32)


def split_rows(value, outer, inner_count):
    return value.reshape(
        (outer, inner_count, value.shape[0] // (outer * inner_count)) + value.shape[1:]
    )


def general(
    inputs,
    lengths,
    offsets,
    cotangent,
    norm_gain,
    norm_shift,
    query_proj,
    query_bias,
    key_proj,
    value_proj,
    value_bias,
    output_proj,
    output_bias,
    second_gain,
    second_shift,
    inner_proj,
    inner_bias,
    outer_proj,
    outer_bias,
):
    count_chrom = lax.axis_size("chrom")
    count_cells = lax.axis_size("cells")
    block_index = lax.axis_index("chrom")
    cells_here, tokens_here, feat_width = inputs.shape
    seq_len = tokens_here * count_chrom
    row_count = cells_here * tokens_here
    inv_root = HEAD_DIM ** (-0.5)
    places = jnp.arange(seq_len, dtype=jnp.int32)
    key_live = places[None, :] < lengths[:, None]
    groups = jnp.sum((places[None, :, None] >= offsets[:, None, :]).astype(jnp.int32), axis=2)
    query_groups = lax.dynamic_slice_in_dim(groups, block_index * tokens_here, tokens_here, 1)
    query_live = lax.dynamic_slice_in_dim(key_live, block_index * tokens_here, tokens_here, 1)
    same_group = (query_groups[:, :, None] == groups[:, None, :]).astype(jnp.float32)
    mask_bias = jnp.where(key_live[:, None, :], group_bias * same_group, -jnp.inf)[:, None]
    gathered = (
        lax.all_gather(norm_gain, "chrom", axis=0, tiled=True),
        lax.all_gather(norm_shift, "chrom", axis=0, tiled=True),
        lax.all_gather(query_proj, "chrom", axis=0, tiled=True),
        lax.all_gather(query_bias, "chrom", axis=0, tiled=True),
        lax.all_gather(key_proj, "chrom", axis=0, tiled=True),
        lax.all_gather(value_proj, "chrom", axis=0, tiled=True),
        lax.all_gather(value_bias, "chrom", axis=0, tiled=True),
        lax.all_gather(output_proj, "chrom", axis=0, tiled=True),
        lax.all_gather(output_bias, "chrom", axis=0, tiled=True),
        lax.all_gather(second_gain, "chrom", axis=0, tiled=True),
        lax.all_gather(second_shift, "chrom", axis=0, tiled=True),
        lax.all_gather(inner_proj, "chrom", axis=0, tiled=True),
        lax.all_gather(inner_bias, "chrom", axis=0, tiled=True),
        lax.all_gather(outer_proj, "chrom", axis=0, tiled=True),
        lax.all_gather(outer_bias, "chrom", axis=0, tiled=True),
    )
    gain_one = gathered[0].astype(jnp.float32)
    shift_one = gathered[1].astype(jnp.float32)
    gain_two = gathered[9].astype(jnp.float32)
    shift_two = gathered[10].astype(jnp.float32)
    states = inputs.astype(jnp.float32).reshape(row_count, feat_width)
    normed_full, norm_back = jax.vjp(layer_norm, states, gain_one, shift_one)
    normed = normed_full.astype(jnp.bfloat16)
    queries = (product(normed, gathered[2]) + gathered[3].astype(jnp.float32)).astype(jnp.bfloat16)
    key_rows = product(normed, gathered[4]).astype(jnp.bfloat16)
    vals = (product(normed, gathered[5]) + gathered[6].astype(jnp.float32)).astype(jnp.bfloat16)
    keys_all, vals_all = (
        lax.all_gather(
            key_rows.reshape(cells_here, tokens_here, feat_width), "chrom", axis=1, tiled=True
        ),
        lax.all_gather(
            vals.reshape(cells_here, tokens_here, feat_width), "chrom", axis=1, tiled=True
        ),
    )
    query_heads = queries.reshape(cells_here, tokens_here, HEADS, HEAD_DIM)
    key_heads = keys_all.reshape(cells_here, seq_len, HEADS, HEAD_DIM)
    val_heads = vals_all.reshape(cells_here, seq_len, HEADS, HEAD_DIM)

    def scores_of():
        raw = (
            jnp.einsum(
                "cqhd,ckhd->chqk", query_heads, key_heads, preferred_element_type=jnp.float32
            )
            * inv_root
        )
        return raw + mask_bias

    masked = scores_of()
    row_max = jnp.max(masked, axis=-1, keepdims=True)
    exp_scores = jnp.exp(masked - row_max)
    exp_total = jnp.sum(exp_scores, axis=-1, keepdims=True)
    attn_probs = exp_scores / exp_total
    log_total = row_max + jnp.log(exp_total)
    mixed_out = jnp.einsum(
        "chqk,ckhd->cqhd",
        attn_probs.astype(jnp.bfloat16),
        val_heads,
        preferred_element_type=jnp.float32,
    )
    mixed_out = mixed_out.astype(jnp.bfloat16).reshape(row_count, feat_width)
    attended = product(mixed_out, gathered[7]) + gathered[8].astype(jnp.float32)
    middle = states + attended
    second_full, second_back = jax.vjp(layer_norm, middle, gain_two, shift_two)
    second = second_full.astype(jnp.bfloat16)
    inner_pre = product(second, gathered[11]) + gathered[12].astype(jnp.float32)
    active_full, gelu_back = jax.vjp(gelu_exact, inner_pre)
    active = active_full.astype(jnp.bfloat16)
    result = middle + product(active, gathered[13]) + gathered[14].astype(jnp.float32)
    live_rows = query_live.reshape(row_count, 1)
    block_out = (
        jnp.where(live_rows, result, 0.0)
        .astype(jnp.bfloat16)
        .reshape(cells_here, tokens_here, feat_width)
    )
    upstream = jnp.where(
        live_rows, cotangent.reshape(row_count, feat_width), jnp.zeros((), jnp.bfloat16)
    )
    outer_bias_grad = column_sum(upstream)
    outer_proj_grad = left_product(active, upstream)
    grad_active = right_back(upstream, gathered[13])
    (grad_inner_full,) = gelu_back(grad_active)
    grad_inner = grad_inner_full.astype(jnp.bfloat16)
    inner_bias_grad = column_sum(grad_inner)
    inner_proj_grad = left_product(second, grad_inner)
    grad_second = right_back(grad_inner, gathered[11])
    grad_middle_norm, second_gain_grad, second_shift_grad = second_back(grad_second)
    grad_middle = upstream.astype(jnp.float32) + grad_middle_norm
    grad_attended = grad_middle.astype(jnp.bfloat16)
    output_bias_grad = column_sum(grad_attended)
    output_proj_grad = left_product(mixed_out, grad_attended)
    grad_mixed = right_back(grad_attended, gathered[7]).astype(jnp.bfloat16)
    grad_mixed = grad_mixed.reshape(cells_here, tokens_here, HEADS, HEAD_DIM)
    attn_again = jnp.exp(scores_of() - log_total)
    grad_probs = jnp.einsum(
        "cqhd,ckhd->chqk", grad_mixed, val_heads, preferred_element_type=jnp.float32
    )
    row_dot = jnp.sum(attn_again * grad_probs, axis=-1, keepdims=True)
    grad_raw = (attn_again * (grad_probs - row_dot)).astype(jnp.bfloat16)
    grad_vals_part = jnp.einsum(
        "chqk,cqhd->ckhd",
        attn_again.astype(jnp.bfloat16),
        grad_mixed,
        preferred_element_type=jnp.float32,
    )
    grad_keys_part = (
        jnp.einsum("chqk,cqhd->ckhd", grad_raw, query_heads, preferred_element_type=jnp.float32)
        * inv_root
    )
    grad_queries = (
        jnp.einsum("chqk,ckhd->cqhd", grad_raw, key_heads, preferred_element_type=jnp.float32)
        * inv_root
    ).astype(jnp.bfloat16)
    grad_queries = grad_queries.reshape(row_count, feat_width)
    grad_keys_sum, grad_vals_sum = (
        lax.psum_scatter(
            grad_keys_part.reshape(cells_here, seq_len, feat_width).astype(jnp.bfloat16),
            "chrom",
            scatter_dimension=1,
            tiled=True,
        ).astype(jnp.float32),
        lax.psum_scatter(
            grad_vals_part.reshape(cells_here, seq_len, feat_width).astype(jnp.bfloat16),
            "chrom",
            scatter_dimension=1,
            tiled=True,
        ).astype(jnp.float32),
    )
    grad_keys = grad_keys_sum.astype(jnp.bfloat16).reshape(row_count, feat_width)
    grad_vals = grad_vals_sum.astype(jnp.bfloat16).reshape(row_count, feat_width)
    query_proj_grad = left_product(normed, grad_queries)
    query_bias_grad = column_sum(grad_queries)
    key_proj_grad = left_product(normed, grad_keys)
    value_proj_grad = left_product(normed, grad_vals)
    value_bias_grad = column_sum(grad_vals)
    grad_normed = (
        right_back(grad_queries, gathered[2])
        + right_back(grad_keys, gathered[4])
        + right_back(grad_vals, gathered[5])
    )
    grad_states_norm, norm_gain_grad, norm_shift_grad = norm_back(grad_normed)
    input_grad = (
        (grad_middle + grad_states_norm)
        .astype(jnp.bfloat16)
        .reshape(cells_here, tokens_here, feat_width)
    )
    grad_list = (
        norm_gain_grad,
        norm_shift_grad,
        query_proj_grad,
        query_bias_grad,
        key_proj_grad,
        value_proj_grad,
        value_bias_grad,
        output_proj_grad,
        output_bias_grad,
        second_gain_grad,
        second_shift_grad,
        inner_proj_grad,
        inner_bias_grad,
        outer_proj_grad,
        outer_bias_grad,
    )
    pieces = tuple((split_rows(member, count_chrom, count_cells) for member in grad_list))
    section_one = (
        lax.psum_scatter(
            pieces[0].astype(jnp.bfloat16), "cells", scatter_dimension=1, tiled=True
        ).astype(jnp.float32),
        lax.psum_scatter(
            pieces[1].astype(jnp.bfloat16), "cells", scatter_dimension=1, tiled=True
        ).astype(jnp.float32),
        lax.psum_scatter(
            pieces[2].astype(jnp.bfloat16), "cells", scatter_dimension=1, tiled=True
        ).astype(jnp.float32),
        lax.psum_scatter(
            pieces[3].astype(jnp.bfloat16), "cells", scatter_dimension=1, tiled=True
        ).astype(jnp.float32),
        lax.psum_scatter(
            pieces[4].astype(jnp.bfloat16), "cells", scatter_dimension=1, tiled=True
        ).astype(jnp.float32),
        lax.psum_scatter(
            pieces[5].astype(jnp.bfloat16), "cells", scatter_dimension=1, tiled=True
        ).astype(jnp.float32),
        lax.psum_scatter(
            pieces[6].astype(jnp.bfloat16), "cells", scatter_dimension=1, tiled=True
        ).astype(jnp.float32),
        lax.psum_scatter(
            pieces[7].astype(jnp.bfloat16), "cells", scatter_dimension=1, tiled=True
        ).astype(jnp.float32),
        lax.psum_scatter(
            pieces[8].astype(jnp.bfloat16), "cells", scatter_dimension=1, tiled=True
        ).astype(jnp.float32),
        lax.psum_scatter(
            pieces[9].astype(jnp.bfloat16), "cells", scatter_dimension=1, tiled=True
        ).astype(jnp.float32),
        lax.psum_scatter(
            pieces[10].astype(jnp.bfloat16), "cells", scatter_dimension=1, tiled=True
        ).astype(jnp.float32),
        lax.psum_scatter(
            pieces[11].astype(jnp.bfloat16), "cells", scatter_dimension=1, tiled=True
        ).astype(jnp.float32),
        lax.psum_scatter(
            pieces[12].astype(jnp.bfloat16), "cells", scatter_dimension=1, tiled=True
        ).astype(jnp.float32),
        lax.psum_scatter(
            pieces[13].astype(jnp.bfloat16), "cells", scatter_dimension=1, tiled=True
        ).astype(jnp.float32),
        lax.psum_scatter(
            pieces[14].astype(jnp.bfloat16), "cells", scatter_dimension=1, tiled=True
        ).astype(jnp.float32),
    )
    section_two = (
        lax.psum_scatter(
            section_one[0].astype(jnp.bfloat16), "chrom", scatter_dimension=0, tiled=True
        ).astype(jnp.float32),
        lax.psum_scatter(
            section_one[1].astype(jnp.bfloat16), "chrom", scatter_dimension=0, tiled=True
        ).astype(jnp.float32),
        lax.psum_scatter(
            section_one[2].astype(jnp.bfloat16), "chrom", scatter_dimension=0, tiled=True
        ).astype(jnp.float32),
        lax.psum_scatter(
            section_one[3].astype(jnp.bfloat16), "chrom", scatter_dimension=0, tiled=True
        ).astype(jnp.float32),
        lax.psum_scatter(
            section_one[4].astype(jnp.bfloat16), "chrom", scatter_dimension=0, tiled=True
        ).astype(jnp.float32),
        lax.psum_scatter(
            section_one[5].astype(jnp.bfloat16), "chrom", scatter_dimension=0, tiled=True
        ).astype(jnp.float32),
        lax.psum_scatter(
            section_one[6].astype(jnp.bfloat16), "chrom", scatter_dimension=0, tiled=True
        ).astype(jnp.float32),
        lax.psum_scatter(
            section_one[7].astype(jnp.bfloat16), "chrom", scatter_dimension=0, tiled=True
        ).astype(jnp.float32),
        lax.psum_scatter(
            section_one[8].astype(jnp.bfloat16), "chrom", scatter_dimension=0, tiled=True
        ).astype(jnp.float32),
        lax.psum_scatter(
            section_one[9].astype(jnp.bfloat16), "chrom", scatter_dimension=0, tiled=True
        ).astype(jnp.float32),
        lax.psum_scatter(
            section_one[10].astype(jnp.bfloat16), "chrom", scatter_dimension=0, tiled=True
        ).astype(jnp.float32),
        lax.psum_scatter(
            section_one[11].astype(jnp.bfloat16), "chrom", scatter_dimension=0, tiled=True
        ).astype(jnp.float32),
        lax.psum_scatter(
            section_one[12].astype(jnp.bfloat16), "chrom", scatter_dimension=0, tiled=True
        ).astype(jnp.float32),
        lax.psum_scatter(
            section_one[13].astype(jnp.bfloat16), "chrom", scatter_dimension=0, tiled=True
        ).astype(jnp.float32),
        lax.psum_scatter(
            section_one[14].astype(jnp.bfloat16), "chrom", scatter_dimension=0, tiled=True
        ).astype(jnp.float32),
    )
    rejoined = (
        lax.all_gather(section_two[0].astype(jnp.bfloat16), "cells", axis=1, tiled=True).astype(
            jnp.float32
        ),
        lax.all_gather(section_two[1].astype(jnp.bfloat16), "cells", axis=1, tiled=True).astype(
            jnp.float32
        ),
        lax.all_gather(section_two[2].astype(jnp.bfloat16), "cells", axis=1, tiled=True).astype(
            jnp.float32
        ),
        lax.all_gather(section_two[3].astype(jnp.bfloat16), "cells", axis=1, tiled=True).astype(
            jnp.float32
        ),
        lax.all_gather(section_two[4].astype(jnp.bfloat16), "cells", axis=1, tiled=True).astype(
            jnp.float32
        ),
        lax.all_gather(section_two[5].astype(jnp.bfloat16), "cells", axis=1, tiled=True).astype(
            jnp.float32
        ),
        lax.all_gather(section_two[6].astype(jnp.bfloat16), "cells", axis=1, tiled=True).astype(
            jnp.float32
        ),
        lax.all_gather(section_two[7].astype(jnp.bfloat16), "cells", axis=1, tiled=True).astype(
            jnp.float32
        ),
        lax.all_gather(section_two[8].astype(jnp.bfloat16), "cells", axis=1, tiled=True).astype(
            jnp.float32
        ),
        lax.all_gather(section_two[9].astype(jnp.bfloat16), "cells", axis=1, tiled=True).astype(
            jnp.float32
        ),
        lax.all_gather(section_two[10].astype(jnp.bfloat16), "cells", axis=1, tiled=True).astype(
            jnp.float32
        ),
        lax.all_gather(section_two[11].astype(jnp.bfloat16), "cells", axis=1, tiled=True).astype(
            jnp.float32
        ),
        lax.all_gather(section_two[12].astype(jnp.bfloat16), "cells", axis=1, tiled=True).astype(
            jnp.float32
        ),
        lax.all_gather(section_two[13].astype(jnp.bfloat16), "cells", axis=1, tiled=True).astype(
            jnp.float32
        ),
        lax.all_gather(section_two[14].astype(jnp.bfloat16), "cells", axis=1, tiled=True).astype(
            jnp.float32
        ),
    )
    final = tuple(
        (
            member.reshape(
                (member.shape[0] * member.shape[1] * member.shape[2],) + member.shape[3:]
            )
            for member in rejoined
        )
    )
    return (block_out, input_grad) + tuple(final)


PLANE = 4
LINE = 4


def rows_of(start, count):
    return pl.ds(pl.multiple_of(start, 16), count)


def cols_of(start, count):
    return pl.ds(pl.multiple_of(start, 128), count)


def gather_kernel(
    small_ref, x_ref, ct_ref, wq_ref, wk_ref, wv_ref, wo_ref, w1_ref, w2_ref,
    smalls, xf, cf, wa, wb, wc, wob,
    sm_s, sm_r, ex_s, ex_r, fw_s, fw_r, un_s, un_r, loc, wo_s, wo_r,
):
    i, z = lax.axis_index("cells"), lax.axis_index("chrom")
    p, c = i // 2, lax.rem(i, 2)
    px, py = lax.rem(p, 2), p // 2
    x_nb, y_nb, core_nb = i + 2 - 4 * px, i + 4 - 8 * py, i + 1 - 2 * c
    p_x, p_y = p + 1 - 2 * px, p + 2 - 4 * py
    right = lax.rem(z + 1, LINE)
    rows = wq_ref.shape[0]
    feat = wq_ref.shape[1]
    half = feat // 2
    hid = w2_ref.shape[0]
    block = x_ref.shape[1]
    part, hid_part = rows // PLANE, hid // 2 // PLANE

    barrier = pltpu.get_barrier_semaphore()
    line_ids = [
        (i - c + lax.rem(c + dc, 2), lax.rem(z + dz, LINE))
        for dc in range(2)
        for dz in range(LINE)
        if dc or dz
    ]
    for who in line_ids + [(x_nb, z), (y_nb, z)]:
        pl.semaphore_signal(barrier, inc=1, device_id=who, device_id_type=pl.DeviceIdType.MESH)
    pl.semaphore_wait(barrier, len(line_ids) + 2)

    def send(src, dst, s, r, who):
        return pltpu.make_async_remote_copy(
            src_ref=src, dst_ref=dst, send_sem=s, recv_sem=r, device_id=who,
            device_id_type=pl.DeviceIdType.MESH,
        )

    small_own = pltpu.make_async_copy(small_ref, smalls.at[z], loc.at[0])
    small_out = [
        send(small_ref, smalls.at[z], sm_s.at[d], sm_r.at[d], (i, lax.rem(z + d + 1, LINE)))
        for d in range(LINE - 1)
    ]

    def exchange(src, dst, which):
        stay = c == z // 2
        mine, outs = None, []
        for k in range(2):
            j = lax.rem(z + k, 2)
            to = dst.at[rows_of(z * block, block), :]
            r = ex_r.at[2 * which + k]
            outs.append(send(src.at[j], to, ex_s.at[2 * which + k], r, (i - c + z // 2, 2 * c + j)))
            if k == 0:
                mine = pltpu.make_async_copy(src.at[j], to, r)

        def start():
            pl.when(stay)(mine.start)
            pl.when(jnp.logical_not(stay))(outs[0].start)
            outs[1].start()

        def arrived():
            pl.when(stay)(mine.wait)
            pl.when(jnp.logical_not(stay))(outs[0].wait_recv)
            outs[1].wait_recv()

        def sent():
            pl.when(jnp.logical_not(stay))(outs[0].wait_send)
            outs[1].wait_send()

        return start, arrived, sent

    def forward(dst, which):
        return [
            send(
                dst.at[rows_of((2 * c + b) * block, block), :],
                dst.at[rows_of((2 * c + b) * block, block), :],
                fw_s.at[2 * which + b], fw_r.at[2 * which + b], (core_nb, z),
            )
            for b in range(2)
        ]

    x_start, x_arrived, x_sent = exchange(x_ref, xf, 0)
    c_start, c_arrived, c_sent = exchange(ct_ref, cf, 1)
    x_fw, c_fw = forward(xf, 0), forward(cf, 1)

    lands = (wa, wb, wc)

    def own_parts(g, row, count):
        if g == 0:
            return [
                (ref.at[rows_of(row, count), cols_of(c * half, half)], cols_of(n * half, half))
                for n, ref in enumerate((wq_ref, wk_ref, wv_ref, wo_ref))
            ]
        if g == 1:
            return [
                (w1_ref.at[rows_of(row, count), cols_of(n * hid + c * (hid // 2), hid // 2)], cols_of(n * (hid // 2), hid // 2))
                for n in range(LINE)
            ]
        return [(w2_ref.at[rows_of(c * (hid // 2) + row, count), :], pl.ds(0, feat))]

    def shape_of(g):
        return (rows, part) if g < 2 else (hid // 2, hid_part)

    def piece(g, s, at):
        shard, count = shape_of(g)
        return lands[g].at[rows_of(s * shard + at * count, count), :]

    def half_piece(g, s, at, side):
        shard, count = shape_of(g)
        width = lands[g].shape[1] // 2
        return lands[g].at[rows_of(s * shard + at * count, count), pl.ds(side * width, width)]

    def shard_at(k):
        return lax.rem(z - k + LINE, LINE)

    class Unit:
        def __init__(self, g, k):
            self.g, self.k, self.n = g, k, g * (LINE - 1) + k - 1

        def sems(self, e):
            return un_s.at[self.n, e], un_r.at[self.n, e]

        def turn(self):
            s = shard_at(self.k - 1)
            return send(piece(self.g, s, p), piece(self.g, s, p), *self.sems(0), (i, right))

        def turn_start(self):
            if self.k > 1:
                self.turn().start()
                return
            shard, count = shape_of(self.g)
            for src, cols in own_parts(self.g, p * count, count):
                dst = lands[self.g].at[rows_of(z * shard + p * count, count), cols]
                send(src, dst, *self.sems(0), (i, right)).start()

        def spread(self):
            s = shard_at(self.k)
            own = piece(self.g, s, p)
            return [
                send(own, own, *self.sems(1), (x_nb, z)),
                send(own, own, *self.sems(2), (y_nb, z)),
            ]

        def cross(self):
            s = shard_at(self.k)
            left = half_piece(self.g, s, p_x, 0)
            rest = half_piece(self.g, s, p_y, 1)
            return [
                send(left, left, *self.sems(3), (y_nb, z)),
                send(rest, rest, *self.sems(4), (x_nb, z)),
            ]

        def arrived(self):
            self.turn().wait_recv()

        def spread_start(self):
            for d in self.spread():
                d.start()

        def cross_start(self):
            for d in self.spread():
                d.wait_recv()
            for d in self.cross():
                d.start()

        def done(self):
            for d in self.cross():
                d.wait_recv()

        def sent(self):
            for d in [self.turn()] + self.spread() + self.cross():
                d.wait_send()

    a, b, w = ([Unit(g, k) for k in range(1, LINE)] for g in range(3))

    def own_start(g):
        shard, _ = shape_of(g)
        for src, cols in own_parts(g, 0, shard):
            pltpu.make_async_copy(src, lands[g].at[rows_of(z * shard, shard), cols], loc.at[1 + g]).start()

    def own_wait(g):
        shard, _ = shape_of(g)
        ref = lands[g].at[rows_of(z * shard, shard), :]
        pltpu.make_async_copy(ref, ref, loc.at[1 + g]).wait()

    small_own.start()
    for d in small_out:
        d.start()
    a[0].turn_start()
    x_start()
    for g in range(3):
        own_start(g)
    a[0].arrived()
    a[1].turn_start()
    a[0].spread_start()
    b[0].turn_start()
    a[1].arrived()
    a[2].turn_start()
    a[1].spread_start()
    a[0].cross_start()
    x_arrived()
    for d in x_fw:
        d.start()
    a[2].arrived()
    a[2].spread_start()
    b[0].arrived()
    b[1].turn_start()
    b[0].spread_start()
    a[1].cross_start()
    a[2].cross_start()
    b[1].arrived()
    b[2].turn_start()
    w[0].turn_start()
    b[1].spread_start()
    b[0].cross_start()
    for u in a:
        u.done()
    own_wait(0)
    wo_own = pltpu.make_async_copy(
        wa.at[rows_of(c * half, half), pl.ds(3 * half, half)], wob.at[:, cols_of(c * half, half)], loc.at[4]
    )
    wo_out = send(
        wa.at[rows_of((1 - c) * half, half), pl.ds(3 * half, half)],
        wob.at[:, cols_of(c * half, half)], wo_s.at[0], wo_r.at[0], (core_nb, z),
    )
    wo_own.start()
    wo_out.start()
    b[2].arrived()
    b[2].spread_start()
    w[0].arrived()
    w[1].turn_start()
    w[0].spread_start()
    c_start()
    b[1].cross_start()
    b[2].cross_start()
    w[1].arrived()
    w[2].turn_start()
    w[1].spread_start()
    w[0].cross_start()
    w[2].arrived()
    w[2].spread_start()
    w[1].cross_start()
    c_arrived()
    for d in c_fw:
        d.start()
    w[2].cross_start()
    for u in b + w:
        u.done()
    for g in (1, 2):
        own_wait(g)
    small_own.wait()
    wo_own.wait()
    for d in small_out + x_fw + c_fw + [wo_out]:
        d.wait()
    x_sent()
    c_sent()
    for u in a + b + w:
        u.sent()


def gather_all(small, x, ct, wq, wk, wv, wo, w1, w2):
    rows, feat = wq.shape
    hid = w2.shape[0]
    seq = x.shape[1] * LINE
    bf = jnp.bfloat16
    dma = pltpu.SemaphoreType.DMA
    anywhere = pl.BlockSpec(memory_space=pl.ANY)
    return pl.pallas_call(
        gather_kernel,
        out_shape=(
            jax.ShapeDtypeStruct((LINE,) + small.shape, bf),
            jax.ShapeDtypeStruct((seq, feat), bf),
            jax.ShapeDtypeStruct((seq, feat), bf),
            jax.ShapeDtypeStruct((rows * LINE, 2 * feat), bf),
            jax.ShapeDtypeStruct((rows * LINE, hid * LINE // 2), bf),
            jax.ShapeDtypeStruct((hid * LINE // 2, feat), bf),
            jax.ShapeDtypeStruct((feat // 2, feat), bf),
        ),
        in_specs=[anywhere] * 9,
        out_specs=(anywhere,) * 7,
        scratch_shapes=[
            dma((3,)), dma((3,)), dma((4,)), dma((4,)), dma((4,)), dma((4,)),
            dma((9, 5)), dma((9, 5)), dma((5,)), dma((1,)), dma((1,)),
        ],
        compiler_params=pltpu.CompilerParams(collective_id=0, has_side_effects=True),
        name="gather_all",
    )(small, x, ct, wq, wk, wv, wo, w1, w2)


def flip(value, step):
    count = lax.axis_size("cells")
    return lax.ppermute(value, "cells", [(n, n ^ step) for n in range(count)])


def take(value, index, axis):
    return lax.dynamic_index_in_dim(value, index, axis, keepdims=False)


def plus(left, right):
    return (left.astype(jnp.float32) + right.astype(jnp.float32)).astype(jnp.bfloat16)


def plane_sum(value, px, py):
    two = value.reshape((2, LINE // 2, 2, 2) + value.shape[2:])
    first, later = two[0], two[1]
    first = plus(take(first, px, 2), flip(take(first, 1 - px, 2), 2))
    later = plus(take(later, py, 1), flip(take(later, 1 - py, 1), 4))
    first = plus(take(first, py, 1), flip(take(first, 1 - py, 1), 4))
    later = plus(take(later, px, 1), flip(take(later, 1 - px, 1), 2))
    return jnp.concatenate([first, later], axis=0)


def reduce_group(value, px, py):
    mine = plane_sum(value, px, py)
    summed = lax.psum_scatter(mine, "chrom", scatter_dimension=0, tiled=True)[0]
    whole = lax.all_gather(summed, "cells", axis=0, tiled=False)
    return whole.reshape((PLANE, 2) + summed.shape)


def send_home(value, core, place):
    half, feat = value.shape
    two = value.reshape(2, half // 2, feat)
    got = []
    for k in range(2):
        pairs = []
        for cells in range(lax.axis_size("cells")):
            for z in range(LINE):
                home, c = cells - cells % 2, cells % 2
                to_z = 2 * c + (z + k) % 2
                pairs.append((cells * LINE + z, (home + z // 2) * LINE + to_z))
        block = take(two, lax.rem(place + k, 2), 0)
        got.append(lax.ppermute(block, ("cells", "chrom"), pairs))
    even = lax.rem(place, 2) == 0
    return jnp.stack([jnp.where(even, got[0], got[1]), jnp.where(even, got[1], got[0])])


def paired_local(
    inputs, lengths, offsets, cotangent, norm_gain, norm_shift, query_proj, query_bias, key_proj, value_proj,
    value_bias, output_proj, output_bias, second_gain, second_shift, inner_proj, inner_bias, outer_proj, outer_bias,
):
    f32, bf = jnp.float32, jnp.bfloat16
    i, z = lax.axis_index("cells"), lax.axis_index("chrom")
    p, c = i // 2, i % 2
    px, py = p % 2, p // 2
    cells_here, block, feat = inputs.shape
    seq = block * LINE
    half_seq, half = seq // 2, feat // 2
    rows = feat // LINE
    hid = outer_proj.shape[0]
    inv_root = HEAD_DIM ** (-0.5)
    heads = HEADS // 2

    vectors = (norm_gain, norm_shift, query_bias, value_bias, output_bias, second_gain, second_shift, outer_bias)
    small = jnp.concatenate([v.reshape(1, rows) for v in vectors] + [inner_bias.reshape(hid // rows, rows)], axis=0)
    small = jnp.pad(small, ((0, 16 - small.shape[0]), (0, 384 - rows)))
    smalls, xf, cf, wa, wb, wc, wob = gather_all(
        small, inputs, cotangent, query_proj, key_proj, value_proj, output_proj, inner_proj, outer_proj
    )
    flat = smalls[:, :8, :rows].astype(f32).transpose(1, 0, 2).reshape(8, feat)
    gain_one, shift_one, bias_q, bias_v, bias_o, gain_two, shift_two, bias_out = (flat[n] for n in range(8))
    bias_in = lax.dynamic_slice_in_dim(smalls[:, 8:12, :rows], 2 * c, 2, 1).astype(f32).reshape(2 * hid)
    bias_q = lax.dynamic_slice_in_dim(bias_q, c * half, half, 0)
    bias_v = lax.dynamic_slice_in_dim(bias_v, c * half, half, 0)

    ragged = jnp.concatenate([lengths[:, None], offsets], axis=1)
    other = flip(ragged, 1)
    ragged = take(jnp.where(z // 2 == c, ragged, other), z % 2, 0)
    length, starts = ragged[0], ragged[1:]
    places = jnp.arange(seq, dtype=jnp.int32)
    live = places < length
    groups = jnp.sum((places[:, None] >= starts[None, :]).astype(jnp.int32), axis=1)
    bias = jnp.where(live[None, :], group_bias * (groups[:, None] == groups[None, :]).astype(f32), -jnp.inf)

    states = xf.astype(f32)
    normed_full, norm_back = jax.vjp(layer_norm, states, gain_one, shift_one)
    normed = normed_full.astype(bf)
    qkv = product(normed, wa[:, : 3 * half])
    queries = (qkv[:, :half] + bias_q).astype(bf)
    key_rows = qkv[:, half : 2 * half].astype(bf)
    vals = (qkv[:, 2 * half :] + bias_v).astype(bf)
    qh = queries.reshape(seq, heads, HEAD_DIM)
    kh = key_rows.reshape(seq, heads, HEAD_DIM)
    vh = vals.reshape(seq, heads, HEAD_DIM)

    def scores_of():
        raw = jnp.einsum("qhd,khd->hqk", qh, kh, preferred_element_type=f32) * inv_root
        return raw + bias[None]

    masked = scores_of()
    row_max = jnp.max(masked, axis=-1, keepdims=True)
    exp_scores = jnp.exp(masked - row_max)
    exp_total = jnp.sum(exp_scores, axis=-1, keepdims=True)
    log_total = row_max + jnp.log(exp_total)
    probs = (exp_scores / exp_total).astype(bf)
    mixed = jnp.einsum("hqk,khd->qhd", probs, vh, preferred_element_type=f32).astype(bf).reshape(seq, half)
    part = product(mixed, wob).astype(bf)
    attended = part.astype(f32) + flip(part, 1).astype(f32) + bias_o
    middle = states + attended
    second_full, second_back = jax.vjp(layer_norm, middle, gain_two, shift_two)
    second = second_full.astype(bf)
    inner = product(second, wb) + bias_in
    active_full, gelu_back = jax.vjp(gelu_exact, inner)
    active = active_full.astype(bf)
    upstream = jnp.where(live[:, None], cf, jnp.zeros((), bf))
    out_part = product(active, wc)
    mine = lax.dynamic_slice_in_dim(out_part, c * half_seq, half_seq, 0)
    theirs = lax.dynamic_slice_in_dim(out_part, (1 - c) * half_seq, half_seq, 0).astype(bf)
    result = (
        lax.dynamic_slice_in_dim(middle, c * half_seq, half_seq, 0) + mine + flip(theirs, 1).astype(f32) + bias_out
    )
    live_half = lax.dynamic_slice_in_dim(live, c * half_seq, half_seq, 0)
    block_out = send_home(jnp.where(live_half[:, None], result, 0.0).astype(bf), c, z)

    outer_grad = left_product(active, upstream).astype(bf)
    outer_sum = reduce_group(outer_grad.reshape(LINE, PLANE, hid // 2 // PLANE, feat), px, py)
    (grad_inner_full,) = gelu_back(right_back(upstream, wc))
    grad_inner = grad_inner_full.astype(bf)
    inner_grad = left_product(second, grad_inner).astype(bf)
    inner_sum = reduce_group(inner_grad.reshape(LINE, PLANE, rows // PLANE, 2 * hid), px, py)
    second_part = right_back(grad_inner, wb).astype(bf)
    grad_second = second_part.astype(f32) + flip(second_part, 1).astype(f32)
    grad_norm, gain_two_grad, shift_two_grad = second_back(grad_second)
    grad_middle = upstream.astype(f32) + grad_norm
    grad_attended = grad_middle.astype(bf)
    out_grad = left_product(mixed, grad_attended).astype(bf)
    grad_mixed = right_back(grad_attended, wob).astype(bf)
    gh = grad_mixed.reshape(seq, heads, HEAD_DIM)
    again = jnp.exp(scores_of() - log_total)
    grad_probs = jnp.einsum("qhd,khd->hqk", gh, vh, preferred_element_type=f32)
    row_dot = jnp.sum(again * grad_probs, axis=-1, keepdims=True)
    grad_raw = (again * (grad_probs - row_dot)).astype(bf)
    dv = jnp.einsum("hqk,qhd->khd", again.astype(bf), gh, preferred_element_type=f32).astype(bf).reshape(seq, half)
    dk = (jnp.einsum("hqk,qhd->khd", grad_raw, qh, preferred_element_type=f32) * inv_root).astype(bf).reshape(seq, half)
    dq = (jnp.einsum("hqk,khd->qhd", grad_raw, kh, preferred_element_type=f32) * inv_root).astype(bf).reshape(seq, half)
    dqkv = jnp.concatenate([dq, dk, dv], axis=1)
    qkv_grad = left_product(normed, dqkv).astype(bf)
    keep = lax.dynamic_slice_in_dim(out_grad, c * half, half, 1)
    swap = flip(lax.dynamic_slice_in_dim(out_grad, (1 - c) * half, half, 1), 1)
    out_cols = jnp.where(c == 0, jnp.concatenate([keep, swap], 0), jnp.concatenate([swap, keep], 0))
    attn_grad = jnp.concatenate([qkv_grad, out_cols], axis=1)
    attn_sum = reduce_group(attn_grad.reshape(LINE, PLANE, rows // PLANE, 2 * feat), px, py)
    normed_part = right_back(dqkv, wa[:, : 3 * half])
    mine = lax.dynamic_slice_in_dim(normed_part, c * half_seq, half_seq, 0)
    theirs = lax.dynamic_slice_in_dim(normed_part, (1 - c) * half_seq, half_seq, 0).astype(bf)
    grad_normed = mine + flip(theirs, 1).astype(f32)
    states_half = lax.dynamic_slice_in_dim(states, c * half_seq, half_seq, 0)
    _, half_back = jax.vjp(layer_norm, states_half, gain_one, shift_one)
    grad_states, gain_one_grad, shift_one_grad = half_back(grad_normed)
    grad_mid_half = lax.dynamic_slice_in_dim(grad_middle, c * half_seq, half_seq, 0)
    input_grad = send_home((grad_mid_half + grad_states).astype(bf), c, z)

    def once(v):
        return jnp.where(c == 0, v, 0.0)

    def placed(v):
        return lax.dynamic_update_slice_in_dim(jnp.zeros((feat,), f32), v, c * half, 0)

    in_bias = jnp.zeros((LINE, 2, hid // 2), f32)
    in_bias = lax.dynamic_update_slice(in_bias, column_sum(grad_inner).reshape(LINE, 1, hid // 2), (0, c, 0))
    packed = jnp.concatenate(
        [
            gain_one_grad, shift_one_grad, placed(column_sum(dq)), placed(column_sum(dv)),
            once(column_sum(grad_attended)), once(gain_two_grad), once(shift_two_grad), once(column_sum(upstream)),
            in_bias.reshape(LINE * hid),
        ]
    ).reshape(12, feat)
    packed = lax.psum(packed, ("cells", "chrom"))

    def shard(v):
        return lax.dynamic_slice_in_dim(v, z * (v.shape[0] // LINE), v.shape[0] // LINE, 0)

    s = [shard(packed[n]) for n in range(8)]
    inner_bias_grad = shard(packed[8:].reshape(LINE * hid))
    w2_grad = outer_sum.transpose(1, 0, 2, 3).reshape(hid, feat).astype(f32)
    w1_grad = inner_sum.reshape(PLANE, 2, rows // PLANE, LINE, hid // 2).transpose(0, 2, 3, 1, 4)
    w1_grad = w1_grad.reshape(rows, LINE * hid).astype(f32)
    wx = attn_sum.reshape(PLANE, 2, rows // PLANE, 4, half).transpose(3, 0, 2, 1, 4).reshape(4, rows, feat)
    wx = [wx[n].astype(f32) for n in range(4)]
    return (
        block_out, input_grad, s[0], s[1], wx[0], s[2], wx[1], wx[2], s[3], wx[3], s[4], s[5], s[6],
        w1_grad, inner_bias_grad, w2_grad, s[7],
    )


def solution(mesh):
    paired = mesh.shape["chrom"] == 4 and mesh.shape["cells"] == 8
    placed = (
        P("cells", "chrom", None),
        P("cells"),
        P("cells", None),
        P("cells", "chrom", None),
        P("chrom"),
        P("chrom"),
        P("chrom", None),
        P("chrom"),
        P("chrom", None),
        P("chrom", None),
        P("chrom"),
        P("chrom", None),
        P("chrom"),
        P("chrom"),
        P("chrom"),
        P("chrom", None),
        P("chrom"),
        P("chrom", None),
        P("chrom"),
    )
    return jax.shard_map(
        paired_local if paired else general,
        mesh=mesh,
        in_specs=placed,
        out_specs=(
            P("cells", "chrom", None),
            P("cells", "chrom", None),
            P("chrom"),
            P("chrom"),
            P("chrom", None),
            P("chrom"),
            P("chrom", None),
            P("chrom", None),
            P("chrom"),
            P("chrom", None),
            P("chrom"),
            P("chrom"),
            P("chrom"),
            P("chrom", None),
            P("chrom"),
            P("chrom", None),
            P("chrom"),
        ),
        check_vma=False,
    )
```

```python
import functools

import jax
import jax.numpy as jnp
from jax import lax
from jax.experimental import pallas as pl
from jax.experimental.pallas import tpu as pltpu
from jax.sharding import PartitionSpec as P

HEADS = 20
HEAD_DIM = 64


eps_norm = 1e-05
group_bias = 1.0


def layer_norm(values, gain, shift):
    center = values - jnp.mean(values, axis=-1, keepdims=True)
    spread = jnp.mean(center * center, axis=-1, keepdims=True)
    return center * lax.rsqrt(spread + eps_norm) * gain + shift


def gelu_exact(values):
    return jax.nn.gelu(values, approximate=False)


def product(left, right):
    return jnp.dot(left, right, preferred_element_type=jnp.float32)


def left_product(left, right):
    return jnp.einsum("ra,rb->ab", left, right, preferred_element_type=jnp.float32)


def right_back(left, right):
    return jnp.einsum("rb,ab->ra", left, right, preferred_element_type=jnp.float32)


def column_sum(values):
    return jnp.sum(values, axis=0, dtype=jnp.float32)


def split_rows(value, outer, inner_count):
    return value.reshape(
        (outer, inner_count, value.shape[0] // (outer * inner_count)) + value.shape[1:]
    )


def general(
    inputs,
    lengths,
    offsets,
    cotangent,
    norm_gain,
    norm_shift,
    query_proj,
    query_bias,
    key_proj,
    value_proj,
    value_bias,
    output_proj,
    output_bias,
    second_gain,
    second_shift,
    inner_proj,
    inner_bias,
    outer_proj,
    outer_bias,
):
    count_chrom = lax.axis_size("chrom")
    count_cells = lax.axis_size("cells")
    block_index = lax.axis_index("chrom")
    cells_here, tokens_here, feat_width = inputs.shape
    seq_len = tokens_here * count_chrom
    row_count = cells_here * tokens_here
    inv_root = HEAD_DIM ** (-0.5)
    places = jnp.arange(seq_len, dtype=jnp.int32)
    key_live = places[None, :] < lengths[:, None]
    groups = jnp.sum((places[None, :, None] >= offsets[:, None, :]).astype(jnp.int32), axis=2)
    query_groups = lax.dynamic_slice_in_dim(groups, block_index * tokens_here, tokens_here, 1)
    query_live = lax.dynamic_slice_in_dim(key_live, block_index * tokens_here, tokens_here, 1)
    same_group = (query_groups[:, :, None] == groups[:, None, :]).astype(jnp.float32)
    mask_bias = jnp.where(key_live[:, None, :], group_bias * same_group, -jnp.inf)[:, None]
    gathered = (
        lax.all_gather(norm_gain, "chrom", axis=0, tiled=True),
        lax.all_gather(norm_shift, "chrom", axis=0, tiled=True),
        lax.all_gather(query_proj, "chrom", axis=0, tiled=True),
        lax.all_gather(query_bias, "chrom", axis=0, tiled=True),
        lax.all_gather(key_proj, "chrom", axis=0, tiled=True),
        lax.all_gather(value_proj, "chrom", axis=0, tiled=True),
        lax.all_gather(value_bias, "chrom", axis=0, tiled=True),
        lax.all_gather(output_proj, "chrom", axis=0, tiled=True),
        lax.all_gather(output_bias, "chrom", axis=0, tiled=True),
        lax.all_gather(second_gain, "chrom", axis=0, tiled=True),
        lax.all_gather(second_shift, "chrom", axis=0, tiled=True),
        lax.all_gather(inner_proj, "chrom", axis=0, tiled=True),
        lax.all_gather(inner_bias, "chrom", axis=0, tiled=True),
        lax.all_gather(outer_proj, "chrom", axis=0, tiled=True),
        lax.all_gather(outer_bias, "chrom", axis=0, tiled=True),
    )
    gain_one = gathered[0].astype(jnp.float32)
    shift_one = gathered[1].astype(jnp.float32)
    gain_two = gathered[9].astype(jnp.float32)
    shift_two = gathered[10].astype(jnp.float32)
    states = inputs.astype(jnp.float32).reshape(row_count, feat_width)
    normed_full, norm_back = jax.vjp(layer_norm, states, gain_one, shift_one)
    normed = normed_full.astype(jnp.bfloat16)
    queries = (product(normed, gathered[2]) + gathered[3].astype(jnp.float32)).astype(jnp.bfloat16)
    key_rows = product(normed, gathered[4]).astype(jnp.bfloat16)
    vals = (product(normed, gathered[5]) + gathered[6].astype(jnp.float32)).astype(jnp.bfloat16)
    keys_all, vals_all = (
        lax.all_gather(
            key_rows.reshape(cells_here, tokens_here, feat_width), "chrom", axis=1, tiled=True
        ),
        lax.all_gather(
            vals.reshape(cells_here, tokens_here, feat_width), "chrom", axis=1, tiled=True
        ),
    )
    query_heads = queries.reshape(cells_here, tokens_here, HEADS, HEAD_DIM)
    key_heads = keys_all.reshape(cells_here, seq_len, HEADS, HEAD_DIM)
    val_heads = vals_all.reshape(cells_here, seq_len, HEADS, HEAD_DIM)

    def scores_of():
        raw = (
            jnp.einsum(
                "cqhd,ckhd->chqk", query_heads, key_heads, preferred_element_type=jnp.float32
            )
            * inv_root
        )
        return raw + mask_bias

    masked = scores_of()
    row_max = jnp.max(masked, axis=-1, keepdims=True)
    exp_scores = jnp.exp(masked - row_max)
    exp_total = jnp.sum(exp_scores, axis=-1, keepdims=True)
    attn_probs = exp_scores / exp_total
    log_total = row_max + jnp.log(exp_total)
    mixed_out = jnp.einsum(
        "chqk,ckhd->cqhd",
        attn_probs.astype(jnp.bfloat16),
        val_heads,
        preferred_element_type=jnp.float32,
    )
    mixed_out = mixed_out.astype(jnp.bfloat16).reshape(row_count, feat_width)
    attended = product(mixed_out, gathered[7]) + gathered[8].astype(jnp.float32)
    middle = states + attended
    second_full, second_back = jax.vjp(layer_norm, middle, gain_two, shift_two)
    second = second_full.astype(jnp.bfloat16)
    inner_pre = product(second, gathered[11]) + gathered[12].astype(jnp.float32)
    active_full, gelu_back = jax.vjp(gelu_exact, inner_pre)
    active = active_full.astype(jnp.bfloat16)
    result = middle + product(active, gathered[13]) + gathered[14].astype(jnp.float32)
    live_rows = query_live.reshape(row_count, 1)
    block_out = (
        jnp.where(live_rows, result, 0.0)
        .astype(jnp.bfloat16)
        .reshape(cells_here, tokens_here, feat_width)
    )
    upstream = jnp.where(
        live_rows, cotangent.reshape(row_count, feat_width), jnp.zeros((), jnp.bfloat16)
    )
    outer_bias_grad = column_sum(upstream)
    outer_proj_grad = left_product(active, upstream)
    grad_active = right_back(upstream, gathered[13])
    (grad_inner_full,) = gelu_back(grad_active)
    grad_inner = grad_inner_full.astype(jnp.bfloat16)
    inner_bias_grad = column_sum(grad_inner)
    inner_proj_grad = left_product(second, grad_inner)
    grad_second = right_back(grad_inner, gathered[11])
    grad_middle_norm, second_gain_grad, second_shift_grad = second_back(grad_second)
    grad_middle = upstream.astype(jnp.float32) + grad_middle_norm
    grad_attended = grad_middle.astype(jnp.bfloat16)
    output_bias_grad = column_sum(grad_attended)
    output_proj_grad = left_product(mixed_out, grad_attended)
    grad_mixed = right_back(grad_attended, gathered[7]).astype(jnp.bfloat16)
    grad_mixed = grad_mixed.reshape(cells_here, tokens_here, HEADS, HEAD_DIM)
    attn_again = jnp.exp(scores_of() - log_total)
    grad_probs = jnp.einsum(
        "cqhd,ckhd->chqk", grad_mixed, val_heads, preferred_element_type=jnp.float32
    )
    row_dot = jnp.sum(attn_again * grad_probs, axis=-1, keepdims=True)
    grad_raw = (attn_again * (grad_probs - row_dot)).astype(jnp.bfloat16)
    grad_vals_part = jnp.einsum(
        "chqk,cqhd->ckhd",
        attn_again.astype(jnp.bfloat16),
        grad_mixed,
        preferred_element_type=jnp.float32,
    )
    grad_keys_part = (
        jnp.einsum("chqk,cqhd->ckhd", grad_raw, query_heads, preferred_element_type=jnp.float32)
        * inv_root
    )
    grad_queries = (
        jnp.einsum("chqk,ckhd->cqhd", grad_raw, key_heads, preferred_element_type=jnp.float32)
        * inv_root
    ).astype(jnp.bfloat16)
    grad_queries = grad_queries.reshape(row_count, feat_width)
    grad_keys_sum, grad_vals_sum = (
        lax.psum_scatter(
            grad_keys_part.reshape(cells_here, seq_len, feat_width).astype(jnp.bfloat16),
            "chrom",
            scatter_dimension=1,
            tiled=True,
        ).astype(jnp.float32),
        lax.psum_scatter(
            grad_vals_part.reshape(cells_here, seq_len, feat_width).astype(jnp.bfloat16),
            "chrom",
            scatter_dimension=1,
            tiled=True,
        ).astype(jnp.float32),
    )
    grad_keys = grad_keys_sum.astype(jnp.bfloat16).reshape(row_count, feat_width)
    grad_vals = grad_vals_sum.astype(jnp.bfloat16).reshape(row_count, feat_width)
    query_proj_grad = left_product(normed, grad_queries)
    query_bias_grad = column_sum(grad_queries)
    key_proj_grad = left_product(normed, grad_keys)
    value_proj_grad = left_product(normed, grad_vals)
    value_bias_grad = column_sum(grad_vals)
    grad_normed = (
        right_back(grad_queries, gathered[2])
        + right_back(grad_keys, gathered[4])
        + right_back(grad_vals, gathered[5])
    )
    grad_states_norm, norm_gain_grad, norm_shift_grad = norm_back(grad_normed)
    input_grad = (
        (grad_middle + grad_states_norm)
        .astype(jnp.bfloat16)
        .reshape(cells_here, tokens_here, feat_width)
    )
    grad_list = (
        norm_gain_grad,
        norm_shift_grad,
        query_proj_grad,
        query_bias_grad,
        key_proj_grad,
        value_proj_grad,
        value_bias_grad,
        output_proj_grad,
        output_bias_grad,
        second_gain_grad,
        second_shift_grad,
        inner_proj_grad,
        inner_bias_grad,
        outer_proj_grad,
        outer_bias_grad,
    )
    pieces = tuple((split_rows(member, count_chrom, count_cells) for member in grad_list))
    section_one = (
        lax.psum_scatter(
            pieces[0].astype(jnp.bfloat16), "cells", scatter_dimension=1, tiled=True
        ).astype(jnp.float32),
        lax.psum_scatter(
            pieces[1].astype(jnp.bfloat16), "cells", scatter_dimension=1, tiled=True
        ).astype(jnp.float32),
        lax.psum_scatter(
            pieces[2].astype(jnp.bfloat16), "cells", scatter_dimension=1, tiled=True
        ).astype(jnp.float32),
        lax.psum_scatter(
            pieces[3].astype(jnp.bfloat16), "cells", scatter_dimension=1, tiled=True
        ).astype(jnp.float32),
        lax.psum_scatter(
            pieces[4].astype(jnp.bfloat16), "cells", scatter_dimension=1, tiled=True
        ).astype(jnp.float32),
        lax.psum_scatter(
            pieces[5].astype(jnp.bfloat16), "cells", scatter_dimension=1, tiled=True
        ).astype(jnp.float32),
        lax.psum_scatter(
            pieces[6].astype(jnp.bfloat16), "cells", scatter_dimension=1, tiled=True
        ).astype(jnp.float32),
        lax.psum_scatter(
            pieces[7].astype(jnp.bfloat16), "cells", scatter_dimension=1, tiled=True
        ).astype(jnp.float32),
        lax.psum_scatter(
            pieces[8].astype(jnp.bfloat16), "cells", scatter_dimension=1, tiled=True
        ).astype(jnp.float32),
        lax.psum_scatter(
            pieces[9].astype(jnp.bfloat16), "cells", scatter_dimension=1, tiled=True
        ).astype(jnp.float32),
        lax.psum_scatter(
            pieces[10].astype(jnp.bfloat16), "cells", scatter_dimension=1, tiled=True
        ).astype(jnp.float32),
        lax.psum_scatter(
            pieces[11].astype(jnp.bfloat16), "cells", scatter_dimension=1, tiled=True
        ).astype(jnp.float32),
        lax.psum_scatter(
            pieces[12].astype(jnp.bfloat16), "cells", scatter_dimension=1, tiled=True
        ).astype(jnp.float32),
        lax.psum_scatter(
            pieces[13].astype(jnp.bfloat16), "cells", scatter_dimension=1, tiled=True
        ).astype(jnp.float32),
        lax.psum_scatter(
            pieces[14].astype(jnp.bfloat16), "cells", scatter_dimension=1, tiled=True
        ).astype(jnp.float32),
    )
    section_two = (
        lax.psum_scatter(
            section_one[0].astype(jnp.bfloat16), "chrom", scatter_dimension=0, tiled=True
        ).astype(jnp.float32),
        lax.psum_scatter(
            section_one[1].astype(jnp.bfloat16), "chrom", scatter_dimension=0, tiled=True
        ).astype(jnp.float32),
        lax.psum_scatter(
            section_one[2].astype(jnp.bfloat16), "chrom", scatter_dimension=0, tiled=True
        ).astype(jnp.float32),
        lax.psum_scatter(
            section_one[3].astype(jnp.bfloat16), "chrom", scatter_dimension=0, tiled=True
        ).astype(jnp.float32),
        lax.psum_scatter(
            section_one[4].astype(jnp.bfloat16), "chrom", scatter_dimension=0, tiled=True
        ).astype(jnp.float32),
        lax.psum_scatter(
            section_one[5].astype(jnp.bfloat16), "chrom", scatter_dimension=0, tiled=True
        ).astype(jnp.float32),
        lax.psum_scatter(
            section_one[6].astype(jnp.bfloat16), "chrom", scatter_dimension=0, tiled=True
        ).astype(jnp.float32),
        lax.psum_scatter(
            section_one[7].astype(jnp.bfloat16), "chrom", scatter_dimension=0, tiled=True
        ).astype(jnp.float32),
        lax.psum_scatter(
            section_one[8].astype(jnp.bfloat16), "chrom", scatter_dimension=0, tiled=True
        ).astype(jnp.float32),
        lax.psum_scatter(
            section_one[9].astype(jnp.bfloat16), "chrom", scatter_dimension=0, tiled=True
        ).astype(jnp.float32),
        lax.psum_scatter(
            section_one[10].astype(jnp.bfloat16), "chrom", scatter_dimension=0, tiled=True
        ).astype(jnp.float32),
        lax.psum_scatter(
            section_one[11].astype(jnp.bfloat16), "chrom", scatter_dimension=0, tiled=True
        ).astype(jnp.float32),
        lax.psum_scatter(
            section_one[12].astype(jnp.bfloat16), "chrom", scatter_dimension=0, tiled=True
        ).astype(jnp.float32),
        lax.psum_scatter(
            section_one[13].astype(jnp.bfloat16), "chrom", scatter_dimension=0, tiled=True
        ).astype(jnp.float32),
        lax.psum_scatter(
            section_one[14].astype(jnp.bfloat16), "chrom", scatter_dimension=0, tiled=True
        ).astype(jnp.float32),
    )
    rejoined = (
        lax.all_gather(section_two[0].astype(jnp.bfloat16), "cells", axis=1, tiled=True).astype(
            jnp.float32
        ),
        lax.all_gather(section_two[1].astype(jnp.bfloat16), "cells", axis=1, tiled=True).astype(
            jnp.float32
        ),
        lax.all_gather(section_two[2].astype(jnp.bfloat16), "cells", axis=1, tiled=True).astype(
            jnp.float32
        ),
        lax.all_gather(section_two[3].astype(jnp.bfloat16), "cells", axis=1, tiled=True).astype(
            jnp.float32
        ),
        lax.all_gather(section_two[4].astype(jnp.bfloat16), "cells", axis=1, tiled=True).astype(
            jnp.float32
        ),
        lax.all_gather(section_two[5].astype(jnp.bfloat16), "cells", axis=1, tiled=True).astype(
            jnp.float32
        ),
        lax.all_gather(section_two[6].astype(jnp.bfloat16), "cells", axis=1, tiled=True).astype(
            jnp.float32
        ),
        lax.all_gather(section_two[7].astype(jnp.bfloat16), "cells", axis=1, tiled=True).astype(
            jnp.float32
        ),
        lax.all_gather(section_two[8].astype(jnp.bfloat16), "cells", axis=1, tiled=True).astype(
            jnp.float32
        ),
        lax.all_gather(section_two[9].astype(jnp.bfloat16), "cells", axis=1, tiled=True).astype(
            jnp.float32
        ),
        lax.all_gather(section_two[10].astype(jnp.bfloat16), "cells", axis=1, tiled=True).astype(
            jnp.float32
        ),
        lax.all_gather(section_two[11].astype(jnp.bfloat16), "cells", axis=1, tiled=True).astype(
            jnp.float32
        ),
        lax.all_gather(section_two[12].astype(jnp.bfloat16), "cells", axis=1, tiled=True).astype(
            jnp.float32
        ),
        lax.all_gather(section_two[13].astype(jnp.bfloat16), "cells", axis=1, tiled=True).astype(
            jnp.float32
        ),
        lax.all_gather(section_two[14].astype(jnp.bfloat16), "cells", axis=1, tiled=True).astype(
            jnp.float32
        ),
    )
    final = tuple(
        (
            member.reshape(
                (member.shape[0] * member.shape[1] * member.shape[2],) + member.shape[3:]
            )
            for member in rejoined
        )
    )
    return (block_out, input_grad) + tuple(final)


PLANE = 4
LINE = 4


def rows_of(start, count):
    return pl.ds(pl.multiple_of(start, 16), count)


def cols_of(start, count):
    return pl.ds(pl.multiple_of(start, 128), count)


VECTORS = 8
TILE = 256


def nt(left, right):
    return lax.dot_general(left, right, (((1,), (1,)), ((), ())), preferred_element_type=jnp.float32)


def nn(left, right):
    return jnp.dot(left, right, preferred_element_type=jnp.float32)


def moments(values):
    center = values - jnp.mean(values, axis=-1, keepdims=True)
    spread = jnp.mean(center * center, axis=-1, keepdims=True)
    return center, lax.rsqrt(spread + eps_norm)


def gelu_and_slope(u):
    gauss = jnp.exp(u * u * -0.5)
    t = 1.0 / (1.0 + jnp.abs(u) * (0.3275911 * 0.5 ** 0.5))
    poly = 0.5 * 1.061405429
    for factor in (-1.453152027, 1.421413741, -0.284496736, 0.254829592):
        poly = poly * t + 0.5 * factor
    tail = poly * t * gauss
    phi_sum = jnp.where(u < 0.0, tail, 1.0 - tail)
    return u * phi_sum, phi_sum + u * gauss * 0.3989422804014327


def forward_kernel(
    small_ref, x_ref, ct_ref, wq_ref, wk_ref, wv_ref, wo_ref, w1_ref, w2_ref, gq_ref, gk_ref,
    vec_o, x_o, ct_o, wa_o, wob_o, wb_o, wc, normed_o, qkv_o, mixed_o, lse_o, middle_o, second_o, active_o, slope_o,
    smalls, vec, bias_in, xf, cf, wa, wol, wob, wb, normed, qkv, gq, gk, kx, mixed, lse, part, part_in, middle, second,
    act, slp,
    sm_s, sm_r, ex_s, ex_r, fw_s, fw_r, ln_s, un_s, un_r, loc, wo_s, wo_r, pa_s, pa_r, out_s, act_s,
):
    f32, bf = jnp.float32, jnp.bfloat16
    i, z = lax.axis_index("cells"), lax.axis_index("chrom")
    p, c = i // 2, lax.rem(i, 2)
    px, py = lax.rem(p, 2), p // 2
    x_nb, y_nb, core_nb = i + 2 - 4 * px, i + 4 - 8 * py, i + 1 - 2 * c
    p_x, p_y = p + 1 - 2 * px, p + 2 - 4 * py
    rows = wq_ref.shape[0]
    feat = wq_ref.shape[1]
    half = feat // 2
    hid = w2_ref.shape[0]
    block = x_ref.shape[1]
    seq = block * LINE
    part_rows, hid_part = rows // PLANE, hid // 2 // PLANE

    barrier = pltpu.get_barrier_semaphore()
    line_ids = [
        (i - c + lax.rem(c + dc, 2), lax.rem(z + dz, LINE))
        for dc in range(2)
        for dz in range(LINE)
        if dc or dz
    ]
    for who in line_ids + [(x_nb, z), (y_nb, z)]:
        pl.semaphore_signal(barrier, inc=1, device_id=who, device_id_type=pl.DeviceIdType.MESH)
    pl.semaphore_wait(barrier, len(line_ids) + 2)

    def send(src, dst, s, r, who):
        return pltpu.make_async_remote_copy(
            src_ref=src, dst_ref=dst, send_sem=s, recv_sem=r, device_id=who,
            device_id_type=pl.DeviceIdType.MESH,
        )

    small_own = pltpu.make_async_copy(small_ref, smalls.at[z], loc.at[0])
    small_out = [
        send(small_ref, smalls.at[z], sm_s.at[d], sm_r.at[d], (i, lax.rem(z + d + 1, LINE)))
        for d in range(LINE - 1)
    ]

    def exchange(src, dst, which):
        stay = c == z // 2
        mine, outs = None, []
        for k in range(2):
            j = lax.rem(z + k, 2)
            to = dst.at[rows_of(z * block, block), :]
            r = ex_r.at[2 * which + k]
            outs.append(send(src.at[j], to, ex_s.at[2 * which + k], r, (i - c + z // 2, 2 * c + j)))
            if k == 0:
                mine = pltpu.make_async_copy(src.at[j], to, r)

        def start():
            pl.when(stay)(mine.start)
            pl.when(jnp.logical_not(stay))(outs[0].start)
            outs[1].start()

        def arrived():
            pl.when(stay)(mine.wait)
            pl.when(jnp.logical_not(stay))(outs[0].wait_recv)
            outs[1].wait_recv()

        def sent():
            pl.when(jnp.logical_not(stay))(outs[0].wait_send)
            outs[1].wait_send()

        return start, arrived, sent

    def forward(dst, which):
        return [
            send(
                dst.at[rows_of((2 * c + b) * block, block), :],
                dst.at[rows_of((2 * c + b) * block, block), :],
                fw_s.at[2 * which + b], fw_r.at[2 * which + b], (core_nb, z),
            )
            for b in range(2)
        ]

    x_start, x_arrived, x_sent = exchange(x_ref, xf, 0)
    c_start, c_arrived, c_sent = exchange(ct_ref, cf, 1)
    x_fw, c_fw = forward(xf, 0), forward(cf, 1)

    lands = (wa, wol, wb, wc)
    groups = range(4)
    partner, inner = z + 1 - 2 * lax.rem(z, 2), 3 - z
    low = z < 2
    middle_chip = jnp.logical_or(z == 1, z == 2)
    slot_shard = (partner, jnp.where(low, 2, 1), jnp.where(low, 3, 0))

    def own_parts(g, row, count):
        if g == 0:
            return [
                (ref.at[rows_of(row, count), cols_of(c * half, half)], pl.ds(n * half, half))
                for n, ref in enumerate((wq_ref, wk_ref, wv_ref))
            ]
        if g == 1:
            return [(wo_ref.at[rows_of(row, count), cols_of(c * half, half)], pl.ds(0, half))]
        if g == 2:
            return [
                (w1_ref.at[rows_of(row, count), cols_of(n * hid + c * (hid // 2), hid // 2)], pl.ds(n * (hid // 2), hid // 2))
                for n in range(LINE)
            ]
        return [(w2_ref.at[rows_of(c * (hid // 2) + row, count), :], pl.ds(0, feat))]

    def shape_of(g):
        return (rows, part_rows) if g < 3 else (hid // 2, hid_part)

    def piece(g, s, at):
        shard, count = shape_of(g)
        return lands[g].at[rows_of(s * shard + at * count, count), :]

    def half_piece(g, s, at, side):
        shard, count = shape_of(g)
        width = lands[g].shape[1]
        cut = width // 256 * 128
        cols = pl.ds(cut, width - cut) if side else pl.ds(0, cut)
        return lands[g].at[rows_of(s * shard + at * count, count), cols]

    def line_send(g, s, slot, e, to):
        return send(piece(g, s, p), piece(g, s, p), ln_s.at[g, e], un_r.at[3 * g + slot, 0], (i, to))

    def first(g):
        shard, count = shape_of(g)
        for src, cols in own_parts(g, p * count, count):
            dst = lands[g].at[rows_of(z * shard + p * count, count), cols]
            send(src, dst, ln_s.at[g, 0], un_r.at[3 * g, 0], (i, partner)).start()

        @pl.when(middle_chip)
        def _():
            for src, cols in own_parts(g, p * count, count):
                dst = lands[g].at[rows_of(z * shard + p * count, count), cols]
                send(src, dst, ln_s.at[g, 1], un_r.at[3 * g + 1, 0], (i, inner)).start()

    def passing(g, slot):
        if slot == 0:
            return line_send(g, slot_shard[0], 2, 2, inner)
        return line_send(g, slot_shard[slot], slot, 2 + slot, partner)

    def spread(g, slot):
        own = piece(g, slot_shard[slot], p)
        u = 3 * g + slot
        return [
            send(own, own, un_s.at[u, 0], un_r.at[u, 1], (x_nb, z)),
            send(own, own, un_s.at[u, 1], un_r.at[u, 2], (y_nb, z)),
        ]

    def cross(g, slot):
        u = 3 * g + slot
        left = half_piece(g, slot_shard[slot], p_x, 0)
        rest = half_piece(g, slot_shard[slot], p_y, 1)
        return [
            send(left, left, un_s.at[u, 2], un_r.at[u, 3], (y_nb, z)),
            send(rest, rest, un_s.at[u, 3], un_r.at[u, 4], (x_nb, z)),
        ]

    def land(g, slot):
        line_send(g, slot_shard[slot], slot, 0, partner).wait_recv()
        pl.when(middle_chip)(passing(g, slot).start)
        for d in spread(g, slot):
            d.start()

    def turn(g, slot):
        for d in spread(g, slot):
            d.wait_recv()
        for d in cross(g, slot):
            d.start()

    def own_start(g):
        shard, _ = shape_of(g)
        for src, cols in own_parts(g, 0, shard):
            to = second.at[pl.ds(0, shard), :] if g == 3 else lands[g].at[rows_of(z * shard, shard), cols]
            pltpu.make_async_copy(src, to, loc.at[1 + g]).start()

    def own_wait(g):
        shard, _ = shape_of(g)
        ref = second.at[pl.ds(0, shard), :] if g == 3 else lands[g].at[rows_of(z * shard, shard), :]
        pltpu.make_async_copy(ref, ref, loc.at[1 + g]).wait()

    def whole(g):
        for slot in range(3):
            for d in cross(g, slot):
                d.wait_recv()
        if g < 3:
            own_wait(g)

    def all_sent(g):
        line_send(g, z, 0, 0, partner).wait_send()

        @pl.when(middle_chip)
        def _():
            line_send(g, z, 1, 1, inner).wait_send()
            for slot in range(3):
                passing(g, slot).wait_send()

        for slot in range(3):
            for d in spread(g, slot) + cross(g, slot):
                d.wait_send()

    outs = []

    def keep(src, dst):
        d = pltpu.make_async_copy(src, dst, out_s.at[len(outs)])
        d.start()
        outs.append(d)

    small_own.start()
    for d in small_out:
        d.start()
    first(0)
    x_start()
    for g in groups:
        own_start(g)
    gq_in = pltpu.make_async_copy(gq_ref, gq, loc.at[6])
    gk_in = pltpu.make_async_copy(gk_ref, gk, loc.at[7])
    gq_in.start()
    gk_in.start()
    first(1)
    land(0, 0)

    small_own.wait()
    for d in small_out:
        d.wait()
    width = smalls.shape[2]
    total = jnp.zeros((smalls.shape[1], feat), f32)
    at = lax.broadcasted_iota(jnp.int32, (width, feat), 0)
    to = lax.broadcasted_iota(jnp.int32, (width, feat), 1)
    for s in range(LINE):
        place = jnp.where(jnp.logical_and(at < rows, to == at + s * rows), 1.0, 0.0).astype(bf)
        total += nn(smalls[s], place)
    vec[...] = total
    at = lax.broadcasted_iota(jnp.int32, (width, hid // 2), 0)
    to = lax.broadcasted_iota(jnp.int32, (width, hid // 2), 1)
    which = lax.broadcasted_iota(jnp.int32, (smalls.shape[1], hid // 2), 0)
    for s in range(LINE):
        line_bias = jnp.zeros((1, hid // 2), f32)
        for n in range(hid // 2 // rows):
            place = jnp.where(jnp.logical_and(at < rows, to == at + n * rows), 1.0, 0.0).astype(bf)
            picked = jnp.where(which == VECTORS + c * (hid // 2 // rows) + n, nn(smalls[s], place), 0.0)
            line_bias += jnp.sum(picked, axis=0, keepdims=True)
        bias_in[:, pl.ds(s * (hid // 2), hid // 2)] = line_bias
    keep(vec, vec_o)

    land(0, 1)
    first(2)
    turn(0, 0)
    x_arrived()
    for d in x_fw:
        d.start()
    land(0, 2)
    turn(0, 1)

    def norm_rows(n, _):
        at = pl.ds(pl.multiple_of(n * 64, 64), 64)
        center, r = moments(xf[at, :].astype(f32))
        normed[at, :] = (center * r * vec[0:1, :] + vec[1:2, :]).astype(bf)
        return _

    def norm_half(h):
        steps = seq // 2 // 64
        lax.fori_loop(h * steps, (h + 1) * steps, norm_rows, 0)

    norm_half(c)
    for d in x_fw:
        d.wait_recv()
    norm_half(1 - c)
    keep(normed, normed_o)
    keep(xf, x_o)
    gq_in.wait()
    gk_in.wait()
    kx[:, 128:] = gk[...]
    land(1, 0)
    land(1, 1)
    turn(0, 2)
    land(1, 2)
    land(2, 0)
    for slot in range(3):
        turn(1, slot)
    whole(0)
    keep(wa, wa_o)

    bias_row = jnp.concatenate(
        [vec[2:3, cols_of(c * half, half)], jnp.zeros((1, half), f32), vec[3:4, cols_of(c * half, half)]], axis=1
    )

    def qkv_cols(start, width):
        got = nn(normed[...], wa[:, pl.ds(start, width)])
        qkv[:, pl.ds(start, width)] = (got + bias_row[:, start : start + width]).astype(bf)

    total_cols = 3 * half
    for n in range(total_cols // TILE):
        qkv_cols(n * TILE, TILE)
        if n == 3:
            land(2, 1)
            first(3)
    if total_cols % TILE:
        qkv_cols(total_cols // TILE * TILE, total_cols % TILE)
    turn(2, 0)
    keep(qkv, qkv_o)

    lane = lax.broadcasted_iota(jnp.int32, (TILE, 128), 1)

    def attend(t):
        k2 = qkv[:, pl.ds(half + t * 128, 128)]
        v2t = jnp.transpose(qkv[:, pl.ds(2 * half + t * 128, 128)])
        kx[:, :128] = k2

        def chunk(n, _):
            at = pl.ds(pl.multiple_of(n * TILE, TILE), TILE)
            q2 = qkv[at, pl.ds(t * 128, 128)] * jnp.array(HEAD_DIM ** (-0.5), bf)
            both = []
            for h in range(2):
                own = lane < HEAD_DIM if h == 0 else lane >= HEAD_DIM
                qx = jnp.concatenate([jnp.where(own, q2, jnp.zeros((), bf)), gq[at, :]], axis=1)
                s = nt(kx[...], qx)
                top = jnp.max(s, axis=0, keepdims=True)
                e = jnp.exp(s - top)
                total = jnp.sum(e, axis=0, keepdims=True)
                o = nn(v2t[h * HEAD_DIM : (h + 1) * HEAD_DIM, :], e.astype(bf))
                both.append(o / total)
                lse[2 * t + h : 2 * t + h + 1, at] = top + jnp.log(total)
            mixed[at, pl.ds(t * 128, 128)] = jnp.transpose(jnp.concatenate(both, axis=0)).astype(bf)
            return _

        lax.fori_loop(0, seq // TILE, chunk, 0)

    attend(0)
    land(2, 2)
    turn(2, 1)
    attend(1)
    whole(1)
    wo_own = pltpu.make_async_copy(
        wol.at[rows_of(c * half, half), :], wob.at[:, cols_of(c * half, half)], loc.at[5]
    )
    wo_out = send(
        wol.at[rows_of((1 - c) * half, half), :],
        wob.at[:, cols_of(c * half, half)], wo_s.at[0], wo_r.at[0], (core_nb, z),
    )
    wo_own.start()
    wo_out.start()
    attend(2)
    land(3, 0)
    turn(2, 2)
    attend(3)
    land(3, 1)
    attend(4)
    turn(3, 0)
    keep(mixed, mixed_o)
    keep(lse, lse_o)
    wo_own.wait()
    wo_out.wait()
    keep(wob, wob_o)

    chunks = seq // TILE
    swaps = []
    for n in range(chunks):
        at = pl.ds(n * TILE, TILE)
        part[at, :] = nn(mixed[at, :], wob[...]).astype(bf)
        d = send(part.at[at, :], part_in.at[at, :], pa_s.at[n], pa_r.at[n], (core_nb, z))
        d.start()
        swaps.append(d)
    land(3, 2)
    c_start()
    own_wait(3)
    out_own = pltpu.make_async_copy(
        second.at[pl.ds(0, hid // 2), :], wc.at[rows_of(z * (hid // 2), hid // 2), :], loc.at[4]
    )
    out_own.start()
    out_own.wait()

    def second_rows(n, _):
        at = pl.ds(pl.multiple_of(n * 64, 64), 64)
        sums = xf[at, :].astype(f32) + (part[at, :].astype(f32) + part_in[at, :].astype(f32) + vec[4:5, :])
        middle[at, :] = sums
        center, r = moments(sums)
        second[at, :] = (center * r * vec[5:6, :] + vec[6:7, :]).astype(bf)
        return _

    for n in range(chunks):
        swaps[n].wait_recv()
        lax.fori_loop(n * TILE // 64, (n + 1) * TILE // 64, second_rows, 0)
    keep(middle, middle_o)
    keep(second, second_o)
    turn(3, 1)
    whole(2)
    keep(wb, wb_o)

    tiles = 2 * hid // TILE

    def tile_out(n, slot):
        cols = pl.ds(n * TILE, TILE)
        return [
            pltpu.make_async_copy(act.at[slot], active_o.at[:, cols], act_s.at[slot, 0]),
            pltpu.make_async_copy(slp.at[slot], slope_o.at[:, cols], act_s.at[slot, 1]),
        ]

    for n in range(tiles):
        slot = n % 2
        cols = pl.ds(n * TILE, TILE)
        if n >= 2:
            for d in tile_out(n - 2, slot):
                d.wait()

        def tile_rows(m, _, cols=cols, slot=slot):
            at = pl.ds(pl.multiple_of(m * TILE, TILE), TILE)
            u = nn(second[at, :], wb[:, cols]) + bias_in[:, cols]
            value, slope = gelu_and_slope(u)
            act[slot, at, :] = value.astype(bf)
            slp[slot, at, :] = slope.astype(bf)
            return _

        lax.fori_loop(0, chunks, tile_rows, 0)
        for d in tile_out(n, slot):
            d.start()
        if n == 3:
            turn(3, 2)
    c_arrived()
    for d in c_fw:
        d.start()
    for n in (tiles - 2, tiles - 1):
        for d in tile_out(n, n % 2):
            d.wait()
    whole(3)
    for d in c_fw:
        d.wait()
    keep(cf, ct_o)
    for d in x_fw + swaps:
        d.wait_send()
    x_sent()
    c_sent()
    for g in groups:
        all_sent(g)
    for d in outs:
        d.wait()


def run_forward(small, x, ct, wq, wk, wv, wo, w1, w2, gq, gk):
    rows, feat = wq.shape
    hid = w2.shape[0]
    seq = x.shape[1] * LINE
    half = feat // 2
    heads = half // HEAD_DIM
    f32, bf = jnp.float32, jnp.bfloat16
    dma = pltpu.SemaphoreType.DMA
    anywhere = pl.BlockSpec(memory_space=pl.ANY)
    made = [
        ((small.shape[0], feat), f32), ((seq, feat), bf), ((seq, feat), bf), ((feat, 3 * half), bf), ((half, feat), bf),
        ((feat, 2 * hid), bf), ((2 * hid, feat), bf), ((seq, feat), bf), ((seq, 3 * half), bf), ((seq, half), bf),
        ((16, seq), f32), ((seq, feat), f32), ((seq, feat), bf), ((seq, 2 * hid), bf), ((seq, 2 * hid), bf),
    ]
    held = [
        ((LINE,) + small.shape, bf), ((small.shape[0], feat), f32), ((1, 2 * hid), f32), ((seq, feat), bf), ((seq, feat), bf),
        ((feat, 3 * half), bf), ((feat, half), bf), ((half, feat), bf), ((feat, 2 * hid), bf), ((seq, feat), bf),
        ((seq, 3 * half), bf), ((seq, 128), bf), ((seq, 128), bf), ((seq, 256), bf), ((seq, half), bf),
        ((16, seq), f32), ((seq, feat), bf), ((seq, feat), bf), ((seq, feat), f32), ((seq, feat), bf),
        ((2, seq, TILE), bf), ((2, seq, TILE), bf),
    ]
    return pl.pallas_call(
        forward_kernel,
        out_shape=tuple(jax.ShapeDtypeStruct(shape, dtype) for shape, dtype in made),
        in_specs=[anywhere] * 11,
        out_specs=(anywhere,) * len(made),
        scratch_shapes=[pltpu.VMEM(shape, dtype) for shape, dtype in held]
        + [
            dma((3,)), dma((3,)), dma((4,)), dma((4,)), dma((4,)), dma((4,)),
            dma((4, 5)), dma((12, 4)), dma((12, 5)), dma((8,)), dma((1,)), dma((1,)),
            dma((4,)), dma((4,)), dma((16,)), dma((2, 2)),
        ],
        compiler_params=pltpu.CompilerParams(
            collective_id=0, has_side_effects=True, vmem_limit_bytes=60 * 1024 * 1024
        ),
        name="forward",
    )(small, x, ct, wq, wk, wv, wo, w1, w2, gq, gk)


def flip(value, step):
    count = lax.axis_size("cells")
    return lax.ppermute(value, "cells", [(n, n ^ step) for n in range(count)])


def take(value, index, axis):
    return lax.dynamic_index_in_dim(value, index, axis, keepdims=False)


def plus(left, right):
    return (left.astype(jnp.float32) + right.astype(jnp.float32)).astype(jnp.bfloat16)


def plane_sum(value, px, py):
    two = value.reshape((2, LINE // 2, 2, 2) + value.shape[2:])
    first, later = two[0], two[1]
    first = plus(take(first, px, 2), flip(take(first, 1 - px, 2), 2))
    later = plus(take(later, py, 1), flip(take(later, 1 - py, 1), 4))
    first = plus(take(first, py, 1), flip(take(first, 1 - py, 1), 4))
    later = plus(take(later, px, 1), flip(take(later, 1 - px, 1), 2))
    return jnp.concatenate([first, later], axis=0)


def reduce_group(value, px, py):
    mine = plane_sum(value, px, py)
    summed = lax.psum_scatter(mine, "chrom", scatter_dimension=0, tiled=True)[0]
    whole = lax.all_gather(summed, "cells", axis=0, tiled=False)
    return whole.reshape((PLANE, 2) + summed.shape)


def send_home(value, core, place):
    half, feat = value.shape
    two = value.reshape(2, half // 2, feat)
    got = []
    for k in range(2):
        pairs = []
        for cells in range(lax.axis_size("cells")):
            for z in range(LINE):
                home, c = cells - cells % 2, cells % 2
                to_z = 2 * c + (z + k) % 2
                pairs.append((cells * LINE + z, (home + z // 2) * LINE + to_z))
        block = take(two, lax.rem(place + k, 2), 0)
        got.append(lax.ppermute(block, ("cells", "chrom"), pairs))
    even = lax.rem(place, 2) == 0
    return jnp.stack([jnp.where(even, got[0], got[1]), jnp.where(even, got[1], got[0])])


def paired_local(
    inputs, lengths, offsets, cotangent, norm_gain, norm_shift, query_proj, query_bias, key_proj, value_proj,
    value_bias, output_proj, output_bias, second_gain, second_shift, inner_proj, inner_bias, outer_proj, outer_bias,
):
    f32, bf = jnp.float32, jnp.bfloat16
    i, z = lax.axis_index("cells"), lax.axis_index("chrom")
    p, c = i // 2, i % 2
    px, py = p % 2, p // 2
    cells_here, block, feat = inputs.shape
    seq = block * LINE
    half_seq, half = seq // 2, feat // 2
    rows = feat // LINE
    hid = outer_proj.shape[0]
    inv_root = HEAD_DIM ** (-0.5)
    heads = HEADS // 2

    vectors = (norm_gain, norm_shift, query_bias, value_bias, output_bias, second_gain, second_shift, outer_bias)
    small = jnp.concatenate([v.reshape(1, rows) for v in vectors] + [inner_bias.reshape(hid // rows, rows)], axis=0)
    small = jnp.pad(small, ((0, 16 - small.shape[0]), (0, 384 - rows)))
    ragged = jnp.concatenate([lengths[:, None], offsets], axis=1)
    other = flip(ragged, 1)
    ragged = take(jnp.where(z // 2 == c, ragged, other), z % 2, 0)
    length, starts = ragged[0], ragged[1:]
    places = jnp.arange(seq, dtype=jnp.int32)
    live = places < length
    groups = jnp.sum((places[:, None] >= starts[None, :]).astype(jnp.int32), axis=1)
    lanes = jnp.arange(128, dtype=jnp.int32)[None, :]
    same = (groups[:, None] == lanes).astype(bf)
    mark_q = jnp.where(lanes == 127, jnp.ones((), bf), same * jnp.array(group_bias, bf))
    mark_k = jnp.where(lanes == 127, jnp.where(live, 0.0, -1e30).astype(bf)[:, None], same)
    (
        vec, xf, cf, wa, wob, wb, wc, normed, qkv, mixed, lse, middle, second, active, slope,
    ) = run_forward(
        small, inputs, cotangent, query_proj, key_proj, value_proj, output_proj, inner_proj, outer_proj, mark_q, mark_k
    )
    gain_one, shift_one, _, _, _, gain_two, shift_two, bias_out = (vec[n] for n in range(8))
    states = xf.astype(f32)
    qh, kh, vh = (qkv[:, n * half : (n + 1) * half].reshape(seq, heads, HEAD_DIM) for n in range(3))
    bias = jnp.where(live[None, :], group_bias * (groups[:, None] == groups[None, :]).astype(f32), -jnp.inf)
    log_total = lse[:heads, :, None]
    _, second_back = jax.vjp(layer_norm, middle, gain_two, shift_two)

    def scores_of():
        raw = jnp.einsum("qhd,khd->hqk", qh, kh, preferred_element_type=f32) * inv_root
        return raw + bias[None]

    upstream = jnp.where(live[:, None], cf, jnp.zeros((), bf))
    out_part = product(active, wc)
    mine = lax.dynamic_slice_in_dim(out_part, c * half_seq, half_seq, 0)
    theirs = lax.dynamic_slice_in_dim(out_part, (1 - c) * half_seq, half_seq, 0).astype(bf)
    result = (
        lax.dynamic_slice_in_dim(middle, c * half_seq, half_seq, 0) + mine + flip(theirs, 1).astype(f32) + bias_out
    )
    live_half = lax.dynamic_slice_in_dim(live, c * half_seq, half_seq, 0)
    block_out = send_home(jnp.where(live_half[:, None], result, 0.0).astype(bf), c, z)

    outer_grad = left_product(active, upstream).astype(bf)
    outer_sum = reduce_group(outer_grad.reshape(LINE, PLANE, hid // 2 // PLANE, feat), px, py)
    grad_inner = (right_back(upstream, wc) * slope.astype(f32)).astype(bf)
    inner_grad = left_product(second, grad_inner).astype(bf)
    inner_sum = reduce_group(inner_grad.reshape(LINE, PLANE, rows // PLANE, 2 * hid), px, py)
    second_part = right_back(grad_inner, wb).astype(bf)
    grad_second = second_part.astype(f32) + flip(second_part, 1).astype(f32)
    grad_norm, gain_two_grad, shift_two_grad = second_back(grad_second)
    grad_middle = upstream.astype(f32) + grad_norm
    grad_attended = grad_middle.astype(bf)
    out_grad = left_product(mixed, grad_attended).astype(bf)
    grad_mixed = right_back(grad_attended, wob).astype(bf)
    gh = grad_mixed.reshape(seq, heads, HEAD_DIM)
    again = jnp.exp(scores_of() - log_total)
    grad_probs = jnp.einsum("qhd,khd->hqk", gh, vh, preferred_element_type=f32)
    row_dot = jnp.sum(again * grad_probs, axis=-1, keepdims=True)
    grad_raw = (again * (grad_probs - row_dot)).astype(bf)
    dv = jnp.einsum("hqk,qhd->khd", again.astype(bf), gh, preferred_element_type=f32).astype(bf).reshape(seq, half)
    dk = (jnp.einsum("hqk,qhd->khd", grad_raw, qh, preferred_element_type=f32) * inv_root).astype(bf).reshape(seq, half)
    dq = (jnp.einsum("hqk,khd->qhd", grad_raw, kh, preferred_element_type=f32) * inv_root).astype(bf).reshape(seq, half)
    dqkv = jnp.concatenate([dq, dk, dv], axis=1)
    qkv_grad = left_product(normed, dqkv).astype(bf)
    keep = lax.dynamic_slice_in_dim(out_grad, c * half, half, 1)
    swap = flip(lax.dynamic_slice_in_dim(out_grad, (1 - c) * half, half, 1), 1)
    out_cols = jnp.where(c == 0, jnp.concatenate([keep, swap], 0), jnp.concatenate([swap, keep], 0))
    attn_grad = jnp.concatenate([qkv_grad, out_cols], axis=1)
    attn_sum = reduce_group(attn_grad.reshape(LINE, PLANE, rows // PLANE, 2 * feat), px, py)
    normed_part = right_back(dqkv, wa)
    mine = lax.dynamic_slice_in_dim(normed_part, c * half_seq, half_seq, 0)
    theirs = lax.dynamic_slice_in_dim(normed_part, (1 - c) * half_seq, half_seq, 0).astype(bf)
    grad_normed = mine + flip(theirs, 1).astype(f32)
    states_half = lax.dynamic_slice_in_dim(states, c * half_seq, half_seq, 0)
    _, half_back = jax.vjp(layer_norm, states_half, gain_one, shift_one)
    grad_states, gain_one_grad, shift_one_grad = half_back(grad_normed)
    grad_mid_half = lax.dynamic_slice_in_dim(grad_middle, c * half_seq, half_seq, 0)
    input_grad = send_home((grad_mid_half + grad_states).astype(bf), c, z)

    def once(v):
        return jnp.where(c == 0, v, 0.0)

    def placed(v):
        return lax.dynamic_update_slice_in_dim(jnp.zeros((feat,), f32), v, c * half, 0)

    in_bias = jnp.zeros((LINE, 2, hid // 2), f32)
    in_bias = lax.dynamic_update_slice(in_bias, column_sum(grad_inner).reshape(LINE, 1, hid // 2), (0, c, 0))
    packed = jnp.concatenate(
        [
            gain_one_grad, shift_one_grad, placed(column_sum(dq)), placed(column_sum(dv)),
            once(column_sum(grad_attended)), once(gain_two_grad), once(shift_two_grad), once(column_sum(upstream)),
            in_bias.reshape(LINE * hid),
        ]
    ).reshape(12, feat)
    packed = lax.psum(packed, ("cells", "chrom"))

    def shard(v):
        return lax.dynamic_slice_in_dim(v, z * (v.shape[0] // LINE), v.shape[0] // LINE, 0)

    s = [shard(packed[n]) for n in range(8)]
    inner_bias_grad = shard(packed[8:].reshape(LINE * hid))
    w2_grad = outer_sum.transpose(1, 0, 2, 3).reshape(hid, feat).astype(f32)
    w1_grad = inner_sum.reshape(PLANE, 2, rows // PLANE, LINE, hid // 2).transpose(0, 2, 3, 1, 4)
    w1_grad = w1_grad.reshape(rows, LINE * hid).astype(f32)
    wx = attn_sum.reshape(PLANE, 2, rows // PLANE, 4, half).transpose(3, 0, 2, 1, 4).reshape(4, rows, feat)
    wx = [wx[n].astype(f32) for n in range(4)]
    return (
        block_out, input_grad, s[0], s[1], wx[0], s[2], wx[1], wx[2], s[3], wx[3], s[4], s[5], s[6],
        w1_grad, inner_bias_grad, w2_grad, s[7],
    )


def solution(mesh):
    paired = mesh.shape["chrom"] == 4 and mesh.shape["cells"] == 8
    placed = (
        P("cells", "chrom", None),
        P("cells"),
        P("cells", None),
        P("cells", "chrom", None),
        P("chrom"),
        P("chrom"),
        P("chrom", None),
        P("chrom"),
        P("chrom", None),
        P("chrom", None),
        P("chrom"),
        P("chrom", None),
        P("chrom"),
        P("chrom"),
        P("chrom"),
        P("chrom", None),
        P("chrom"),
        P("chrom", None),
        P("chrom"),
    )
    return jax.shard_map(
        paired_local if paired else general,
        mesh=mesh,
        in_specs=placed,
        out_specs=(
            P("cells", "chrom", None),
            P("cells", "chrom", None),
            P("chrom"),
            P("chrom"),
            P("chrom", None),
            P("chrom"),
            P("chrom", None),
            P("chrom", None),
            P("chrom"),
            P("chrom", None),
            P("chrom"),
            P("chrom"),
            P("chrom"),
            P("chrom", None),
            P("chrom"),
            P("chrom", None),
            P("chrom"),
        ),
        check_vma=False,
    )
```

```python
import functools

import jax
import jax.numpy as jnp
from jax import lax
from jax.experimental import pallas as pl
from jax.experimental.pallas import tpu as pltpu
from jax.sharding import PartitionSpec as P

HEADS = 20
HEAD_DIM = 64


eps_norm = 1e-05
group_bias = 1.0


def layer_norm(values, gain, shift):
    center = values - jnp.mean(values, axis=-1, keepdims=True)
    spread = jnp.mean(center * center, axis=-1, keepdims=True)
    return center * lax.rsqrt(spread + eps_norm) * gain + shift


def gelu_exact(values):
    return jax.nn.gelu(values, approximate=False)


def product(left, right):
    return jnp.dot(left, right, preferred_element_type=jnp.float32)


def left_product(left, right):
    return jnp.einsum("ra,rb->ab", left, right, preferred_element_type=jnp.float32)


def right_back(left, right):
    return jnp.einsum("rb,ab->ra", left, right, preferred_element_type=jnp.float32)


def column_sum(values):
    return jnp.sum(values, axis=0, dtype=jnp.float32)


def split_rows(value, outer, inner_count):
    return value.reshape(
        (outer, inner_count, value.shape[0] // (outer * inner_count)) + value.shape[1:]
    )


def general(
    inputs,
    lengths,
    offsets,
    cotangent,
    norm_gain,
    norm_shift,
    query_proj,
    query_bias,
    key_proj,
    value_proj,
    value_bias,
    output_proj,
    output_bias,
    second_gain,
    second_shift,
    inner_proj,
    inner_bias,
    outer_proj,
    outer_bias,
):
    count_chrom = lax.axis_size("chrom")
    count_cells = lax.axis_size("cells")
    block_index = lax.axis_index("chrom")
    cells_here, tokens_here, feat_width = inputs.shape
    seq_len = tokens_here * count_chrom
    row_count = cells_here * tokens_here
    inv_root = HEAD_DIM ** (-0.5)
    places = jnp.arange(seq_len, dtype=jnp.int32)
    key_live = places[None, :] < lengths[:, None]
    groups = jnp.sum((places[None, :, None] >= offsets[:, None, :]).astype(jnp.int32), axis=2)
    query_groups = lax.dynamic_slice_in_dim(groups, block_index * tokens_here, tokens_here, 1)
    query_live = lax.dynamic_slice_in_dim(key_live, block_index * tokens_here, tokens_here, 1)
    same_group = (query_groups[:, :, None] == groups[:, None, :]).astype(jnp.float32)
    mask_bias = jnp.where(key_live[:, None, :], group_bias * same_group, -jnp.inf)[:, None]
    gathered = (
        lax.all_gather(norm_gain, "chrom", axis=0, tiled=True),
        lax.all_gather(norm_shift, "chrom", axis=0, tiled=True),
        lax.all_gather(query_proj, "chrom", axis=0, tiled=True),
        lax.all_gather(query_bias, "chrom", axis=0, tiled=True),
        lax.all_gather(key_proj, "chrom", axis=0, tiled=True),
        lax.all_gather(value_proj, "chrom", axis=0, tiled=True),
        lax.all_gather(value_bias, "chrom", axis=0, tiled=True),
        lax.all_gather(output_proj, "chrom", axis=0, tiled=True),
        lax.all_gather(output_bias, "chrom", axis=0, tiled=True),
        lax.all_gather(second_gain, "chrom", axis=0, tiled=True),
        lax.all_gather(second_shift, "chrom", axis=0, tiled=True),
        lax.all_gather(inner_proj, "chrom", axis=0, tiled=True),
        lax.all_gather(inner_bias, "chrom", axis=0, tiled=True),
        lax.all_gather(outer_proj, "chrom", axis=0, tiled=True),
        lax.all_gather(outer_bias, "chrom", axis=0, tiled=True),
    )
    gain_one = gathered[0].astype(jnp.float32)
    shift_one = gathered[1].astype(jnp.float32)
    gain_two = gathered[9].astype(jnp.float32)
    shift_two = gathered[10].astype(jnp.float32)
    states = inputs.astype(jnp.float32).reshape(row_count, feat_width)
    normed_full, norm_back = jax.vjp(layer_norm, states, gain_one, shift_one)
    normed = normed_full.astype(jnp.bfloat16)
    queries = (product(normed, gathered[2]) + gathered[3].astype(jnp.float32)).astype(jnp.bfloat16)
    key_rows = product(normed, gathered[4]).astype(jnp.bfloat16)
    vals = (product(normed, gathered[5]) + gathered[6].astype(jnp.float32)).astype(jnp.bfloat16)
    keys_all, vals_all = (
        lax.all_gather(
            key_rows.reshape(cells_here, tokens_here, feat_width), "chrom", axis=1, tiled=True
        ),
        lax.all_gather(
            vals.reshape(cells_here, tokens_here, feat_width), "chrom", axis=1, tiled=True
        ),
    )
    query_heads = queries.reshape(cells_here, tokens_here, HEADS, HEAD_DIM)
    key_heads = keys_all.reshape(cells_here, seq_len, HEADS, HEAD_DIM)
    val_heads = vals_all.reshape(cells_here, seq_len, HEADS, HEAD_DIM)

    def scores_of():
        raw = (
            jnp.einsum(
                "cqhd,ckhd->chqk", query_heads, key_heads, preferred_element_type=jnp.float32
            )
            * inv_root
        )
        return raw + mask_bias

    masked = scores_of()
    row_max = jnp.max(masked, axis=-1, keepdims=True)
    exp_scores = jnp.exp(masked - row_max)
    exp_total = jnp.sum(exp_scores, axis=-1, keepdims=True)
    attn_probs = exp_scores / exp_total
    log_total = row_max + jnp.log(exp_total)
    mixed_out = jnp.einsum(
        "chqk,ckhd->cqhd",
        attn_probs.astype(jnp.bfloat16),
        val_heads,
        preferred_element_type=jnp.float32,
    )
    mixed_out = mixed_out.astype(jnp.bfloat16).reshape(row_count, feat_width)
    attended = product(mixed_out, gathered[7]) + gathered[8].astype(jnp.float32)
    middle = states + attended
    second_full, second_back = jax.vjp(layer_norm, middle, gain_two, shift_two)
    second = second_full.astype(jnp.bfloat16)
    inner_pre = product(second, gathered[11]) + gathered[12].astype(jnp.float32)
    active_full, gelu_back = jax.vjp(gelu_exact, inner_pre)
    active = active_full.astype(jnp.bfloat16)
    result = middle + product(active, gathered[13]) + gathered[14].astype(jnp.float32)
    live_rows = query_live.reshape(row_count, 1)
    block_out = (
        jnp.where(live_rows, result, 0.0)
        .astype(jnp.bfloat16)
        .reshape(cells_here, tokens_here, feat_width)
    )
    upstream = jnp.where(
        live_rows, cotangent.reshape(row_count, feat_width), jnp.zeros((), jnp.bfloat16)
    )
    outer_bias_grad = column_sum(upstream)
    outer_proj_grad = left_product(active, upstream)
    grad_active = right_back(upstream, gathered[13])
    (grad_inner_full,) = gelu_back(grad_active)
    grad_inner = grad_inner_full.astype(jnp.bfloat16)
    inner_bias_grad = column_sum(grad_inner)
    inner_proj_grad = left_product(second, grad_inner)
    grad_second = right_back(grad_inner, gathered[11])
    grad_middle_norm, second_gain_grad, second_shift_grad = second_back(grad_second)
    grad_middle = upstream.astype(jnp.float32) + grad_middle_norm
    grad_attended = grad_middle.astype(jnp.bfloat16)
    output_bias_grad = column_sum(grad_attended)
    output_proj_grad = left_product(mixed_out, grad_attended)
    grad_mixed = right_back(grad_attended, gathered[7]).astype(jnp.bfloat16)
    grad_mixed = grad_mixed.reshape(cells_here, tokens_here, HEADS, HEAD_DIM)
    attn_again = jnp.exp(scores_of() - log_total)
    grad_probs = jnp.einsum(
        "cqhd,ckhd->chqk", grad_mixed, val_heads, preferred_element_type=jnp.float32
    )
    row_dot = jnp.sum(attn_again * grad_probs, axis=-1, keepdims=True)
    grad_raw = (attn_again * (grad_probs - row_dot)).astype(jnp.bfloat16)
    grad_vals_part = jnp.einsum(
        "chqk,cqhd->ckhd",
        attn_again.astype(jnp.bfloat16),
        grad_mixed,
        preferred_element_type=jnp.float32,
    )
    grad_keys_part = (
        jnp.einsum("chqk,cqhd->ckhd", grad_raw, query_heads, preferred_element_type=jnp.float32)
        * inv_root
    )
    grad_queries = (
        jnp.einsum("chqk,ckhd->cqhd", grad_raw, key_heads, preferred_element_type=jnp.float32)
        * inv_root
    ).astype(jnp.bfloat16)
    grad_queries = grad_queries.reshape(row_count, feat_width)
    grad_keys_sum, grad_vals_sum = (
        lax.psum_scatter(
            grad_keys_part.reshape(cells_here, seq_len, feat_width).astype(jnp.bfloat16),
            "chrom",
            scatter_dimension=1,
            tiled=True,
        ).astype(jnp.float32),
        lax.psum_scatter(
            grad_vals_part.reshape(cells_here, seq_len, feat_width).astype(jnp.bfloat16),
            "chrom",
            scatter_dimension=1,
            tiled=True,
        ).astype(jnp.float32),
    )
    grad_keys = grad_keys_sum.astype(jnp.bfloat16).reshape(row_count, feat_width)
    grad_vals = grad_vals_sum.astype(jnp.bfloat16).reshape(row_count, feat_width)
    query_proj_grad = left_product(normed, grad_queries)
    query_bias_grad = column_sum(grad_queries)
    key_proj_grad = left_product(normed, grad_keys)
    value_proj_grad = left_product(normed, grad_vals)
    value_bias_grad = column_sum(grad_vals)
    grad_normed = (
        right_back(grad_queries, gathered[2])
        + right_back(grad_keys, gathered[4])
        + right_back(grad_vals, gathered[5])
    )
    grad_states_norm, norm_gain_grad, norm_shift_grad = norm_back(grad_normed)
    input_grad = (
        (grad_middle + grad_states_norm)
        .astype(jnp.bfloat16)
        .reshape(cells_here, tokens_here, feat_width)
    )
    grad_list = (
        norm_gain_grad,
        norm_shift_grad,
        query_proj_grad,
        query_bias_grad,
        key_proj_grad,
        value_proj_grad,
        value_bias_grad,
        output_proj_grad,
        output_bias_grad,
        second_gain_grad,
        second_shift_grad,
        inner_proj_grad,
        inner_bias_grad,
        outer_proj_grad,
        outer_bias_grad,
    )
    pieces = tuple((split_rows(member, count_chrom, count_cells) for member in grad_list))
    section_one = (
        lax.psum_scatter(
            pieces[0].astype(jnp.bfloat16), "cells", scatter_dimension=1, tiled=True
        ).astype(jnp.float32),
        lax.psum_scatter(
            pieces[1].astype(jnp.bfloat16), "cells", scatter_dimension=1, tiled=True
        ).astype(jnp.float32),
        lax.psum_scatter(
            pieces[2].astype(jnp.bfloat16), "cells", scatter_dimension=1, tiled=True
        ).astype(jnp.float32),
        lax.psum_scatter(
            pieces[3].astype(jnp.bfloat16), "cells", scatter_dimension=1, tiled=True
        ).astype(jnp.float32),
        lax.psum_scatter(
            pieces[4].astype(jnp.bfloat16), "cells", scatter_dimension=1, tiled=True
        ).astype(jnp.float32),
        lax.psum_scatter(
            pieces[5].astype(jnp.bfloat16), "cells", scatter_dimension=1, tiled=True
        ).astype(jnp.float32),
        lax.psum_scatter(
            pieces[6].astype(jnp.bfloat16), "cells", scatter_dimension=1, tiled=True
        ).astype(jnp.float32),
        lax.psum_scatter(
            pieces[7].astype(jnp.bfloat16), "cells", scatter_dimension=1, tiled=True
        ).astype(jnp.float32),
        lax.psum_scatter(
            pieces[8].astype(jnp.bfloat16), "cells", scatter_dimension=1, tiled=True
        ).astype(jnp.float32),
        lax.psum_scatter(
            pieces[9].astype(jnp.bfloat16), "cells", scatter_dimension=1, tiled=True
        ).astype(jnp.float32),
        lax.psum_scatter(
            pieces[10].astype(jnp.bfloat16), "cells", scatter_dimension=1, tiled=True
        ).astype(jnp.float32),
        lax.psum_scatter(
            pieces[11].astype(jnp.bfloat16), "cells", scatter_dimension=1, tiled=True
        ).astype(jnp.float32),
        lax.psum_scatter(
            pieces[12].astype(jnp.bfloat16), "cells", scatter_dimension=1, tiled=True
        ).astype(jnp.float32),
        lax.psum_scatter(
            pieces[13].astype(jnp.bfloat16), "cells", scatter_dimension=1, tiled=True
        ).astype(jnp.float32),
        lax.psum_scatter(
            pieces[14].astype(jnp.bfloat16), "cells", scatter_dimension=1, tiled=True
        ).astype(jnp.float32),
    )
    section_two = (
        lax.psum_scatter(
            section_one[0].astype(jnp.bfloat16), "chrom", scatter_dimension=0, tiled=True
        ).astype(jnp.float32),
        lax.psum_scatter(
            section_one[1].astype(jnp.bfloat16), "chrom", scatter_dimension=0, tiled=True
        ).astype(jnp.float32),
        lax.psum_scatter(
            section_one[2].astype(jnp.bfloat16), "chrom", scatter_dimension=0, tiled=True
        ).astype(jnp.float32),
        lax.psum_scatter(
            section_one[3].astype(jnp.bfloat16), "chrom", scatter_dimension=0, tiled=True
        ).astype(jnp.float32),
        lax.psum_scatter(
            section_one[4].astype(jnp.bfloat16), "chrom", scatter_dimension=0, tiled=True
        ).astype(jnp.float32),
        lax.psum_scatter(
            section_one[5].astype(jnp.bfloat16), "chrom", scatter_dimension=0, tiled=True
        ).astype(jnp.float32),
        lax.psum_scatter(
            section_one[6].astype(jnp.bfloat16), "chrom", scatter_dimension=0, tiled=True
        ).astype(jnp.float32),
        lax.psum_scatter(
            section_one[7].astype(jnp.bfloat16), "chrom", scatter_dimension=0, tiled=True
        ).astype(jnp.float32),
        lax.psum_scatter(
            section_one[8].astype(jnp.bfloat16), "chrom", scatter_dimension=0, tiled=True
        ).astype(jnp.float32),
        lax.psum_scatter(
            section_one[9].astype(jnp.bfloat16), "chrom", scatter_dimension=0, tiled=True
        ).astype(jnp.float32),
        lax.psum_scatter(
            section_one[10].astype(jnp.bfloat16), "chrom", scatter_dimension=0, tiled=True
        ).astype(jnp.float32),
        lax.psum_scatter(
            section_one[11].astype(jnp.bfloat16), "chrom", scatter_dimension=0, tiled=True
        ).astype(jnp.float32),
        lax.psum_scatter(
            section_one[12].astype(jnp.bfloat16), "chrom", scatter_dimension=0, tiled=True
        ).astype(jnp.float32),
        lax.psum_scatter(
            section_one[13].astype(jnp.bfloat16), "chrom", scatter_dimension=0, tiled=True
        ).astype(jnp.float32),
        lax.psum_scatter(
            section_one[14].astype(jnp.bfloat16), "chrom", scatter_dimension=0, tiled=True
        ).astype(jnp.float32),
    )
    rejoined = (
        lax.all_gather(section_two[0].astype(jnp.bfloat16), "cells", axis=1, tiled=True).astype(
            jnp.float32
        ),
        lax.all_gather(section_two[1].astype(jnp.bfloat16), "cells", axis=1, tiled=True).astype(
            jnp.float32
        ),
        lax.all_gather(section_two[2].astype(jnp.bfloat16), "cells", axis=1, tiled=True).astype(
            jnp.float32
        ),
        lax.all_gather(section_two[3].astype(jnp.bfloat16), "cells", axis=1, tiled=True).astype(
            jnp.float32
        ),
        lax.all_gather(section_two[4].astype(jnp.bfloat16), "cells", axis=1, tiled=True).astype(
            jnp.float32
        ),
        lax.all_gather(section_two[5].astype(jnp.bfloat16), "cells", axis=1, tiled=True).astype(
            jnp.float32
        ),
        lax.all_gather(section_two[6].astype(jnp.bfloat16), "cells", axis=1, tiled=True).astype(
            jnp.float32
        ),
        lax.all_gather(section_two[7].astype(jnp.bfloat16), "cells", axis=1, tiled=True).astype(
            jnp.float32
        ),
        lax.all_gather(section_two[8].astype(jnp.bfloat16), "cells", axis=1, tiled=True).astype(
            jnp.float32
        ),
        lax.all_gather(section_two[9].astype(jnp.bfloat16), "cells", axis=1, tiled=True).astype(
            jnp.float32
        ),
        lax.all_gather(section_two[10].astype(jnp.bfloat16), "cells", axis=1, tiled=True).astype(
            jnp.float32
        ),
        lax.all_gather(section_two[11].astype(jnp.bfloat16), "cells", axis=1, tiled=True).astype(
            jnp.float32
        ),
        lax.all_gather(section_two[12].astype(jnp.bfloat16), "cells", axis=1, tiled=True).astype(
            jnp.float32
        ),
        lax.all_gather(section_two[13].astype(jnp.bfloat16), "cells", axis=1, tiled=True).astype(
            jnp.float32
        ),
        lax.all_gather(section_two[14].astype(jnp.bfloat16), "cells", axis=1, tiled=True).astype(
            jnp.float32
        ),
    )
    final = tuple(
        (
            member.reshape(
                (member.shape[0] * member.shape[1] * member.shape[2],) + member.shape[3:]
            )
            for member in rejoined
        )
    )
    return (block_out, input_grad) + tuple(final)


PLANE = 4
LINE = 4
VMEM_LIMIT = 62 * 1024 * 1024


def rows_of(start, count):
    return pl.ds(pl.multiple_of(start, 16), count)


def cols_of(start, count):
    return pl.ds(pl.multiple_of(start, 128), count)


VECTORS = 8
TILE = 256


def nt(left, right):
    return lax.dot_general(left, right, (((1,), (1,)), ((), ())), preferred_element_type=jnp.float32)


def nn(left, right):
    return jnp.dot(left, right, preferred_element_type=jnp.float32)


def moments(values):
    center = values - jnp.mean(values, axis=-1, keepdims=True)
    spread = jnp.mean(center * center, axis=-1, keepdims=True)
    return center, lax.rsqrt(spread + eps_norm)


def gelu_and_slope(u):
    gauss = jnp.exp(u * u * -0.5)
    t = 1.0 / (1.0 + jnp.abs(u) * (0.3275911 * 0.5 ** 0.5))
    poly = 0.5 * 1.061405429
    for factor in (-1.453152027, 1.421413741, -0.284496736, 0.254829592):
        poly = poly * t + 0.5 * factor
    tail = poly * t * gauss
    phi_sum = jnp.where(u < 0.0, tail, 1.0 - tail)
    return u * phi_sum, phi_sum + u * gauss * 0.3989422804014327


def forward_kernel(
    small_ref, x_ref, ct_ref, wq_ref, wk_ref, wv_ref, wo_ref, w1_ref, w2_ref, gq_ref, gk_ref,
    vec_o, x_o, ct_o, wa_o, wob_o, wb_o, wc, normed_o, qkv_o, mixed_o, lse_o, middle_o, second_o, active_o, slope_o,
    smalls, vec, bias_in, xf, cf, wa, wol, wob, wb, normed, qkv, gq, gk, kx, mixed, lse, part, part_in, middle, second,
    act, slp,
    sm_s, sm_r, ex_s, ex_r, fw_s, fw_r, ln_s, un_s, un_r, loc, wo_s, wo_r, pa_s, pa_r, out_s, act_s,
):
    f32, bf = jnp.float32, jnp.bfloat16
    i, z = lax.axis_index("cells"), lax.axis_index("chrom")
    p, c = i // 2, lax.rem(i, 2)
    px, py = lax.rem(p, 2), p // 2
    x_nb, y_nb, core_nb = i + 2 - 4 * px, i + 4 - 8 * py, i + 1 - 2 * c
    p_x, p_y = p + 1 - 2 * px, p + 2 - 4 * py
    rows = wq_ref.shape[0]
    feat = wq_ref.shape[1]
    half = feat // 2
    hid = w2_ref.shape[0]
    block = x_ref.shape[1]
    seq = block * LINE
    part_rows, hid_part = rows // PLANE, hid // 2 // PLANE

    barrier = pltpu.get_barrier_semaphore()
    line_ids = [
        (i - c + lax.rem(c + dc, 2), lax.rem(z + dz, LINE))
        for dc in range(2)
        for dz in range(LINE)
        if dc or dz
    ]
    for who in line_ids + [(x_nb, z), (y_nb, z)]:
        pl.semaphore_signal(barrier, inc=1, device_id=who, device_id_type=pl.DeviceIdType.MESH)
    pl.semaphore_wait(barrier, len(line_ids) + 2)

    def send(src, dst, s, r, who):
        return pltpu.make_async_remote_copy(
            src_ref=src, dst_ref=dst, send_sem=s, recv_sem=r, device_id=who,
            device_id_type=pl.DeviceIdType.MESH,
        )

    small_own = pltpu.make_async_copy(small_ref, smalls.at[z], loc.at[0])
    small_out = [
        send(small_ref, smalls.at[z], sm_s.at[d], sm_r.at[d], (i, lax.rem(z + d + 1, LINE)))
        for d in range(LINE - 1)
    ]

    def exchange(src, dst, which):
        stay = c == z // 2
        mine, outs = None, []
        for k in range(2):
            j = lax.rem(z + k, 2)
            to = dst.at[rows_of(z * block, block), :]
            r = ex_r.at[2 * which + k]
            outs.append(send(src.at[j], to, ex_s.at[2 * which + k], r, (i - c + z // 2, 2 * c + j)))
            if k == 0:
                mine = pltpu.make_async_copy(src.at[j], to, r)

        def start():
            pl.when(stay)(mine.start)
            pl.when(jnp.logical_not(stay))(outs[0].start)
            outs[1].start()

        def arrived():
            pl.when(stay)(mine.wait)
            pl.when(jnp.logical_not(stay))(outs[0].wait_recv)
            outs[1].wait_recv()

        def sent():
            pl.when(jnp.logical_not(stay))(outs[0].wait_send)
            outs[1].wait_send()

        return start, arrived, sent

    def forward(dst, which):
        return [
            send(
                dst.at[rows_of((2 * c + b) * block, block), :],
                dst.at[rows_of((2 * c + b) * block, block), :],
                fw_s.at[2 * which + b], fw_r.at[2 * which + b], (core_nb, z),
            )
            for b in range(2)
        ]

    x_start, x_arrived, x_sent = exchange(x_ref, xf, 0)
    c_start, c_arrived, c_sent = exchange(ct_ref, cf, 1)
    x_fw, c_fw = forward(xf, 0), forward(cf, 1)

    lands = (wa, wol, wb, wc)
    groups = range(4)
    partner, inner = z + 1 - 2 * lax.rem(z, 2), 3 - z
    low = z < 2
    middle_chip = jnp.logical_or(z == 1, z == 2)
    slot_shard = (partner, jnp.where(low, 2, 1), jnp.where(low, 3, 0))

    def own_parts(g, row, count):
        if g == 0:
            return [
                (ref.at[rows_of(row, count), cols_of(c * half, half)], pl.ds(n * half, half))
                for n, ref in enumerate((wq_ref, wk_ref, wv_ref))
            ]
        if g == 1:
            return [(wo_ref.at[rows_of(row, count), cols_of(c * half, half)], pl.ds(0, half))]
        if g == 2:
            return [
                (w1_ref.at[rows_of(row, count), cols_of(n * hid + c * (hid // 2), hid // 2)], pl.ds(n * (hid // 2), hid // 2))
                for n in range(LINE)
            ]
        return [(w2_ref.at[rows_of(c * (hid // 2) + row, count), :], pl.ds(0, feat))]

    def shape_of(g):
        return (rows, part_rows) if g < 3 else (hid // 2, hid_part)

    def piece(g, s, at):
        shard, count = shape_of(g)
        return lands[g].at[rows_of(s * shard + at * count, count), :]

    def half_piece(g, s, at, side):
        shard, count = shape_of(g)
        width = lands[g].shape[1]
        cut = width // 256 * 128
        cols = pl.ds(cut, width - cut) if side else pl.ds(0, cut)
        return lands[g].at[rows_of(s * shard + at * count, count), cols]

    def line_send(g, s, slot, e, to):
        return send(piece(g, s, p), piece(g, s, p), ln_s.at[g, e], un_r.at[3 * g + slot, 0], (i, to))

    def first(g):
        shard, count = shape_of(g)
        for src, cols in own_parts(g, p * count, count):
            dst = lands[g].at[rows_of(z * shard + p * count, count), cols]
            send(src, dst, ln_s.at[g, 0], un_r.at[3 * g, 0], (i, partner)).start()

        @pl.when(middle_chip)
        def _():
            for src, cols in own_parts(g, p * count, count):
                dst = lands[g].at[rows_of(z * shard + p * count, count), cols]
                send(src, dst, ln_s.at[g, 1], un_r.at[3 * g + 1, 0], (i, inner)).start()

    def passing(g, slot):
        if slot == 0:
            return line_send(g, slot_shard[0], 2, 2, inner)
        return line_send(g, slot_shard[slot], slot, 2 + slot, partner)

    def spread(g, slot):
        own = piece(g, slot_shard[slot], p)
        u = 3 * g + slot
        return [
            send(own, own, un_s.at[u, 0], un_r.at[u, 1], (x_nb, z)),
            send(own, own, un_s.at[u, 1], un_r.at[u, 2], (y_nb, z)),
        ]

    def cross(g, slot):
        u = 3 * g + slot
        left = half_piece(g, slot_shard[slot], p_x, 0)
        rest = half_piece(g, slot_shard[slot], p_y, 1)
        return [
            send(left, left, un_s.at[u, 2], un_r.at[u, 3], (y_nb, z)),
            send(rest, rest, un_s.at[u, 3], un_r.at[u, 4], (x_nb, z)),
        ]

    def land(g, slot):
        line_send(g, slot_shard[slot], slot, 0, partner).wait_recv()
        pl.when(middle_chip)(passing(g, slot).start)
        for d in spread(g, slot):
            d.start()

    def turn(g, slot):
        for d in spread(g, slot):
            d.wait_recv()
        for d in cross(g, slot):
            d.start()

    def own_start(g):
        shard, _ = shape_of(g)
        for src, cols in own_parts(g, 0, shard):
            to = second.at[pl.ds(0, shard), :] if g == 3 else lands[g].at[rows_of(z * shard, shard), cols]
            pltpu.make_async_copy(src, to, loc.at[1 + g]).start()

    def own_wait(g):
        shard, _ = shape_of(g)
        ref = second.at[pl.ds(0, shard), :] if g == 3 else lands[g].at[rows_of(z * shard, shard), :]
        pltpu.make_async_copy(ref, ref, loc.at[1 + g]).wait()

    def whole(g):
        for slot in range(3):
            for d in cross(g, slot):
                d.wait_recv()
        if g < 3:
            own_wait(g)

    def all_sent(g):
        line_send(g, z, 0, 0, partner).wait_send()

        @pl.when(middle_chip)
        def _():
            line_send(g, z, 1, 1, inner).wait_send()
            for slot in range(3):
                passing(g, slot).wait_send()

        for slot in range(3):
            for d in spread(g, slot) + cross(g, slot):
                d.wait_send()

    outs = []

    def keep(src, dst):
        d = pltpu.make_async_copy(src, dst, out_s.at[len(outs)])
        d.start()
        outs.append(d)

    small_own.start()
    for d in small_out:
        d.start()
    first(0)
    x_start()
    for g in groups:
        own_start(g)
    gq_in = pltpu.make_async_copy(gq_ref, gq, loc.at[6])
    gk_in = pltpu.make_async_copy(gk_ref, gk, loc.at[7])
    gq_in.start()
    gk_in.start()
    first(1)
    land(0, 0)

    small_own.wait()
    for d in small_out:
        d.wait()
    width = smalls.shape[2]
    total = jnp.zeros((smalls.shape[1], feat), f32)
    at = lax.broadcasted_iota(jnp.int32, (width, feat), 0)
    to = lax.broadcasted_iota(jnp.int32, (width, feat), 1)
    for s in range(LINE):
        place = jnp.where(jnp.logical_and(at < rows, to == at + s * rows), 1.0, 0.0).astype(bf)
        total += nn(smalls[s], place)
    vec[...] = total
    at = lax.broadcasted_iota(jnp.int32, (width, hid // 2), 0)
    to = lax.broadcasted_iota(jnp.int32, (width, hid // 2), 1)
    which = lax.broadcasted_iota(jnp.int32, (smalls.shape[1], hid // 2), 0)
    for s in range(LINE):
        line_bias = jnp.zeros((1, hid // 2), f32)
        for n in range(hid // 2 // rows):
            place = jnp.where(jnp.logical_and(at < rows, to == at + n * rows), 1.0, 0.0).astype(bf)
            picked = jnp.where(which == VECTORS + c * (hid // 2 // rows) + n, nn(smalls[s], place), 0.0)
            line_bias += jnp.sum(picked, axis=0, keepdims=True)
        bias_in[:, pl.ds(s * (hid // 2), hid // 2)] = line_bias
    keep(vec, vec_o)

    land(0, 1)
    first(2)
    turn(0, 0)
    x_arrived()
    for d in x_fw:
        d.start()
    land(0, 2)
    turn(0, 1)

    def norm_rows(n, _):
        at = pl.ds(pl.multiple_of(n * 64, 64), 64)
        center, r = moments(xf[at, :].astype(f32))
        normed[at, :] = (center * r * vec[0:1, :] + vec[1:2, :]).astype(bf)
        return _

    def norm_half(h):
        steps = seq // 2 // 64
        lax.fori_loop(h * steps, (h + 1) * steps, norm_rows, 0)

    norm_half(c)
    for d in x_fw:
        d.wait_recv()
    norm_half(1 - c)
    keep(normed, normed_o)
    keep(xf, x_o)
    gq_in.wait()
    gk_in.wait()
    kx[:, 128:] = gk[...]
    land(1, 0)
    land(1, 1)
    turn(0, 2)
    land(1, 2)
    land(2, 0)
    for slot in range(3):
        turn(1, slot)
    whole(0)
    keep(wa, wa_o)

    bias_row = jnp.concatenate(
        [vec[2:3, cols_of(c * half, half)], jnp.zeros((1, half), f32), vec[3:4, cols_of(c * half, half)]], axis=1
    )

    def qkv_cols(start, width):
        got = nn(normed[...], wa[:, pl.ds(start, width)])
        qkv[:, pl.ds(start, width)] = (got + bias_row[:, start : start + width]).astype(bf)

    total_cols = 3 * half
    for n in range(total_cols // TILE):
        qkv_cols(n * TILE, TILE)
        if n == 3:
            land(2, 1)
            first(3)
    if total_cols % TILE:
        qkv_cols(total_cols // TILE * TILE, total_cols % TILE)
    turn(2, 0)
    keep(qkv, qkv_o)

    lane = lax.broadcasted_iota(jnp.int32, (TILE, 128), 1)

    def attend(t):
        k2 = qkv[:, pl.ds(half + t * 128, 128)]
        v2t = jnp.transpose(qkv[:, pl.ds(2 * half + t * 128, 128)])
        kx[:, :128] = k2

        def chunk(n, _):
            at = pl.ds(pl.multiple_of(n * TILE, TILE), TILE)
            q2 = qkv[at, pl.ds(t * 128, 128)] * jnp.array(HEAD_DIM ** (-0.5), bf)
            both = []
            for h in range(2):
                own = lane < HEAD_DIM if h == 0 else lane >= HEAD_DIM
                qx = jnp.concatenate([jnp.where(own, q2, jnp.zeros((), bf)), gq[at, :]], axis=1)
                s = nt(kx[...], qx)
                top = jnp.max(s, axis=0, keepdims=True)
                e = jnp.exp(s - top)
                total = jnp.sum(e, axis=0, keepdims=True)
                o = nn(v2t[h * HEAD_DIM : (h + 1) * HEAD_DIM, :], e.astype(bf))
                both.append(o / total)
                lse[2 * t + h : 2 * t + h + 1, at] = top + jnp.log(total)
            mixed[at, pl.ds(t * 128, 128)] = jnp.transpose(jnp.concatenate(both, axis=0)).astype(bf)
            return _

        lax.fori_loop(0, seq // TILE, chunk, 0)

    attend(0)
    land(2, 2)
    turn(2, 1)
    attend(1)
    whole(1)
    wo_own = pltpu.make_async_copy(
        wol.at[rows_of(c * half, half), :], wob.at[:, cols_of(c * half, half)], loc.at[5]
    )
    wo_out = send(
        wol.at[rows_of((1 - c) * half, half), :],
        wob.at[:, cols_of(c * half, half)], wo_s.at[0], wo_r.at[0], (core_nb, z),
    )
    wo_own.start()
    wo_out.start()
    attend(2)
    land(3, 0)
    turn(2, 2)
    attend(3)
    land(3, 1)
    attend(4)
    turn(3, 0)
    keep(mixed, mixed_o)
    keep(lse, lse_o)
    wo_own.wait()
    wo_out.wait()
    keep(wob, wob_o)

    chunks = seq // TILE
    swaps = []
    for n in range(chunks):
        at = pl.ds(n * TILE, TILE)
        part[at, :] = nn(mixed[at, :], wob[...]).astype(bf)
        d = send(part.at[at, :], part_in.at[at, :], pa_s.at[n], pa_r.at[n], (core_nb, z))
        d.start()
        swaps.append(d)
    land(3, 2)
    c_start()
    own_wait(3)
    out_own = pltpu.make_async_copy(
        second.at[pl.ds(0, hid // 2), :], wc.at[rows_of(z * (hid // 2), hid // 2), :], loc.at[4]
    )
    out_own.start()
    out_own.wait()

    def second_rows(n, _):
        at = pl.ds(pl.multiple_of(n * 64, 64), 64)
        sums = xf[at, :].astype(f32) + (part[at, :].astype(f32) + part_in[at, :].astype(f32) + vec[4:5, :])
        middle[at, :] = sums.astype(bf)
        center, r = moments(sums)
        second[at, :] = (center * r * vec[5:6, :] + vec[6:7, :]).astype(bf)
        return _

    for n in range(chunks):
        swaps[n].wait_recv()
        lax.fori_loop(n * TILE // 64, (n + 1) * TILE // 64, second_rows, 0)
    keep(middle, middle_o)
    keep(second, second_o)
    turn(3, 1)
    whole(2)
    keep(wb, wb_o)

    tiles = 2 * hid // TILE

    def tile_out(n, slot):
        cols = pl.ds(n * TILE, TILE)
        return [
            pltpu.make_async_copy(act.at[slot], active_o.at[:, cols], act_s.at[slot, 0]),
            pltpu.make_async_copy(slp.at[slot], slope_o.at[:, cols], act_s.at[slot, 1]),
        ]

    for n in range(tiles):
        slot = n % 2
        cols = pl.ds(n * TILE, TILE)
        if n >= 2:
            for d in tile_out(n - 2, slot):
                d.wait()

        def tile_rows(m, _, cols=cols, slot=slot):
            at = pl.ds(pl.multiple_of(m * TILE, TILE), TILE)
            u = nn(second[at, :], wb[:, cols]) + bias_in[:, cols]
            value, slope = gelu_and_slope(u)
            act[slot, at, :] = value.astype(bf)
            slp[slot, at, :] = slope.astype(bf)
            return _

        lax.fori_loop(0, chunks, tile_rows, 0)
        for d in tile_out(n, slot):
            d.start()
        if n == 3:
            turn(3, 2)
    c_arrived()
    for d in c_fw:
        d.start()
    for n in (tiles - 2, tiles - 1):
        for d in tile_out(n, n % 2):
            d.wait()
    whole(3)
    for d in c_fw:
        d.wait()
    keep(cf, ct_o)
    for d in x_fw + swaps:
        d.wait_send()
    x_sent()
    c_sent()
    for g in groups:
        all_sent(g)
    for d in outs:
        d.wait()


def run_forward(small, x, ct, wq, wk, wv, wo, w1, w2, gq, gk):
    rows, feat = wq.shape
    hid = w2.shape[0]
    seq = x.shape[1] * LINE
    half = feat // 2
    heads = half // HEAD_DIM
    f32, bf = jnp.float32, jnp.bfloat16
    dma = pltpu.SemaphoreType.DMA
    anywhere = pl.BlockSpec(memory_space=pl.ANY)
    made = [
        ((small.shape[0], feat), f32), ((seq, feat), bf), ((seq, feat), bf), ((feat, 3 * half), bf), ((half, feat), bf),
        ((feat, 2 * hid), bf), ((2 * hid, feat), bf), ((seq, feat), bf), ((seq, 3 * half), bf), ((seq, half), bf),
        ((16, seq), f32), ((seq, feat), bf), ((seq, feat), bf), ((seq, 2 * hid), bf), ((seq, 2 * hid), bf),
    ]
    held = [
        ((LINE,) + small.shape, bf), ((small.shape[0], feat), f32), ((1, 2 * hid), f32), ((seq, feat), bf), ((seq, feat), bf),
        ((feat, 3 * half), bf), ((feat, half), bf), ((half, feat), bf), ((feat, 2 * hid), bf), ((seq, feat), bf),
        ((seq, 3 * half), bf), ((seq, 128), bf), ((seq, 128), bf), ((seq, 256), bf), ((seq, half), bf),
        ((16, seq), f32), ((seq, feat), bf), ((seq, feat), bf), ((seq, feat), bf), ((seq, feat), bf),
        ((2, seq, TILE), bf), ((2, seq, TILE), bf),
    ]
    return pl.pallas_call(
        forward_kernel,
        out_shape=tuple(jax.ShapeDtypeStruct(shape, dtype) for shape, dtype in made),
        in_specs=[anywhere] * 11,
        out_specs=(anywhere,) * len(made),
        scratch_shapes=[pltpu.VMEM(shape, dtype) for shape, dtype in held]
        + [
            dma((3,)), dma((3,)), dma((4,)), dma((4,)), dma((4,)), dma((4,)),
            dma((4, 5)), dma((12, 4)), dma((12, 5)), dma((8,)), dma((1,)), dma((1,)),
            dma((4,)), dma((4,)), dma((16,)), dma((2, 2)),
        ],
        compiler_params=pltpu.CompilerParams(
            collective_id=0, has_side_effects=True, vmem_limit_bytes=VMEM_LIMIT
        ),
        name="forward",
    )(small, x, ct, wq, wk, wv, wo, w1, w2, gq, gk)


def tn(left, right):
    return lax.dot_general(left, right, (((0,), (0,)), ((), ())), preferred_element_type=jnp.float32)


def backward_kernel(
    vec_ref, x_ref, ct_ref, wa_ref, wob_ref, wb_ref, wc_ref, normed_ref, qkv_ref, mixed_ref, lse_ref, middle_ref,
    second_ref, active_ref, slope_ref, gq_ref, gk_ref,
    block_o, input_o, w2_o, w1_o, q_o, k_o, v_o, o_o, small_o,
    vec, up, big, two, three, wts, dc, db, do, r1c, r2c, zc, r1b, r2b, zb, r1o, r2a, za, kx, gq, gk, lse, half_in, home,
    acc, stage, sums, sums_in, bias_row, dkv,
    ld, us, ur, hs, hr, cs, cr, ss, sr, os, free_x, free_y,
):
    f32, bf = jnp.float32, jnp.bfloat16
    i, z = lax.axis_index("cells"), lax.axis_index("chrom")
    p, c = i // 2, lax.rem(i, 2)
    px, py = lax.rem(p, 2), p // 2
    x_nb, y_nb, core_nb = i + 2 - 4 * px, i + 4 - 8 * py, i + 1 - 2 * c
    p_x, p_y = p + 1 - 2 * px, p + 2 - 4 * py
    seq, feat = up.shape
    half, half_seq, block = feat // 2, seq // 2, seq // LINE
    rows = feat // LINE
    hid = wc_ref.shape[0] // 2
    chunks = seq // TILE
    mesh_id = pl.DeviceIdType.MESH

    barrier = pltpu.get_barrier_semaphore()
    line_ids = [
        (i - c + lax.rem(c + dc_, 2), lax.rem(z + dz, LINE))
        for dc_ in range(2)
        for dz in range(LINE)
        if dc_ or dz
    ]
    for who in line_ids + [(x_nb, z), (y_nb, z)]:
        pl.semaphore_signal(barrier, inc=1, device_id=who, device_id_type=mesh_id)

    loads = {}

    def load(name, pairs):
        n = len(loads)
        copies = [pltpu.make_async_copy(src, dst, ld.at[n, m]) for m, (src, dst) in enumerate(pairs)]
        loads[name] = copies
        for d in copies:
            d.start()

    def loaded(*names):
        for name in names:
            for d in loads[name]:
                d.wait()

    load("ct", [(ct_ref, up)])
    load("marks", [(gk_ref, gk), (gq_ref, gq), (vec_ref, vec), (lse_ref, lse)])
    load("active", [(active_ref, big)])
    load("wc", [(wc_ref, wts)])
    load("mid half", [(middle_ref.at[rows_of(c * half_seq, half_seq), :], home)])
    load("slope", [(slope_ref, db.at[pl.ds(0, seq), :])])
    load("second", [(second_ref, two)])

    def send(src, dst, s, r, who):
        return pltpu.make_async_remote_copy(
            src_ref=src, dst_ref=dst, send_sem=s, recv_sem=r, device_id=who, device_id_type=mesh_id
        )

    class Unit:
        def __init__(self, n, d, col, r, w, r1, r2, zl, parts):
            self.n, self.d, self.col, self.r, self.w = n, d, col, r, w
            self.r1_at, self.r2_at, self.z_at, self.parts = r1, r2, zl, parts

        def region(self, base, row, count=1):
            ref, row0, col0 = base
            return ref.at[rows_of(row0 + row * self.r, count * self.r), pl.ds(col0, self.w)]

        def own(self, s, a, b):
            return self.region((self.d, 0, self.col), (s * 2 + a) * 2 + b)

        def r1(self, side, m, n):
            return self.region(self.r1_at, (side * 2 + m) * 2 + n)

        def r2(self, s):
            return self.region(self.r2_at, s)

        def zl(self, d):
            return self.region(self.z_at, d)

        def sems(self, e):
            return us.at[self.n, e], ur.at[self.n, e]

        def total(self, e, count):
            ref = self.region(self.r1_at, 0, count)
            return send(ref, ref, *self.sems(e), (x_nb, z))

        def step1(self, s):
            for n in range(2):
                if s < 2:
                    send(self.own(s, n, 1 - px), self.r1(0, s, n), *self.sems(0), (x_nb, z)).start()
                else:
                    send(self.own(s, 1 - py, n), self.r1(1, s - 2, n), *self.sems(1), (y_nb, z)).start()

        def step1_all(self):
            for s in (0, 2, 1, 3):
                self.step1(s)

        def add(self, to, *more):
            value = to[...].astype(f32)
            for ref in more:
                value = value + ref[...].astype(f32)
            to[...] = value.astype(bf)

        def step2(self):
            self.total(0, 4).wait_recv()
            for m in range(2):
                for n in range(2):
                    self.add(self.r1(0, m, n), self.own(m, n, px))
                send(self.r1(0, m, 1 - py), self.r2(m), *self.sems(2), (y_nb, z)).start()
            self.total(1, 4).wait_recv()
            for m in range(2):
                for n in range(2):
                    self.add(self.r1(1, m, n), self.own(2 + m, py, n))
                send(self.r1(1, m, 1 - px), self.r2(2 + m), *self.sems(3), (x_nb, z)).start()

        def line(self):
            self.total(2, 2).wait_recv()
            for m in range(2):
                self.add(self.r2(m), self.r1(0, m, py))
            self.total(3, 2).wait_recv()
            for m in range(2):
                self.add(self.r2(2 + m), self.r1(1, m, px))
            for d in range(LINE - 1):
                to = lax.rem(z + d + 1, LINE)
                send(self.r2(to), self.zl(d), *self.sems(4 + d), (i, to)).start()

        def spread(self):
            for d in range(LINE - 1):
                self.total(4 + d, 1).wait_recv()
            self.add(self.r2(z), *[self.zl(d) for d in range(LINE - 1)])
            for off, width, place in self.parts:
                ref, row0, col0 = self.r2_at
                src = ref.at[rows_of(row0 + z * self.r, self.r), pl.ds(col0 + off, width)]
                dst = place(p, 0, width)
                send(src, dst, *self.sems(7), (x_nb, z)).start()
                send(src, dst, *self.sems(8), (y_nb, z)).start()
                pltpu.make_async_copy(src, dst, os.at[self.n]).start()

        def cross(self):
            self.total(7, 1).wait_recv()
            self.total(8, 1).wait_recv()
            for off, width, place in self.parts:
                cut = width // 256 * 128
                left, rest = place(p_x, 0, cut), place(p_y, cut, width - cut)
                send(left, left, *self.sems(9), (y_nb, z)).start()
                send(rest, rest, *self.sems(10), (x_nb, z)).start()

        def crossed(self, e):
            off = 0
            for _, width, _place in self.parts:
                cut = width // 256 * 128
                off += cut if e == 9 else width - cut
            ref, row0, col0 = self.r1_at
            ref = ref.at[rows_of(row0, self.r), pl.ds(col0, off)]
            return send(ref, ref, *self.sems(e), (x_nb, z))

        def to_core(self):
            self.crossed(9).wait_recv()
            self.crossed(10).wait_recv()
            ref = self.region(self.r1_at, 0)
            pltpu.make_async_copy(ref, ref, os.at[self.n]).wait()
            for off, width, place in self.parts:
                mine = place(None, 0, width)
                send(mine, mine, *self.sems(11), (core_nb, z)).start()

        def step2_sent(self):
            self.total(2, 2).wait_send()
            self.total(3, 2).wait_send()

        def end(self):
            self.total(11, 4).wait()
            for e in range(4, 9):
                self.total(e, 1).wait_send()
            self.crossed(9).wait_send()
            self.crossed(10).wait_send()

        def step1_sent(self):
            self.total(0, 4).wait_send()
            self.total(1, 4).wait_send()

    def place_w2(at, off, width):
        first, count = (0, half) if at is None else (at * (hid // 2 // PLANE), hid // 2 // PLANE)
        return w2_o.at[rows_of(c * (hid // 2) + first, count), pl.ds(off, width)]

    def place_w1(n):
        def place(at, off, width):
            first, count = (0, rows) if at is None else (at * (rows // PLANE), rows // PLANE)
            return w1_o.at[rows_of(first, count), cols_of(n * hid + c * (hid // 2) + off, width)]

        return place

    def place_of(ref):
        def place(at, off, width):
            first, count = (0, rows) if at is None else (at * (rows // PLANE), rows // PLANE)
            return ref.at[rows_of(first, count), cols_of(c * half + off, width)]

        return place

    r_big, r_small = hid // 2 // PLANE, rows // PLANE
    unit_c = Unit(0, dc, 0, r_big, feat, (r1c, 0, 0), (r2c, 0, 0), (zc, 0, 0), [(0, feat, place_w2)])
    unit_b = [
        Unit(
            1 + n, db, n * hid, r_small, hid, (r1b, 0, n * hid), (r2b, 0, n * hid), (zb, 0, n * hid),
            [(m * (hid // 2), hid // 2, place_w1(2 * n + m)) for m in range(2)],
        )
        for n in range(2)
    ]
    unit_o = Unit(3, do, 0, r_small, half, (r1o, 0, 0), (r2a, 0, 0), (za, 0, 0), [(0, half, place_of(o_o))])
    spots = ((0, 0), (0, half), (8 * r_small, 0))
    unit_a = [
        Unit(
            4 + n, db, n * half, r_small, half, (r1c,) + spots[n], (r2a, 0, (1 + n) * half), (za, 0, (1 + n) * half),
            [(0, half, place_of(ref))],
        )
        for n, ref in enumerate((q_o, k_o, v_o))
    ]

    def going_home(src, dst, e):
        stay = c == z // 2
        mine, outs = None, []
        for k in range(2):
            b = lax.rem(z + k, 2)
            part = src.at[rows_of(b * block, block), :]
            to = dst.at[lax.rem(z, 2)]
            outs.append(send(part, to, hs.at[e, k], hr.at[e, k], (i - c + z // 2, 2 * c + b)))
            if k == 0:
                mine = pltpu.make_async_copy(part, to, hr.at[e, k])

        def start():
            pl.when(stay)(mine.start)
            pl.when(jnp.logical_not(stay))(outs[0].start)
            outs[1].start()

        def sent():
            pl.when(stay)(mine.wait)
            pl.when(jnp.logical_not(stay))(outs[0].wait_send)
            outs[1].wait_send()

        def arrived():
            pl.when(jnp.logical_not(stay))(outs[0].wait_recv)
            outs[1].wait_recv()

        return start, sent, arrived

    block_start, block_sent, block_arrived = going_home(home, block_o, 0)
    input_start, input_sent, input_arrived = going_home(home, input_o, 1)

    sums[0] = jnp.zeros(sums.shape[1:], f32)
    loaded("ct", "marks")

    def mask_rows(n, total):
        at = pl.ds(pl.multiple_of(n * TILE, TILE), TILE)
        gone = gk[at, 127:128].astype(f32) < 0.0
        value = jnp.where(gone, 0.0, up[at, :].astype(f32))
        up[at, :] = value.astype(bf)
        return total + jnp.sum(value, axis=0, keepdims=True)

    up_sum = lax.fori_loop(0, chunks, mask_rows, jnp.zeros((1, feat), f32))
    first_core = jnp.where(c == 0, 1.0, 0.0)
    sums[0, 7:8, :] = up_sum * first_core
    loaded("active")
    pl.semaphore_wait(barrier, len(line_ids) + 2)
    wide = hid // 2
    for s in (0, 2, 1, 3):
        dc[s * wide : (s + 1) * wide, :] = tn(big[:, s * wide : (s + 1) * wide], up[...]).astype(bf)
        unit_c.step1(s)

    loaded("wc", "mid half")
    swaps = []
    for n in range(half_seq // TILE):
        at = rows_of((1 - c) * half_seq + n * TILE, TILE)
        to = pl.ds(n * TILE, TILE)
        got = nn(big[at, :], wts[...]).astype(bf)
        for m in range(2):
            held = pl.ds(m * half_seq + n * TILE, TILE)
            do[held, :] = got[:, m * half : (m + 1) * half]
            send(
                do.at[held, :], half_in.at[to, pl.ds(m * half, half)], cs.at[n], cr.at[n], (core_nb, z)
            ).start()
        swaps.append(send(half_in.at[to, :], half_in.at[to, :], cs.at[n], cr.at[n], (core_nb, z)))
    for n in range(half_seq // TILE):
        at = rows_of(c * half_seq + n * TILE, TILE)
        to = pl.ds(n * TILE, TILE)
        acc[...] = nn(big[at, :], wts[...])
        swaps[n].wait_recv()
        gone = gk[at, 127:128].astype(f32) < 0.0
        value = home[to, :].astype(f32) + acc[...] + half_in[to, :].astype(f32) + vec[7:8, :]
        home[to, :] = jnp.where(gone, 0.0, value).astype(bf)
    block_start()

    loaded("slope")

    def inner_tile(n, _):
        cols = pl.ds(pl.multiple_of(n * TILE, TILE), TILE)
        got = (nt(up[...], wts[cols, :]) * db[pl.ds(0, seq), cols].astype(f32)).astype(bf)
        big[:, cols] = got
        bias_row[:, cols] = jnp.sum(got.astype(f32), axis=0, keepdims=True)
        return _

    lax.fori_loop(0, 2 * hid // TILE, inner_tile, 0)
    for s in range(LINE):
        sums[0, 8 + s : 9 + s, cols_of(c * wide, wide)] = bias_row[:, s * wide : (s + 1) * wide]
    load("wb", [(wb_ref.at[:, pl.ds(n * hid, hid)], wts.at[pl.ds(n * feat, feat), :]) for n in range(2)])
    loaded("second")
    for n in range(2):

        def inner_rows(m, _, n=n):
            at = pl.ds(pl.multiple_of(m * TILE, TILE), TILE)
            db[at, pl.ds(n * hid, hid)] = tn(two[:, at], big[:, pl.ds(n * hid, hid)]).astype(bf)
            return _

        lax.fori_loop(0, feat // TILE, inner_rows, 0)
        unit_b[n].step1_all()

    loaded("wb")
    for d in swaps:
        d.wait_send()
    gs_swaps = []
    for n in range(chunks):
        at = pl.ds(n * TILE, TILE)
        two[at, :] = (nt(big[at, pl.ds(0, hid)], wts[pl.ds(0, feat), :]) + nt(big[at, pl.ds(hid, hid)], wts[pl.ds(feat, feat), :])).astype(bf)
        d = send(two.at[at, :], three.at[at, :], cs.at[2 + n], cr.at[2 + n], (core_nb, z))
        d.start()
        gs_swaps.append(d)
    load("qkv", [(qkv_ref, big.at[:, pl.ds(0, 3 * half)]), (mixed_ref, big.at[:, pl.ds(3 * half, half)])])
    load(
        "wa",
        [
            (wa_ref.at[:, pl.ds(0, feat)], wts.at[pl.ds(0, feat), :]),
            (wa_ref.at[:, pl.ds(feat, half)], wts.at[pl.ds(feat, feat), pl.ds(0, half)]),
            (wob_ref.at[:, pl.ds(0, half)], wts.at[pl.ds(feat, half), pl.ds(half, half)]),
            (wob_ref.at[:, pl.ds(half, half)], wts.at[pl.ds(feat + half, half), pl.ds(half, half)]),
        ],
    )
    unit_c.step2()
    unit_c.step1_sent()
    load("middle", [(middle_ref, dc.at[pl.ds(0, seq), :])])
    loaded("middle")

    def back_rows(n, carry):
        gain_sum, shift_sum, out_sum = carry
        at = pl.ds(pl.multiple_of(n * 64, 64), 64)
        g = two[at, :].astype(f32) + three[at, :].astype(f32)
        center, r = moments(dc[at, :].astype(f32))
        hat = center * r
        gh = g * hat
        h = g * vec[5:6, :]
        first = jnp.mean(h, axis=-1, keepdims=True)
        slant = jnp.mean(h * hat, axis=-1, keepdims=True)
        got = (up[at, :].astype(f32) + r * (h - first - hat * slant)).astype(bf)
        two[at, :] = got
        return (
            gain_sum + jnp.sum(gh, axis=0, keepdims=True),
            shift_sum + jnp.sum(g, axis=0, keepdims=True),
            out_sum + jnp.sum(got.astype(f32), axis=0, keepdims=True),
        )

    zero_row = jnp.zeros((1, feat), f32)
    carry = (zero_row, zero_row, zero_row)
    for n in range(chunks):
        gs_swaps[n].wait()
        carry = lax.fori_loop(n * TILE // 64, (n + 1) * TILE // 64, back_rows, carry)
    sums[0, 5:6, :] = carry[0] * first_core
    sums[0, 6:7, :] = carry[1] * first_core
    sums[0, 4:5, :] = carry[2] * first_core
    load("normed", [(normed_ref, three)])
    load("x", [(x_ref.at[rows_of(c * half_seq, half_seq), :], up.at[pl.ds(0, half_seq), :])])

    loaded("qkv", "wa")
    stage[...] = tn(big[:, pl.ds(3 * half, half)], two[:, cols_of((1 - c) * half, half)]).astype(bf)
    o_swap = send(stage, do.at[rows_of(c * half, half), :], cs.at[6], cr.at[6], (core_nb, z))
    o_swap.start()
    do[rows_of(c * half, half), :] = tn(big[:, pl.ds(3 * half, half)], two[:, cols_of(c * half, half)]).astype(bf)
    o_swap.wait_recv()
    unit_o.step1_all()
    grad_mixed = (pl.ds(seq, seq), half)
    for n in range(chunks):
        at = pl.ds(n * TILE, TILE)
        dc[pl.ds(seq + n * TILE, TILE), pl.ds(half, half)] = (
            nt(two[at, pl.ds(0, half)], wts[pl.ds(feat, half), pl.ds(half, half)])
            + nt(two[at, pl.ds(half, half)], wts[pl.ds(feat + half, half), pl.ds(half, half)])
        ).astype(bf)
    kx[:, 128:] = gk[...]

    lane = lax.broadcasted_iota(jnp.int32, (TILE, 128), 1)
    root = HEAD_DIM ** (-0.5)

    def attend_back(t):
        k2 = big[:, pl.ds(half + t * 128, 128)]
        k2t = jnp.transpose(k2)
        kx[:, :128] = k2
        dkv[...] = jnp.zeros(dkv.shape, f32)

        def chunk(n, _):
            at = pl.ds(pl.multiple_of(n * TILE, TILE), TILE)
            g_at = pl.ds(pl.multiple_of(seq + n * TILE, TILE), TILE)
            q2 = big[at, pl.ds(t * 128, 128)] * jnp.array(root, bf)
            g2 = dc[g_at, pl.ds(half + t * 128, 128)]
            both = []
            for h in range(2):
                own = lane < HEAD_DIM if h == 0 else lane >= HEAD_DIM
                qm = jnp.where(own, q2, jnp.zeros((), bf))
                gm = jnp.where(own, g2, jnp.zeros((), bf))
                s = nt(kx[...], jnp.concatenate([qm, gq[at, :]], axis=1))
                prob = jnp.exp(s - lse[2 * t + h : 2 * t + h + 1, at])
                grad = nt(big[:, pl.ds(2 * half + t * 128, 128)], gm)
                both_of = prob * grad
                dot = jnp.sum(both_of, axis=0, keepdims=True)
                ds = (both_of - prob * dot).astype(bf)
                dkv[0] += nn(ds, qm)
                dkv[1] += nn(prob.astype(bf), gm)
                both.append(nn(k2t[h * HEAD_DIM : (h + 1) * HEAD_DIM, :], ds))
            dc[at, pl.ds(t * 128, 128)] = (jnp.transpose(jnp.concatenate(both, axis=0)) * root).astype(bf)
            return _

        lax.fori_loop(0, chunks, chunk, 0)
        dc[pl.ds(0, seq), pl.ds(half + t * 128, 128)] = dkv[0].astype(bf)
        dc[pl.ds(seq, seq), pl.ds(t * 128, 128)] = dkv[1].astype(bf)

    attend_back(0)
    unit_b[0].step2()
    attend_back(1)
    unit_c.line()
    unit_c.step2_sent()
    pl.semaphore_signal(free_x, inc=1, device_id=(x_nb, z), device_id_type=mesh_id)
    pl.semaphore_signal(free_y, inc=1, device_id=(y_nb, z), device_id_type=mesh_id)
    attend_back(2)
    unit_b[1].step2()
    unit_o.step2()
    attend_back(3)
    unit_b[0].line()
    attend_back(4)
    unit_b[1].line()
    unit_o.line()
    sums[0, 2:3, cols_of(c * half, half)] = jnp.sum(dc[pl.ds(0, seq), pl.ds(0, half)].astype(f32), axis=0, keepdims=True)
    sums[0, 3:4, cols_of(c * half, half)] = jnp.sum(dc[pl.ds(seq, seq), pl.ds(0, half)].astype(f32), axis=0, keepdims=True)

    loaded("normed")
    for u in unit_b:
        u.step1_sent()

    def qk_rows(m, _):
        at = pl.ds(pl.multiple_of(m * TILE, TILE), TILE)
        db[at, pl.ds(0, feat)] = tn(three[:, at], dc[pl.ds(0, seq), :]).astype(bf)
        return _

    def v_rows(m, _):
        at = pl.ds(pl.multiple_of(m * TILE, TILE), TILE)
        db[at, pl.ds(feat, half)] = tn(three[:, at], dc[pl.ds(seq, seq), pl.ds(0, half)]).astype(bf)
        return _

    lax.fori_loop(0, feat // TILE, qk_rows, 0)
    pl.semaphore_wait(free_x, 1)
    pl.semaphore_wait(free_y, 1)
    unit_a[0].step1_all()
    unit_a[1].step1_all()
    lax.fori_loop(0, feat // TILE, v_rows, 0)
    unit_a[2].step1_all()
    unit_c.spread()

    def first_part(at):
        at_v = rows_of(at + seq, TILE)
        return nt(dc[rows_of(at, TILE), :], wts[pl.ds(0, feat), :]) + nt(
            dc[at_v, pl.ds(0, half)], wts[pl.ds(feat, feat), pl.ds(0, half)]
        )

    loaded("x")
    gn_swaps = []
    for n in range(half_seq // TILE):
        to = pl.ds(half_seq + n * TILE, TILE)
        up[to, :] = first_part((1 - c) * half_seq + n * TILE).astype(bf)
        d = send(up.at[to, :], half_in.at[pl.ds(n * TILE, TILE), :], cs.at[7 + n], cr.at[7 + n], (core_nb, z))
        d.start()
        gn_swaps.append(d)
    unit_c.cross()
    block_sent()
    carry = (zero_row, zero_row)
    for n in range(half_seq // TILE):
        acc[...] = first_part(c * half_seq + n * TILE)
        gn_swaps[n].wait_recv()

        def first_rows(m, carry, n=n):
            gain_sum, shift_sum = carry
            at = pl.ds(pl.multiple_of(m * 64, 64), 64)
            here = pl.ds(pl.multiple_of(n * TILE + m * 64, 64), 64)
            g = acc[at, :] + half_in[here, :].astype(f32)
            center, r = moments(up[here, :].astype(f32))
            hat = center * r
            gh = g * hat
            h = g * vec[0:1, :]
            first = jnp.mean(h, axis=-1, keepdims=True)
            slant = jnp.mean(h * hat, axis=-1, keepdims=True)
            got = two[rows_of(c * half_seq + n * TILE + m * 64, 64), :].astype(f32) + r * (h - first - hat * slant)
            home[here, :] = got.astype(bf)
            return (
                gain_sum + jnp.sum(gh, axis=0, keepdims=True),
                shift_sum + jnp.sum(g, axis=0, keepdims=True),
            )

        carry = lax.fori_loop(0, TILE // 64, first_rows, carry)
    sums[0, 0:1, :] = carry[0]
    sums[0, 1:2, :] = carry[1]
    input_start()

    def small_step(n, who):
        d = send(sums.at[n], sums_in.at[n], ss.at[n], sr.at[n], who)
        d.start()
        return d

    small = [small_step(0, (core_nb, z))]
    unit_b[0].spread()
    unit_c.to_core()
    small[0].wait_recv()
    sums[1] = sums[0] + sums_in[0]
    small.append(small_step(1, (x_nb, z)))
    unit_b[1].spread()
    unit_a[0].step2()
    unit_b[0].cross()
    small[1].wait_recv()
    sums[2] = sums[1] + sums_in[1]
    small.append(small_step(2, (y_nb, z)))
    unit_a[1].step2()
    unit_b[1].cross()
    unit_o.spread()
    small[2].wait_recv()
    sums[3] = sums[2] + sums_in[2]
    for d in range(LINE - 1):
        small.append(
            send(sums.at[3], sums_in.at[3 + d], ss.at[3 + d], sr.at[3 + d], (i, lax.rem(z + d + 1, LINE)))
        )
        small[-1].start()
    unit_a[2].step2()
    unit_b[0].to_core()
    unit_a[0].line()
    unit_b[1].to_core()
    unit_o.cross()
    unit_a[1].line()
    for d in range(LINE - 1):
        small[3 + d].wait_recv()
    sums[4] = sums[3] + ((sums_in[3] + sums_in[4]) + sums_in[5])
    small_out = pltpu.make_async_copy(sums.at[4], small_o, os.at[7])
    small_out.start()
    unit_a[2].line()
    unit_o.to_core()
    unit_a[0].spread()
    unit_a[1].spread()
    unit_a[0].cross()
    unit_a[2].spread()
    unit_a[1].cross()
    unit_a[0].to_core()
    unit_a[2].cross()
    unit_a[1].to_core()
    unit_a[2].to_core()
    small_out.wait()
    for d in small + gn_swaps + [o_swap]:
        d.wait_send()
    input_sent()
    block_arrived()
    input_arrived()
    units = [unit_c] + unit_b + [unit_o] + unit_a
    for u in units[1:]:
        u.step2_sent()
    for u in [unit_o] + unit_a:
        u.step1_sent()
    for u in units:
        u.end()


def run_backward(vec, x, ct, wa, wob, wb, wc, normed, qkv, mixed, lse, middle, second, active, slope, gq, gk):
    seq, feat = x.shape
    half = feat // 2
    hid = wc.shape[0] // 2
    rows = feat // LINE
    r_big, r_small = hid // 2 // PLANE, rows // PLANE
    f32, bf = jnp.float32, jnp.bfloat16
    dma = pltpu.SemaphoreType.DMA
    anywhere = pl.BlockSpec(memory_space=pl.ANY)
    made = [
        ((2, seq // LINE, feat), bf), ((2, seq // LINE, feat), bf), ((hid, feat), bf), ((rows, LINE * hid), bf),
        ((rows, feat), bf), ((rows, feat), bf), ((rows, feat), bf), ((rows, feat), bf), ((16, feat), f32),
    ]
    held = [
        (vec.shape, f32), ((seq, feat), bf), ((seq, 2 * hid), bf), ((seq, feat), bf), ((seq, feat), bf),
        ((2 * hid, feat), bf), ((2 * hid, feat), bf), ((feat, 2 * hid), bf), ((feat, half), bf),
        ((8 * r_big, feat), bf), ((4 * r_big, feat), bf), ((3 * r_big, feat), bf),
        ((8 * r_small, 2 * hid), bf), ((4 * r_small, 2 * hid), bf), ((3 * r_small, 2 * hid), bf),
        ((8 * r_small, half), bf), ((4 * r_small, 4 * half), bf), ((3 * r_small, 4 * half), bf),
        ((seq, 256), bf), ((seq, 128), bf), ((seq, 128), bf), ((16, seq), f32),
        ((seq // 2, feat), bf), ((seq // 2, feat), bf), ((TILE, feat), f32), ((half, half), bf),
        ((5, 16, feat), f32), ((6, 16, feat), f32), ((1, 2 * hid), f32), ((2, seq, 128), f32),
    ]
    return pl.pallas_call(
        backward_kernel,
        out_shape=tuple(jax.ShapeDtypeStruct(shape, dtype) for shape, dtype in made),
        in_specs=[anywhere] * 17,
        out_specs=(anywhere,) * len(made),
        scratch_shapes=[pltpu.VMEM(shape, dtype) for shape, dtype in held]
        + [
            dma((14, 4)), dma((7, 12)), dma((7, 12)), dma((2, 2)), dma((2, 2)), dma((9,)), dma((9,)), dma((6,)), dma((6,)),
            dma((8,)), pltpu.SemaphoreType.REGULAR, pltpu.SemaphoreType.REGULAR,
        ],
        compiler_params=pltpu.CompilerParams(
            collective_id=1, has_side_effects=True, vmem_limit_bytes=VMEM_LIMIT
        ),
        name="backward",
    )(vec, x, ct, wa, wob, wb, wc, normed, qkv, mixed, lse, middle, second, active, slope, gq, gk)


def flip(value, step):
    count = lax.axis_size("cells")
    return lax.ppermute(value, "cells", [(n, n ^ step) for n in range(count)])


def take(value, index, axis):
    return lax.dynamic_index_in_dim(value, index, axis, keepdims=False)


def paired_local(
    inputs, lengths, offsets, cotangent, norm_gain, norm_shift, query_proj, query_bias, key_proj, value_proj,
    value_bias, output_proj, output_bias, second_gain, second_shift, inner_proj, inner_bias, outer_proj, outer_bias,
):
    f32, bf = jnp.float32, jnp.bfloat16
    i, z = lax.axis_index("cells"), lax.axis_index("chrom")
    p, c = i // 2, i % 2
    px, py = p % 2, p // 2
    cells_here, block, feat = inputs.shape
    seq = block * LINE
    half_seq, half = seq // 2, feat // 2
    rows = feat // LINE
    hid = outer_proj.shape[0]
    inv_root = HEAD_DIM ** (-0.5)
    heads = HEADS // 2

    vectors = (norm_gain, norm_shift, query_bias, value_bias, output_bias, second_gain, second_shift, outer_bias)
    small = jnp.concatenate([v.reshape(1, rows) for v in vectors] + [inner_bias.reshape(hid // rows, rows)], axis=0)
    small = jnp.pad(small, ((0, 16 - small.shape[0]), (0, 384 - rows)))
    ragged = jnp.concatenate([lengths[:, None], offsets], axis=1)
    other = flip(ragged, 1)
    ragged = take(jnp.where(z // 2 == c, ragged, other), z % 2, 0)
    length, starts = ragged[0], ragged[1:]
    places = jnp.arange(seq, dtype=jnp.int32)
    live = places < length
    groups = jnp.sum((places[:, None] >= starts[None, :]).astype(jnp.int32), axis=1)
    lanes = jnp.arange(128, dtype=jnp.int32)[None, :]
    same = (groups[:, None] == lanes).astype(bf)
    mark_q = jnp.where(lanes == 127, jnp.ones((), bf), same * jnp.array(group_bias, bf))
    mark_k = jnp.where(lanes == 127, jnp.where(live, 0.0, -1e30).astype(bf)[:, None], same)
    (
        vec, xf, cf, wa, wob, wb, wc, normed, qkv, mixed, lse, middle, second, active, slope,
    ) = run_forward(
        small, inputs, cotangent, query_proj, key_proj, value_proj, output_proj, inner_proj, outer_proj, mark_q, mark_k
    )
    block_out, input_grad, w2_grad, w1_grad, q_grad, k_grad, v_grad, o_grad, sums = run_backward(
        vec, xf, cf, wa, wob, wb, wc, normed, qkv, mixed, lse, middle, second, active, slope, mark_q, mark_k
    )

    def shard(n):
        return lax.dynamic_slice_in_dim(sums[n], z * rows, rows, 0)

    inner_bias_grad = take(sums[8:12], z, 0)
    return (
        block_out, input_grad, shard(0), shard(1), q_grad.astype(f32), shard(2), k_grad.astype(f32),
        v_grad.astype(f32), shard(3), o_grad.astype(f32), shard(4), shard(5), shard(6), w1_grad.astype(f32),
        inner_bias_grad, w2_grad.astype(f32), shard(7),
    )


def solution(mesh):
    paired = mesh.shape["chrom"] == 4 and mesh.shape["cells"] == 8
    placed = (
        P("cells", "chrom", None),
        P("cells"),
        P("cells", None),
        P("cells", "chrom", None),
        P("chrom"),
        P("chrom"),
        P("chrom", None),
        P("chrom"),
        P("chrom", None),
        P("chrom", None),
        P("chrom"),
        P("chrom", None),
        P("chrom"),
        P("chrom"),
        P("chrom"),
        P("chrom", None),
        P("chrom"),
        P("chrom", None),
        P("chrom"),
    )
    return jax.shard_map(
        paired_local if paired else general,
        mesh=mesh,
        in_specs=placed,
        out_specs=(
            P("cells", "chrom", None),
            P("cells", "chrom", None),
            P("chrom"),
            P("chrom"),
            P("chrom", None),
            P("chrom"),
            P("chrom", None),
            P("chrom", None),
            P("chrom"),
            P("chrom", None),
            P("chrom"),
            P("chrom"),
            P("chrom"),
            P("chrom", None),
            P("chrom"),
            P("chrom", None),
            P("chrom"),
        ),
        check_vma=False,
    )
```

```python
import functools

import jax
import jax.numpy as jnp
from jax import lax
from jax.experimental import pallas as pl
from jax.experimental.pallas import tpu as pltpu
from jax.sharding import PartitionSpec as P

HEADS = 20
HEAD_DIM = 64


eps_norm = 1e-05
group_bias = 1.0


def layer_norm(values, gain, shift):
    center = values - jnp.mean(values, axis=-1, keepdims=True)
    spread = jnp.mean(center * center, axis=-1, keepdims=True)
    return center * lax.rsqrt(spread + eps_norm) * gain + shift


def gelu_exact(values):
    return jax.nn.gelu(values, approximate=False)


def product(left, right):
    return jnp.dot(left, right, preferred_element_type=jnp.float32)


def left_product(left, right):
    return jnp.einsum("ra,rb->ab", left, right, preferred_element_type=jnp.float32)


def right_back(left, right):
    return jnp.einsum("rb,ab->ra", left, right, preferred_element_type=jnp.float32)


def column_sum(values):
    return jnp.sum(values, axis=0, dtype=jnp.float32)


def split_rows(value, outer, inner_count):
    return value.reshape(
        (outer, inner_count, value.shape[0] // (outer * inner_count)) + value.shape[1:]
    )


def general(
    inputs,
    lengths,
    offsets,
    cotangent,
    norm_gain,
    norm_shift,
    query_proj,
    query_bias,
    key_proj,
    value_proj,
    value_bias,
    output_proj,
    output_bias,
    second_gain,
    second_shift,
    inner_proj,
    inner_bias,
    outer_proj,
    outer_bias,
):
    count_chrom = lax.axis_size("chrom")
    count_cells = lax.axis_size("cells")
    block_index = lax.axis_index("chrom")
    cells_here, tokens_here, feat_width = inputs.shape
    seq_len = tokens_here * count_chrom
    row_count = cells_here * tokens_here
    inv_root = HEAD_DIM ** (-0.5)
    places = jnp.arange(seq_len, dtype=jnp.int32)
    key_live = places[None, :] < lengths[:, None]
    groups = jnp.sum((places[None, :, None] >= offsets[:, None, :]).astype(jnp.int32), axis=2)
    query_groups = lax.dynamic_slice_in_dim(groups, block_index * tokens_here, tokens_here, 1)
    query_live = lax.dynamic_slice_in_dim(key_live, block_index * tokens_here, tokens_here, 1)
    same_group = (query_groups[:, :, None] == groups[:, None, :]).astype(jnp.float32)
    mask_bias = jnp.where(key_live[:, None, :], group_bias * same_group, -jnp.inf)[:, None]
    gathered = (
        lax.all_gather(norm_gain, "chrom", axis=0, tiled=True),
        lax.all_gather(norm_shift, "chrom", axis=0, tiled=True),
        lax.all_gather(query_proj, "chrom", axis=0, tiled=True),
        lax.all_gather(query_bias, "chrom", axis=0, tiled=True),
        lax.all_gather(key_proj, "chrom", axis=0, tiled=True),
        lax.all_gather(value_proj, "chrom", axis=0, tiled=True),
        lax.all_gather(value_bias, "chrom", axis=0, tiled=True),
        lax.all_gather(output_proj, "chrom", axis=0, tiled=True),
        lax.all_gather(output_bias, "chrom", axis=0, tiled=True),
        lax.all_gather(second_gain, "chrom", axis=0, tiled=True),
        lax.all_gather(second_shift, "chrom", axis=0, tiled=True),
        lax.all_gather(inner_proj, "chrom", axis=0, tiled=True),
        lax.all_gather(inner_bias, "chrom", axis=0, tiled=True),
        lax.all_gather(outer_proj, "chrom", axis=0, tiled=True),
        lax.all_gather(outer_bias, "chrom", axis=0, tiled=True),
    )
    gain_one = gathered[0].astype(jnp.float32)
    shift_one = gathered[1].astype(jnp.float32)
    gain_two = gathered[9].astype(jnp.float32)
    shift_two = gathered[10].astype(jnp.float32)
    states = inputs.astype(jnp.float32).reshape(row_count, feat_width)
    normed_full, norm_back = jax.vjp(layer_norm, states, gain_one, shift_one)
    normed = normed_full.astype(jnp.bfloat16)
    queries = (product(normed, gathered[2]) + gathered[3].astype(jnp.float32)).astype(jnp.bfloat16)
    key_rows = product(normed, gathered[4]).astype(jnp.bfloat16)
    vals = (product(normed, gathered[5]) + gathered[6].astype(jnp.float32)).astype(jnp.bfloat16)
    keys_all, vals_all = (
        lax.all_gather(
            key_rows.reshape(cells_here, tokens_here, feat_width), "chrom", axis=1, tiled=True
        ),
        lax.all_gather(
            vals.reshape(cells_here, tokens_here, feat_width), "chrom", axis=1, tiled=True
        ),
    )
    query_heads = queries.reshape(cells_here, tokens_here, HEADS, HEAD_DIM)
    key_heads = keys_all.reshape(cells_here, seq_len, HEADS, HEAD_DIM)
    val_heads = vals_all.reshape(cells_here, seq_len, HEADS, HEAD_DIM)

    def scores_of():
        raw = (
            jnp.einsum(
                "cqhd,ckhd->chqk", query_heads, key_heads, preferred_element_type=jnp.float32
            )
            * inv_root
        )
        return raw + mask_bias

    masked = scores_of()
    row_max = jnp.max(masked, axis=-1, keepdims=True)
    exp_scores = jnp.exp(masked - row_max)
    exp_total = jnp.sum(exp_scores, axis=-1, keepdims=True)
    attn_probs = exp_scores / exp_total
    log_total = row_max + jnp.log(exp_total)
    mixed_out = jnp.einsum(
        "chqk,ckhd->cqhd",
        attn_probs.astype(jnp.bfloat16),
        val_heads,
        preferred_element_type=jnp.float32,
    )
    mixed_out = mixed_out.astype(jnp.bfloat16).reshape(row_count, feat_width)
    attended = product(mixed_out, gathered[7]) + gathered[8].astype(jnp.float32)
    middle = states + attended
    second_full, second_back = jax.vjp(layer_norm, middle, gain_two, shift_two)
    second = second_full.astype(jnp.bfloat16)
    inner_pre = product(second, gathered[11]) + gathered[12].astype(jnp.float32)
    active_full, gelu_back = jax.vjp(gelu_exact, inner_pre)
    active = active_full.astype(jnp.bfloat16)
    result = middle + product(active, gathered[13]) + gathered[14].astype(jnp.float32)
    live_rows = query_live.reshape(row_count, 1)
    block_out = (
        jnp.where(live_rows, result, 0.0)
        .astype(jnp.bfloat16)
        .reshape(cells_here, tokens_here, feat_width)
    )
    upstream = jnp.where(
        live_rows, cotangent.reshape(row_count, feat_width), jnp.zeros((), jnp.bfloat16)
    )
    outer_bias_grad = column_sum(upstream)
    outer_proj_grad = left_product(active, upstream)
    grad_active = right_back(upstream, gathered[13])
    (grad_inner_full,) = gelu_back(grad_active)
    grad_inner = grad_inner_full.astype(jnp.bfloat16)
    inner_bias_grad = column_sum(grad_inner)
    inner_proj_grad = left_product(second, grad_inner)
    grad_second = right_back(grad_inner, gathered[11])
    grad_middle_norm, second_gain_grad, second_shift_grad = second_back(grad_second)
    grad_middle = upstream.astype(jnp.float32) + grad_middle_norm
    grad_attended = grad_middle.astype(jnp.bfloat16)
    output_bias_grad = column_sum(grad_attended)
    output_proj_grad = left_product(mixed_out, grad_attended)
    grad_mixed = right_back(grad_attended, gathered[7]).astype(jnp.bfloat16)
    grad_mixed = grad_mixed.reshape(cells_here, tokens_here, HEADS, HEAD_DIM)
    attn_again = jnp.exp(scores_of() - log_total)
    grad_probs = jnp.einsum(
        "cqhd,ckhd->chqk", grad_mixed, val_heads, preferred_element_type=jnp.float32
    )
    row_dot = jnp.sum(attn_again * grad_probs, axis=-1, keepdims=True)
    grad_raw = (attn_again * (grad_probs - row_dot)).astype(jnp.bfloat16)
    grad_vals_part = jnp.einsum(
        "chqk,cqhd->ckhd",
        attn_again.astype(jnp.bfloat16),
        grad_mixed,
        preferred_element_type=jnp.float32,
    )
    grad_keys_part = (
        jnp.einsum("chqk,cqhd->ckhd", grad_raw, query_heads, preferred_element_type=jnp.float32)
        * inv_root
    )
    grad_queries = (
        jnp.einsum("chqk,ckhd->cqhd", grad_raw, key_heads, preferred_element_type=jnp.float32)
        * inv_root
    ).astype(jnp.bfloat16)
    grad_queries = grad_queries.reshape(row_count, feat_width)
    grad_keys_sum, grad_vals_sum = (
        lax.psum_scatter(
            grad_keys_part.reshape(cells_here, seq_len, feat_width).astype(jnp.bfloat16),
            "chrom",
            scatter_dimension=1,
            tiled=True,
        ).astype(jnp.float32),
        lax.psum_scatter(
            grad_vals_part.reshape(cells_here, seq_len, feat_width).astype(jnp.bfloat16),
            "chrom",
            scatter_dimension=1,
            tiled=True,
        ).astype(jnp.float32),
    )
    grad_keys = grad_keys_sum.astype(jnp.bfloat16).reshape(row_count, feat_width)
    grad_vals = grad_vals_sum.astype(jnp.bfloat16).reshape(row_count, feat_width)
    query_proj_grad = left_product(normed, grad_queries)
    query_bias_grad = column_sum(grad_queries)
    key_proj_grad = left_product(normed, grad_keys)
    value_proj_grad = left_product(normed, grad_vals)
    value_bias_grad = column_sum(grad_vals)
    grad_normed = (
        right_back(grad_queries, gathered[2])
        + right_back(grad_keys, gathered[4])
        + right_back(grad_vals, gathered[5])
    )
    grad_states_norm, norm_gain_grad, norm_shift_grad = norm_back(grad_normed)
    input_grad = (
        (grad_middle + grad_states_norm)
        .astype(jnp.bfloat16)
        .reshape(cells_here, tokens_here, feat_width)
    )
    grad_list = (
        norm_gain_grad,
        norm_shift_grad,
        query_proj_grad,
        query_bias_grad,
        key_proj_grad,
        value_proj_grad,
        value_bias_grad,
        output_proj_grad,
        output_bias_grad,
        second_gain_grad,
        second_shift_grad,
        inner_proj_grad,
        inner_bias_grad,
        outer_proj_grad,
        outer_bias_grad,
    )
    pieces = tuple((split_rows(member, count_chrom, count_cells) for member in grad_list))
    section_one = (
        lax.psum_scatter(
            pieces[0].astype(jnp.bfloat16), "cells", scatter_dimension=1, tiled=True
        ).astype(jnp.float32),
        lax.psum_scatter(
            pieces[1].astype(jnp.bfloat16), "cells", scatter_dimension=1, tiled=True
        ).astype(jnp.float32),
        lax.psum_scatter(
            pieces[2].astype(jnp.bfloat16), "cells", scatter_dimension=1, tiled=True
        ).astype(jnp.float32),
        lax.psum_scatter(
            pieces[3].astype(jnp.bfloat16), "cells", scatter_dimension=1, tiled=True
        ).astype(jnp.float32),
        lax.psum_scatter(
            pieces[4].astype(jnp.bfloat16), "cells", scatter_dimension=1, tiled=True
        ).astype(jnp.float32),
        lax.psum_scatter(
            pieces[5].astype(jnp.bfloat16), "cells", scatter_dimension=1, tiled=True
        ).astype(jnp.float32),
        lax.psum_scatter(
            pieces[6].astype(jnp.bfloat16), "cells", scatter_dimension=1, tiled=True
        ).astype(jnp.float32),
        lax.psum_scatter(
            pieces[7].astype(jnp.bfloat16), "cells", scatter_dimension=1, tiled=True
        ).astype(jnp.float32),
        lax.psum_scatter(
            pieces[8].astype(jnp.bfloat16), "cells", scatter_dimension=1, tiled=True
        ).astype(jnp.float32),
        lax.psum_scatter(
            pieces[9].astype(jnp.bfloat16), "cells", scatter_dimension=1, tiled=True
        ).astype(jnp.float32),
        lax.psum_scatter(
            pieces[10].astype(jnp.bfloat16), "cells", scatter_dimension=1, tiled=True
        ).astype(jnp.float32),
        lax.psum_scatter(
            pieces[11].astype(jnp.bfloat16), "cells", scatter_dimension=1, tiled=True
        ).astype(jnp.float32),
        lax.psum_scatter(
            pieces[12].astype(jnp.bfloat16), "cells", scatter_dimension=1, tiled=True
        ).astype(jnp.float32),
        lax.psum_scatter(
            pieces[13].astype(jnp.bfloat16), "cells", scatter_dimension=1, tiled=True
        ).astype(jnp.float32),
        lax.psum_scatter(
            pieces[14].astype(jnp.bfloat16), "cells", scatter_dimension=1, tiled=True
        ).astype(jnp.float32),
    )
    section_two = (
        lax.psum_scatter(
            section_one[0].astype(jnp.bfloat16), "chrom", scatter_dimension=0, tiled=True
        ).astype(jnp.float32),
        lax.psum_scatter(
            section_one[1].astype(jnp.bfloat16), "chrom", scatter_dimension=0, tiled=True
        ).astype(jnp.float32),
        lax.psum_scatter(
            section_one[2].astype(jnp.bfloat16), "chrom", scatter_dimension=0, tiled=True
        ).astype(jnp.float32),
        lax.psum_scatter(
            section_one[3].astype(jnp.bfloat16), "chrom", scatter_dimension=0, tiled=True
        ).astype(jnp.float32),
        lax.psum_scatter(
            section_one[4].astype(jnp.bfloat16), "chrom", scatter_dimension=0, tiled=True
        ).astype(jnp.float32),
        lax.psum_scatter(
            section_one[5].astype(jnp.bfloat16), "chrom", scatter_dimension=0, tiled=True
        ).astype(jnp.float32),
        lax.psum_scatter(
            section_one[6].astype(jnp.bfloat16), "chrom", scatter_dimension=0, tiled=True
        ).astype(jnp.float32),
        lax.psum_scatter(
            section_one[7].astype(jnp.bfloat16), "chrom", scatter_dimension=0, tiled=True
        ).astype(jnp.float32),
        lax.psum_scatter(
            section_one[8].astype(jnp.bfloat16), "chrom", scatter_dimension=0, tiled=True
        ).astype(jnp.float32),
        lax.psum_scatter(
            section_one[9].astype(jnp.bfloat16), "chrom", scatter_dimension=0, tiled=True
        ).astype(jnp.float32),
        lax.psum_scatter(
            section_one[10].astype(jnp.bfloat16), "chrom", scatter_dimension=0, tiled=True
        ).astype(jnp.float32),
        lax.psum_scatter(
            section_one[11].astype(jnp.bfloat16), "chrom", scatter_dimension=0, tiled=True
        ).astype(jnp.float32),
        lax.psum_scatter(
            section_one[12].astype(jnp.bfloat16), "chrom", scatter_dimension=0, tiled=True
        ).astype(jnp.float32),
        lax.psum_scatter(
            section_one[13].astype(jnp.bfloat16), "chrom", scatter_dimension=0, tiled=True
        ).astype(jnp.float32),
        lax.psum_scatter(
            section_one[14].astype(jnp.bfloat16), "chrom", scatter_dimension=0, tiled=True
        ).astype(jnp.float32),
    )
    rejoined = (
        lax.all_gather(section_two[0].astype(jnp.bfloat16), "cells", axis=1, tiled=True).astype(
            jnp.float32
        ),
        lax.all_gather(section_two[1].astype(jnp.bfloat16), "cells", axis=1, tiled=True).astype(
            jnp.float32
        ),
        lax.all_gather(section_two[2].astype(jnp.bfloat16), "cells", axis=1, tiled=True).astype(
            jnp.float32
        ),
        lax.all_gather(section_two[3].astype(jnp.bfloat16), "cells", axis=1, tiled=True).astype(
            jnp.float32
        ),
        lax.all_gather(section_two[4].astype(jnp.bfloat16), "cells", axis=1, tiled=True).astype(
            jnp.float32
        ),
        lax.all_gather(section_two[5].astype(jnp.bfloat16), "cells", axis=1, tiled=True).astype(
            jnp.float32
        ),
        lax.all_gather(section_two[6].astype(jnp.bfloat16), "cells", axis=1, tiled=True).astype(
            jnp.float32
        ),
        lax.all_gather(section_two[7].astype(jnp.bfloat16), "cells", axis=1, tiled=True).astype(
            jnp.float32
        ),
        lax.all_gather(section_two[8].astype(jnp.bfloat16), "cells", axis=1, tiled=True).astype(
            jnp.float32
        ),
        lax.all_gather(section_two[9].astype(jnp.bfloat16), "cells", axis=1, tiled=True).astype(
            jnp.float32
        ),
        lax.all_gather(section_two[10].astype(jnp.bfloat16), "cells", axis=1, tiled=True).astype(
            jnp.float32
        ),
        lax.all_gather(section_two[11].astype(jnp.bfloat16), "cells", axis=1, tiled=True).astype(
            jnp.float32
        ),
        lax.all_gather(section_two[12].astype(jnp.bfloat16), "cells", axis=1, tiled=True).astype(
            jnp.float32
        ),
        lax.all_gather(section_two[13].astype(jnp.bfloat16), "cells", axis=1, tiled=True).astype(
            jnp.float32
        ),
        lax.all_gather(section_two[14].astype(jnp.bfloat16), "cells", axis=1, tiled=True).astype(
            jnp.float32
        ),
    )
    final = tuple(
        (
            member.reshape(
                (member.shape[0] * member.shape[1] * member.shape[2],) + member.shape[3:]
            )
            for member in rejoined
        )
    )
    return (block_out, input_grad) + tuple(final)


PLANE = 4
LINE = 4
VMEM_LIMIT = 62 * 1024 * 1024


def rows_of(start, count):
    return pl.ds(pl.multiple_of(start, 16), count)


def cols_of(start, count):
    return pl.ds(pl.multiple_of(start, 128), count)


VECTORS = 8
TILE = 256


def nt(left, right):
    return lax.dot_general(left, right, (((1,), (1,)), ((), ())), preferred_element_type=jnp.float32)


def nn(left, right):
    return jnp.dot(left, right, preferred_element_type=jnp.float32)


def moments(values):
    center = values - jnp.mean(values, axis=-1, keepdims=True)
    spread = jnp.mean(center * center, axis=-1, keepdims=True)
    return center, lax.rsqrt(spread + eps_norm)


def gelu_and_slope(u):
    gauss = jnp.exp(u * u * -0.5)
    t = 1.0 / (1.0 + jnp.abs(u) * (0.3275911 * 0.5 ** 0.5))
    poly = 0.5 * 1.061405429
    for factor in (-1.453152027, 1.421413741, -0.284496736, 0.254829592):
        poly = poly * t + 0.5 * factor
    tail = poly * t * gauss
    phi_sum = jnp.where(u < 0.0, tail, 1.0 - tail)
    return u * phi_sum, phi_sum + u * gauss * 0.3989422804014327


def forward_kernel(
    small_ref, rag_ref, x_ref, ct_ref, wq_ref, wk_ref, wv_ref, wo_ref, w1_ref, w2_ref,
    gq_o, gk_o, vec_o, x_o, ct_o, wa_o, wob_o, wb_o, wc, normed_o, qkv_o, mixed_o, lse_o, middle_o, second_o, active_o, slope_o,
    smalls, rag, vec, bias_in, xf, cf, wa, wol, wob, wb, normed, qkv, gq, gk, kx, mixed, lse, part, part_in, middle, second,
    act, slp,
    sm_s, sm_r, ex_s, ex_r, fw_s, fw_r, ln_s, un_s, un_r, loc, wo_s, wo_r, pa_s, pa_r, out_s, act_s,
):
    f32, bf = jnp.float32, jnp.bfloat16
    i, z = lax.axis_index("cells"), lax.axis_index("chrom")
    p, c = i // 2, lax.rem(i, 2)
    px, py = lax.rem(p, 2), p // 2
    x_nb, y_nb, core_nb = i + 2 - 4 * px, i + 4 - 8 * py, i + 1 - 2 * c
    p_x, p_y = p + 1 - 2 * px, p + 2 - 4 * py
    rows = wq_ref.shape[0]
    feat = wq_ref.shape[1]
    half = feat // 2
    hid = w2_ref.shape[0]
    block = x_ref.shape[1]
    seq = block * LINE
    part_rows, hid_part = rows // PLANE, hid // 2 // PLANE

    barrier = pltpu.get_barrier_semaphore()
    line_ids = [
        (i - c + lax.rem(c + dc, 2), lax.rem(z + dz, LINE))
        for dc in range(2)
        for dz in range(LINE)
        if dc or dz
    ]
    for who in line_ids + [(x_nb, z), (y_nb, z)]:
        pl.semaphore_signal(barrier, inc=1, device_id=who, device_id_type=pl.DeviceIdType.MESH)
    pl.semaphore_wait(barrier, len(line_ids) + 2)

    def send(src, dst, s, r, who):
        return pltpu.make_async_remote_copy(
            src_ref=src, dst_ref=dst, send_sem=s, recv_sem=r, device_id=who,
            device_id_type=pl.DeviceIdType.MESH,
        )

    small_own = pltpu.make_async_copy(small_ref, smalls.at[z], loc.at[0])
    small_out = [
        send(small_ref, smalls.at[z], sm_s.at[d], sm_r.at[d], (i, lax.rem(z + d + 1, LINE)))
        for d in range(LINE - 1)
    ]

    rag_own = pltpu.make_async_copy(rag_ref.at[lax.rem(z, 2)], rag.at[0], loc.at[6])
    rag_out = send(rag_ref.at[lax.rem(z, 2)], rag.at[1], wo_s.at[1], wo_r.at[1], (core_nb, z))

    def exchange(src, dst, which):
        stay = c == z // 2
        mine, outs = None, []
        for k in range(2):
            j = lax.rem(z + k, 2)
            to = dst.at[rows_of(z * block, block), :]
            r = ex_r.at[2 * which + k]
            outs.append(send(src.at[j], to, ex_s.at[2 * which + k], r, (i - c + z // 2, 2 * c + j)))
            if k == 0:
                mine = pltpu.make_async_copy(src.at[j], to, r)

        def start():
            pl.when(stay)(mine.start)
            pl.when(jnp.logical_not(stay))(outs[0].start)
            outs[1].start()

        def arrived():
            pl.when(stay)(mine.wait)
            pl.when(jnp.logical_not(stay))(outs[0].wait_recv)
            outs[1].wait_recv()

        def sent():
            pl.when(jnp.logical_not(stay))(outs[0].wait_send)
            outs[1].wait_send()

        return start, arrived, sent

    def forward(dst, which):
        return [
            send(
                dst.at[rows_of((2 * c + b) * block, block), :],
                dst.at[rows_of((2 * c + b) * block, block), :],
                fw_s.at[2 * which + b], fw_r.at[2 * which + b], (core_nb, z),
            )
            for b in range(2)
        ]

    x_start, x_arrived, x_sent = exchange(x_ref, xf, 0)
    c_start, c_arrived, c_sent = exchange(ct_ref, cf, 1)
    x_fw, c_fw = forward(xf, 0), forward(cf, 1)

    lands = (wa, wol, wb, wc)
    groups = range(4)
    partner, inner = z + 1 - 2 * lax.rem(z, 2), 3 - z
    low = z < 2
    middle_chip = jnp.logical_or(z == 1, z == 2)
    slot_shard = (partner, jnp.where(low, 2, 1), jnp.where(low, 3, 0))

    def own_parts(g, row, count):
        if g == 0:
            return [
                (ref.at[rows_of(row, count), cols_of(c * half, half)], pl.ds(n * half, half))
                for n, ref in enumerate((wq_ref, wk_ref, wv_ref))
            ]
        if g == 1:
            return [(wo_ref.at[rows_of(row, count), cols_of(c * half, half)], pl.ds(0, half))]
        if g == 2:
            return [
                (w1_ref.at[rows_of(row, count), cols_of(n * hid + c * (hid // 2), hid // 2)], pl.ds(n * (hid // 2), hid // 2))
                for n in range(LINE)
            ]
        return [(w2_ref.at[rows_of(c * (hid // 2) + row, count), :], pl.ds(0, feat))]

    def shape_of(g):
        return (rows, part_rows) if g < 3 else (hid // 2, hid_part)

    def piece(g, s, at):
        shard, count = shape_of(g)
        return lands[g].at[rows_of(s * shard + at * count, count), :]

    def half_piece(g, s, at, side):
        shard, count = shape_of(g)
        width = lands[g].shape[1]
        cut = width // 256 * 128
        cols = pl.ds(cut, width - cut) if side else pl.ds(0, cut)
        return lands[g].at[rows_of(s * shard + at * count, count), cols]

    def line_send(g, s, slot, e, to):
        return send(piece(g, s, p), piece(g, s, p), ln_s.at[g, e], un_r.at[3 * g + slot, 0], (i, to))

    def first(g):
        shard, count = shape_of(g)
        for src, cols in own_parts(g, p * count, count):
            dst = lands[g].at[rows_of(z * shard + p * count, count), cols]
            send(src, dst, ln_s.at[g, 0], un_r.at[3 * g, 0], (i, partner)).start()

        @pl.when(middle_chip)
        def _():
            for src, cols in own_parts(g, p * count, count):
                dst = lands[g].at[rows_of(z * shard + p * count, count), cols]
                send(src, dst, ln_s.at[g, 1], un_r.at[3 * g + 1, 0], (i, inner)).start()

    def passing(g, slot):
        if slot == 0:
            return line_send(g, slot_shard[0], 2, 2, inner)
        return line_send(g, slot_shard[slot], slot, 2 + slot, partner)

    def spread(g, slot):
        own = piece(g, slot_shard[slot], p)
        u = 3 * g + slot
        return [
            send(own, own, un_s.at[u, 0], un_r.at[u, 1], (x_nb, z)),
            send(own, own, un_s.at[u, 1], un_r.at[u, 2], (y_nb, z)),
        ]

    def cross(g, slot):
        u = 3 * g + slot
        left = half_piece(g, slot_shard[slot], p_x, 0)
        rest = half_piece(g, slot_shard[slot], p_y, 1)
        return [
            send(left, left, un_s.at[u, 2], un_r.at[u, 3], (y_nb, z)),
            send(rest, rest, un_s.at[u, 3], un_r.at[u, 4], (x_nb, z)),
        ]

    def land(g, slot):
        line_send(g, slot_shard[slot], slot, 0, partner).wait_recv()
        pl.when(middle_chip)(passing(g, slot).start)
        for d in spread(g, slot):
            d.start()

    def turn(g, slot):
        for d in spread(g, slot):
            d.wait_recv()
        for d in cross(g, slot):
            d.start()

    def own_start(g):
        shard, _ = shape_of(g)
        for src, cols in own_parts(g, 0, shard):
            to = second.at[pl.ds(0, shard), :] if g == 3 else lands[g].at[rows_of(z * shard, shard), cols]
            pltpu.make_async_copy(src, to, loc.at[1 + g]).start()

    def own_wait(g):
        shard, _ = shape_of(g)
        ref = second.at[pl.ds(0, shard), :] if g == 3 else lands[g].at[rows_of(z * shard, shard), :]
        pltpu.make_async_copy(ref, ref, loc.at[1 + g]).wait()

    def whole(g):
        for slot in range(3):
            for d in cross(g, slot):
                d.wait_recv()
        if g < 3:
            own_wait(g)

    def all_sent(g):
        line_send(g, z, 0, 0, partner).wait_send()

        @pl.when(middle_chip)
        def _():
            line_send(g, z, 1, 1, inner).wait_send()
            for slot in range(3):
                passing(g, slot).wait_send()

        for slot in range(3):
            for d in spread(g, slot) + cross(g, slot):
                d.wait_send()

    outs = []

    def keep(src, dst):
        d = pltpu.make_async_copy(src, dst, out_s.at[len(outs)])
        d.start()
        outs.append(d)

    def begin():
        small_own.start()
        rag_own.start()
        rag_out.start()
        for d in small_out:
            d.start()

    def vectors():
        small_own.wait()
        for d in small_out:
            d.wait()
        width = smalls.shape[2]
        total = jnp.zeros((smalls.shape[1], feat), f32)
        at = lax.broadcasted_iota(jnp.int32, (width, feat), 0)
        to = lax.broadcasted_iota(jnp.int32, (width, feat), 1)
        for s in range(LINE):
            place = jnp.where(jnp.logical_and(at < rows, to == at + s * rows), 1.0, 0.0).astype(bf)
            total += nn(smalls[s], place)
        vec[...] = total
        at = lax.broadcasted_iota(jnp.int32, (width, hid // 2), 0)
        to = lax.broadcasted_iota(jnp.int32, (width, hid // 2), 1)
        which = lax.broadcasted_iota(jnp.int32, (smalls.shape[1], hid // 2), 0)
        for s in range(LINE):
            line_bias = jnp.zeros((1, hid // 2), f32)
            for n in range(hid // 2 // rows):
                place = jnp.where(jnp.logical_and(at < rows, to == at + n * rows), 1.0, 0.0).astype(bf)
                picked = jnp.where(which == VECTORS + c * (hid // 2 // rows) + n, nn(smalls[s], place), 0.0)
                line_bias += jnp.sum(picked, axis=0, keepdims=True)
            bias_in[:, pl.ds(s * (hid // 2), hid // 2)] = line_bias
        keep(vec, vec_o)

        rag_own.wait()
        rag_out.wait()
        bounds = jnp.where(c == z // 2, rag[0], rag[1])
        lanes = lax.broadcasted_iota(jnp.int32, (TILE, 128), 1)
        for n in range(seq // TILE):
            at = pl.ds(n * TILE, TILE)
            token = lax.broadcasted_iota(jnp.int32, (TILE, 128), 0) + n * TILE
            same = jnp.logical_and(token >= bounds[0:1, :], token < bounds[1:2, :])
            dead = jnp.where(token < bounds[2:3, :], 0.0, -1e30)
            gq[at, :] = jnp.where(lanes == 127, 1.0, jnp.where(same, group_bias, 0.0)).astype(bf)
            gk[at, :] = jnp.where(lanes == 127, dead, jnp.where(same, 1.0, 0.0)).astype(bf)
        kx[:, 128:] = gk[...]
        keep(gq, gq_o)
        keep(gk, gk_o)

    def x_spread():
        x_arrived()
        for d in x_fw:
            d.start()

    def norm_rows(n, _):
        at = pl.ds(pl.multiple_of(n * 64, 64), 64)
        center, r = moments(xf[at, :].astype(f32))
        normed[at, :] = (center * r * vec[0:1, :] + vec[1:2, :]).astype(bf)
        return _

    def norm_own():
        steps = seq // 2 // 64
        lax.fori_loop(c * steps, (c + 1) * steps, norm_rows, 0)

    def norm_other():
        steps = seq // 2 // 64
        for d in x_fw:
            d.wait_recv()
        lax.fori_loop((1 - c) * steps, (2 - c) * steps, norm_rows, 0)
        keep(normed, normed_o)
        keep(xf, x_o)

    def project(start, stop):
        bias_row = jnp.concatenate(
            [vec[2:3, cols_of(c * half, half)], jnp.zeros((1, half), f32), vec[3:4, cols_of(c * half, half)]], axis=1
        )
        for at in range(start, stop, TILE):
            width = min(TILE, stop - at)
            got = nn(normed[...], wa[:, pl.ds(at, width)])
            qkv[:, pl.ds(at, width)] = (got + bias_row[:, at : at + width]).astype(bf)
        if stop == 3 * half:
            keep(qkv, qkv_o)
            keep(wa, wa_o)

    lane = lax.broadcasted_iota(jnp.int32, (TILE, 128), 1)

    def attend(t):
        k2 = qkv[:, pl.ds(half + t * 128, 128)]
        v2t = jnp.transpose(qkv[:, pl.ds(2 * half + t * 128, 128)])
        kx[:, :128] = k2

        def chunk(n, _):
            at = pl.ds(pl.multiple_of(n * TILE, TILE), TILE)
            q2 = qkv[at, pl.ds(t * 128, 128)] * jnp.array(HEAD_DIM ** (-0.5), bf)
            both = []
            for h in range(2):
                own = lane < HEAD_DIM if h == 0 else lane >= HEAD_DIM
                qx = jnp.concatenate([jnp.where(own, q2, jnp.zeros((), bf)), gq[at, :]], axis=1)
                s = nt(kx[...], qx)
                top = jnp.max(s, axis=0, keepdims=True)
                e = jnp.exp(s - top)
                total = jnp.sum(e, axis=0, keepdims=True)
                o = nn(v2t[h * HEAD_DIM : (h + 1) * HEAD_DIM, :], e.astype(bf))
                both.append(o / total)
                lse[2 * t + h : 2 * t + h + 1, at] = top + jnp.log(total)
            mixed[at, pl.ds(t * 128, 128)] = jnp.transpose(jnp.concatenate(both, axis=0)).astype(bf)
            return _

        lax.fori_loop(0, seq // TILE, chunk, 0)
        if t == half // 128 - 1:
            keep(mixed, mixed_o)
            keep(lse, lse_o)

    wo_own = pltpu.make_async_copy(
        wol.at[rows_of(c * half, half), :], wob.at[:, cols_of(c * half, half)], loc.at[5]
    )
    wo_out = send(
        wol.at[rows_of((1 - c) * half, half), :],
        wob.at[:, cols_of(c * half, half)], wo_s.at[0], wo_r.at[0], (core_nb, z),
    )

    def wo_swap():
        wo_own.start()
        wo_out.start()

    def wo_ready():
        wo_own.wait()
        wo_out.wait()
        keep(wob, wob_o)

    chunks = seq // TILE
    swaps = [
        send(part.at[pl.ds(n * TILE, TILE), :], part_in.at[pl.ds(n * TILE, TILE), :], pa_s.at[n], pa_r.at[n], (core_nb, z))
        for n in range(chunks)
    ]

    def output_rows(n):
        at = pl.ds(n * TILE, TILE)
        part[at, :] = nn(mixed[at, :], wob[...]).astype(bf)
        swaps[n].start()

    def own_outer():
        own_wait(3)
        out_own = pltpu.make_async_copy(
            second.at[pl.ds(0, hid // 2), :], wc.at[rows_of(z * (hid // 2), hid // 2), :], loc.at[4]
        )
        out_own.start()
        out_own.wait()

    def second_rows(n, _):
        at = pl.ds(pl.multiple_of(n * 64, 64), 64)
        sums = xf[at, :].astype(f32) + (part[at, :].astype(f32) + part_in[at, :].astype(f32) + vec[4:5, :])
        middle[at, :] = sums.astype(bf)
        center, r = moments(sums)
        second[at, :] = (center * r * vec[5:6, :] + vec[6:7, :]).astype(bf)
        return _

    def second_norm(n):
        swaps[n].wait_recv()
        lax.fori_loop(n * TILE // 64, (n + 1) * TILE // 64, second_rows, 0)
        if n == chunks - 1:
            keep(middle, middle_o)
            keep(second, second_o)

    tiles = 2 * hid // TILE

    def tile_out(n, slot):
        cols = pl.ds(n * TILE, TILE)
        return [
            pltpu.make_async_copy(act.at[slot], active_o.at[:, cols], act_s.at[slot, 0]),
            pltpu.make_async_copy(slp.at[slot], slope_o.at[:, cols], act_s.at[slot, 1]),
        ]

    def inner_tile(n):
        slot = n % 2
        cols = pl.ds(n * TILE, TILE)
        if n >= 2:
            for d in tile_out(n - 2, slot):
                d.wait()

        def tile_rows(m, _):
            at = pl.ds(pl.multiple_of(m * TILE, TILE), TILE)
            u = nn(second[at, :], wb[:, cols]) + bias_in[:, cols]
            value, slope = gelu_and_slope(u)
            act[slot, at, :] = value.astype(bf)
            slp[slot, at, :] = slope.astype(bf)
            return _

        lax.fori_loop(0, chunks, tile_rows, 0)
        for d in tile_out(n, slot):
            d.start()
        if n == tiles - 1:
            keep(wb, wb_o)

    def c_spread():
        c_arrived()
        for d in c_fw:
            d.start()

    begin()
    first(0)
    for g in groups:
        own_start(g)
    first(1)
    land(1, 1)
    land(1, 0)
    land(0, 0)
    land(0, 1)
    x_start()
    land(1, 2)
    turn(0, 0)
    land(0, 2)
    first(2)
    turn(0, 1)
    vectors()
    turn(1, 1)
    x_spread()
    first(3)
    turn(0, 2)
    turn(1, 2)
    turn(1, 0)
    norm_own()
    norm_other()
    land(2, 0)
    whole(0)
    project(0, 512)
    project(512, 1024)
    project(1024, 1536)
    project(1536, 3 * half)
    land(3, 0)
    land(2, 1)
    attend(0)
    whole(1)
    turn(2, 0)
    attend(1)
    land(2, 2)
    attend(2)
    turn(2, 1)
    land(3, 2)
    attend(3)
    wo_swap()
    attend(4)
    turn(2, 2)
    land(3, 1)
    wo_ready()
    c_start()
    output_rows(0)
    output_rows(1)
    output_rows(2)
    output_rows(3)
    turn(3, 0)
    turn(3, 2)
    own_outer()
    second_norm(0)
    second_norm(1)
    whole(2)
    second_norm(2)
    second_norm(3)
    inner_tile(0)
    inner_tile(1)
    inner_tile(2)
    inner_tile(3)
    inner_tile(4)
    turn(3, 1)
    inner_tile(5)
    inner_tile(6)
    inner_tile(7)
    c_spread()
    inner_tile(8)
    inner_tile(9)
    whole(3)
    for n in (tiles - 2, tiles - 1):
        for d in tile_out(n, n % 2):
            d.wait()
    for d in c_fw:
        d.wait()
    keep(cf, ct_o)
    for d in x_fw + swaps:
        d.wait_send()
    x_sent()
    c_sent()
    for g in groups:
        all_sent(g)
    for d in outs:
        d.wait()


def run_forward(small, bounds, x, ct, wq, wk, wv, wo, w1, w2):
    rows, feat = wq.shape
    hid = w2.shape[0]
    seq = x.shape[1] * LINE
    half = feat // 2
    heads = half // HEAD_DIM
    f32, bf = jnp.float32, jnp.bfloat16
    dma = pltpu.SemaphoreType.DMA
    anywhere = pl.BlockSpec(memory_space=pl.ANY)
    made = [
        ((seq, 128), bf), ((seq, 128), bf),
        ((small.shape[0], feat), f32), ((seq, feat), bf), ((seq, feat), bf), ((feat, 3 * half), bf), ((half, feat), bf),
        ((feat, 2 * hid), bf), ((2 * hid, feat), bf), ((seq, feat), bf), ((seq, 3 * half), bf), ((seq, half), bf),
        ((16, seq), f32), ((seq, feat), bf), ((seq, feat), bf), ((seq, 2 * hid), bf), ((seq, 2 * hid), bf),
    ]
    held = [
        ((LINE,) + small.shape, bf), (bounds.shape, jnp.int32), ((small.shape[0], feat), f32), ((1, 2 * hid), f32), ((seq, feat), bf), ((seq, feat), bf),
        ((feat, 3 * half), bf), ((feat, half), bf), ((half, feat), bf), ((feat, 2 * hid), bf), ((seq, feat), bf),
        ((seq, 3 * half), bf), ((seq, 128), bf), ((seq, 128), bf), ((seq, 256), bf), ((seq, half), bf),
        ((16, seq), f32), ((seq, feat), bf), ((seq, feat), bf), ((seq, feat), bf), ((seq, feat), bf),
        ((2, seq, TILE), bf), ((2, seq, TILE), bf),
    ]
    return pl.pallas_call(
        forward_kernel,
        out_shape=tuple(jax.ShapeDtypeStruct(shape, dtype) for shape, dtype in made),
        in_specs=[anywhere] * 10,
        out_specs=(anywhere,) * len(made),
        scratch_shapes=[pltpu.VMEM(shape, dtype) for shape, dtype in held]
        + [
            dma((3,)), dma((3,)), dma((4,)), dma((4,)), dma((4,)), dma((4,)),
            dma((4, 5)), dma((12, 4)), dma((12, 5)), dma((7,)), dma((2,)), dma((2,)),
            dma((4,)), dma((4,)), dma((16,)), dma((2, 2)),
        ],
        compiler_params=pltpu.CompilerParams(
            collective_id=0, has_side_effects=True, vmem_limit_bytes=VMEM_LIMIT
        ),
        name="forward",
    )(small, bounds, x, ct, wq, wk, wv, wo, w1, w2)


def tn(left, right):
    return lax.dot_general(left, right, (((0,), (0,)), ((), ())), preferred_element_type=jnp.float32)


def backward_kernel(
    vec_ref, x_ref, ct_ref, wa_ref, wob_ref, wb_ref, wc_ref, normed_ref, qkv_ref, mixed_ref, lse_ref, middle_ref,
    second_ref, active_ref, slope_ref, gq_ref, gk_ref,
    block_o, input_o, w2_o, w1_o, q_o, k_o, v_o, o_o, small_o,
    vec, up, big, two, three, wts, dc, db, do, r1c, r2c, zc, r1b, r2b, zb, r1o, r2a, za, kx, gq, gk, lse, half_in, home,
    acc, stage, sums, sums_in, bias_row, dkv,
    ld, us, ur, hs, hr, cs, cr, ss, sr, os, free_x, free_y,
):
    f32, bf = jnp.float32, jnp.bfloat16
    i, z = lax.axis_index("cells"), lax.axis_index("chrom")
    p, c = i // 2, lax.rem(i, 2)
    px, py = lax.rem(p, 2), p // 2
    x_nb, y_nb, core_nb = i + 2 - 4 * px, i + 4 - 8 * py, i + 1 - 2 * c
    p_x, p_y = p + 1 - 2 * px, p + 2 - 4 * py
    seq, feat = up.shape
    half, half_seq, block = feat // 2, seq // 2, seq // LINE
    rows = feat // LINE
    hid = wc_ref.shape[0] // 2
    chunks = seq // TILE
    mesh_id = pl.DeviceIdType.MESH

    barrier = pltpu.get_barrier_semaphore()
    line_ids = [
        (i - c + lax.rem(c + dc_, 2), lax.rem(z + dz, LINE))
        for dc_ in range(2)
        for dz in range(LINE)
        if dc_ or dz
    ]
    for who in line_ids + [(x_nb, z), (y_nb, z)]:
        pl.semaphore_signal(barrier, inc=1, device_id=who, device_id_type=mesh_id)

    loads = {}

    def load(name, pairs):
        n = len(loads)
        copies = [pltpu.make_async_copy(src, dst, ld.at[n, m]) for m, (src, dst) in enumerate(pairs)]
        loads[name] = copies
        for d in copies:
            d.start()

    here = set()

    def loaded(*names):
        for name in names:
            for d in loads[name] if name not in here else ():
                d.wait()
            here.add(name)

    load("ct", [(ct_ref, up)])
    load("marks", [(gk_ref, gk), (gq_ref, gq), (vec_ref, vec), (lse_ref, lse)])
    load("active", [(active_ref, big)])
    load("wc", [(wc_ref, wts)])
    load("mid half", [(middle_ref.at[rows_of(c * half_seq, half_seq), :], home)])
    load("slope", [(slope_ref, db.at[pl.ds(0, seq), :])])
    load("second", [(second_ref, two)])

    def send(src, dst, s, r, who):
        return pltpu.make_async_remote_copy(
            src_ref=src, dst_ref=dst, send_sem=s, recv_sem=r, device_id=who, device_id_type=mesh_id
        )

    class Unit:
        def __init__(self, n, d, col, r, w, r1, r2, zl, parts):
            self.n, self.d, self.col, self.r, self.w = n, d, col, r, w
            self.r1_at, self.r2_at, self.z_at, self.parts = r1, r2, zl, parts

        def region(self, base, row, count=1):
            ref, row0, col0 = base
            return ref.at[rows_of(row0 + row * self.r, count * self.r), pl.ds(col0, self.w)]

        def own(self, s, a, b):
            return self.region((self.d, 0, self.col), (s * 2 + a) * 2 + b)

        def r1(self, side, m, n):
            return self.region(self.r1_at, (side * 2 + m) * 2 + n)

        def r2(self, s):
            return self.region(self.r2_at, s)

        def zl(self, d):
            return self.region(self.z_at, d)

        def sems(self, e):
            return us.at[self.n, e], ur.at[self.n, e]

        def total(self, e, count):
            ref = self.region(self.r1_at, 0, count)
            return send(ref, ref, *self.sems(e), (x_nb, z))

        def step1(self, s):
            for n in range(2):
                if s < 2:
                    send(self.own(s, n, 1 - px), self.r1(0, s, n), *self.sems(0), (x_nb, z)).start()
                else:
                    send(self.own(s, 1 - py, n), self.r1(1, s - 2, n), *self.sems(1), (y_nb, z)).start()

        def step1_all(self):
            for s in (0, 2, 1, 3):
                self.step1(s)

        def add(self, to, *more):
            value = to[...].astype(f32)
            for ref in more:
                value = value + ref[...].astype(f32)
            to[...] = value.astype(bf)

        def step2(self):
            self.total(0, 4).wait_recv()
            for m in range(2):
                for n in range(2):
                    self.add(self.r1(0, m, n), self.own(m, n, px))
                send(self.r1(0, m, 1 - py), self.r2(m), *self.sems(2), (y_nb, z)).start()
            self.total(1, 4).wait_recv()
            for m in range(2):
                for n in range(2):
                    self.add(self.r1(1, m, n), self.own(2 + m, py, n))
                send(self.r1(1, m, 1 - px), self.r2(2 + m), *self.sems(3), (x_nb, z)).start()

        def line(self):
            self.total(2, 2).wait_recv()
            for m in range(2):
                self.add(self.r2(m), self.r1(0, m, py))
            self.total(3, 2).wait_recv()
            for m in range(2):
                self.add(self.r2(2 + m), self.r1(1, m, px))
            for d in range(LINE - 1):
                to = lax.rem(z + d + 1, LINE)
                send(self.r2(to), self.zl(d), *self.sems(4 + d), (i, to)).start()

        def spread(self):
            for d in range(LINE - 1):
                self.total(4 + d, 1).wait_recv()
            self.add(self.r2(z), *[self.zl(d) for d in range(LINE - 1)])
            for off, width, place in self.parts:
                ref, row0, col0 = self.r2_at
                src = ref.at[rows_of(row0 + z * self.r, self.r), pl.ds(col0 + off, width)]
                dst = place(p, 0, width)
                send(src, dst, *self.sems(7), (x_nb, z)).start()
                send(src, dst, *self.sems(8), (y_nb, z)).start()
                pltpu.make_async_copy(src, dst, os.at[self.n]).start()

        def cross(self):
            self.total(7, 1).wait_recv()
            self.total(8, 1).wait_recv()
            for off, width, place in self.parts:
                cut = width // 256 * 128
                left, rest = place(p_x, 0, cut), place(p_y, cut, width - cut)
                send(left, left, *self.sems(9), (y_nb, z)).start()
                send(rest, rest, *self.sems(10), (x_nb, z)).start()

        def crossed(self, e):
            off = 0
            for _, width, _place in self.parts:
                cut = width // 256 * 128
                off += cut if e == 9 else width - cut
            ref, row0, col0 = self.r1_at
            ref = ref.at[rows_of(row0, self.r), pl.ds(col0, off)]
            return send(ref, ref, *self.sems(e), (x_nb, z))

        def to_core(self):
            self.crossed(9).wait_recv()
            self.crossed(10).wait_recv()
            ref = self.region(self.r1_at, 0)
            pltpu.make_async_copy(ref, ref, os.at[self.n]).wait()
            for off, width, place in self.parts:
                mine = place(None, 0, width)
                send(mine, mine, *self.sems(11), (core_nb, z)).start()

        def step2_sent(self):
            self.total(2, 2).wait_send()
            self.total(3, 2).wait_send()

        def end(self):
            self.total(11, 4).wait()
            for e in range(4, 9):
                self.total(e, 1).wait_send()
            self.crossed(9).wait_send()
            self.crossed(10).wait_send()

        def step1_sent(self):
            self.total(0, 4).wait_send()
            self.total(1, 4).wait_send()

    def place_w2(at, off, width):
        first, count = (0, half) if at is None else (at * (hid // 2 // PLANE), hid // 2 // PLANE)
        return w2_o.at[rows_of(c * (hid // 2) + first, count), pl.ds(off, width)]

    def place_w1(n):
        def place(at, off, width):
            first, count = (0, rows) if at is None else (at * (rows // PLANE), rows // PLANE)
            return w1_o.at[rows_of(first, count), cols_of(n * hid + c * (hid // 2) + off, width)]

        return place

    def place_of(ref):
        def place(at, off, width):
            first, count = (0, rows) if at is None else (at * (rows // PLANE), rows // PLANE)
            return ref.at[rows_of(first, count), cols_of(c * half + off, width)]

        return place

    r_big, r_small = hid // 2 // PLANE, rows // PLANE
    unit_c = Unit(0, dc, 0, r_big, feat, (r1c, 0, 0), (r2c, 0, 0), (zc, 0, 0), [(0, feat, place_w2)])
    unit_b = [
        Unit(
            1 + n, db, n * hid, r_small, hid, (r1b, 0, n * hid), (r2b, 0, n * hid), (zb, 0, n * hid),
            [(m * (hid // 2), hid // 2, place_w1(2 * n + m)) for m in range(2)],
        )
        for n in range(2)
    ]
    unit_o = Unit(3, do, 0, r_small, half, (r1o, 0, 0), (r2a, 0, 0), (za, 0, 0), [(0, half, place_of(o_o))])
    spots = ((0, 0), (0, half), (8 * r_small, 0))
    unit_a = [
        Unit(
            4 + n, db, n * half, r_small, half, (r1c,) + spots[n], (r2a, 0, (1 + n) * half), (za, 0, (1 + n) * half),
            [(0, half, place_of(ref))],
        )
        for n, ref in enumerate((q_o, k_o, v_o))
    ]

    def going_home(src, dst, e):
        stay = c == z // 2
        mine, outs = None, []
        for k in range(2):
            b = lax.rem(z + k, 2)
            part = src.at[rows_of(b * block, block), :]
            to = dst.at[lax.rem(z, 2)]
            outs.append(send(part, to, hs.at[e, k], hr.at[e, k], (i - c + z // 2, 2 * c + b)))
            if k == 0:
                mine = pltpu.make_async_copy(part, to, hr.at[e, k])

        def start():
            pl.when(stay)(mine.start)
            pl.when(jnp.logical_not(stay))(outs[0].start)
            outs[1].start()

        def sent():
            pl.when(stay)(mine.wait)
            pl.when(jnp.logical_not(stay))(outs[0].wait_send)
            outs[1].wait_send()

        def arrived():
            pl.when(jnp.logical_not(stay))(outs[0].wait_recv)
            outs[1].wait_recv()

        return start, sent, arrived

    block_start, block_sent, block_arrived = going_home(home, block_o, 0)
    input_start, input_sent, input_arrived = going_home(home, input_o, 1)

    first_core = jnp.where(c == 0, 1.0, 0.0)
    zero_row = jnp.zeros((1, feat), f32)
    wide = hid // 2

    def mask():
        sums[0] = jnp.zeros(sums.shape[1:], f32)
        loaded("ct", "marks")

        def mask_rows(n, total):
            at = pl.ds(pl.multiple_of(n * TILE, TILE), TILE)
            gone = gk[at, 127:128].astype(f32) < 0.0
            value = jnp.where(gone, 0.0, up[at, :].astype(f32))
            up[at, :] = value.astype(bf)
            return total + jnp.sum(value, axis=0, keepdims=True)

        up_sum = lax.fori_loop(0, chunks, mask_rows, zero_row)
        sums[0, 7:8, :] = up_sum * first_core
        loaded("active")

    def outer_rows(s):
        dc[s * wide : (s + 1) * wide, :] = tn(big[:, s * wide : (s + 1) * wide], up[...]).astype(bf)
        unit_c.step1(s)

    swaps = [
        send(half_in.at[pl.ds(n * TILE, TILE), :], half_in.at[pl.ds(n * TILE, TILE), :], cs.at[n], cr.at[n], (core_nb, z))
        for n in range(half_seq // TILE)
    ]

    def block_other():
        loaded("wc", "mid half")
        for n in range(half_seq // TILE):
            at = rows_of((1 - c) * half_seq + n * TILE, TILE)
            to = pl.ds(n * TILE, TILE)
            got = nn(big[at, :], wts[...]).astype(bf)
            for m in range(2):
                held = pl.ds(m * half_seq + n * TILE, TILE)
                do[held, :] = got[:, m * half : (m + 1) * half]
                send(
                    do.at[held, :], half_in.at[to, pl.ds(m * half, half)], cs.at[n], cr.at[n], (core_nb, z)
                ).start()

    def block_own():
        for n in range(half_seq // TILE):
            at = rows_of(c * half_seq + n * TILE, TILE)
            to = pl.ds(n * TILE, TILE)
            acc[...] = nn(big[at, :], wts[...])
            swaps[n].wait_recv()
            gone = gk[at, 127:128].astype(f32) < 0.0
            value = home[to, :].astype(f32) + acc[...] + half_in[to, :].astype(f32) + vec[7:8, :]
            home[to, :] = jnp.where(gone, 0.0, value).astype(bf)

    def through_gelu():
        loaded("wc", "slope")

        def tile(n, _):
            cols = pl.ds(pl.multiple_of(n * TILE, TILE), TILE)
            got = (nt(up[...], wts[cols, :]) * db[pl.ds(0, seq), cols].astype(f32)).astype(bf)
            big[:, cols] = got
            bias_row[:, cols] = jnp.sum(got.astype(f32), axis=0, keepdims=True)
            return _

        lax.fori_loop(0, 2 * hid // TILE, tile, 0)
        for s in range(LINE):
            sums[0, 8 + s : 9 + s, cols_of(c * wide, wide)] = bias_row[:, s * wide : (s + 1) * wide]
        load("wb", [(wb_ref.at[:, pl.ds(n * hid, hid)], wts.at[pl.ds(n * feat, feat), :]) for n in range(2)])
        loaded("second")

    def inner_grad(n):
        def inner_rows(m, _):
            at = pl.ds(pl.multiple_of(m * TILE, TILE), TILE)
            db[at, pl.ds(n * hid, hid)] = tn(two[:, at], big[:, pl.ds(n * hid, hid)]).astype(bf)
            return _

        lax.fori_loop(0, feat // TILE, inner_rows, 0)

    gs_swaps = [
        send(two.at[pl.ds(n * TILE, TILE), :], three.at[pl.ds(n * TILE, TILE), :], cs.at[2 + n], cr.at[2 + n], (core_nb, z))
        for n in range(chunks)
    ]

    def to_second(n):
        if n == 0:
            loaded("wb")
            for d in swaps:
                d.wait_send()
        at = pl.ds(n * TILE, TILE)
        two[at, :] = (
            nt(big[at, pl.ds(0, hid)], wts[pl.ds(0, feat), :]) + nt(big[at, pl.ds(hid, hid)], wts[pl.ds(feat, feat), :])
        ).astype(bf)
        gs_swaps[n].start()
        if n == chunks - 1:
            load("qkv", [(qkv_ref, big.at[:, pl.ds(0, 3 * half)]), (mixed_ref, big.at[:, pl.ds(3 * half, half)])])
            load(
                "wa",
                [
                    (wa_ref.at[:, pl.ds(0, feat)], wts.at[pl.ds(0, feat), :]),
                    (wa_ref.at[:, pl.ds(feat, half)], wts.at[pl.ds(feat, feat), pl.ds(0, half)]),
                    (wob_ref.at[:, pl.ds(0, half)], wts.at[pl.ds(feat, half), pl.ds(half, half)]),
                    (wob_ref.at[:, pl.ds(half, half)], wts.at[pl.ds(feat + half, half), pl.ds(half, half)]),
                ],
            )

    def middle_load():
        unit_c.step1_sent()
        load("middle", [(middle_ref, dc.at[pl.ds(0, seq), :])])

    def back_rows(n, carry):
        gain_sum, shift_sum, out_sum = carry
        at = pl.ds(pl.multiple_of(n * 64, 64), 64)
        g = two[at, :].astype(f32) + three[at, :].astype(f32)
        center, r = moments(dc[at, :].astype(f32))
        hat = center * r
        gh = g * hat
        h = g * vec[5:6, :]
        first = jnp.mean(h, axis=-1, keepdims=True)
        slant = jnp.mean(h * hat, axis=-1, keepdims=True)
        got = (up[at, :].astype(f32) + r * (h - first - hat * slant)).astype(bf)
        two[at, :] = got
        return (
            gain_sum + jnp.sum(gh, axis=0, keepdims=True),
            shift_sum + jnp.sum(g, axis=0, keepdims=True),
            out_sum + jnp.sum(got.astype(f32), axis=0, keepdims=True),
        )

    def second_back():
        loaded("middle")
        carry = (zero_row, zero_row, zero_row)
        for n in range(chunks):
            gs_swaps[n].wait()
            carry = lax.fori_loop(n * TILE // 64, (n + 1) * TILE // 64, back_rows, carry)
        sums[0, 5:6, :] = carry[0] * first_core
        sums[0, 6:7, :] = carry[1] * first_core
        sums[0, 4:5, :] = carry[2] * first_core
        load("normed", [(normed_ref, three)])
        load("x", [(x_ref.at[rows_of(c * half_seq, half_seq), :], up.at[pl.ds(0, half_seq), :])])

    o_swap = send(stage, do.at[rows_of(c * half, half), :], cs.at[6], cr.at[6], (core_nb, z))

    def output_grad():
        loaded("qkv", "wa")
        stage[...] = tn(big[:, pl.ds(3 * half, half)], two[:, cols_of((1 - c) * half, half)]).astype(bf)
        o_swap.start()
        do[rows_of(c * half, half), :] = tn(big[:, pl.ds(3 * half, half)], two[:, cols_of(c * half, half)]).astype(bf)

    def mixed_grad():
        for n in range(chunks):
            at = pl.ds(n * TILE, TILE)
            dc[pl.ds(seq + n * TILE, TILE), pl.ds(half, half)] = (
                nt(two[at, pl.ds(0, half)], wts[pl.ds(feat, half), pl.ds(half, half)])
                + nt(two[at, pl.ds(half, half)], wts[pl.ds(feat + half, half), pl.ds(half, half)])
            ).astype(bf)
        kx[:, 128:] = gk[...]

    lane = lax.broadcasted_iota(jnp.int32, (TILE, 128), 1)
    root = HEAD_DIM ** (-0.5)

    def attend_back(t):
        k2 = big[:, pl.ds(half + t * 128, 128)]
        k2t = jnp.transpose(k2)
        kx[:, :128] = k2
        dkv[...] = jnp.zeros(dkv.shape, f32)

        def chunk(n, _):
            at = pl.ds(pl.multiple_of(n * TILE, TILE), TILE)
            g_at = pl.ds(pl.multiple_of(seq + n * TILE, TILE), TILE)
            q2 = big[at, pl.ds(t * 128, 128)] * jnp.array(root, bf)
            g2 = dc[g_at, pl.ds(half + t * 128, 128)]
            both = []
            for h in range(2):
                own = lane < HEAD_DIM if h == 0 else lane >= HEAD_DIM
                qm = jnp.where(own, q2, jnp.zeros((), bf))
                gm = jnp.where(own, g2, jnp.zeros((), bf))
                s = nt(kx[...], jnp.concatenate([qm, gq[at, :]], axis=1))
                prob = jnp.exp(s - lse[2 * t + h : 2 * t + h + 1, at])
                grad = nt(big[:, pl.ds(2 * half + t * 128, 128)], gm)
                both_of = prob * grad
                dot = jnp.sum(both_of, axis=0, keepdims=True)
                ds = (both_of - prob * dot).astype(bf)
                dkv[0] += nn(ds, qm)
                dkv[1] += nn(prob.astype(bf), gm)
                both.append(nn(k2t[h * HEAD_DIM : (h + 1) * HEAD_DIM, :], ds))
            dc[at, pl.ds(t * 128, 128)] = (jnp.transpose(jnp.concatenate(both, axis=0)) * root).astype(bf)
            return _

        lax.fori_loop(0, chunks, chunk, 0)
        dc[pl.ds(0, seq), pl.ds(half + t * 128, 128)] = dkv[0].astype(bf)
        dc[pl.ds(seq, seq), pl.ds(t * 128, 128)] = dkv[1].astype(bf)
        if t == half // 128 - 1:
            sums[0, 2:3, cols_of(c * half, half)] = jnp.sum(
                dc[pl.ds(0, seq), pl.ds(0, half)].astype(f32), axis=0, keepdims=True
            )
            sums[0, 3:4, cols_of(c * half, half)] = jnp.sum(
                dc[pl.ds(seq, seq), pl.ds(0, half)].astype(f32), axis=0, keepdims=True
            )

    def free_landing():
        unit_c.step2_sent()
        pl.semaphore_signal(free_x, inc=1, device_id=(x_nb, z), device_id_type=mesh_id)
        pl.semaphore_signal(free_y, inc=1, device_id=(y_nb, z), device_id_type=mesh_id)

    def landing_free():
        pl.semaphore_wait(free_x, 1)
        pl.semaphore_wait(free_y, 1)

    def query_key_grad():
        loaded("normed")
        for u in unit_b:
            u.step1_sent()

        def qk_rows(m, _):
            at = pl.ds(pl.multiple_of(m * TILE, TILE), TILE)
            db[at, pl.ds(0, feat)] = tn(three[:, at], dc[pl.ds(0, seq), :]).astype(bf)
            return _

        lax.fori_loop(0, feat // TILE, qk_rows, 0)

    def value_grad():
        def v_rows(m, _):
            at = pl.ds(pl.multiple_of(m * TILE, TILE), TILE)
            db[at, pl.ds(feat, half)] = tn(three[:, at], dc[pl.ds(seq, seq), pl.ds(0, half)]).astype(bf)
            return _

        lax.fori_loop(0, feat // TILE, v_rows, 0)

    def first_part(at):
        at_v = rows_of(at + seq, TILE)
        return nt(dc[rows_of(at, TILE), :], wts[pl.ds(0, feat), :]) + nt(
            dc[at_v, pl.ds(0, half)], wts[pl.ds(feat, feat), pl.ds(0, half)]
        )

    gn_swaps = [
        send(
            up.at[pl.ds(half_seq + n * TILE, TILE), :], half_in.at[pl.ds(n * TILE, TILE), :], cs.at[7 + n], cr.at[7 + n],
            (core_nb, z),
        )
        for n in range(half_seq // TILE)
    ]

    def to_first(n):
        if n == 0:
            loaded("x")
        up[pl.ds(half_seq + n * TILE, TILE), :] = first_part((1 - c) * half_seq + n * TILE).astype(bf)
        gn_swaps[n].start()

    first_sums = [zero_row, zero_row]

    def first_back(n):
        if n == 0:
            block_sent()
        acc[...] = first_part(c * half_seq + n * TILE)
        gn_swaps[n].wait_recv()

        def first_rows(m, carry):
            gain_sum, shift_sum = carry
            at = pl.ds(pl.multiple_of(m * 64, 64), 64)
            here = pl.ds(pl.multiple_of(n * TILE + m * 64, 64), 64)
            g = acc[at, :] + half_in[here, :].astype(f32)
            center, r = moments(up[here, :].astype(f32))
            hat = center * r
            gh = g * hat
            h = g * vec[0:1, :]
            first = jnp.mean(h, axis=-1, keepdims=True)
            slant = jnp.mean(h * hat, axis=-1, keepdims=True)
            got = two[rows_of(c * half_seq + n * TILE + m * 64, 64), :].astype(f32) + r * (h - first - hat * slant)
            home[here, :] = got.astype(bf)
            return (
                gain_sum + jnp.sum(gh, axis=0, keepdims=True),
                shift_sum + jnp.sum(g, axis=0, keepdims=True),
            )

        first_sums[:] = lax.fori_loop(0, TILE // 64, first_rows, tuple(first_sums))
        if n == half_seq // TILE - 1:
            sums[0, 0:1, :] = first_sums[0]
            sums[0, 1:2, :] = first_sums[1]

    small_who = [(core_nb, z), (x_nb, z), (y_nb, z)]
    small = [send(sums.at[n], sums_in.at[n], ss.at[n], sr.at[n], small_who[n]) for n in range(3)] + [
        send(sums.at[3], sums_in.at[3 + d], ss.at[3 + d], sr.at[3 + d], (i, lax.rem(z + d + 1, LINE)))
        for d in range(LINE - 1)
    ]
    small_out = pltpu.make_async_copy(sums.at[4], small_o, os.at[7])

    def small_step(n):
        if n > 0:
            small[n - 1].wait_recv()
            sums[n] = sums[n - 1] + sums_in[n - 1]
        for d in small[3:] if n == 3 else small[n : n + 1]:
            d.start()

    def small_end():
        for d in range(LINE - 1):
            small[3 + d].wait_recv()
        sums[4] = sums[3] + ((sums_in[3] + sums_in[4]) + sums_in[5])
        small_out.start()

    (unit_b0, unit_b1), (unit_q, unit_k, unit_v) = unit_b, unit_a

    pl.semaphore_wait(barrier, len(line_ids) + 2)
    mask()
    outer_rows(0)
    outer_rows(2)
    block_other()
    outer_rows(1)
    outer_rows(3)
    block_own()
    through_gelu()
    block_start()
    inner_grad(0)
    inner_grad(1)
    to_second(0)
    unit_c.step2()
    middle_load()
    to_second(1)
    to_second(2)
    to_second(3)
    unit_b0.step1_all()
    second_back()
    unit_b1.step1_all()
    output_grad()
    mixed_grad()
    unit_c.line()
    free_landing()
    attend_back(0)
    attend_back(1)
    unit_b0.step2()
    attend_back(2)
    attend_back(3)
    unit_b1.step2()
    attend_back(4)
    unit_b0.line()
    to_first(0)
    o_swap.wait_recv()
    to_first(1)
    unit_o.step1_all()
    query_key_grad()
    unit_b1.line()
    value_grad()
    landing_free()
    unit_v.step1_all()
    unit_o.step2()
    unit_v.step2()
    unit_o.line()
    unit_q.step1_all()
    unit_k.step1_all()
    unit_q.step2()
    unit_v.line()
    unit_k.step2()
    unit_o.spread()
    unit_q.line()
    unit_b1.spread()
    unit_k.line()
    first_back(0)
    unit_b0.spread()
    first_back(1)
    small_step(0)
    unit_v.spread()
    unit_q.spread()
    unit_c.spread()
    small_step(1)
    unit_b1.cross()
    input_start()
    unit_b0.cross()
    unit_k.spread()
    small_step(2)
    unit_o.cross()
    unit_c.cross()
    unit_q.cross()
    small_step(3)
    unit_v.cross()
    unit_k.cross()
    unit_v.to_core()
    small_end()
    unit_q.to_core()
    unit_b1.to_core()
    unit_k.to_core()
    unit_c.to_core()
    unit_b0.to_core()
    unit_o.to_core()
    small_out.wait()
    for d in small + gn_swaps + [o_swap]:
        d.wait_send()
    input_sent()
    block_arrived()
    input_arrived()
    units = [unit_c] + unit_b + [unit_o] + unit_a
    for u in units[1:]:
        u.step2_sent()
    for u in [unit_o] + unit_a:
        u.step1_sent()
    for u in units:
        u.end()


def run_backward(vec, x, ct, wa, wob, wb, wc, normed, qkv, mixed, lse, middle, second, active, slope, gq, gk):
    seq, feat = x.shape
    half = feat // 2
    hid = wc.shape[0] // 2
    rows = feat // LINE
    r_big, r_small = hid // 2 // PLANE, rows // PLANE
    f32, bf = jnp.float32, jnp.bfloat16
    dma = pltpu.SemaphoreType.DMA
    anywhere = pl.BlockSpec(memory_space=pl.ANY)
    made = [
        ((2, seq // LINE, feat), bf), ((2, seq // LINE, feat), bf), ((hid, feat), bf), ((rows, LINE * hid), bf),
        ((rows, feat), bf), ((rows, feat), bf), ((rows, feat), bf), ((rows, feat), bf), ((16, feat), f32),
    ]
    held = [
        (vec.shape, f32), ((seq, feat), bf), ((seq, 2 * hid), bf), ((seq, feat), bf), ((seq, feat), bf),
        ((2 * hid, feat), bf), ((2 * hid, feat), bf), ((feat, 2 * hid), bf), ((feat, half), bf),
        ((8 * r_big, feat), bf), ((4 * r_big, feat), bf), ((3 * r_big, feat), bf),
        ((8 * r_small, 2 * hid), bf), ((4 * r_small, 2 * hid), bf), ((3 * r_small, 2 * hid), bf),
        ((8 * r_small, half), bf), ((4 * r_small, 4 * half), bf), ((3 * r_small, 4 * half), bf),
        ((seq, 256), bf), ((seq, 128), bf), ((seq, 128), bf), ((16, seq), f32),
        ((seq // 2, feat), bf), ((seq // 2, feat), bf), ((TILE, feat), f32), ((half, half), bf),
        ((5, 16, feat), f32), ((6, 16, feat), f32), ((1, 2 * hid), f32), ((2, seq, 128), f32),
    ]
    return pl.pallas_call(
        backward_kernel,
        out_shape=tuple(jax.ShapeDtypeStruct(shape, dtype) for shape, dtype in made),
        in_specs=[anywhere] * 17,
        out_specs=(anywhere,) * len(made),
        scratch_shapes=[pltpu.VMEM(shape, dtype) for shape, dtype in held]
        + [
            dma((14, 4)), dma((7, 12)), dma((7, 12)), dma((2, 2)), dma((2, 2)), dma((9,)), dma((9,)), dma((6,)), dma((6,)),
            dma((8,)), pltpu.SemaphoreType.REGULAR, pltpu.SemaphoreType.REGULAR,
        ],
        compiler_params=pltpu.CompilerParams(
            collective_id=1, has_side_effects=True, vmem_limit_bytes=VMEM_LIMIT
        ),
        name="backward",
    )(vec, x, ct, wa, wob, wb, wc, normed, qkv, mixed, lse, middle, second, active, slope, gq, gk)


def finish_kernel(
    block_ref, input_ref, w2_ref, w1_ref, q_ref, k_ref, v_ref, o_ref, small_ref,
    block_o, input_o, gain_o, shift_o, q_o, bq_o, k_o, v_o, bv_o, o_o, bo_o, gain_two_o, shift_two_o, w1_o, b1_o, w2_o, b2_o,
    held, wide, blocks, sums, ins, outs,
):
    z = lax.axis_index("chrom")
    rows, feat = q_ref.shape
    tiles = [(ref, to, pl.ds(0, rows), pl.ds(0, feat)) for ref, to in ((q_ref, q_o), (k_ref, k_o), (v_ref, v_o), (o_ref, o_o))]
    tiles += [(w1_ref, w1_o, pl.ds(0, rows), pl.ds(n * feat, feat)) for n in range(w1_ref.shape[1] // feat)]
    tiles += [(w2_ref, w2_o, pl.ds(n * rows, rows), pl.ds(0, feat)) for n in range(w2_ref.shape[0] // rows)]
    small_in = pltpu.make_async_copy(small_ref, sums, ins.at[len(tiles)])
    small_in.start()
    loads = [pltpu.make_async_copy(ref.at[at, cols], held.at[n], ins.at[n]) for n, (ref, _, at, cols) in enumerate(tiles)]
    loads += [
        pltpu.make_async_copy(ref, blocks.at[n], ins.at[len(tiles) + 1 + n]) for n, ref in enumerate((block_ref, input_ref))
    ]
    for d in loads:
        d.start()
    small_in.wait()
    spots = (gain_o, shift_o, bq_o, bv_o, bo_o, gain_two_o, shift_two_o, b2_o)
    for n, to in enumerate(spots):
        value = sums[n : n + 1, 0:rows]
        for s in range(1, LINE):
            value = jnp.where(z == s, sums[n : n + 1, s * rows : (s + 1) * rows], value)
        to[...] = value[0, :]
    value = sums[VECTORS : VECTORS + 1, :]
    for s in range(1, LINE):
        value = jnp.where(z == s, sums[VECTORS + s : VECTORS + s + 1, :], value)
    b1_o[...] = value[0, :]
    stores = []
    for n, (_, to, at, cols) in enumerate(tiles):
        loads[n].wait()
        wide[n] = held[n].astype(jnp.float32)
        stores.append(pltpu.make_async_copy(wide.at[n], to.at[at, cols], outs.at[n]))
        stores[-1].start()
    for n, to in enumerate((block_o, input_o)):
        loads[len(tiles) + n].wait()
        stores.append(pltpu.make_async_copy(blocks.at[n], to, outs.at[len(tiles) + n]))
        stores[-1].start()
    for d in stores:
        d.wait()


def finish(block_out, input_grad, w2, w1, q, k, v, o, sums):
    f32 = jnp.float32
    rows, feat = q.shape
    hid = w2.shape[0]
    tiles = 4 + w1.shape[1] // feat + hid // rows
    anywhere, here = pl.BlockSpec(memory_space=pl.ANY), pl.BlockSpec(memory_space=pltpu.VMEM)
    matrix, vector = jax.ShapeDtypeStruct((rows, feat), f32), jax.ShapeDtypeStruct((rows,), f32)
    block = jax.ShapeDtypeStruct(block_out.shape, block_out.dtype)
    made = (
        block, block, vector, vector, matrix, vector, matrix, matrix, vector, matrix, vector, vector, vector,
        jax.ShapeDtypeStruct(w1.shape, f32), jax.ShapeDtypeStruct((hid,), f32), jax.ShapeDtypeStruct(w2.shape, f32), vector,
    )
    return pl.pallas_call(
        finish_kernel,
        out_shape=made,
        in_specs=[anywhere] * 9,
        out_specs=tuple(here if len(m.shape) == 1 else anywhere for m in made),
        scratch_shapes=[
            pltpu.VMEM((tiles, rows, feat), q.dtype), pltpu.VMEM((tiles, rows, feat), f32),
            pltpu.VMEM((2,) + block_out.shape, block_out.dtype), pltpu.VMEM(sums.shape, f32),
            pltpu.SemaphoreType.DMA((tiles + 3,)), pltpu.SemaphoreType.DMA((tiles + 2,)),
        ],
        compiler_params=pltpu.CompilerParams(vmem_limit_bytes=VMEM_LIMIT),
        name="finish",
    )(block_out, input_grad, w2, w1, q, k, v, o, sums)


def paired_local(
    inputs, lengths, offsets, cotangent, norm_gain, norm_shift, query_proj, query_bias, key_proj, value_proj,
    value_bias, output_proj, output_bias, second_gain, second_shift, inner_proj, inner_bias, outer_proj, outer_bias,
):
    cells_here, _, feat = inputs.shape
    rows = feat // LINE
    hid = outer_proj.shape[0]

    vectors = (norm_gain, norm_shift, query_bias, value_bias, output_bias, second_gain, second_shift, outer_bias)
    entries = vectors + tuple(inner_bias[n * rows : (n + 1) * rows] for n in range(hid // rows))
    row = lax.broadcasted_iota(jnp.int32, (16, rows), 0)
    small = jnp.zeros((16, rows), entries[0].dtype)
    for n, entry in enumerate(entries):
        small = jnp.where(row == n, entry[None, :], small)
    small = jnp.pad(small, ((0, 0), (0, 384 - rows)))
    lanes, count = 128, offsets.shape[1]
    first = jnp.pad(offsets, ((0, 0), (1, lanes - 1 - count)), constant_values=2 ** 30)
    end = jnp.pad(offsets, ((0, 0), (0, lanes - count)), constant_values=2 ** 30)
    group = lax.broadcasted_iota(jnp.int32, (cells_here, 8, lanes), 2)
    kind = lax.broadcasted_iota(jnp.int32, (cells_here, 8, lanes), 1)
    first = jnp.where(group == 0, 0, first[:, None, :])
    bounds = jnp.where(kind == 0, first, jnp.where(kind == 1, end[:, None, :], lengths[:, None, None]))
    (
        mark_q, mark_k, vec, xf, cf, wa, wob, wb, wc, normed, qkv, mixed, lse, middle, second, active, slope,
    ) = run_forward(
        small, bounds, inputs, cotangent, query_proj, key_proj, value_proj, output_proj, inner_proj, outer_proj
    )
    grads = run_backward(
        vec, xf, cf, wa, wob, wb, wc, normed, qkv, mixed, lse, middle, second, active, slope, mark_q, mark_k
    )
    return finish(*grads)


def solution(mesh):
    paired = mesh.shape["chrom"] == 4 and mesh.shape["cells"] == 8
    placed = (
        P("cells", "chrom", None),
        P("cells"),
        P("cells", None),
        P("cells", "chrom", None),
        P("chrom"),
        P("chrom"),
        P("chrom", None),
        P("chrom"),
        P("chrom", None),
        P("chrom", None),
        P("chrom"),
        P("chrom", None),
        P("chrom"),
        P("chrom"),
        P("chrom"),
        P("chrom", None),
        P("chrom"),
        P("chrom", None),
        P("chrom"),
    )
    return jax.shard_map(
        paired_local if paired else general,
        mesh=mesh,
        in_specs=placed,
        out_specs=(
            P("cells", "chrom", None),
            P("cells", "chrom", None),
            P("chrom"),
            P("chrom"),
            P("chrom", None),
            P("chrom"),
            P("chrom", None),
            P("chrom", None),
            P("chrom"),
            P("chrom", None),
            P("chrom"),
            P("chrom"),
            P("chrom"),
            P("chrom", None),
            P("chrom"),
            P("chrom", None),
            P("chrom"),
        ),
        check_vma=False,
    )
```

```python
import functools

import jax
import jax.numpy as jnp
from jax import lax
from jax.experimental import pallas as pl
from jax.experimental.pallas import tpu as pltpu
from jax.sharding import PartitionSpec as P

HEADS = 20
HEAD_DIM = 64


eps_norm = 1e-05
group_bias = 1.0


def layer_norm(values, gain, shift):
    center = values - jnp.mean(values, axis=-1, keepdims=True)
    spread = jnp.mean(center * center, axis=-1, keepdims=True)
    return center * lax.rsqrt(spread + eps_norm) * gain + shift


def gelu_exact(values):
    return jax.nn.gelu(values, approximate=False)


def product(left, right):
    return jnp.dot(left, right, preferred_element_type=jnp.float32)


def left_product(left, right):
    return jnp.einsum("ra,rb->ab", left, right, preferred_element_type=jnp.float32)


def right_back(left, right):
    return jnp.einsum("rb,ab->ra", left, right, preferred_element_type=jnp.float32)


def column_sum(values):
    return jnp.sum(values, axis=0, dtype=jnp.float32)


def split_rows(value, outer, inner_count):
    return value.reshape(
        (outer, inner_count, value.shape[0] // (outer * inner_count)) + value.shape[1:]
    )


def general(
    inputs,
    lengths,
    offsets,
    cotangent,
    norm_gain,
    norm_shift,
    query_proj,
    query_bias,
    key_proj,
    value_proj,
    value_bias,
    output_proj,
    output_bias,
    second_gain,
    second_shift,
    inner_proj,
    inner_bias,
    outer_proj,
    outer_bias,
):
    count_chrom = lax.axis_size("chrom")
    count_cells = lax.axis_size("cells")
    block_index = lax.axis_index("chrom")
    cells_here, tokens_here, feat_width = inputs.shape
    seq_len = tokens_here * count_chrom
    row_count = cells_here * tokens_here
    inv_root = HEAD_DIM ** (-0.5)
    places = jnp.arange(seq_len, dtype=jnp.int32)
    key_live = places[None, :] < lengths[:, None]
    groups = jnp.sum((places[None, :, None] >= offsets[:, None, :]).astype(jnp.int32), axis=2)
    query_groups = lax.dynamic_slice_in_dim(groups, block_index * tokens_here, tokens_here, 1)
    query_live = lax.dynamic_slice_in_dim(key_live, block_index * tokens_here, tokens_here, 1)
    same_group = (query_groups[:, :, None] == groups[:, None, :]).astype(jnp.float32)
    mask_bias = jnp.where(key_live[:, None, :], group_bias * same_group, -jnp.inf)[:, None]
    gathered = (
        lax.all_gather(norm_gain, "chrom", axis=0, tiled=True),
        lax.all_gather(norm_shift, "chrom", axis=0, tiled=True),
        lax.all_gather(query_proj, "chrom", axis=0, tiled=True),
        lax.all_gather(query_bias, "chrom", axis=0, tiled=True),
        lax.all_gather(key_proj, "chrom", axis=0, tiled=True),
        lax.all_gather(value_proj, "chrom", axis=0, tiled=True),
        lax.all_gather(value_bias, "chrom", axis=0, tiled=True),
        lax.all_gather(output_proj, "chrom", axis=0, tiled=True),
        lax.all_gather(output_bias, "chrom", axis=0, tiled=True),
        lax.all_gather(second_gain, "chrom", axis=0, tiled=True),
        lax.all_gather(second_shift, "chrom", axis=0, tiled=True),
        lax.all_gather(inner_proj, "chrom", axis=0, tiled=True),
        lax.all_gather(inner_bias, "chrom", axis=0, tiled=True),
        lax.all_gather(outer_proj, "chrom", axis=0, tiled=True),
        lax.all_gather(outer_bias, "chrom", axis=0, tiled=True),
    )
    gain_one = gathered[0].astype(jnp.float32)
    shift_one = gathered[1].astype(jnp.float32)
    gain_two = gathered[9].astype(jnp.float32)
    shift_two = gathered[10].astype(jnp.float32)
    states = inputs.astype(jnp.float32).reshape(row_count, feat_width)
    normed_full, norm_back = jax.vjp(layer_norm, states, gain_one, shift_one)
    normed = normed_full.astype(jnp.bfloat16)
    queries = (product(normed, gathered[2]) + gathered[3].astype(jnp.float32)).astype(jnp.bfloat16)
    key_rows = product(normed, gathered[4]).astype(jnp.bfloat16)
    vals = (product(normed, gathered[5]) + gathered[6].astype(jnp.float32)).astype(jnp.bfloat16)
    keys_all, vals_all = (
        lax.all_gather(
            key_rows.reshape(cells_here, tokens_here, feat_width), "chrom", axis=1, tiled=True
        ),
        lax.all_gather(
            vals.reshape(cells_here, tokens_here, feat_width), "chrom", axis=1, tiled=True
        ),
    )
    query_heads = queries.reshape(cells_here, tokens_here, HEADS, HEAD_DIM)
    key_heads = keys_all.reshape(cells_here, seq_len, HEADS, HEAD_DIM)
    val_heads = vals_all.reshape(cells_here, seq_len, HEADS, HEAD_DIM)

    def scores_of():
        raw = (
            jnp.einsum(
                "cqhd,ckhd->chqk", query_heads, key_heads, preferred_element_type=jnp.float32
            )
            * inv_root
        )
        return raw + mask_bias

    masked = scores_of()
    row_max = jnp.max(masked, axis=-1, keepdims=True)
    exp_scores = jnp.exp(masked - row_max)
    exp_total = jnp.sum(exp_scores, axis=-1, keepdims=True)
    attn_probs = exp_scores / exp_total
    log_total = row_max + jnp.log(exp_total)
    mixed_out = jnp.einsum(
        "chqk,ckhd->cqhd",
        attn_probs.astype(jnp.bfloat16),
        val_heads,
        preferred_element_type=jnp.float32,
    )
    mixed_out = mixed_out.astype(jnp.bfloat16).reshape(row_count, feat_width)
    attended = product(mixed_out, gathered[7]) + gathered[8].astype(jnp.float32)
    middle = states + attended
    second_full, second_back = jax.vjp(layer_norm, middle, gain_two, shift_two)
    second = second_full.astype(jnp.bfloat16)
    inner_pre = product(second, gathered[11]) + gathered[12].astype(jnp.float32)
    active_full, gelu_back = jax.vjp(gelu_exact, inner_pre)
    active = active_full.astype(jnp.bfloat16)
    result = middle + product(active, gathered[13]) + gathered[14].astype(jnp.float32)
    live_rows = query_live.reshape(row_count, 1)
    block_out = (
        jnp.where(live_rows, result, 0.0)
        .astype(jnp.bfloat16)
        .reshape(cells_here, tokens_here, feat_width)
    )
    upstream = jnp.where(
        live_rows, cotangent.reshape(row_count, feat_width), jnp.zeros((), jnp.bfloat16)
    )
    outer_bias_grad = column_sum(upstream)
    outer_proj_grad = left_product(active, upstream)
    grad_active = right_back(upstream, gathered[13])
    (grad_inner_full,) = gelu_back(grad_active)
    grad_inner = grad_inner_full.astype(jnp.bfloat16)
    inner_bias_grad = column_sum(grad_inner)
    inner_proj_grad = left_product(second, grad_inner)
    grad_second = right_back(grad_inner, gathered[11])
    grad_middle_norm, second_gain_grad, second_shift_grad = second_back(grad_second)
    grad_middle = upstream.astype(jnp.float32) + grad_middle_norm
    grad_attended = grad_middle.astype(jnp.bfloat16)
    output_bias_grad = column_sum(grad_attended)
    output_proj_grad = left_product(mixed_out, grad_attended)
    grad_mixed = right_back(grad_attended, gathered[7]).astype(jnp.bfloat16)
    grad_mixed = grad_mixed.reshape(cells_here, tokens_here, HEADS, HEAD_DIM)
    attn_again = jnp.exp(scores_of() - log_total)
    grad_probs = jnp.einsum(
        "cqhd,ckhd->chqk", grad_mixed, val_heads, preferred_element_type=jnp.float32
    )
    row_dot = jnp.sum(attn_again * grad_probs, axis=-1, keepdims=True)
    grad_raw = (attn_again * (grad_probs - row_dot)).astype(jnp.bfloat16)
    grad_vals_part = jnp.einsum(
        "chqk,cqhd->ckhd",
        attn_again.astype(jnp.bfloat16),
        grad_mixed,
        preferred_element_type=jnp.float32,
    )
    grad_keys_part = (
        jnp.einsum("chqk,cqhd->ckhd", grad_raw, query_heads, preferred_element_type=jnp.float32)
        * inv_root
    )
    grad_queries = (
        jnp.einsum("chqk,ckhd->cqhd", grad_raw, key_heads, preferred_element_type=jnp.float32)
        * inv_root
    ).astype(jnp.bfloat16)
    grad_queries = grad_queries.reshape(row_count, feat_width)
    grad_keys_sum, grad_vals_sum = (
        lax.psum_scatter(
            grad_keys_part.reshape(cells_here, seq_len, feat_width).astype(jnp.bfloat16),
            "chrom",
            scatter_dimension=1,
            tiled=True,
        ).astype(jnp.float32),
        lax.psum_scatter(
            grad_vals_part.reshape(cells_here, seq_len, feat_width).astype(jnp.bfloat16),
            "chrom",
            scatter_dimension=1,
            tiled=True,
        ).astype(jnp.float32),
    )
    grad_keys = grad_keys_sum.astype(jnp.bfloat16).reshape(row_count, feat_width)
    grad_vals = grad_vals_sum.astype(jnp.bfloat16).reshape(row_count, feat_width)
    query_proj_grad = left_product(normed, grad_queries)
    query_bias_grad = column_sum(grad_queries)
    key_proj_grad = left_product(normed, grad_keys)
    value_proj_grad = left_product(normed, grad_vals)
    value_bias_grad = column_sum(grad_vals)
    grad_normed = (
        right_back(grad_queries, gathered[2])
        + right_back(grad_keys, gathered[4])
        + right_back(grad_vals, gathered[5])
    )
    grad_states_norm, norm_gain_grad, norm_shift_grad = norm_back(grad_normed)
    input_grad = (
        (grad_middle + grad_states_norm)
        .astype(jnp.bfloat16)
        .reshape(cells_here, tokens_here, feat_width)
    )
    grad_list = (
        norm_gain_grad,
        norm_shift_grad,
        query_proj_grad,
        query_bias_grad,
        key_proj_grad,
        value_proj_grad,
        value_bias_grad,
        output_proj_grad,
        output_bias_grad,
        second_gain_grad,
        second_shift_grad,
        inner_proj_grad,
        inner_bias_grad,
        outer_proj_grad,
        outer_bias_grad,
    )
    pieces = tuple((split_rows(member, count_chrom, count_cells) for member in grad_list))
    section_one = (
        lax.psum_scatter(
            pieces[0].astype(jnp.bfloat16), "cells", scatter_dimension=1, tiled=True
        ).astype(jnp.float32),
        lax.psum_scatter(
            pieces[1].astype(jnp.bfloat16), "cells", scatter_dimension=1, tiled=True
        ).astype(jnp.float32),
        lax.psum_scatter(
            pieces[2].astype(jnp.bfloat16), "cells", scatter_dimension=1, tiled=True
        ).astype(jnp.float32),
        lax.psum_scatter(
            pieces[3].astype(jnp.bfloat16), "cells", scatter_dimension=1, tiled=True
        ).astype(jnp.float32),
        lax.psum_scatter(
            pieces[4].astype(jnp.bfloat16), "cells", scatter_dimension=1, tiled=True
        ).astype(jnp.float32),
        lax.psum_scatter(
            pieces[5].astype(jnp.bfloat16), "cells", scatter_dimension=1, tiled=True
        ).astype(jnp.float32),
        lax.psum_scatter(
            pieces[6].astype(jnp.bfloat16), "cells", scatter_dimension=1, tiled=True
        ).astype(jnp.float32),
        lax.psum_scatter(
            pieces[7].astype(jnp.bfloat16), "cells", scatter_dimension=1, tiled=True
        ).astype(jnp.float32),
        lax.psum_scatter(
            pieces[8].astype(jnp.bfloat16), "cells", scatter_dimension=1, tiled=True
        ).astype(jnp.float32),
        lax.psum_scatter(
            pieces[9].astype(jnp.bfloat16), "cells", scatter_dimension=1, tiled=True
        ).astype(jnp.float32),
        lax.psum_scatter(
            pieces[10].astype(jnp.bfloat16), "cells", scatter_dimension=1, tiled=True
        ).astype(jnp.float32),
        lax.psum_scatter(
            pieces[11].astype(jnp.bfloat16), "cells", scatter_dimension=1, tiled=True
        ).astype(jnp.float32),
        lax.psum_scatter(
            pieces[12].astype(jnp.bfloat16), "cells", scatter_dimension=1, tiled=True
        ).astype(jnp.float32),
        lax.psum_scatter(
            pieces[13].astype(jnp.bfloat16), "cells", scatter_dimension=1, tiled=True
        ).astype(jnp.float32),
        lax.psum_scatter(
            pieces[14].astype(jnp.bfloat16), "cells", scatter_dimension=1, tiled=True
        ).astype(jnp.float32),
    )
    section_two = (
        lax.psum_scatter(
            section_one[0].astype(jnp.bfloat16), "chrom", scatter_dimension=0, tiled=True
        ).astype(jnp.float32),
        lax.psum_scatter(
            section_one[1].astype(jnp.bfloat16), "chrom", scatter_dimension=0, tiled=True
        ).astype(jnp.float32),
        lax.psum_scatter(
            section_one[2].astype(jnp.bfloat16), "chrom", scatter_dimension=0, tiled=True
        ).astype(jnp.float32),
        lax.psum_scatter(
            section_one[3].astype(jnp.bfloat16), "chrom", scatter_dimension=0, tiled=True
        ).astype(jnp.float32),
        lax.psum_scatter(
            section_one[4].astype(jnp.bfloat16), "chrom", scatter_dimension=0, tiled=True
        ).astype(jnp.float32),
        lax.psum_scatter(
            section_one[5].astype(jnp.bfloat16), "chrom", scatter_dimension=0, tiled=True
        ).astype(jnp.float32),
        lax.psum_scatter(
            section_one[6].astype(jnp.bfloat16), "chrom", scatter_dimension=0, tiled=True
        ).astype(jnp.float32),
        lax.psum_scatter(
            section_one[7].astype(jnp.bfloat16), "chrom", scatter_dimension=0, tiled=True
        ).astype(jnp.float32),
        lax.psum_scatter(
            section_one[8].astype(jnp.bfloat16), "chrom", scatter_dimension=0, tiled=True
        ).astype(jnp.float32),
        lax.psum_scatter(
            section_one[9].astype(jnp.bfloat16), "chrom", scatter_dimension=0, tiled=True
        ).astype(jnp.float32),
        lax.psum_scatter(
            section_one[10].astype(jnp.bfloat16), "chrom", scatter_dimension=0, tiled=True
        ).astype(jnp.float32),
        lax.psum_scatter(
            section_one[11].astype(jnp.bfloat16), "chrom", scatter_dimension=0, tiled=True
        ).astype(jnp.float32),
        lax.psum_scatter(
            section_one[12].astype(jnp.bfloat16), "chrom", scatter_dimension=0, tiled=True
        ).astype(jnp.float32),
        lax.psum_scatter(
            section_one[13].astype(jnp.bfloat16), "chrom", scatter_dimension=0, tiled=True
        ).astype(jnp.float32),
        lax.psum_scatter(
            section_one[14].astype(jnp.bfloat16), "chrom", scatter_dimension=0, tiled=True
        ).astype(jnp.float32),
    )
    rejoined = (
        lax.all_gather(section_two[0].astype(jnp.bfloat16), "cells", axis=1, tiled=True).astype(
            jnp.float32
        ),
        lax.all_gather(section_two[1].astype(jnp.bfloat16), "cells", axis=1, tiled=True).astype(
            jnp.float32
        ),
        lax.all_gather(section_two[2].astype(jnp.bfloat16), "cells", axis=1, tiled=True).astype(
            jnp.float32
        ),
        lax.all_gather(section_two[3].astype(jnp.bfloat16), "cells", axis=1, tiled=True).astype(
            jnp.float32
        ),
        lax.all_gather(section_two[4].astype(jnp.bfloat16), "cells", axis=1, tiled=True).astype(
            jnp.float32
        ),
        lax.all_gather(section_two[5].astype(jnp.bfloat16), "cells", axis=1, tiled=True).astype(
            jnp.float32
        ),
        lax.all_gather(section_two[6].astype(jnp.bfloat16), "cells", axis=1, tiled=True).astype(
            jnp.float32
        ),
        lax.all_gather(section_two[7].astype(jnp.bfloat16), "cells", axis=1, tiled=True).astype(
            jnp.float32
        ),
        lax.all_gather(section_two[8].astype(jnp.bfloat16), "cells", axis=1, tiled=True).astype(
            jnp.float32
        ),
        lax.all_gather(section_two[9].astype(jnp.bfloat16), "cells", axis=1, tiled=True).astype(
            jnp.float32
        ),
        lax.all_gather(section_two[10].astype(jnp.bfloat16), "cells", axis=1, tiled=True).astype(
            jnp.float32
        ),
        lax.all_gather(section_two[11].astype(jnp.bfloat16), "cells", axis=1, tiled=True).astype(
            jnp.float32
        ),
        lax.all_gather(section_two[12].astype(jnp.bfloat16), "cells", axis=1, tiled=True).astype(
            jnp.float32
        ),
        lax.all_gather(section_two[13].astype(jnp.bfloat16), "cells", axis=1, tiled=True).astype(
            jnp.float32
        ),
        lax.all_gather(section_two[14].astype(jnp.bfloat16), "cells", axis=1, tiled=True).astype(
            jnp.float32
        ),
    )
    final = tuple(
        (
            member.reshape(
                (member.shape[0] * member.shape[1] * member.shape[2],) + member.shape[3:]
            )
            for member in rejoined
        )
    )
    return (block_out, input_grad) + tuple(final)


PLANE = 4
LINE = 4
VMEM_LIMIT = 62 * 1024 * 1024


def rows_of(start, count):
    return pl.ds(pl.multiple_of(start, 16), count)


def cols_of(start, count):
    return pl.ds(pl.multiple_of(start, 128), count)


VECTORS = 8
TILE = 256


def nt(left, right):
    return lax.dot_general(left, right, (((1,), (1,)), ((), ())), preferred_element_type=jnp.float32)


def nn(left, right):
    return jnp.dot(left, right, preferred_element_type=jnp.float32)


def moments(values):
    center = values - jnp.mean(values, axis=-1, keepdims=True)
    spread = jnp.mean(center * center, axis=-1, keepdims=True)
    return center, lax.rsqrt(spread + eps_norm)


def gelu_and_slope(u):
    gauss = jnp.exp(u * u * -0.5)
    t = 1.0 / (1.0 + jnp.abs(u) * (0.3275911 * 0.5 ** 0.5))
    poly = 0.5 * 1.061405429
    for factor in (-1.453152027, 1.421413741, -0.284496736, 0.254829592):
        poly = poly * t + 0.5 * factor
    tail = poly * t * gauss
    phi_sum = jnp.where(u < 0.0, tail, 1.0 - tail)
    return u * phi_sum, phi_sum + u * gauss * 0.3989422804014327


def tn(left, right):
    return lax.dot_general(left, right, (((0,), (0,)), ((), ())), preferred_element_type=jnp.float32)


def layer_kernel(
    len_ref, off_ref, v0, v1, v2, v3, v4, v5, v6, v7, b_ref, x_ref, ct_ref, wq_ref, wk_ref, wv_ref, wo_ref, w1_ref, w2_ref,
    block_o, input_o, w2_o, w1_o, q_o, k_o, v_o, o_o, small_o, x_o, normed_o, qkv_o, wa_o, wob_o,
    small_ref, rag_ref, smalls, rag, vec, bias_in, xf, up, dc, do, wb, wts, big, db, two, three, r1c, r2c, zc, r1o, r2a, za, kx, gq, gk, lse,
    half_in, home, acc, sums, sums_in,
    sm_s, sm_r, ex_s, ex_r, fw_s, fw_r, ln_s, un_s, un_r, loc, wo_s, wo_r, pa_s, pa_r, out_s,
    ld, us, ur, hs, hr, cs, cr, ss, sr, os, free_x, free_y, freed_x, freed_y, freed_z,
):
    f32, bf = jnp.float32, jnp.bfloat16
    i, z = lax.axis_index("cells"), lax.axis_index("chrom")
    p, c = i // 2, lax.rem(i, 2)
    px, py = lax.rem(p, 2), p // 2
    x_nb, y_nb, core_nb = i + 2 - 4 * px, i + 4 - 8 * py, i + 1 - 2 * c
    p_x, p_y = p + 1 - 2 * px, p + 2 - 4 * py
    rows = wq_ref.shape[0]
    feat = wq_ref.shape[1]
    half = feat // 2
    hid = w2_ref.shape[0]
    block = x_ref.shape[1]
    seq = block * LINE
    half_seq = seq // 2
    chunks = seq // TILE
    wide = hid // 2
    mesh_id = pl.DeviceIdType.MESH
    part_rows, hid_part = rows // PLANE, hid // 2 // PLANE

    small_ref[...] = jnp.zeros(small_ref.shape, bf)
    for n, ref in enumerate((v0, v1, v2, v3, v4, v5, v6, v7)):
        small_ref[n : n + 1, 0:rows] = ref[...][None, :]
    for n in range(hid // rows):
        small_ref[VECTORS + n : VECTORS + n + 1, 0:rows] = b_ref[n * rows : (n + 1) * rows][None, :]
    count = off_ref.shape[1]
    never = 2 ** 30
    for n in range(rag_ref.shape[0]):
        rag_ref[n] = jnp.full(rag_ref.shape[1:], never, jnp.int32)
        rag_ref[n, 1:2, 0:count] = off_ref[n : n + 1, :]
        end = rag_ref[n, 1:2, :]
        group = lax.broadcasted_iota(jnp.int32, end.shape, 1)
        rag_ref[n, 0:1, :] = jnp.where(group == 0, 0, pltpu.roll(end, 1, 1))
        rag_ref[n, 2:3, :] = jnp.full(end.shape, len_ref[n], jnp.int32)

    barrier = pltpu.get_barrier_semaphore()
    line_ids = [
        (i - c + lax.rem(c + dc, 2), lax.rem(z + dz, LINE))
        for dc in range(2)
        for dz in range(LINE)
        if dc or dz
    ]
    for who in line_ids + [(x_nb, z), (y_nb, z)]:
        pl.semaphore_signal(barrier, inc=1, device_id=who, device_id_type=pl.DeviceIdType.MESH)
    pl.semaphore_wait(barrier, len(line_ids) + 2)

    def send(src, dst, s, r, who):
        return pltpu.make_async_remote_copy(
            src_ref=src, dst_ref=dst, send_sem=s, recv_sem=r, device_id=who,
            device_id_type=pl.DeviceIdType.MESH,
        )

    small_own = pltpu.make_async_copy(small_ref, smalls.at[z], loc.at[0])
    small_out = [
        send(small_ref, smalls.at[z], sm_s.at[d], sm_r.at[d], (i, lax.rem(z + d + 1, LINE)))
        for d in range(LINE - 1)
    ]

    rag_own = pltpu.make_async_copy(rag_ref.at[lax.rem(z, 2)], rag.at[0], loc.at[6])
    rag_out = send(rag_ref.at[lax.rem(z, 2)], rag.at[1], wo_s.at[1], wo_r.at[1], (core_nb, z))

    def exchange(src, dst, which):
        stay = c == z // 2
        mine, outs = None, []
        for k in range(2):
            j = lax.rem(z + k, 2)
            to = dst.at[rows_of(z * block, block), :]
            r = ex_r.at[2 * which + k]
            outs.append(send(src.at[j], to, ex_s.at[2 * which + k], r, (i - c + z // 2, 2 * c + j)))
            if k == 0:
                mine = pltpu.make_async_copy(src.at[j], to, r)

        def start():
            pl.when(stay)(mine.start)
            pl.when(jnp.logical_not(stay))(outs[0].start)
            outs[1].start()

        def arrived():
            pl.when(stay)(mine.wait)
            pl.when(jnp.logical_not(stay))(outs[0].wait_recv)
            outs[1].wait_recv()

        def sent():
            pl.when(jnp.logical_not(stay))(outs[0].wait_send)
            outs[1].wait_send()

        return start, arrived, sent

    def forward(dst, which):
        return [
            send(
                dst.at[rows_of((2 * c + b) * block, block), :],
                dst.at[rows_of((2 * c + b) * block, block), :],
                fw_s.at[2 * which + b], fw_r.at[2 * which + b], (core_nb, z),
            )
            for b in range(2)
        ]

    x_start, x_arrived, x_sent = exchange(x_ref, xf, 0)
    c_start, c_arrived, c_sent = exchange(ct_ref, up, 1)
    x_fw, c_fw = forward(xf, 0), forward(up, 1)

    wa, wol = dc.at[:, pl.ds(0, 3 * half)], dc.at[:, pl.ds(3 * half, half)]
    lands = (wa, wol, wb, wts)
    groups = range(4)
    partner, inner = z + 1 - 2 * lax.rem(z, 2), 3 - z
    low = z < 2
    middle_chip = jnp.logical_or(z == 1, z == 2)
    slot_shard = (partner, jnp.where(low, 2, 1), jnp.where(low, 3, 0))

    def own_parts(g, row, count):
        if g == 0:
            return [
                (ref.at[rows_of(row, count), cols_of(c * half, half)], pl.ds(n * half, half))
                for n, ref in enumerate((wq_ref, wk_ref, wv_ref))
            ]
        if g == 1:
            return [(wo_ref.at[rows_of(row, count), cols_of(c * half, half)], pl.ds(0, half))]
        if g == 2:
            return [
                (w1_ref.at[rows_of(row, count), cols_of(n * hid + c * (hid // 2), hid // 2)], pl.ds(n * (hid // 2), hid // 2))
                for n in range(LINE)
            ]
        return [(w2_ref.at[rows_of(c * (hid // 2) + row, count), :], pl.ds(0, feat))]

    def shape_of(g):
        return (rows, part_rows) if g < 3 else (hid // 2, hid_part)

    def piece(g, s, at):
        shard, count = shape_of(g)
        return lands[g].at[rows_of(s * shard + at * count, count), :]

    def half_piece(g, s, at, side):
        shard, count = shape_of(g)
        width = lands[g].shape[1]
        cut = width // 256 * 128
        cols = pl.ds(cut, width - cut) if side else pl.ds(0, cut)
        return lands[g].at[rows_of(s * shard + at * count, count), cols]

    def line_send(g, s, slot, e, to):
        return send(piece(g, s, p), piece(g, s, p), ln_s.at[g, e], un_r.at[3 * g + slot, 0], (i, to))

    def first(g):
        shard, count = shape_of(g)
        for src, cols in own_parts(g, p * count, count):
            dst = lands[g].at[rows_of(z * shard + p * count, count), cols]
            send(src, dst, ln_s.at[g, 0], un_r.at[3 * g, 0], (i, partner)).start()

        @pl.when(middle_chip)
        def _():
            for src, cols in own_parts(g, p * count, count):
                dst = lands[g].at[rows_of(z * shard + p * count, count), cols]
                send(src, dst, ln_s.at[g, 1], un_r.at[3 * g + 1, 0], (i, inner)).start()

    def passing(g, slot):
        if slot == 0:
            return line_send(g, slot_shard[0], 2, 2, inner)
        return line_send(g, slot_shard[slot], slot, 2 + slot, partner)

    def spread(g, slot):
        own = piece(g, slot_shard[slot], p)
        u = 3 * g + slot
        return [
            send(own, own, un_s.at[u, 0], un_r.at[u, 1], (x_nb, z)),
            send(own, own, un_s.at[u, 1], un_r.at[u, 2], (y_nb, z)),
        ]

    def cross(g, slot):
        u = 3 * g + slot
        left = half_piece(g, slot_shard[slot], p_x, 0)
        rest = half_piece(g, slot_shard[slot], p_y, 1)
        return [
            send(left, left, un_s.at[u, 2], un_r.at[u, 3], (y_nb, z)),
            send(rest, rest, un_s.at[u, 3], un_r.at[u, 4], (x_nb, z)),
        ]

    def land(g, slot):
        line_send(g, slot_shard[slot], slot, 0, partner).wait_recv()
        pl.when(middle_chip)(passing(g, slot).start)
        for d in spread(g, slot):
            d.start()

    def turn(g, slot):
        for d in spread(g, slot):
            d.wait_recv()
        for d in cross(g, slot):
            d.start()

    def own_start(g):
        shard, _ = shape_of(g)
        for src, cols in own_parts(g, 0, shard):
            pltpu.make_async_copy(src, lands[g].at[rows_of(z * shard, shard), cols], loc.at[1 + g]).start()

    def own_wait(g):
        shard, _ = shape_of(g)
        ref = lands[g].at[rows_of(z * shard, shard), :]
        pltpu.make_async_copy(ref, ref, loc.at[1 + g]).wait()

    def whole(g):
        for slot in range(3):
            for d in cross(g, slot):
                d.wait_recv()
        own_wait(g)

    def all_sent(g):
        line_send(g, z, 0, 0, partner).wait_send()

        @pl.when(middle_chip)
        def _():
            line_send(g, z, 1, 1, inner).wait_send()
            for slot in range(3):
                passing(g, slot).wait_send()

        for slot in range(3):
            for d in spread(g, slot) + cross(g, slot):
                d.wait_send()

    kept = {}

    def keep(name, src, dst):
        kept[name] = pltpu.make_async_copy(src, dst, out_s.at[len(kept)])
        kept[name].start()

    def begin():
        small_own.start()
        rag_own.start()
        rag_out.start()
        for d in small_out:
            d.start()

    def vectors():
        small_own.wait()
        for d in small_out:
            d.wait()
        width = smalls.shape[2]
        total = jnp.zeros((smalls.shape[1], feat), f32)
        at = lax.broadcasted_iota(jnp.int32, (width, feat), 0)
        to = lax.broadcasted_iota(jnp.int32, (width, feat), 1)
        for s in range(LINE):
            place = jnp.where(jnp.logical_and(at < rows, to == at + s * rows), 1.0, 0.0).astype(bf)
            total += nn(smalls[s], place)
        vec[...] = total
        at = lax.broadcasted_iota(jnp.int32, (width, hid // 2), 0)
        to = lax.broadcasted_iota(jnp.int32, (width, hid // 2), 1)
        which = lax.broadcasted_iota(jnp.int32, (smalls.shape[1], hid // 2), 0)
        for s in range(LINE):
            line_bias = jnp.zeros((1, hid // 2), f32)
            for n in range(hid // 2 // rows):
                place = jnp.where(jnp.logical_and(at < rows, to == at + n * rows), 1.0, 0.0).astype(bf)
                picked = jnp.where(which == VECTORS + c * (hid // 2 // rows) + n, nn(smalls[s], place), 0.0)
                line_bias += jnp.sum(picked, axis=0, keepdims=True)
            bias_in[:, pl.ds(s * (hid // 2), hid // 2)] = line_bias
        rag_own.wait()
        rag_out.wait()
        bounds = jnp.where(c == z // 2, rag[0], rag[1])
        lanes = lax.broadcasted_iota(jnp.int32, (TILE, 128), 1)
        for n in range(seq // TILE):
            at = pl.ds(n * TILE, TILE)
            token = lax.broadcasted_iota(jnp.int32, (TILE, 128), 0) + n * TILE
            same = jnp.logical_and(token >= bounds[0:1, :], token < bounds[1:2, :])
            dead = jnp.where(token < bounds[2:3, :], 0.0, -1e30)
            gq[at, :] = jnp.where(lanes == 127, 1.0, jnp.where(same, group_bias, 0.0)).astype(bf)
            gk[at, :] = jnp.where(lanes == 127, dead, jnp.where(same, 1.0, 0.0)).astype(bf)
        kx[:, 128:] = gk[...]

    def x_spread():
        x_arrived()
        for d in x_fw:
            d.start()

    def norm_rows(n, _):
        at = pl.ds(pl.multiple_of(n * 64, 64), 64)
        center, r = moments(xf[at, :].astype(f32))
        db[at, pl.ds(0, feat)] = (center * r * vec[0:1, :] + vec[1:2, :]).astype(bf)
        return _

    def norm_own():
        steps = seq // 2 // 64
        lax.fori_loop(c * steps, (c + 1) * steps, norm_rows, 0)

    def norm_other():
        steps = seq // 2 // 64
        for d in x_fw:
            d.wait_recv()
        lax.fori_loop((1 - c) * steps, (2 - c) * steps, norm_rows, 0)
        keep("normed", db.at[pl.ds(0, seq), pl.ds(0, feat)], normed_o)
        keep("x", xf.at[rows_of(c * half_seq, half_seq), :], x_o)

    def project(start, stop):
        bias_row = jnp.concatenate(
            [vec[2:3, cols_of(c * half, half)], jnp.zeros((1, half), f32), vec[3:4, cols_of(c * half, half)]], axis=1
        )
        for at in range(start, stop, TILE):
            width = min(TILE, stop - at)
            got = nn(db[pl.ds(0, seq), pl.ds(0, feat)], dc[:, pl.ds(at, width)])
            big[:, pl.ds(at, width)] = (got + bias_row[:, at : at + width]).astype(bf)
        if stop == 3 * half:
            keep("wa", wa, wa_o)

    lane = lax.broadcasted_iota(jnp.int32, (TILE, 128), 1)

    def attend(t):
        k2 = big[:, pl.ds(half + t * 128, 128)]
        v2t = jnp.transpose(big[:, pl.ds(2 * half + t * 128, 128)])
        kx[:, :128] = k2

        def chunk(n, _):
            at = pl.ds(pl.multiple_of(n * TILE, TILE), TILE)
            q2 = big[at, pl.ds(t * 128, 128)] * jnp.array(HEAD_DIM ** (-0.5), bf)
            both = []
            for h in range(2):
                own = lane < HEAD_DIM if h == 0 else lane >= HEAD_DIM
                qx = jnp.concatenate([jnp.where(own, q2, jnp.zeros((), bf)), gq[at, :]], axis=1)
                s = nt(kx[...], qx)
                top = jnp.max(s, axis=0, keepdims=True)
                e = jnp.exp(s - top)
                total = jnp.sum(e, axis=0, keepdims=True)
                o = nn(v2t[h * HEAD_DIM : (h + 1) * HEAD_DIM, :], e.astype(bf))
                both.append(o / total)
                lse[2 * t + h : 2 * t + h + 1, at] = top + jnp.log(total)
            big[at, pl.ds(3 * half + t * 128, 128)] = jnp.transpose(jnp.concatenate(both, axis=0)).astype(bf)
            return _

        lax.fori_loop(0, seq // TILE, chunk, 0)
        if t == half // 128 - 1:
            keep("qkv", big, qkv_o)

    wo_own = pltpu.make_async_copy(
        wol.at[rows_of(c * half, half), :], do.at[rows_of(c * half, half), :], loc.at[5]
    )
    wo_out = send(
        wol.at[rows_of((1 - c) * half, half), :],
        do.at[rows_of(c * half, half), :], wo_s.at[0], wo_r.at[0], (core_nb, z),
    )

    def wo_swap():
        wo_own.start()
        wo_out.start()

    def wo_ready():
        wo_own.wait()
        wo_out.wait()
        keep("wob", do, wob_o)

    part = db.at[pl.ds(0, seq), pl.ds(feat, feat)]
    part_swaps = [
        send(part.at[pl.ds(n * TILE, TILE), :], three.at[pl.ds(n * TILE, TILE), :], pa_s.at[n], pa_r.at[n], (core_nb, z))
        for n in range(chunks)
    ]

    def output_rows(n):
        at = pl.ds(n * TILE, TILE)
        for m in range(2):
            db[at, pl.ds(feat + m * half, half)] = nn(
                big[at, pl.ds(3 * half, half)], do[pl.ds(m * half, half), :]
            ).astype(bf)
        part_swaps[n].start()

    def second_rows(n, _):
        at = pl.ds(pl.multiple_of(n * 64, 64), 64)
        total = xf[at, :].astype(f32) + (
            db[at, pl.ds(feat, feat)].astype(f32) + three[at, :].astype(f32) + vec[4:5, :]
        )
        xf[at, :] = total.astype(bf)
        center, r = moments(total)
        two[at, :] = (center * r * vec[5:6, :] + vec[6:7, :]).astype(bf)
        return _

    def second_norm(n):
        if n == 0:
            kept["x"].wait()
            for d in x_fw:
                d.wait_send()
        part_swaps[n].wait()
        lax.fori_loop(n * TILE // 64, (n + 1) * TILE // 64, second_rows, 0)

    tiles = 2 * hid // TILE

    def inner_tile(n):
        if n == 0:
            for name in ("qkv", "normed"):
                kept[name].wait()
        cols = pl.ds(n * TILE, TILE)

        def tile_rows(m, _):
            at = pl.ds(pl.multiple_of(m * TILE, TILE), TILE)
            u = nn(two[at, :], wb[:, cols]) + bias_in[:, cols]
            value, slope = gelu_and_slope(u)
            big[at, cols] = value.astype(bf)
            db[at, cols] = slope.astype(bf)
            return _

        lax.fori_loop(0, chunks, tile_rows, 0)

    def c_spread():
        c_arrived()
        for d in c_fw:
            d.start()

    loads = {}

    def load(name, pairs):
        n = len(loads)
        copies = [pltpu.make_async_copy(src, dst, ld.at[n, m]) for m, (src, dst) in enumerate(pairs)]
        loads[name] = copies
        for d in copies:
            d.start()

    here = set()

    def loaded(*names):
        for name in names:
            for d in loads[name] if name not in here else ():
                d.wait()
            here.add(name)

    class Unit:
        def __init__(self, n, d, col, r, w, r1, r2, zl, parts):
            self.n, self.d, self.col, self.r, self.w = n, d, col, r, w
            self.r1_at, self.r2_at, self.z_at, self.parts = r1, r2, zl, parts

        def region(self, base, row, count=1):
            ref, row0, col0 = base
            return ref.at[rows_of(row0 + row * self.r, count * self.r), pl.ds(col0, self.w)]

        def own(self, s, a, b):
            if self.col is None:
                return self.region((self.d, 0, s // 2 * self.w), (s % 2 * 2 + a) * 2 + b)
            return self.region((self.d, 0, self.col), (s * 2 + a) * 2 + b)

        def r1(self, side, m, n):
            return self.region(self.r1_at, (side * 2 + m) * 2 + n)

        def r2(self, s):
            return self.region(self.r2_at, s)

        def zl(self, d):
            return self.region(self.z_at, d)

        def sems(self, e):
            return us.at[self.n, e], ur.at[self.n, e]

        def total(self, e, count):
            ref = self.region(self.r1_at, 0, count)
            return send(ref, ref, *self.sems(e), (x_nb, z))

        def step1(self, s):
            for n in range(2):
                if s < 2:
                    send(self.own(s, n, 1 - px), self.r1(0, s, n), *self.sems(0), (x_nb, z)).start()
                else:
                    send(self.own(s, 1 - py, n), self.r1(1, s - 2, n), *self.sems(1), (y_nb, z)).start()

        def step1_all(self):
            for s in (0, 2, 1, 3):
                self.step1(s)

        def add(self, to, *more):
            value = to[...].astype(f32)
            for ref in more:
                value = value + ref[...].astype(f32)
            to[...] = value.astype(bf)

        def step2(self):
            self.total(0, 4).wait_recv()
            for m in range(2):
                for n in range(2):
                    self.add(self.r1(0, m, n), self.own(m, n, px))
                send(self.r1(0, m, 1 - py), self.r2(m), *self.sems(2), (y_nb, z)).start()
            self.total(1, 4).wait_recv()
            for m in range(2):
                for n in range(2):
                    self.add(self.r1(1, m, n), self.own(2 + m, py, n))
                send(self.r1(1, m, 1 - px), self.r2(2 + m), *self.sems(3), (x_nb, z)).start()

        def line(self):
            self.total(2, 2).wait_recv()
            for m in range(2):
                self.add(self.r2(m), self.r1(0, m, py))
            self.total(3, 2).wait_recv()
            for m in range(2):
                self.add(self.r2(2 + m), self.r1(1, m, px))
            for d in range(LINE - 1):
                to = lax.rem(z + d + 1, LINE)
                send(self.r2(to), self.zl(d), *self.sems(4 + d), (i, to)).start()

        def spread(self):
            for d in range(LINE - 1):
                self.total(4 + d, 1).wait_recv()
            self.add(self.r2(z), *[self.zl(d) for d in range(LINE - 1)])
            for off, width, place in self.parts:
                ref, row0, col0 = self.r2_at
                src = ref.at[rows_of(row0 + z * self.r, self.r), pl.ds(col0 + off, width)]
                dst = place(p, 0, width)
                send(src, dst, *self.sems(7), (x_nb, z)).start()
                send(src, dst, *self.sems(8), (y_nb, z)).start()
                pltpu.make_async_copy(src, dst, os.at[self.n]).start()

        def cross(self):
            self.total(7, 1).wait_recv()
            self.total(8, 1).wait_recv()
            for off, width, place in self.parts:
                cut = width // 256 * 128
                left, rest = place(p_x, 0, cut), place(p_y, cut, width - cut)
                send(left, left, *self.sems(9), (y_nb, z)).start()
                send(rest, rest, *self.sems(10), (x_nb, z)).start()

        def crossed(self, e):
            off = 0
            for _, width, _place in self.parts:
                cut = width // 256 * 128
                off += cut if e == 9 else width - cut
            ref, row0, col0 = self.r1_at
            ref = ref.at[rows_of(row0, self.r), pl.ds(col0, off)]
            return send(ref, ref, *self.sems(e), (x_nb, z))

        def to_core(self):
            self.crossed(9).wait_recv()
            self.crossed(10).wait_recv()
            ref = self.region(self.r1_at, 0)
            pltpu.make_async_copy(ref, ref, os.at[self.n]).wait()
            for off, width, place in self.parts:
                mine = place(None, 0, width)
                send(mine, mine, *self.sems(11), (core_nb, z)).start()

        def step2_sent(self):
            self.total(2, 2).wait_send()
            self.total(3, 2).wait_send()

        def end(self):
            self.total(11, 4).wait()
            for e in range(4, 9):
                self.total(e, 1).wait_send()
            self.crossed(9).wait_send()
            self.crossed(10).wait_send()

        def step1_sent(self):
            self.total(0, 4).wait_send()
            self.total(1, 4).wait_send()

    def place_w2(at, off, width):
        first, count = (0, half) if at is None else (at * (hid // 2 // PLANE), hid // 2 // PLANE)
        return w2_o.at[rows_of(c * (hid // 2) + first, count), pl.ds(off, width)]

    def place_w1(n):
        def place(at, off, width):
            first, count = (0, rows) if at is None else (at * (rows // PLANE), rows // PLANE)
            return w1_o.at[rows_of(first, count), cols_of(n * hid + c * (hid // 2) + off, width)]

        return place

    def place_of(ref):
        def place(at, off, width):
            first, count = (0, rows) if at is None else (at * (rows // PLANE), rows // PLANE)
            return ref.at[rows_of(first, count), cols_of(c * half + off, width)]

        return place

    r_big, r_small = hid // 2 // PLANE, rows // PLANE
    unit_c = Unit(0, dc, None, r_big, feat, (r1c, 0, 0), (r2c, 0, 0), (zc, 0, 0), [(0, feat, place_w2)])
    unit_b = [
        Unit(
            1 + n, db, n * hid, r_small, hid, (wb, 0, n * hid), (wb, 8 * r_small, n * hid), (wb, 12 * r_small, n * hid),
            [(m * (hid // 2), hid // 2, place_w1(2 * n + m)) for m in range(2)],
        )
        for n in range(2)
    ]
    unit_o = Unit(3, do, 0, r_small, half, (r1o, 0, 0), (r2a, 0, 0), (za, 0, 0), [(0, half, place_of(o_o))])
    spots = ((0, 0), (0, half), (8 * r_small, 0))
    unit_a = [
        Unit(
            4 + n, db, n * half, r_small, half, (r1c,) + spots[n], (r2a, 0, (1 + n) * half), (za, 0, (1 + n) * half),
            [(0, half, place_of(ref))],
        )
        for n, ref in enumerate((q_o, k_o, v_o))
    ]

    def going_home(src, dst, e):
        stay = c == z // 2
        mine, outs = None, []
        for k in range(2):
            b = lax.rem(z + k, 2)
            part = src.at[rows_of(b * block, block), :]
            to = dst.at[lax.rem(z, 2)]
            outs.append(send(part, to, hs.at[e, k], hr.at[e, k], (i - c + z // 2, 2 * c + b)))
            if k == 0:
                mine = pltpu.make_async_copy(part, to, hr.at[e, k])

        def start():
            pl.when(stay)(mine.start)
            pl.when(jnp.logical_not(stay))(outs[0].start)
            outs[1].start()

        def sent():
            pl.when(stay)(mine.wait)
            pl.when(jnp.logical_not(stay))(outs[0].wait_send)
            outs[1].wait_send()

        def arrived():
            pl.when(jnp.logical_not(stay))(outs[0].wait_recv)
            outs[1].wait_recv()

        return start, sent, arrived

    block_start, block_sent, block_arrived = going_home(home, block_o, 0)
    input_start, input_sent, input_arrived = going_home(home, input_o, 1)

    first_core = jnp.where(c == 0, 1.0, 0.0)
    zero_row = jnp.zeros((1, feat), f32)

    def mask():
        sums[0] = jnp.zeros(sums.shape[1:], f32)
        for d in c_fw:
            d.wait()

        def mask_rows(n, total):
            at = pl.ds(pl.multiple_of(n * TILE, TILE), TILE)
            gone = gk[at, 127:128].astype(f32) < 0.0
            value = jnp.where(gone, 0.0, up[at, :].astype(f32))
            up[at, :] = value.astype(bf)
            return total + jnp.sum(value, axis=0, keepdims=True)

        up_sum = lax.fori_loop(0, chunks, mask_rows, zero_row)
        sums[0, 7:8, :] = up_sum * first_core
        kept["wa"].wait()
        for g in (0, 1):
            all_sent(g)

    def outer_rows(s):
        dc[s % 2 * wide : (s % 2 + 1) * wide, s // 2 * feat : (s // 2 + 1) * feat] = tn(big[:, s * wide : (s + 1) * wide], up[...]).astype(bf)
        unit_c.step1(s)

    swaps = [
        send(half_in.at[pl.ds(n * TILE, TILE), :], half_in.at[pl.ds(n * TILE, TILE), :], cs.at[n], cr.at[n], (core_nb, z))
        for n in range(half_seq // TILE)
    ]

    def block_other():
        kept["wob"].wait()
        for n in range(half_seq // TILE):
            at = rows_of((1 - c) * half_seq + n * TILE, TILE)
            to = pl.ds(n * TILE, TILE)
            got = nn(big[at, :], wts[...]).astype(bf)
            for m in range(2):
                held = pl.ds(m * half_seq + n * TILE, TILE)
                do[held, :] = got[:, m * half : (m + 1) * half]
                send(
                    do.at[held, :], half_in.at[to, pl.ds(m * half, half)], cs.at[n], cr.at[n], (core_nb, z)
                ).start()

    def block_own():
        for n in range(half_seq // TILE):
            at = rows_of(c * half_seq + n * TILE, TILE)
            to = pl.ds(n * TILE, TILE)
            acc[...] = nn(big[at, :], wts[...])
            swaps[n].wait_recv()
            gone = gk[at, 127:128].astype(f32) < 0.0
            value = xf[at, :].astype(f32) + acc[...] + half_in[to, :].astype(f32) + vec[7:8, :]
            home[to, :] = jnp.where(gone, 0.0, value).astype(bf)

    def through_gelu():
        def tile(n, _):
            cols = pl.ds(pl.multiple_of(n * TILE, TILE), TILE)
            got = (nt(up[...], wts[cols, :]) * db[pl.ds(0, seq), cols].astype(f32)).astype(bf)
            big[:, cols] = got
            bias_in[:, cols] = jnp.sum(got.astype(f32), axis=0, keepdims=True)
            return _

        lax.fori_loop(0, 2 * hid // TILE, tile, 0)
        for s in range(LINE):
            sums[0, 8 + s : 9 + s, cols_of(c * wide, wide)] = bias_in[:, s * wide : (s + 1) * wide]

    def inner_grad(n):
        def inner_rows(m, _):
            at = pl.ds(pl.multiple_of(m * TILE, TILE), TILE)
            db[at, pl.ds(n * hid, hid)] = tn(two[:, at], big[:, pl.ds(n * hid, hid)]).astype(bf)
            return _

        lax.fori_loop(0, feat // TILE, inner_rows, 0)

    gs_swaps = [
        send(db.at[pl.ds(n * TILE, TILE), pl.ds(0, feat)], three.at[pl.ds(n * TILE, TILE), :], cs.at[2 + n], cr.at[2 + n], (core_nb, z))
        for n in range(chunks)
    ]

    def to_second(n):
        if n == 0:
            for d in swaps:
                d.wait_send()
        at = pl.ds(n * TILE, TILE)
        db[at, pl.ds(0, feat)] = nt(big[at, :], wb[...]).astype(bf)
        gs_swaps[n].start()
        if n == chunks - 1:
            all_sent(2)
            pl.semaphore_signal(freed_x, inc=1, device_id=(x_nb, z), device_id_type=mesh_id)
            pl.semaphore_signal(freed_y, inc=1, device_id=(y_nb, z), device_id_type=mesh_id)
            for d in range(1, LINE):
                pl.semaphore_signal(
                    freed_z, inc=1, device_id=(i, lax.rem(z + d, LINE)), device_id_type=mesh_id
                )

    def inner_free():
        pl.semaphore_wait(freed_x, 1)
        pl.semaphore_wait(freed_y, 1)
        pl.semaphore_wait(freed_z, LINE - 1)

    def weights_load():
        all_sent(3)
        load(
            "wa",
            [
                (wa_o.at[:, pl.ds(0, feat)], wts.at[pl.ds(0, feat), :]),
                (wa_o.at[:, pl.ds(feat, half)], wts.at[pl.ds(feat, feat), pl.ds(0, half)]),
                (wob_o, wts.at[pl.ds(feat, feat), pl.ds(half, half)]),
            ],
        )

    def qkv_load():
        load("qkv", [(qkv_o, big)])
        load("normed", [(normed_o, two)])

    def back_rows(n, carry):
        gain_sum, shift_sum, out_sum = carry
        at = pl.ds(pl.multiple_of(n * 64, 64), 64)
        g = db[at, pl.ds(0, feat)].astype(f32) + three[at, :].astype(f32)
        center, r = moments(xf[at, :].astype(f32))
        hat = center * r
        gh = g * hat
        h = g * vec[5:6, :]
        first = jnp.mean(h, axis=-1, keepdims=True)
        slant = jnp.mean(h * hat, axis=-1, keepdims=True)
        got = (up[at, :].astype(f32) + r * (h - first - hat * slant)).astype(bf)
        three[at, :] = got
        return (
            gain_sum + jnp.sum(gh, axis=0, keepdims=True),
            shift_sum + jnp.sum(g, axis=0, keepdims=True),
            out_sum + jnp.sum(got.astype(f32), axis=0, keepdims=True),
        )

    def second_back():
        carry = (zero_row, zero_row, zero_row)
        for n in range(chunks):
            gs_swaps[n].wait()
            carry = lax.fori_loop(n * TILE // 64, (n + 1) * TILE // 64, back_rows, carry)
        sums[0, 5:6, :] = carry[0] * first_core
        sums[0, 6:7, :] = carry[1] * first_core
        sums[0, 4:5, :] = carry[2] * first_core
        load("x", [(x_o, up.at[pl.ds(0, half_seq), :])])

    stage = dc.at[pl.ds(0, half), pl.ds(0, half)]
    o_swap = send(stage, do.at[rows_of(c * half, half), :], cs.at[6], cr.at[6], (core_nb, z))

    def output_grad():
        loaded("qkv")
        unit_c.step1_sent()
        dc[pl.ds(0, half), pl.ds(0, half)] = tn(
            big[:, pl.ds(3 * half, half)], three[:, cols_of((1 - c) * half, half)]
        ).astype(bf)
        o_swap.start()
        do[rows_of(c * half, half), :] = tn(big[:, pl.ds(3 * half, half)], three[:, cols_of(c * half, half)]).astype(bf)

    def mixed_grad():
        loaded("wa")
        for n in range(chunks):
            at = pl.ds(n * TILE, TILE)
            dc[at, pl.ds(3 * half, half)] = (
                nt(three[at, pl.ds(0, half)], wts[pl.ds(feat, half), pl.ds(half, half)])
                + nt(three[at, pl.ds(half, half)], wts[pl.ds(feat + half, half), pl.ds(half, half)])
            ).astype(bf)

    root = HEAD_DIM ** (-0.5)

    def attend_back(t):
        k2 = big[:, pl.ds(half + t * 128, 128)]
        k2t = jnp.transpose(k2)
        kx[:, :128] = k2
        acc[...] = jnp.zeros(acc.shape, f32)

        def chunk(n, _):
            at = pl.ds(pl.multiple_of(n * TILE, TILE), TILE)
            q2 = big[at, pl.ds(t * 128, 128)] * jnp.array(root, bf)
            g2 = dc[at, pl.ds(3 * half + t * 128, 128)]
            both = []
            for h in range(2):
                own = lane < HEAD_DIM if h == 0 else lane >= HEAD_DIM
                qm = jnp.where(own, q2, jnp.zeros((), bf))
                gm = jnp.where(own, g2, jnp.zeros((), bf))
                s = nt(kx[...], jnp.concatenate([qm, gq[at, :]], axis=1))
                prob = jnp.exp(s - lse[2 * t + h : 2 * t + h + 1, at])
                grad = nt(big[:, pl.ds(2 * half + t * 128, 128)], gm)
                both_of = prob * grad
                dot = jnp.sum(both_of, axis=0, keepdims=True)
                ds = (both_of - prob * dot).astype(bf)
                for which, got in enumerate((nn(ds, qm), nn(prob.astype(bf), gm))):
                    for m in range(chunks):
                        acc[:, pl.ds((which * chunks + m) * 128, 128)] += got[m * TILE : (m + 1) * TILE]
                both.append(nn(k2t[h * HEAD_DIM : (h + 1) * HEAD_DIM, :], ds))
            dc[at, pl.ds(t * 128, 128)] = (jnp.transpose(jnp.concatenate(both, axis=0)) * root).astype(bf)
            return _

        lax.fori_loop(0, chunks, chunk, 0)
        for which in range(2):
            for m in range(chunks):
                dc[pl.ds(m * TILE, TILE), pl.ds((1 + which) * half + t * 128, 128)] = acc[
                    :, pl.ds((which * chunks + m) * 128, 128)
                ].astype(bf)
        if t == half // 128 - 1:
            sums[0, 2:3, cols_of(c * half, half)] = jnp.sum(
                dc[pl.ds(0, seq), pl.ds(0, half)].astype(f32), axis=0, keepdims=True
            )
            sums[0, 3:4, cols_of(c * half, half)] = jnp.sum(
                dc[pl.ds(0, seq), pl.ds(2 * half, half)].astype(f32), axis=0, keepdims=True
            )

    def free_landing():
        unit_c.step2_sent()
        pl.semaphore_signal(free_x, inc=1, device_id=(x_nb, z), device_id_type=mesh_id)
        pl.semaphore_signal(free_y, inc=1, device_id=(y_nb, z), device_id_type=mesh_id)

    def landing_free():
        pl.semaphore_wait(free_x, 1)
        pl.semaphore_wait(free_y, 1)

    def query_key_grad():
        loaded("normed")
        for u in unit_b:
            u.step1_sent()

        def qk_rows(m, _):
            at = pl.ds(pl.multiple_of(m * TILE, TILE), TILE)
            db[at, pl.ds(0, feat)] = tn(two[:, at], dc[pl.ds(0, seq), pl.ds(0, feat)]).astype(bf)
            return _

        lax.fori_loop(0, feat // TILE, qk_rows, 0)

    def value_grad():
        def v_rows(m, _):
            at = pl.ds(pl.multiple_of(m * TILE, TILE), TILE)
            db[at, pl.ds(feat, half)] = tn(two[:, at], dc[pl.ds(0, seq), pl.ds(feat, half)]).astype(bf)
            return _

        lax.fori_loop(0, feat // TILE, v_rows, 0)

    def first_part(at):
        at = rows_of(at, TILE)
        return nt(dc[at, pl.ds(0, feat)], wts[pl.ds(0, feat), :]) + nt(
            dc[at, pl.ds(feat, half)], wts[pl.ds(feat, feat), pl.ds(0, half)]
        )

    gn_swaps = [
        send(
            up.at[pl.ds(half_seq + n * TILE, TILE), :], half_in.at[pl.ds(n * TILE, TILE), :], cs.at[7 + n], cr.at[7 + n],
            (core_nb, z),
        )
        for n in range(half_seq // TILE)
    ]

    def to_first(n):
        if n == 0:
            loaded("x")
        up[pl.ds(half_seq + n * TILE, TILE), :] = first_part((1 - c) * half_seq + n * TILE).astype(bf)
        gn_swaps[n].start()

    first_sums = [zero_row, zero_row]

    def first_back(n):
        if n == 0:
            block_sent()
        acc[...] = first_part(c * half_seq + n * TILE)
        gn_swaps[n].wait_recv()

        def first_rows(m, carry):
            gain_sum, shift_sum = carry
            at = pl.ds(pl.multiple_of(m * 64, 64), 64)
            here = pl.ds(pl.multiple_of(n * TILE + m * 64, 64), 64)
            g = acc[at, :] + half_in[here, :].astype(f32)
            center, r = moments(up[here, :].astype(f32))
            hat = center * r
            gh = g * hat
            h = g * vec[0:1, :]
            first = jnp.mean(h, axis=-1, keepdims=True)
            slant = jnp.mean(h * hat, axis=-1, keepdims=True)
            got = three[rows_of(c * half_seq + n * TILE + m * 64, 64), :].astype(f32) + r * (h - first - hat * slant)
            home[here, :] = got.astype(bf)
            return (
                gain_sum + jnp.sum(gh, axis=0, keepdims=True),
                shift_sum + jnp.sum(g, axis=0, keepdims=True),
            )

        first_sums[:] = lax.fori_loop(0, TILE // 64, first_rows, tuple(first_sums))
        if n == half_seq // TILE - 1:
            sums[0, 0:1, :] = first_sums[0]
            sums[0, 1:2, :] = first_sums[1]

    small_who = [(core_nb, z), (x_nb, z), (y_nb, z)]
    small = [send(sums.at[n], sums_in.at[n], ss.at[n], sr.at[n], small_who[n]) for n in range(3)] + [
        send(sums.at[3], sums_in.at[3 + d], ss.at[3 + d], sr.at[3 + d], (i, lax.rem(z + d + 1, LINE)))
        for d in range(LINE - 1)
    ]
    sums_out = pltpu.make_async_copy(sums.at[4], small_o, os.at[7])

    def small_step(n):
        if n > 0:
            small[n - 1].wait_recv()
            sums[n] = sums[n - 1] + sums_in[n - 1]
        for d in small[3:] if n == 3 else small[n : n + 1]:
            d.start()

    def small_end():
        for d in range(LINE - 1):
            small[3 + d].wait_recv()
        sums[4] = sums[3] + ((sums_in[3] + sums_in[4]) + sums_in[5])
        sums_out.start()

    (unit_b0, unit_b1), (unit_q, unit_k, unit_v) = unit_b, unit_a

    begin()
    first(0)
    for g in groups:
        own_start(g)
    first(1)
    land(1, 0)
    first(2)
    land(1, 1)
    turn(1, 0)
    land(0, 0)
    land(0, 1)
    vectors()
    x_start()
    turn(0, 0)
    turn(0, 1)
    land(0, 2)
    land(1, 2)
    turn(0, 2)
    first(3)
    turn(1, 1)
    land(2, 0)
    x_spread()
    norm_own()
    norm_other()
    whole(0)
    project(0, 512)
    turn(1, 2)
    project(512, 1024)
    project(1024, 1536)
    project(1536, 3 * half)
    turn(2, 0)
    land(2, 1)
    attend(0)
    attend(1)
    whole(1)
    land(2, 2)
    land(3, 0)
    wo_swap()
    attend(2)
    wo_ready()
    attend(3)
    turn(2, 1)
    turn(2, 2)
    land(3, 2)
    attend(4)
    output_rows(0)
    output_rows(1)
    land(3, 1)
    c_start()
    output_rows(2)
    output_rows(3)
    turn(3, 0)
    second_norm(0)
    second_norm(1)
    second_norm(2)
    second_norm(3)
    whole(2)
    inner_tile(0)
    inner_tile(1)
    inner_tile(2)
    inner_tile(3)
    inner_tile(4)
    inner_tile(5)
    inner_tile(6)
    inner_tile(7)
    inner_tile(8)
    c_spread()
    turn(3, 1)
    inner_tile(9)
    turn(3, 2)
    mask()
    outer_rows(0)
    outer_rows(2)
    whole(3)
    block_other()
    outer_rows(1)
    block_own()
    outer_rows(3)
    through_gelu()
    weights_load()
    to_second(0)
    to_second(1)
    block_start()
    to_second(2)
    to_second(3)
    unit_c.step2()
    second_back()
    inner_grad(0)
    inner_grad(1)
    qkv_load()
    inner_free()
    unit_b1.step1_all()
    output_grad()
    mixed_grad()
    o_swap.wait()
    unit_b0.step1_all()
    attend_back(0)
    unit_c.line()
    free_landing()
    attend_back(1)
    attend_back(2)
    unit_b1.step2()
    attend_back(3)
    unit_o.step1_all()
    attend_back(4)
    unit_b0.step2()
    unit_b1.line()
    query_key_grad()
    to_first(0)
    to_first(1)
    landing_free()
    unit_q.step1_all()
    unit_k.step1_all()
    unit_o.step2()
    value_grad()
    unit_b0.line()
    unit_k.step2()
    unit_o.line()
    unit_q.step2()
    unit_k.line()
    unit_v.step1_all()
    unit_q.line()
    unit_c.spread()
    unit_v.step2()
    unit_b0.spread()
    first_back(0)
    unit_b1.spread()
    unit_q.spread()
    unit_o.spread()
    unit_v.line()
    first_back(1)
    small_step(0)
    input_start()
    unit_k.spread()
    unit_c.cross()
    unit_o.cross()
    small_step(1)
    unit_b0.cross()
    unit_v.spread()
    unit_k.cross()
    small_step(2)
    unit_b1.cross()
    unit_c.to_core()
    unit_q.cross()
    small_step(3)
    unit_v.cross()
    unit_b1.to_core()
    unit_b0.to_core()
    small_end()
    unit_q.to_core()
    unit_k.to_core()
    unit_o.to_core()
    unit_v.to_core()
    sums_out.wait()
    for d in small + gn_swaps:
        d.wait_send()
    x_sent()
    c_sent()
    input_sent()
    block_arrived()
    input_arrived()
    units = [unit_c] + unit_b + [unit_o] + unit_a
    for u in units[1:]:
        u.step2_sent()
    for u in [unit_o] + unit_a:
        u.step1_sent()
    for u in units:
        u.end()


def run_layer(lengths, offsets, vectors, inner_bias, x, ct, wq, wk, wv, wo, w1, w2):
    rows, feat = wq.shape
    hid = w2.shape[0]
    seq = x.shape[1] * LINE
    half = feat // 2
    r_big, r_small = hid // 2 // PLANE, rows // PLANE
    f32, bf = jnp.float32, jnp.bfloat16
    dma, plain = pltpu.SemaphoreType.DMA, pltpu.SemaphoreType.REGULAR
    anywhere = pl.BlockSpec(memory_space=pl.ANY)
    here, scalars = pl.BlockSpec(memory_space=pltpu.VMEM), pl.BlockSpec(memory_space=pltpu.SMEM)
    small, bounds = (16, 384), (lengths.shape[0], 8, 128)
    made = [
        (x.shape, bf), (x.shape, bf), ((hid, feat), bf), ((rows, LINE * hid), bf),
        ((rows, feat), bf), ((rows, feat), bf), ((rows, feat), bf), ((rows, feat), bf), ((16, feat), f32),
        ((seq // 2, feat), bf), ((seq, feat), bf), ((seq, 4 * half), bf), ((feat, 3 * half), bf), ((feat, half), bf),
    ]
    held = [
        (small, bf), (bounds, jnp.int32), ((LINE,) + small, bf), (bounds, jnp.int32), ((small[0], feat), f32), ((1, 2 * hid), f32),
        ((seq, feat), bf), ((seq, feat), bf), ((feat, 4 * half), bf), ((feat, half), bf), ((feat, 2 * hid), bf),
        ((2 * hid, feat), bf), ((seq, 2 * hid), bf), ((feat, 2 * hid), bf), ((seq, feat), bf), ((seq, feat), bf),
        ((8 * r_big, feat), bf), ((4 * r_big, feat), bf), ((3 * r_big, feat), bf),
        ((8 * r_small, half), bf), ((4 * r_small, 4 * half), bf), ((3 * r_small, 4 * half), bf),
        ((seq, 256), bf), ((seq, 128), bf), ((seq, 128), bf), ((half // HEAD_DIM, seq), f32),
        ((seq // 2, feat), bf), ((seq // 2, feat), bf), ((TILE, feat), f32),
        ((5, 16, feat), f32), ((6, 16, feat), f32),
    ]
    out = pl.pallas_call(
        layer_kernel,
        out_shape=tuple(jax.ShapeDtypeStruct(shape, dtype) for shape, dtype in made),
        in_specs=[scalars] + [here] * (2 + len(vectors)) + [anywhere] * 8,
        out_specs=(anywhere,) * len(made),
        scratch_shapes=[pltpu.VMEM(shape, dtype) for shape, dtype in held]
        + [
            dma((3,)), dma((3,)), dma((4,)), dma((4,)), dma((4,)), dma((4,)),
            dma((4, 5)), dma((12, 4)), dma((12, 5)), dma((7,)), dma((2,)), dma((2,)), dma((4,)), dma((4,)), dma((5,)),
            dma((4, 3)), dma((7, 12)), dma((7, 12)), dma((2, 2)), dma((2, 2)), dma((9,)), dma((9,)), dma((6,)), dma((6,)),
            dma((8,)), plain, plain, plain, plain, plain,
        ],
        compiler_params=pltpu.CompilerParams(
            collective_id=0, has_side_effects=True, vmem_limit_bytes=VMEM_LIMIT
        ),
        name="layer",
    )(lengths, offsets, *vectors, inner_bias, x, ct, wq, wk, wv, wo, w1, w2)
    return out[:9]


def finish_kernel(
    block_ref, input_ref, w2_ref, w1_ref, q_ref, k_ref, v_ref, o_ref, small_ref,
    block_o, input_o, gain_o, shift_o, q_o, bq_o, k_o, v_o, bv_o, o_o, bo_o, gain_two_o, shift_two_o, w1_o, b1_o, w2_o, b2_o,
    held, wide, blocks, sums, ins, outs,
):
    z = lax.axis_index("chrom")
    rows, feat = q_ref.shape
    tiles = [(ref, to, pl.ds(0, rows), pl.ds(0, feat)) for ref, to in ((q_ref, q_o), (k_ref, k_o), (v_ref, v_o), (o_ref, o_o))]
    tiles += [(w1_ref, w1_o, pl.ds(0, rows), pl.ds(n * feat, feat)) for n in range(w1_ref.shape[1] // feat)]
    tiles += [(w2_ref, w2_o, pl.ds(n * rows, rows), pl.ds(0, feat)) for n in range(w2_ref.shape[0] // rows)]
    small_in = pltpu.make_async_copy(small_ref, sums, ins.at[len(tiles)])
    small_in.start()
    loads = [pltpu.make_async_copy(ref.at[at, cols], held.at[n], ins.at[n]) for n, (ref, _, at, cols) in enumerate(tiles)]
    loads += [
        pltpu.make_async_copy(ref, blocks.at[n], ins.at[len(tiles) + 1 + n]) for n, ref in enumerate((block_ref, input_ref))
    ]
    for d in loads:
        d.start()
    small_in.wait()
    spots = (gain_o, shift_o, bq_o, bv_o, bo_o, gain_two_o, shift_two_o, b2_o)
    for n, to in enumerate(spots):
        value = sums[n : n + 1, 0:rows]
        for s in range(1, LINE):
            value = jnp.where(z == s, sums[n : n + 1, s * rows : (s + 1) * rows], value)
        to[...] = value[0, :]
    value = sums[VECTORS : VECTORS + 1, :]
    for s in range(1, LINE):
        value = jnp.where(z == s, sums[VECTORS + s : VECTORS + s + 1, :], value)
    b1_o[...] = value[0, :]
    stores = []
    for n, (_, to, at, cols) in enumerate(tiles):
        loads[n].wait()
        wide[n] = held[n].astype(jnp.float32)
        stores.append(pltpu.make_async_copy(wide.at[n], to.at[at, cols], outs.at[n]))
        stores[-1].start()
    for n, to in enumerate((block_o, input_o)):
        loads[len(tiles) + n].wait()
        stores.append(pltpu.make_async_copy(blocks.at[n], to, outs.at[len(tiles) + n]))
        stores[-1].start()
    for d in stores:
        d.wait()


def finish(block_out, input_grad, w2, w1, q, k, v, o, sums):
    f32 = jnp.float32
    rows, feat = q.shape
    hid = w2.shape[0]
    tiles = 4 + w1.shape[1] // feat + hid // rows
    anywhere, here = pl.BlockSpec(memory_space=pl.ANY), pl.BlockSpec(memory_space=pltpu.VMEM)
    matrix, vector = jax.ShapeDtypeStruct((rows, feat), f32), jax.ShapeDtypeStruct((rows,), f32)
    block = jax.ShapeDtypeStruct(block_out.shape, block_out.dtype)
    made = (
        block, block, vector, vector, matrix, vector, matrix, matrix, vector, matrix, vector, vector, vector,
        jax.ShapeDtypeStruct(w1.shape, f32), jax.ShapeDtypeStruct((hid,), f32), jax.ShapeDtypeStruct(w2.shape, f32), vector,
    )
    return pl.pallas_call(
        finish_kernel,
        out_shape=made,
        in_specs=[anywhere] * 9,
        out_specs=tuple(here if len(m.shape) == 1 else anywhere for m in made),
        scratch_shapes=[
            pltpu.VMEM((tiles, rows, feat), q.dtype), pltpu.VMEM((tiles, rows, feat), f32),
            pltpu.VMEM((2,) + block_out.shape, block_out.dtype), pltpu.VMEM(sums.shape, f32),
            pltpu.SemaphoreType.DMA((tiles + 3,)), pltpu.SemaphoreType.DMA((tiles + 2,)),
        ],
        compiler_params=pltpu.CompilerParams(vmem_limit_bytes=VMEM_LIMIT),
        name="finish",
    )(block_out, input_grad, w2, w1, q, k, v, o, sums)


def paired_local(
    inputs, lengths, offsets, cotangent, norm_gain, norm_shift, query_proj, query_bias, key_proj, value_proj,
    value_bias, output_proj, output_bias, second_gain, second_shift, inner_proj, inner_bias, outer_proj, outer_bias,
):
    vectors = (norm_gain, norm_shift, query_bias, value_bias, output_bias, second_gain, second_shift, outer_bias)
    grads = run_layer(
        lengths, offsets, vectors, inner_bias, inputs, cotangent,
        query_proj, key_proj, value_proj, output_proj, inner_proj, outer_proj,
    )
    return finish(*grads)


def solution(mesh):
    paired = mesh.shape["chrom"] == 4 and mesh.shape["cells"] == 8
    placed = (
        P("cells", "chrom", None),
        P("cells"),
        P("cells", None),
        P("cells", "chrom", None),
        P("chrom"),
        P("chrom"),
        P("chrom", None),
        P("chrom"),
        P("chrom", None),
        P("chrom", None),
        P("chrom"),
        P("chrom", None),
        P("chrom"),
        P("chrom"),
        P("chrom"),
        P("chrom", None),
        P("chrom"),
        P("chrom", None),
        P("chrom"),
    )
    return jax.shard_map(
        paired_local if paired else general,
        mesh=mesh,
        in_specs=placed,
        out_specs=(
            P("cells", "chrom", None),
            P("cells", "chrom", None),
            P("chrom"),
            P("chrom"),
            P("chrom", None),
            P("chrom"),
            P("chrom", None),
            P("chrom", None),
            P("chrom"),
            P("chrom", None),
            P("chrom"),
            P("chrom"),
            P("chrom"),
            P("chrom", None),
            P("chrom"),
            P("chrom", None),
            P("chrom"),
        ),
        check_vma=False,
    )
```

```python
import functools

import jax
import jax.numpy as jnp
from jax import lax
from jax.experimental import pallas as pl
from jax.experimental.pallas import tpu as pltpu
from jax.sharding import PartitionSpec as P

HEADS = 20
HEAD_DIM = 64


eps_norm = 1e-05
group_bias = 1.0


def layer_norm(values, gain, shift):
    center = values - jnp.mean(values, axis=-1, keepdims=True)
    spread = jnp.mean(center * center, axis=-1, keepdims=True)
    return center * lax.rsqrt(spread + eps_norm) * gain + shift


def gelu_exact(values):
    return jax.nn.gelu(values, approximate=False)


def product(left, right):
    return jnp.dot(left, right, preferred_element_type=jnp.float32)


def left_product(left, right):
    return jnp.einsum("ra,rb->ab", left, right, preferred_element_type=jnp.float32)


def right_back(left, right):
    return jnp.einsum("rb,ab->ra", left, right, preferred_element_type=jnp.float32)


def column_sum(values):
    return jnp.sum(values, axis=0, dtype=jnp.float32)


def split_rows(value, outer, inner_count):
    return value.reshape(
        (outer, inner_count, value.shape[0] // (outer * inner_count)) + value.shape[1:]
    )


def general(
    inputs,
    lengths,
    offsets,
    cotangent,
    norm_gain,
    norm_shift,
    query_proj,
    query_bias,
    key_proj,
    value_proj,
    value_bias,
    output_proj,
    output_bias,
    second_gain,
    second_shift,
    inner_proj,
    inner_bias,
    outer_proj,
    outer_bias,
):
    count_chrom = lax.axis_size("chrom")
    count_cells = lax.axis_size("cells")
    block_index = lax.axis_index("chrom")
    cells_here, tokens_here, feat_width = inputs.shape
    seq_len = tokens_here * count_chrom
    row_count = cells_here * tokens_here
    inv_root = HEAD_DIM ** (-0.5)
    places = jnp.arange(seq_len, dtype=jnp.int32)
    key_live = places[None, :] < lengths[:, None]
    groups = jnp.sum((places[None, :, None] >= offsets[:, None, :]).astype(jnp.int32), axis=2)
    query_groups = lax.dynamic_slice_in_dim(groups, block_index * tokens_here, tokens_here, 1)
    query_live = lax.dynamic_slice_in_dim(key_live, block_index * tokens_here, tokens_here, 1)
    same_group = (query_groups[:, :, None] == groups[:, None, :]).astype(jnp.float32)
    mask_bias = jnp.where(key_live[:, None, :], group_bias * same_group, -jnp.inf)[:, None]
    gathered = (
        lax.all_gather(norm_gain, "chrom", axis=0, tiled=True),
        lax.all_gather(norm_shift, "chrom", axis=0, tiled=True),
        lax.all_gather(query_proj, "chrom", axis=0, tiled=True),
        lax.all_gather(query_bias, "chrom", axis=0, tiled=True),
        lax.all_gather(key_proj, "chrom", axis=0, tiled=True),
        lax.all_gather(value_proj, "chrom", axis=0, tiled=True),
        lax.all_gather(value_bias, "chrom", axis=0, tiled=True),
        lax.all_gather(output_proj, "chrom", axis=0, tiled=True),
        lax.all_gather(output_bias, "chrom", axis=0, tiled=True),
        lax.all_gather(second_gain, "chrom", axis=0, tiled=True),
        lax.all_gather(second_shift, "chrom", axis=0, tiled=True),
        lax.all_gather(inner_proj, "chrom", axis=0, tiled=True),
        lax.all_gather(inner_bias, "chrom", axis=0, tiled=True),
        lax.all_gather(outer_proj, "chrom", axis=0, tiled=True),
        lax.all_gather(outer_bias, "chrom", axis=0, tiled=True),
    )
    gain_one = gathered[0].astype(jnp.float32)
    shift_one = gathered[1].astype(jnp.float32)
    gain_two = gathered[9].astype(jnp.float32)
    shift_two = gathered[10].astype(jnp.float32)
    states = inputs.astype(jnp.float32).reshape(row_count, feat_width)
    normed_full, norm_back = jax.vjp(layer_norm, states, gain_one, shift_one)
    normed = normed_full.astype(jnp.bfloat16)
    queries = (product(normed, gathered[2]) + gathered[3].astype(jnp.float32)).astype(jnp.bfloat16)
    key_rows = product(normed, gathered[4]).astype(jnp.bfloat16)
    vals = (product(normed, gathered[5]) + gathered[6].astype(jnp.float32)).astype(jnp.bfloat16)
    keys_all, vals_all = (
        lax.all_gather(
            key_rows.reshape(cells_here, tokens_here, feat_width), "chrom", axis=1, tiled=True
        ),
        lax.all_gather(
            vals.reshape(cells_here, tokens_here, feat_width), "chrom", axis=1, tiled=True
        ),
    )
    query_heads = queries.reshape(cells_here, tokens_here, HEADS, HEAD_DIM)
    key_heads = keys_all.reshape(cells_here, seq_len, HEADS, HEAD_DIM)
    val_heads = vals_all.reshape(cells_here, seq_len, HEADS, HEAD_DIM)

    def scores_of():
        raw = (
            jnp.einsum(
                "cqhd,ckhd->chqk", query_heads, key_heads, preferred_element_type=jnp.float32
            )
            * inv_root
        )
        return raw + mask_bias

    masked = scores_of()
    row_max = jnp.max(masked, axis=-1, keepdims=True)
    exp_scores = jnp.exp(masked - row_max)
    exp_total = jnp.sum(exp_scores, axis=-1, keepdims=True)
    attn_probs = exp_scores / exp_total
    log_total = row_max + jnp.log(exp_total)
    mixed_out = jnp.einsum(
        "chqk,ckhd->cqhd",
        attn_probs.astype(jnp.bfloat16),
        val_heads,
        preferred_element_type=jnp.float32,
    )
    mixed_out = mixed_out.astype(jnp.bfloat16).reshape(row_count, feat_width)
    attended = product(mixed_out, gathered[7]) + gathered[8].astype(jnp.float32)
    middle = states + attended
    second_full, second_back = jax.vjp(layer_norm, middle, gain_two, shift_two)
    second = second_full.astype(jnp.bfloat16)
    inner_pre = product(second, gathered[11]) + gathered[12].astype(jnp.float32)
    active_full, gelu_back = jax.vjp(gelu_exact, inner_pre)
    active = active_full.astype(jnp.bfloat16)
    result = middle + product(active, gathered[13]) + gathered[14].astype(jnp.float32)
    live_rows = query_live.reshape(row_count, 1)
    block_out = (
        jnp.where(live_rows, result, 0.0)
        .astype(jnp.bfloat16)
        .reshape(cells_here, tokens_here, feat_width)
    )
    upstream = jnp.where(
        live_rows, cotangent.reshape(row_count, feat_width), jnp.zeros((), jnp.bfloat16)
    )
    outer_bias_grad = column_sum(upstream)
    outer_proj_grad = left_product(active, upstream)
    grad_active = right_back(upstream, gathered[13])
    (grad_inner_full,) = gelu_back(grad_active)
    grad_inner = grad_inner_full.astype(jnp.bfloat16)
    inner_bias_grad = column_sum(grad_inner)
    inner_proj_grad = left_product(second, grad_inner)
    grad_second = right_back(grad_inner, gathered[11])
    grad_middle_norm, second_gain_grad, second_shift_grad = second_back(grad_second)
    grad_middle = upstream.astype(jnp.float32) + grad_middle_norm
    grad_attended = grad_middle.astype(jnp.bfloat16)
    output_bias_grad = column_sum(grad_attended)
    output_proj_grad = left_product(mixed_out, grad_attended)
    grad_mixed = right_back(grad_attended, gathered[7]).astype(jnp.bfloat16)
    grad_mixed = grad_mixed.reshape(cells_here, tokens_here, HEADS, HEAD_DIM)
    attn_again = jnp.exp(scores_of() - log_total)
    grad_probs = jnp.einsum(
        "cqhd,ckhd->chqk", grad_mixed, val_heads, preferred_element_type=jnp.float32
    )
    row_dot = jnp.sum(attn_again * grad_probs, axis=-1, keepdims=True)
    grad_raw = (attn_again * (grad_probs - row_dot)).astype(jnp.bfloat16)
    grad_vals_part = jnp.einsum(
        "chqk,cqhd->ckhd",
        attn_again.astype(jnp.bfloat16),
        grad_mixed,
        preferred_element_type=jnp.float32,
    )
    grad_keys_part = (
        jnp.einsum("chqk,cqhd->ckhd", grad_raw, query_heads, preferred_element_type=jnp.float32)
        * inv_root
    )
    grad_queries = (
        jnp.einsum("chqk,ckhd->cqhd", grad_raw, key_heads, preferred_element_type=jnp.float32)
        * inv_root
    ).astype(jnp.bfloat16)
    grad_queries = grad_queries.reshape(row_count, feat_width)
    grad_keys_sum, grad_vals_sum = (
        lax.psum_scatter(
            grad_keys_part.reshape(cells_here, seq_len, feat_width).astype(jnp.bfloat16),
            "chrom",
            scatter_dimension=1,
            tiled=True,
        ).astype(jnp.float32),
        lax.psum_scatter(
            grad_vals_part.reshape(cells_here, seq_len, feat_width).astype(jnp.bfloat16),
            "chrom",
            scatter_dimension=1,
            tiled=True,
        ).astype(jnp.float32),
    )
    grad_keys = grad_keys_sum.astype(jnp.bfloat16).reshape(row_count, feat_width)
    grad_vals = grad_vals_sum.astype(jnp.bfloat16).reshape(row_count, feat_width)
    query_proj_grad = left_product(normed, grad_queries)
    query_bias_grad = column_sum(grad_queries)
    key_proj_grad = left_product(normed, grad_keys)
    value_proj_grad = left_product(normed, grad_vals)
    value_bias_grad = column_sum(grad_vals)
    grad_normed = (
        right_back(grad_queries, gathered[2])
        + right_back(grad_keys, gathered[4])
        + right_back(grad_vals, gathered[5])
    )
    grad_states_norm, norm_gain_grad, norm_shift_grad = norm_back(grad_normed)
    input_grad = (
        (grad_middle + grad_states_norm)
        .astype(jnp.bfloat16)
        .reshape(cells_here, tokens_here, feat_width)
    )
    grad_list = (
        norm_gain_grad,
        norm_shift_grad,
        query_proj_grad,
        query_bias_grad,
        key_proj_grad,
        value_proj_grad,
        value_bias_grad,
        output_proj_grad,
        output_bias_grad,
        second_gain_grad,
        second_shift_grad,
        inner_proj_grad,
        inner_bias_grad,
        outer_proj_grad,
        outer_bias_grad,
    )
    pieces = tuple((split_rows(member, count_chrom, count_cells) for member in grad_list))
    section_one = (
        lax.psum_scatter(
            pieces[0].astype(jnp.bfloat16), "cells", scatter_dimension=1, tiled=True
        ).astype(jnp.float32),
        lax.psum_scatter(
            pieces[1].astype(jnp.bfloat16), "cells", scatter_dimension=1, tiled=True
        ).astype(jnp.float32),
        lax.psum_scatter(
            pieces[2].astype(jnp.bfloat16), "cells", scatter_dimension=1, tiled=True
        ).astype(jnp.float32),
        lax.psum_scatter(
            pieces[3].astype(jnp.bfloat16), "cells", scatter_dimension=1, tiled=True
        ).astype(jnp.float32),
        lax.psum_scatter(
            pieces[4].astype(jnp.bfloat16), "cells", scatter_dimension=1, tiled=True
        ).astype(jnp.float32),
        lax.psum_scatter(
            pieces[5].astype(jnp.bfloat16), "cells", scatter_dimension=1, tiled=True
        ).astype(jnp.float32),
        lax.psum_scatter(
            pieces[6].astype(jnp.bfloat16), "cells", scatter_dimension=1, tiled=True
        ).astype(jnp.float32),
        lax.psum_scatter(
            pieces[7].astype(jnp.bfloat16), "cells", scatter_dimension=1, tiled=True
        ).astype(jnp.float32),
        lax.psum_scatter(
            pieces[8].astype(jnp.bfloat16), "cells", scatter_dimension=1, tiled=True
        ).astype(jnp.float32),
        lax.psum_scatter(
            pieces[9].astype(jnp.bfloat16), "cells", scatter_dimension=1, tiled=True
        ).astype(jnp.float32),
        lax.psum_scatter(
            pieces[10].astype(jnp.bfloat16), "cells", scatter_dimension=1, tiled=True
        ).astype(jnp.float32),
        lax.psum_scatter(
            pieces[11].astype(jnp.bfloat16), "cells", scatter_dimension=1, tiled=True
        ).astype(jnp.float32),
        lax.psum_scatter(
            pieces[12].astype(jnp.bfloat16), "cells", scatter_dimension=1, tiled=True
        ).astype(jnp.float32),
        lax.psum_scatter(
            pieces[13].astype(jnp.bfloat16), "cells", scatter_dimension=1, tiled=True
        ).astype(jnp.float32),
        lax.psum_scatter(
            pieces[14].astype(jnp.bfloat16), "cells", scatter_dimension=1, tiled=True
        ).astype(jnp.float32),
    )
    section_two = (
        lax.psum_scatter(
            section_one[0].astype(jnp.bfloat16), "chrom", scatter_dimension=0, tiled=True
        ).astype(jnp.float32),
        lax.psum_scatter(
            section_one[1].astype(jnp.bfloat16), "chrom", scatter_dimension=0, tiled=True
        ).astype(jnp.float32),
        lax.psum_scatter(
            section_one[2].astype(jnp.bfloat16), "chrom", scatter_dimension=0, tiled=True
        ).astype(jnp.float32),
        lax.psum_scatter(
            section_one[3].astype(jnp.bfloat16), "chrom", scatter_dimension=0, tiled=True
        ).astype(jnp.float32),
        lax.psum_scatter(
            section_one[4].astype(jnp.bfloat16), "chrom", scatter_dimension=0, tiled=True
        ).astype(jnp.float32),
        lax.psum_scatter(
            section_one[5].astype(jnp.bfloat16), "chrom", scatter_dimension=0, tiled=True
        ).astype(jnp.float32),
        lax.psum_scatter(
            section_one[6].astype(jnp.bfloat16), "chrom", scatter_dimension=0, tiled=True
        ).astype(jnp.float32),
        lax.psum_scatter(
            section_one[7].astype(jnp.bfloat16), "chrom", scatter_dimension=0, tiled=True
        ).astype(jnp.float32),
        lax.psum_scatter(
            section_one[8].astype(jnp.bfloat16), "chrom", scatter_dimension=0, tiled=True
        ).astype(jnp.float32),
        lax.psum_scatter(
            section_one[9].astype(jnp.bfloat16), "chrom", scatter_dimension=0, tiled=True
        ).astype(jnp.float32),
        lax.psum_scatter(
            section_one[10].astype(jnp.bfloat16), "chrom", scatter_dimension=0, tiled=True
        ).astype(jnp.float32),
        lax.psum_scatter(
            section_one[11].astype(jnp.bfloat16), "chrom", scatter_dimension=0, tiled=True
        ).astype(jnp.float32),
        lax.psum_scatter(
            section_one[12].astype(jnp.bfloat16), "chrom", scatter_dimension=0, tiled=True
        ).astype(jnp.float32),
        lax.psum_scatter(
            section_one[13].astype(jnp.bfloat16), "chrom", scatter_dimension=0, tiled=True
        ).astype(jnp.float32),
        lax.psum_scatter(
            section_one[14].astype(jnp.bfloat16), "chrom", scatter_dimension=0, tiled=True
        ).astype(jnp.float32),
    )
    rejoined = (
        lax.all_gather(section_two[0].astype(jnp.bfloat16), "cells", axis=1, tiled=True).astype(
            jnp.float32
        ),
        lax.all_gather(section_two[1].astype(jnp.bfloat16), "cells", axis=1, tiled=True).astype(
            jnp.float32
        ),
        lax.all_gather(section_two[2].astype(jnp.bfloat16), "cells", axis=1, tiled=True).astype(
            jnp.float32
        ),
        lax.all_gather(section_two[3].astype(jnp.bfloat16), "cells", axis=1, tiled=True).astype(
            jnp.float32
        ),
        lax.all_gather(section_two[4].astype(jnp.bfloat16), "cells", axis=1, tiled=True).astype(
            jnp.float32
        ),
        lax.all_gather(section_two[5].astype(jnp.bfloat16), "cells", axis=1, tiled=True).astype(
            jnp.float32
        ),
        lax.all_gather(section_two[6].astype(jnp.bfloat16), "cells", axis=1, tiled=True).astype(
            jnp.float32
        ),
        lax.all_gather(section_two[7].astype(jnp.bfloat16), "cells", axis=1, tiled=True).astype(
            jnp.float32
        ),
        lax.all_gather(section_two[8].astype(jnp.bfloat16), "cells", axis=1, tiled=True).astype(
            jnp.float32
        ),
        lax.all_gather(section_two[9].astype(jnp.bfloat16), "cells", axis=1, tiled=True).astype(
            jnp.float32
        ),
        lax.all_gather(section_two[10].astype(jnp.bfloat16), "cells", axis=1, tiled=True).astype(
            jnp.float32
        ),
        lax.all_gather(section_two[11].astype(jnp.bfloat16), "cells", axis=1, tiled=True).astype(
            jnp.float32
        ),
        lax.all_gather(section_two[12].astype(jnp.bfloat16), "cells", axis=1, tiled=True).astype(
            jnp.float32
        ),
        lax.all_gather(section_two[13].astype(jnp.bfloat16), "cells", axis=1, tiled=True).astype(
            jnp.float32
        ),
        lax.all_gather(section_two[14].astype(jnp.bfloat16), "cells", axis=1, tiled=True).astype(
            jnp.float32
        ),
    )
    final = tuple(
        (
            member.reshape(
                (member.shape[0] * member.shape[1] * member.shape[2],) + member.shape[3:]
            )
            for member in rejoined
        )
    )
    return (block_out, input_grad) + tuple(final)


PLANE = 4
LINE = 4
VMEM_LIMIT = 65000 * 1024


def rows_of(start, count):
    return pl.ds(pl.multiple_of(start, 16), count)


def cols_of(start, count):
    return pl.ds(pl.multiple_of(start, 128), count)


VECTORS = 8
TILE = 256
AHEAD = 1024
BACK = 512


def nt(left, right):
    return lax.dot_general(left, right, (((1,), (1,)), ((), ())), preferred_element_type=jnp.float32)


def nn(left, right):
    return jnp.dot(left, right, preferred_element_type=jnp.float32)


def moments(values):
    center = values - jnp.mean(values, axis=-1, keepdims=True)
    spread = jnp.mean(center * center, axis=-1, keepdims=True)
    return center, lax.rsqrt(spread + eps_norm)


def gelu_and_slope(u):
    gauss = jnp.exp(u * u * -0.5)
    t = 1.0 / (1.0 + jnp.abs(u) * (0.3275911 * 0.5 ** 0.5))
    poly = 0.5 * 1.061405429
    for factor in (-1.453152027, 1.421413741, -0.284496736, 0.254829592):
        poly = poly * t + 0.5 * factor
    tail = poly * t * gauss
    phi_sum = jnp.where(u < 0.0, tail, 1.0 - tail)
    return u * phi_sum, phi_sum + u * gauss * 0.3989422804014327


def tn(left, right):
    return lax.dot_general(left, right, (((0,), (0,)), ((), ())), preferred_element_type=jnp.float32)


def layer_kernel(
    len_ref, off_ref, v0, v1, v2, v3, v4, v5, v6, v7, b_ref, x_ref, ct_ref, wq_ref, wk_ref, wv_ref, wo_ref, w1_ref, w2_ref,
    block_o, input_o, w2_o, w1_o, q_o, k_o, v_o, o_o, small_o, x_o, normed_o, qkv_o, wa_o, wob_o,
    small_ref, rag_ref, smalls, rag, vec, bias_in, xf, up, dc, do, wb, wts, big, db, two, three, r1c, r2c, zc, r2a, za, kx, lse,
    half_in, home, acc, sums, sums_in,
    sm_s, sm_r, ex_s, ex_r, fw_s, fw_r, ln_s, un_s, un_r, loc, wo_s, wo_r, pa_s, pa_r, out_s,
    ld, us, ur, hs, hr, cs, cr, ss, sr, os, free_x, free_y, freed_x, freed_y, freed_z,
):
    f32, bf = jnp.float32, jnp.bfloat16
    i, z = lax.axis_index("cells"), lax.axis_index("chrom")
    p, c = i // 2, lax.rem(i, 2)
    px, py = lax.rem(p, 2), p // 2
    x_nb, y_nb, core_nb = i + 2 - 4 * px, i + 4 - 8 * py, i + 1 - 2 * c
    p_x, p_y = p + 1 - 2 * px, p + 2 - 4 * py
    rows = wq_ref.shape[0]
    feat = wq_ref.shape[1]
    half = feat // 2
    hid = w2_ref.shape[0]
    block = x_ref.shape[1]
    seq = block * LINE
    half_seq = seq // 2
    chunks = seq // TILE
    wide = hid // 2
    mesh_id = pl.DeviceIdType.MESH
    part_rows, hid_part = rows // PLANE, hid // 2 // PLANE

    small_ref[...] = jnp.zeros(small_ref.shape, bf)
    for n, ref in enumerate((v0, v1, v2, v3, v4, v5, v6, v7)):
        small_ref[n : n + 1, 0:rows] = ref[...][None, :]
    for n in range(hid // rows):
        small_ref[VECTORS + n : VECTORS + n + 1, 0:rows] = b_ref[n * rows : (n + 1) * rows][None, :]
    count = off_ref.shape[1]
    never = 2 ** 30
    for n in range(rag_ref.shape[0]):
        rag_ref[n] = jnp.full(rag_ref.shape[1:], never, jnp.int32)
        rag_ref[n, 1:2, 0:count] = off_ref[n : n + 1, :]
        end = rag_ref[n, 1:2, :]
        group = lax.broadcasted_iota(jnp.int32, end.shape, 1)
        rag_ref[n, 0:1, :] = jnp.where(group == 0, 0, pltpu.roll(end, 1, 1))
        rag_ref[n, 2:3, :] = jnp.full(end.shape, len_ref[n], jnp.int32)

    barrier = pltpu.get_barrier_semaphore()
    line_ids = [
        (i - c + lax.rem(c + dc, 2), lax.rem(z + dz, LINE))
        for dc in range(2)
        for dz in range(LINE)
        if dc or dz
    ]
    for who in line_ids + [(x_nb, z), (y_nb, z)]:
        pl.semaphore_signal(barrier, inc=1, device_id=who, device_id_type=pl.DeviceIdType.MESH)
    pl.semaphore_wait(barrier, len(line_ids) + 2)

    def send(src, dst, s, r, who):
        return pltpu.make_async_remote_copy(
            src_ref=src, dst_ref=dst, send_sem=s, recv_sem=r, device_id=who,
            device_id_type=pl.DeviceIdType.MESH,
        )

    small_own = pltpu.make_async_copy(small_ref, smalls.at[z], loc.at[0])
    small_out = [
        send(small_ref, smalls.at[z], sm_s.at[d], sm_r.at[d], (i, lax.rem(z + d + 1, LINE)))
        for d in range(LINE - 1)
    ]

    rag_own = pltpu.make_async_copy(rag_ref.at[lax.rem(z, 2)], rag.at[0], loc.at[6])
    rag_out = send(rag_ref.at[lax.rem(z, 2)], rag.at[1], wo_s.at[1], wo_r.at[1], (core_nb, z))

    def exchange(src, dst, which):
        stay = c == z // 2
        mine, outs = None, []
        for k in range(2):
            j = lax.rem(z + k, 2)
            to = dst.at[rows_of(z * block, block), :]
            r = ex_r.at[2 * which + k]
            outs.append(send(src.at[j], to, ex_s.at[2 * which + k], r, (i - c + z // 2, 2 * c + j)))
            if k == 0:
                mine = pltpu.make_async_copy(src.at[j], to, r)

        def start():
            pl.when(stay)(mine.start)
            pl.when(jnp.logical_not(stay))(outs[0].start)
            outs[1].start()

        def arrived():
            pl.when(stay)(mine.wait)
            pl.when(jnp.logical_not(stay))(outs[0].wait_recv)
            outs[1].wait_recv()

        def sent():
            pl.when(jnp.logical_not(stay))(outs[0].wait_send)
            outs[1].wait_send()

        return start, arrived, sent

    def forward(dst, which):
        return [
            send(
                dst.at[rows_of((2 * c + b) * block, block), :],
                dst.at[rows_of((2 * c + b) * block, block), :],
                fw_s.at[2 * which + b], fw_r.at[2 * which + b], (core_nb, z),
            )
            for b in range(2)
        ]

    x_start, x_arrived, x_sent = exchange(x_ref, xf, 0)
    c_start, c_arrived, c_sent = exchange(ct_ref, up, 1)
    x_fw, c_fw = forward(xf, 0), forward(up, 1)

    wa, wol = dc.at[:, pl.ds(0, 3 * half)], dc.at[:, pl.ds(3 * half, half)]
    lands = (wa, wol, wb, wts)
    groups = range(4)
    partner, inner = z + 1 - 2 * lax.rem(z, 2), 3 - z
    low = z < 2
    middle_chip = jnp.logical_or(z == 1, z == 2)
    slot_shard = (partner, jnp.where(low, 2, 1), jnp.where(low, 3, 0))

    def own_parts(g, row, count):
        if g == 0:
            return [
                (ref.at[rows_of(row, count), cols_of(c * half, half)], pl.ds(n * half, half))
                for n, ref in enumerate((wq_ref, wk_ref, wv_ref))
            ]
        if g == 1:
            return [(wo_ref.at[rows_of(row, count), cols_of(c * half, half)], pl.ds(0, half))]
        if g == 2:
            return [
                (w1_ref.at[rows_of(row, count), cols_of(n * hid + c * (hid // 2), hid // 2)], pl.ds(n * (hid // 2), hid // 2))
                for n in range(LINE)
            ]
        return [(w2_ref.at[rows_of(c * (hid // 2) + row, count), :], pl.ds(0, feat))]

    def shape_of(g):
        return (rows, part_rows) if g < 3 else (hid // 2, hid_part)

    def piece(g, s, at):
        shard, count = shape_of(g)
        return lands[g].at[rows_of(s * shard + at * count, count), :]

    def half_piece(g, s, at, side):
        shard, count = shape_of(g)
        width = lands[g].shape[1]
        cut = width // 256 * 128
        cols = pl.ds(cut, width - cut) if side else pl.ds(0, cut)
        return lands[g].at[rows_of(s * shard + at * count, count), cols]

    def line_send(g, s, slot, e, to):
        return send(piece(g, s, p), piece(g, s, p), ln_s.at[g, e], un_r.at[3 * g + slot, 0], (i, to))

    def first(g):
        shard, count = shape_of(g)
        for src, cols in own_parts(g, p * count, count):
            dst = lands[g].at[rows_of(z * shard + p * count, count), cols]
            send(src, dst, ln_s.at[g, 0], un_r.at[3 * g, 0], (i, partner)).start()

        @pl.when(middle_chip)
        def _():
            for src, cols in own_parts(g, p * count, count):
                dst = lands[g].at[rows_of(z * shard + p * count, count), cols]
                send(src, dst, ln_s.at[g, 1], un_r.at[3 * g + 1, 0], (i, inner)).start()

    def passing(g, slot):
        if slot == 0:
            return line_send(g, slot_shard[0], 2, 2, inner)
        return line_send(g, slot_shard[slot], slot, 2 + slot, partner)

    def spread(g, slot):
        own = piece(g, slot_shard[slot], p)
        u = 3 * g + slot
        return [
            send(own, own, un_s.at[u, 0], un_r.at[u, 1], (x_nb, z)),
            send(own, own, un_s.at[u, 1], un_r.at[u, 2], (y_nb, z)),
        ]

    def cross(g, slot):
        u = 3 * g + slot
        left = half_piece(g, slot_shard[slot], p_x, 0)
        rest = half_piece(g, slot_shard[slot], p_y, 1)
        return [
            send(left, left, un_s.at[u, 2], un_r.at[u, 3], (y_nb, z)),
            send(rest, rest, un_s.at[u, 3], un_r.at[u, 4], (x_nb, z)),
        ]

    def land(g, slot):
        line_send(g, slot_shard[slot], slot, 0, partner).wait_recv()
        pl.when(middle_chip)(passing(g, slot).start)
        for d in spread(g, slot):
            d.start()

    def turn(g, slot):
        for d in spread(g, slot):
            d.wait_recv()
        for d in cross(g, slot):
            d.start()

    def own_start(g):
        shard, _ = shape_of(g)
        for src, cols in own_parts(g, 0, shard):
            pltpu.make_async_copy(src, lands[g].at[rows_of(z * shard, shard), cols], loc.at[1 + g]).start()

    def own_wait(g):
        shard, _ = shape_of(g)
        ref = lands[g].at[rows_of(z * shard, shard), :]
        pltpu.make_async_copy(ref, ref, loc.at[1 + g]).wait()

    def whole(g):
        for slot in range(3):
            for d in cross(g, slot):
                d.wait_recv()
        own_wait(g)

    def all_sent(g):
        line_send(g, z, 0, 0, partner).wait_send()

        @pl.when(middle_chip)
        def _():
            line_send(g, z, 1, 1, inner).wait_send()
            for slot in range(3):
                passing(g, slot).wait_send()

        for slot in range(3):
            for d in spread(g, slot) + cross(g, slot):
                d.wait_send()

    kept = {}

    def keep(name, src, dst):
        kept[name] = pltpu.make_async_copy(src, dst, out_s.at[len(kept)])
        kept[name].start()

    def begin():
        small_own.start()
        rag_own.start()
        rag_out.start()
        for d in small_out:
            d.start()

    def vectors():
        small_own.wait()
        for d in small_out:
            d.wait()
        width = smalls.shape[2]
        total = jnp.zeros((smalls.shape[1], feat), f32)
        at = lax.broadcasted_iota(jnp.int32, (width, feat), 0)
        to = lax.broadcasted_iota(jnp.int32, (width, feat), 1)
        for s in range(LINE):
            place = jnp.where(jnp.logical_and(at < rows, to == at + s * rows), 1.0, 0.0).astype(bf)
            total += nn(smalls[s], place)
        vec[...] = total
        at = lax.broadcasted_iota(jnp.int32, (width, hid // 2), 0)
        to = lax.broadcasted_iota(jnp.int32, (width, hid // 2), 1)
        which = lax.broadcasted_iota(jnp.int32, (smalls.shape[1], hid // 2), 0)
        for s in range(LINE):
            line_bias = jnp.zeros((1, hid // 2), f32)
            for n in range(hid // 2 // rows):
                place = jnp.where(jnp.logical_and(at < rows, to == at + n * rows), 1.0, 0.0).astype(bf)
                picked = jnp.where(which == VECTORS + c * (hid // 2 // rows) + n, nn(smalls[s], place), 0.0)
                line_bias += jnp.sum(picked, axis=0, keepdims=True)
            bias_in[:, pl.ds(s * (hid // 2), hid // 2)] = line_bias
        rag_own.wait()
        rag_out.wait()
        bounds = jnp.where(c == z // 2, rag[0], rag[1])
        lanes = lax.broadcasted_iota(jnp.int32, (TILE, 128), 1)
        for n in range(seq // TILE):
            at = pl.ds(n * TILE, TILE)
            token = lax.broadcasted_iota(jnp.int32, (TILE, 128), 0) + n * TILE
            same = jnp.logical_and(token >= bounds[0:1, :], token < bounds[1:2, :])
            dead = jnp.where(token < bounds[2:3, :], 0.0, -1e30)
            kx[at, pl.ds(128, 128)] = jnp.where(lanes == 127, dead, jnp.where(same, 1.0, 0.0)).astype(bf)

    def query_mark(at, lane):
        same = kx[at, pl.ds(128, 128)] * jnp.array(group_bias, bf)
        return jnp.where(lane == 127, jnp.ones((), bf), same)

    def x_spread():
        x_arrived()
        for d in x_fw:
            d.start()

    def norm_rows(n, _):
        at = pl.ds(pl.multiple_of(n * 64, 64), 64)
        center, r = moments(xf[at, :].astype(f32))
        db[at, pl.ds(0, feat)] = (center * r * vec[0:1, :] + vec[1:2, :]).astype(bf)
        return _

    def norm_own():
        steps = seq // 2 // 64
        lax.fori_loop(c * steps, (c + 1) * steps, norm_rows, 0)

    def norm_other():
        steps = seq // 2 // 64
        for d in x_fw:
            d.wait_recv()
        lax.fori_loop((1 - c) * steps, (2 - c) * steps, norm_rows, 0)
        keep("normed", db.at[pl.ds(0, seq), pl.ds(0, feat)], normed_o)
        keep("x", xf.at[rows_of(c * half_seq, half_seq), :], x_o)

    def project(start, stop):
        bias_row = jnp.concatenate(
            [vec[2:3, cols_of(c * half, half)], jnp.zeros((1, half), f32), vec[3:4, cols_of(c * half, half)]], axis=1
        )
        for at in range(start, stop, TILE):
            width = min(TILE, stop - at)
            got = nn(db[pl.ds(0, seq), pl.ds(0, feat)], dc[:, pl.ds(at, width)])
            big[:, pl.ds(at, width)] = (got + bias_row[:, at : at + width]).astype(bf)
        if stop == 3 * half:
            keep("wa", wa, wa_o)

    def attend(t):
        lane = lax.broadcasted_iota(jnp.int32, (AHEAD, 128), 1)
        k2 = big[:, pl.ds(half + t * 128, 128)]
        v2t = jnp.transpose(big[:, pl.ds(2 * half + t * 128, 128)])
        kx[:, :128] = k2

        def chunk(n, _):
            at = pl.ds(pl.multiple_of(n * AHEAD, AHEAD), AHEAD)
            q2 = big[at, pl.ds(t * 128, 128)] * jnp.array(HEAD_DIM ** (-0.5), bf)
            mark = query_mark(at, lane)
            both = []
            for h in range(2):
                own = lane < HEAD_DIM if h == 0 else lane >= HEAD_DIM
                qx = jnp.concatenate([jnp.where(own, q2, jnp.zeros((), bf)), mark], axis=1)
                s = nt(kx[...], qx)
                top = jnp.max(s, axis=0, keepdims=True)
                e = jnp.exp(s - top)
                total = jnp.sum(e, axis=0, keepdims=True)
                o = nn(v2t[h * HEAD_DIM : (h + 1) * HEAD_DIM, :], e.astype(bf))
                both.append(o / total)
                lse[2 * t + h : 2 * t + h + 1, at] = top + jnp.log(total)
            big[at, pl.ds(3 * half + t * 128, 128)] = jnp.transpose(jnp.concatenate(both, axis=0)).astype(bf)
            return _

        lax.fori_loop(0, seq // AHEAD, chunk, 0)
        if t == half // 128 - 1:
            keep("qkv", big, qkv_o)

    wo_own = pltpu.make_async_copy(
        wol.at[rows_of(c * half, half), :], do.at[rows_of(c * half, half), :], loc.at[5]
    )
    wo_out = send(
        wol.at[rows_of((1 - c) * half, half), :],
        do.at[rows_of(c * half, half), :], wo_s.at[0], wo_r.at[0], (core_nb, z),
    )

    def wo_swap():
        wo_own.start()
        wo_out.start()

    def wo_ready():
        wo_own.wait()
        wo_out.wait()
        keep("wob", do, wob_o)

    part = db.at[pl.ds(0, seq), pl.ds(feat, feat)]
    part_swaps = [
        send(part.at[pl.ds(n * TILE, TILE), :], three.at[pl.ds(n * TILE, TILE), :], pa_s.at[n], pa_r.at[n], (core_nb, z))
        for n in range(chunks)
    ]

    def output_rows(n):
        at = pl.ds(n * TILE, TILE)
        for m in range(2):
            db[at, pl.ds(feat + m * half, half)] = nn(
                big[at, pl.ds(3 * half, half)], do[pl.ds(m * half, half), :]
            ).astype(bf)
        part_swaps[n].start()

    def second_rows(n, _):
        at = pl.ds(pl.multiple_of(n * 64, 64), 64)
        total = xf[at, :].astype(f32) + (
            db[at, pl.ds(feat, feat)].astype(f32) + three[at, :].astype(f32) + vec[4:5, :]
        )
        xf[at, :] = total.astype(bf)
        center, r = moments(total)
        two[at, :] = (center * r * vec[5:6, :] + vec[6:7, :]).astype(bf)
        return _

    def second_norm(n):
        if n == 0:
            kept["x"].wait()
            for d in x_fw:
                d.wait_send()
        part_swaps[n].wait()
        lax.fori_loop(n * TILE // 64, (n + 1) * TILE // 64, second_rows, 0)

    tiles = 2 * hid // TILE

    def inner_tile(n):
        if n == 0:
            for name in ("qkv", "normed"):
                kept[name].wait()
        cols = pl.ds(n * TILE, TILE)

        def tile_rows(m, _):
            at = pl.ds(pl.multiple_of(m * TILE, TILE), TILE)
            u = nn(two[at, :], wb[:, cols]) + bias_in[:, cols]
            value, slope = gelu_and_slope(u)
            big[at, cols] = value.astype(bf)
            db[at, cols] = slope.astype(bf)
            return _

        lax.fori_loop(0, chunks, tile_rows, 0, unroll=4)

    def c_spread():
        c_arrived()
        for d in c_fw:
            d.start()

    loads = {}

    def load(name, pairs):
        n = len(loads)
        copies = [pltpu.make_async_copy(src, dst, ld.at[n, m]) for m, (src, dst) in enumerate(pairs)]
        loads[name] = copies
        for d in copies:
            d.start()

    here = set()

    def loaded(*names):
        for name in names:
            for d in loads[name] if name not in here else ():
                d.wait()
            here.add(name)

    class Unit:
        def __init__(self, n, d, col, r, w, r1, r2, zl, parts):
            self.n, self.d, self.col, self.r, self.w = n, d, col, r, w
            self.r1_at, self.r2_at, self.z_at, self.parts = r1, r2, zl, parts

        def region(self, base, row, count=1):
            ref, row0, col0 = base
            return ref.at[rows_of(row0 + row * self.r, count * self.r), pl.ds(col0, self.w)]

        def own(self, s, a, b):
            if self.col is None:
                return self.region((self.d, 0, s // 2 * self.w), (s % 2 * 2 + a) * 2 + b)
            return self.region((self.d, 0, self.col), (s * 2 + a) * 2 + b)

        def r1(self, side, m, n):
            return self.region(self.r1_at, (side * 2 + m) * 2 + n)

        def r2(self, s):
            return self.region(self.r2_at, s)

        def zl(self, d):
            return self.region(self.z_at, d)

        def sems(self, e):
            return us.at[self.n, e], ur.at[self.n, e]

        def total(self, e, count):
            ref = self.region(self.r1_at, 0, count)
            return send(ref, ref, *self.sems(e), (x_nb, z))

        def step1(self, s):
            for n in range(2):
                if s < 2:
                    send(self.own(s, n, 1 - px), self.r1(0, s, n), *self.sems(0), (x_nb, z)).start()
                else:
                    send(self.own(s, 1 - py, n), self.r1(1, s - 2, n), *self.sems(1), (y_nb, z)).start()

        def step1_all(self):
            for s in (0, 2, 1, 3):
                self.step1(s)

        def add(self, to, *more):
            value = to[...].astype(f32)
            for ref in more:
                value = value + ref[...].astype(f32)
            to[...] = value.astype(bf)

        def step2(self):
            self.total(0, 4).wait_recv()
            for m in range(2):
                for n in range(2):
                    self.add(self.r1(0, m, n), self.own(m, n, px))
                send(self.r1(0, m, 1 - py), self.r2(m), *self.sems(2), (y_nb, z)).start()
            self.total(1, 4).wait_recv()
            for m in range(2):
                for n in range(2):
                    self.add(self.r1(1, m, n), self.own(2 + m, py, n))
                send(self.r1(1, m, 1 - px), self.r2(2 + m), *self.sems(3), (x_nb, z)).start()

        def line(self):
            self.total(2, 2).wait_recv()
            for m in range(2):
                self.add(self.r2(m), self.r1(0, m, py))
            self.total(3, 2).wait_recv()
            for m in range(2):
                self.add(self.r2(2 + m), self.r1(1, m, px))
            for d in range(LINE - 1):
                to = lax.rem(z + d + 1, LINE)
                send(self.r2(to), self.zl(d), *self.sems(4 + d), (i, to)).start()

        def spread(self):
            for d in range(LINE - 1):
                self.total(4 + d, 1).wait_recv()
            self.add(self.r2(z), *[self.zl(d) for d in range(LINE - 1)])
            for off, width, place in self.parts:
                ref, row0, col0 = self.r2_at
                src = ref.at[rows_of(row0 + z * self.r, self.r), pl.ds(col0 + off, width)]
                dst = place(p, 0, width)
                send(src, dst, *self.sems(7), (x_nb, z)).start()
                send(src, dst, *self.sems(8), (y_nb, z)).start()
                pltpu.make_async_copy(src, dst, os.at[self.n]).start()

        def cross(self):
            self.total(7, 1).wait_recv()
            self.total(8, 1).wait_recv()
            for off, width, place in self.parts:
                cut = width // 256 * 128
                left, rest = place(p_x, 0, cut), place(p_y, cut, width - cut)
                send(left, left, *self.sems(9), (y_nb, z)).start()
                send(rest, rest, *self.sems(10), (x_nb, z)).start()

        def crossed(self, e):
            off = 0
            for _, width, _place in self.parts:
                cut = width // 256 * 128
                off += cut if e == 9 else width - cut
            ref, row0, col0 = self.r1_at
            ref = ref.at[rows_of(row0, self.r), pl.ds(col0, off)]
            return send(ref, ref, *self.sems(e), (x_nb, z))

        def to_core(self):
            self.crossed(9).wait_recv()
            self.crossed(10).wait_recv()
            ref = self.region(self.r1_at, 0)
            pltpu.make_async_copy(ref, ref, os.at[self.n]).wait()
            for off, width, place in self.parts:
                mine = place(None, 0, width)
                send(mine, mine, *self.sems(11), (core_nb, z)).start()

        def step2_sent(self):
            self.total(2, 2).wait_send()
            self.total(3, 2).wait_send()

        def end(self):
            self.total(11, 4).wait()
            for e in range(4, 9):
                self.total(e, 1).wait_send()
            self.crossed(9).wait_send()
            self.crossed(10).wait_send()

        def step1_sent(self):
            self.total(0, 4).wait_send()
            self.total(1, 4).wait_send()

    def place_w2(at, off, width):
        first, count = (0, half) if at is None else (at * (hid // 2 // PLANE), hid // 2 // PLANE)
        return w2_o.at[rows_of(c * (hid // 2) + first, count), pl.ds(off, width)]

    def place_w1(n):
        def place(at, off, width):
            first, count = (0, rows) if at is None else (at * (rows // PLANE), rows // PLANE)
            return w1_o.at[rows_of(first, count), cols_of(n * hid + c * (hid // 2) + off, width)]

        return place

    def place_of(ref):
        def place(at, off, width):
            first, count = (0, rows) if at is None else (at * (rows // PLANE), rows // PLANE)
            return ref.at[rows_of(first, count), cols_of(c * half + off, width)]

        return place

    r_big, r_small = hid // 2 // PLANE, rows // PLANE
    unit_c = Unit(0, dc, None, r_big, feat, (r1c, 0, 0), (r2c, 0, 0), (zc, 0, 0), [(0, feat, place_w2)])
    unit_b = [
        Unit(
            1 + n, db, n * hid, r_small, hid, (wb, 0, n * hid), (wb, 8 * r_small, n * hid), (wb, 12 * r_small, n * hid),
            [(m * (hid // 2), hid // 2, place_w1(2 * n + m)) for m in range(2)],
        )
        for n in range(2)
    ]
    spots = ((0, 0), (0, half), (8 * r_small, 0), (8 * r_small, half))
    unit_o = Unit(3, do, 0, r_small, half, (r1c,) + spots[3], (r2a, 0, 0), (za, 0, 0), [(0, half, place_of(o_o))])
    unit_a = [
        Unit(
            4 + n, db, n * half, r_small, half, (r1c,) + spots[n], (r2a, 0, (1 + n) * half), (za, 0, (1 + n) * half),
            [(0, half, place_of(ref))],
        )
        for n, ref in enumerate((q_o, k_o, v_o))
    ]

    def going_home(src, dst, e):
        stay = c == z // 2
        mine, outs = None, []
        for k in range(2):
            b = lax.rem(z + k, 2)
            part = src.at[rows_of(b * block, block), :]
            to = dst.at[lax.rem(z, 2)]
            outs.append(send(part, to, hs.at[e, k], hr.at[e, k], (i - c + z // 2, 2 * c + b)))
            if k == 0:
                mine = pltpu.make_async_copy(part, to, hr.at[e, k])

        def start():
            pl.when(stay)(mine.start)
            pl.when(jnp.logical_not(stay))(outs[0].start)
            outs[1].start()

        def sent():
            pl.when(stay)(mine.wait)
            pl.when(jnp.logical_not(stay))(outs[0].wait_send)
            outs[1].wait_send()

        def arrived():
            pl.when(jnp.logical_not(stay))(outs[0].wait_recv)
            outs[1].wait_recv()

        return start, sent, arrived

    block_start, block_sent, block_arrived = going_home(home, block_o, 0)
    input_start, input_sent, input_arrived = going_home(home, input_o, 1)

    first_core = jnp.where(c == 0, 1.0, 0.0)
    zero_row = jnp.zeros((1, feat), f32)

    def mask():
        sums[0] = jnp.zeros(sums.shape[1:], f32)
        for d in c_fw:
            d.wait()

        def mask_rows(n, total):
            at = pl.ds(pl.multiple_of(n * TILE, TILE), TILE)
            gone = kx[at, 255:256].astype(f32) < 0.0
            value = jnp.where(gone, 0.0, up[at, :].astype(f32))
            up[at, :] = value.astype(bf)
            return total + jnp.sum(value, axis=0, keepdims=True)

        up_sum = lax.fori_loop(0, chunks, mask_rows, zero_row)
        sums[0, 7:8, :] = up_sum * first_core
        kept["wa"].wait()
        for g in (0, 1):
            all_sent(g)

    def outer_rows(s):
        dc[s % 2 * wide : (s % 2 + 1) * wide, s // 2 * feat : (s // 2 + 1) * feat] = tn(big[:, s * wide : (s + 1) * wide], up[...]).astype(bf)
        unit_c.step1(s)

    swaps = [
        send(half_in.at[pl.ds(n * TILE, TILE), :], half_in.at[pl.ds(n * TILE, TILE), :], cs.at[n], cr.at[n], (core_nb, z))
        for n in range(half_seq // TILE)
    ]

    def block_other():
        kept["wob"].wait()
        for n in range(half_seq // TILE):
            at = rows_of((1 - c) * half_seq + n * TILE, TILE)
            to = pl.ds(n * TILE, TILE)
            got = nn(big[at, :], wts[...]).astype(bf)
            for m in range(2):
                held = pl.ds(m * half_seq + n * TILE, TILE)
                do[held, :] = got[:, m * half : (m + 1) * half]
                send(
                    do.at[held, :], half_in.at[to, pl.ds(m * half, half)], cs.at[n], cr.at[n], (core_nb, z)
                ).start()

    def block_own():
        for n in range(half_seq // TILE):
            at = rows_of(c * half_seq + n * TILE, TILE)
            to = pl.ds(n * TILE, TILE)
            acc[...] = nn(big[at, :], wts[...])
            swaps[n].wait_recv()
            gone = kx[at, 255:256].astype(f32) < 0.0
            value = xf[at, :].astype(f32) + acc[...] + half_in[to, :].astype(f32) + vec[7:8, :]
            home[to, :] = jnp.where(gone, 0.0, value).astype(bf)

    def through_gelu():
        def tile(n, _):
            cols = pl.ds(pl.multiple_of(n * TILE, TILE), TILE)
            got = (nt(up[...], wts[cols, :]) * db[pl.ds(0, seq), cols].astype(f32)).astype(bf)
            big[:, cols] = got
            bias_in[:, cols] = jnp.sum(got.astype(f32), axis=0, keepdims=True)
            return _

        lax.fori_loop(0, 2 * hid // TILE, tile, 0)
        for s in range(LINE):
            sums[0, 8 + s : 9 + s, cols_of(c * wide, wide)] = bias_in[:, s * wide : (s + 1) * wide]

    def inner_grad(n):
        def inner_rows(m, _):
            at = pl.ds(pl.multiple_of(m * TILE, TILE), TILE)
            db[at, pl.ds(n * hid, hid)] = tn(two[:, at], big[:, pl.ds(n * hid, hid)]).astype(bf)
            return _

        lax.fori_loop(0, feat // TILE, inner_rows, 0)

    gs_swaps = [
        send(db.at[pl.ds(n * TILE, TILE), pl.ds(0, feat)], three.at[pl.ds(n * TILE, TILE), :], cs.at[2 + n], cr.at[2 + n], (core_nb, z))
        for n in range(chunks)
    ]

    def to_second(n):
        if n == 0:
            for d in swaps:
                d.wait_send()
        at = pl.ds(n * TILE, TILE)
        db[at, pl.ds(0, feat)] = nt(big[at, :], wb[...]).astype(bf)
        gs_swaps[n].start()
        if n == chunks - 1:
            all_sent(2)
            pl.semaphore_signal(freed_x, inc=1, device_id=(x_nb, z), device_id_type=mesh_id)
            pl.semaphore_signal(freed_y, inc=1, device_id=(y_nb, z), device_id_type=mesh_id)
            for d in range(1, LINE):
                pl.semaphore_signal(
                    freed_z, inc=1, device_id=(i, lax.rem(z + d, LINE)), device_id_type=mesh_id
                )

    def inner_free():
        pl.semaphore_wait(freed_x, 1)
        pl.semaphore_wait(freed_y, 1)
        pl.semaphore_wait(freed_z, LINE - 1)

    def weights_load():
        all_sent(3)
        load(
            "wa",
            [
                (wa_o.at[:, pl.ds(0, feat)], wts.at[pl.ds(0, feat), :]),
                (wa_o.at[:, pl.ds(feat, half)], wts.at[pl.ds(feat, feat), pl.ds(0, half)]),
                (wob_o, wts.at[pl.ds(feat, feat), pl.ds(half, half)]),
            ],
        )

    def qkv_load():
        load("qkv", [(qkv_o, big)])
        load("normed", [(normed_o, two)])

    def back_rows(n, carry):
        gain_sum, shift_sum, out_sum = carry
        at = pl.ds(pl.multiple_of(n * 64, 64), 64)
        g = db[at, pl.ds(0, feat)].astype(f32) + three[at, :].astype(f32)
        center, r = moments(xf[at, :].astype(f32))
        hat = center * r
        gh = g * hat
        h = g * vec[5:6, :]
        first = jnp.mean(h, axis=-1, keepdims=True)
        slant = jnp.mean(h * hat, axis=-1, keepdims=True)
        got = (up[at, :].astype(f32) + r * (h - first - hat * slant)).astype(bf)
        three[at, :] = got
        return (
            gain_sum + jnp.sum(gh, axis=0, keepdims=True),
            shift_sum + jnp.sum(g, axis=0, keepdims=True),
            out_sum + jnp.sum(got.astype(f32), axis=0, keepdims=True),
        )

    def second_back():
        carry = (zero_row, zero_row, zero_row)
        for n in range(chunks):
            gs_swaps[n].wait()
            carry = lax.fori_loop(n * TILE // 64, (n + 1) * TILE // 64, back_rows, carry)
        sums[0, 5:6, :] = carry[0] * first_core
        sums[0, 6:7, :] = carry[1] * first_core
        sums[0, 4:5, :] = carry[2] * first_core
        load("x", [(x_o, up.at[pl.ds(0, half_seq), :])])

    stage = dc.at[pl.ds(0, half), pl.ds(0, half)]
    o_swap = send(stage, do.at[rows_of(c * half, half), :], cs.at[6], cr.at[6], (core_nb, z))

    def output_grad():
        loaded("qkv")
        unit_c.step1_sent()
        dc[pl.ds(0, half), pl.ds(0, half)] = tn(
            big[:, pl.ds(3 * half, half)], three[:, cols_of((1 - c) * half, half)]
        ).astype(bf)
        o_swap.start()
        do[rows_of(c * half, half), :] = tn(big[:, pl.ds(3 * half, half)], three[:, cols_of(c * half, half)]).astype(bf)

    def mixed_grad():
        loaded("wa")
        for n in range(chunks):
            at = pl.ds(n * TILE, TILE)
            dc[at, pl.ds(3 * half, half)] = (
                nt(three[at, pl.ds(0, half)], wts[pl.ds(feat, half), pl.ds(half, half)])
                + nt(three[at, pl.ds(half, half)], wts[pl.ds(feat + half, half), pl.ds(half, half)])
            ).astype(bf)

    root = HEAD_DIM ** (-0.5)

    def attend_back(t):
        lane = lax.broadcasted_iota(jnp.int32, (BACK, 128), 1)
        k2 = big[:, pl.ds(half + t * 128, 128)]
        k2t = jnp.transpose(k2)
        kx[:, :128] = k2
        acc[...] = jnp.zeros(acc.shape, f32)

        def chunk(n, _):
            at = pl.ds(pl.multiple_of(n * BACK, BACK), BACK)
            q2 = big[at, pl.ds(t * 128, 128)] * jnp.array(root, bf)
            mark = query_mark(at, lane)
            g2 = dc[at, pl.ds(3 * half + t * 128, 128)]
            both = []
            for h in range(2):
                own = lane < HEAD_DIM if h == 0 else lane >= HEAD_DIM
                qm = jnp.where(own, q2, jnp.zeros((), bf))
                gm = jnp.where(own, g2, jnp.zeros((), bf))
                s = nt(kx[...], jnp.concatenate([qm, mark], axis=1))
                prob = jnp.exp(s - lse[2 * t + h : 2 * t + h + 1, at])
                grad = nt(big[:, pl.ds(2 * half + t * 128, 128)], gm)
                both_of = prob * grad
                dot = jnp.sum(both_of, axis=0, keepdims=True)
                ds = (both_of - prob * dot).astype(bf)
                for which, got in enumerate((nn(ds, qm), nn(prob.astype(bf), gm))):
                    for m in range(chunks):
                        acc[:, pl.ds((which * chunks + m) * 128, 128)] += got[m * TILE : (m + 1) * TILE]
                both.append(nn(k2t[h * HEAD_DIM : (h + 1) * HEAD_DIM, :], ds))
            dc[at, pl.ds(t * 128, 128)] = (jnp.transpose(jnp.concatenate(both, axis=0)) * root).astype(bf)
            return _

        lax.fori_loop(0, seq // BACK, chunk, 0)
        for which in range(2):
            for m in range(chunks):
                dc[pl.ds(m * TILE, TILE), pl.ds((1 + which) * half + t * 128, 128)] = acc[
                    :, pl.ds((which * chunks + m) * 128, 128)
                ].astype(bf)
        if t == half // 128 - 1:
            sums[0, 2:3, cols_of(c * half, half)] = jnp.sum(
                dc[pl.ds(0, seq), pl.ds(0, half)].astype(f32), axis=0, keepdims=True
            )
            sums[0, 3:4, cols_of(c * half, half)] = jnp.sum(
                dc[pl.ds(0, seq), pl.ds(2 * half, half)].astype(f32), axis=0, keepdims=True
            )

    def free_landing():
        unit_c.step2_sent()
        pl.semaphore_signal(free_x, inc=1, device_id=(x_nb, z), device_id_type=mesh_id)
        pl.semaphore_signal(free_y, inc=1, device_id=(y_nb, z), device_id_type=mesh_id)

    def landing_free():
        pl.semaphore_wait(free_x, 1)
        pl.semaphore_wait(free_y, 1)

    def query_key_grad():
        loaded("normed")
        for u in unit_b:
            u.step1_sent()

        def qk_rows(m, _):
            at = pl.ds(pl.multiple_of(m * TILE, TILE), TILE)
            db[at, pl.ds(0, feat)] = tn(two[:, at], dc[pl.ds(0, seq), pl.ds(0, feat)]).astype(bf)
            return _

        lax.fori_loop(0, feat // TILE, qk_rows, 0)

    def value_grad():
        def v_rows(m, _):
            at = pl.ds(pl.multiple_of(m * TILE, TILE), TILE)
            db[at, pl.ds(feat, half)] = tn(two[:, at], dc[pl.ds(0, seq), pl.ds(feat, half)]).astype(bf)
            return _

        lax.fori_loop(0, feat // TILE, v_rows, 0)

    def first_part(at):
        at = rows_of(at, TILE)
        return nt(dc[at, pl.ds(0, feat)], wts[pl.ds(0, feat), :]) + nt(
            dc[at, pl.ds(feat, half)], wts[pl.ds(feat, feat), pl.ds(0, half)]
        )

    gn_swaps = [
        send(
            up.at[pl.ds(half_seq + n * TILE, TILE), :], half_in.at[pl.ds(n * TILE, TILE), :], cs.at[7 + n], cr.at[7 + n],
            (core_nb, z),
        )
        for n in range(half_seq // TILE)
    ]

    def to_first(n):
        if n == 0:
            loaded("x")
        up[pl.ds(half_seq + n * TILE, TILE), :] = first_part((1 - c) * half_seq + n * TILE).astype(bf)
        gn_swaps[n].start()

    first_sums = [zero_row, zero_row]

    def first_back(n):
        if n == 0:
            block_sent()
        acc[...] = first_part(c * half_seq + n * TILE)
        gn_swaps[n].wait_recv()

        def first_rows(m, carry):
            gain_sum, shift_sum = carry
            at = pl.ds(pl.multiple_of(m * 64, 64), 64)
            here = pl.ds(pl.multiple_of(n * TILE + m * 64, 64), 64)
            g = acc[at, :] + half_in[here, :].astype(f32)
            center, r = moments(up[here, :].astype(f32))
            hat = center * r
            gh = g * hat
            h = g * vec[0:1, :]
            first = jnp.mean(h, axis=-1, keepdims=True)
            slant = jnp.mean(h * hat, axis=-1, keepdims=True)
            got = three[rows_of(c * half_seq + n * TILE + m * 64, 64), :].astype(f32) + r * (h - first - hat * slant)
            home[here, :] = got.astype(bf)
            return (
                gain_sum + jnp.sum(gh, axis=0, keepdims=True),
                shift_sum + jnp.sum(g, axis=0, keepdims=True),
            )

        first_sums[:] = lax.fori_loop(0, TILE // 64, first_rows, tuple(first_sums))
        if n == half_seq // TILE - 1:
            sums[0, 0:1, :] = first_sums[0]
            sums[0, 1:2, :] = first_sums[1]

    small_who = [(core_nb, z), (x_nb, z), (y_nb, z)]
    small = [send(sums.at[0], sums_in.at[n], ss.at[n], sr.at[n], small_who[n]) for n in range(3)] + [
        send(sums.at[0], sums_in.at[3 + d], ss.at[3 + d], sr.at[3 + d], (i, lax.rem(z + d + 1, LINE)))
        for d in range(LINE - 1)
    ]
    sums_out = pltpu.make_async_copy(sums.at[0], small_o, os.at[7])

    def small_step(n):
        if n > 0:
            small[n - 1].wait()
            sums[0] = sums[0] + sums_in[n - 1]
        for d in small[3:] if n == 3 else small[n : n + 1]:
            d.start()

    def small_end():
        for d in range(LINE - 1):
            small[3 + d].wait()
        sums[0] = sums[0] + ((sums_in[3] + sums_in[4]) + sums_in[5])
        sums_out.start()

    (unit_b0, unit_b1), (unit_q, unit_k, unit_v) = unit_b, unit_a

    begin()
    first(0)
    for g in groups:
        own_start(g)
    first(1)
    land(0, 1)
    land(0, 0)
    land(1, 0)
    first(2)
    turn(0, 1)
    land(0, 2)
    land(1, 2)
    land(1, 1)
    x_start()
    turn(0, 0)
    vectors()
    turn(0, 2)
    land(2, 0)
    land(2, 1)
    turn(1, 2)
    turn(1, 0)
    first(3)
    x_spread()
    whole(0)
    turn(1, 1)
    norm_own()
    norm_other()
    turn(2, 1)
    project(0, 512)
    turn(2, 0)
    project(512, 1024)
    project(1024, 1536)
    project(1536, 3 * half)
    whole(1)
    land(3, 0)
    wo_swap()
    land(2, 2)
    attend(0)
    wo_ready()
    land(3, 1)
    attend(1)
    attend(2)
    c_start()
    attend(3)
    attend(4)
    output_rows(0)
    output_rows(1)
    output_rows(2)
    output_rows(3)
    turn(2, 2)
    turn(3, 0)
    second_norm(0)
    second_norm(1)
    second_norm(2)
    second_norm(3)
    land(3, 2)
    turn(3, 1)
    whole(2)
    inner_tile(0)
    inner_tile(1)
    inner_tile(2)
    inner_tile(3)
    inner_tile(4)
    inner_tile(5)
    inner_tile(6)
    c_spread()
    inner_tile(7)
    inner_tile(8)
    inner_tile(9)
    turn(3, 2)
    mask()
    outer_rows(0)
    outer_rows(2)
    outer_rows(1)
    outer_rows(3)
    whole(3)
    block_other()
    block_own()
    through_gelu()
    weights_load()
    to_second(0)
    to_second(1)
    to_second(2)
    to_second(3)
    unit_c.step2()
    second_back()
    block_start()
    inner_grad(0)
    inner_free()
    unit_b0.step1_all()
    inner_grad(1)
    qkv_load()
    output_grad()
    o_swap.wait()
    mixed_grad()
    attend_back(0)
    unit_c.line()
    free_landing()
    unit_b1.step1_all()
    attend_back(1)
    attend_back(2)
    unit_b0.step2()
    landing_free()
    unit_o.step1_all()
    attend_back(3)
    unit_b1.step2()
    attend_back(4)
    query_key_grad()
    unit_q.step1_all()
    to_first(0)
    unit_b0.line()
    value_grad()
    unit_b1.line()
    unit_o.step2()
    unit_k.step1_all()
    unit_q.step2()
    unit_v.step1_all()
    to_first(1)
    unit_o.line()
    unit_q.line()
    unit_k.step2()
    unit_v.step2()
    unit_b1.spread()
    unit_o.spread()
    unit_k.line()
    unit_c.spread()
    unit_q.spread()
    unit_v.line()
    unit_o.cross()
    first_back(0)
    first_back(1)
    small_step(0)
    unit_k.spread()
    input_start()
    unit_q.cross()
    unit_b0.spread()
    small_step(1)
    unit_v.spread()
    unit_b1.cross()
    unit_q.to_core()
    small_step(2)
    unit_c.cross()
    unit_v.cross()
    unit_b0.cross()
    small_step(3)
    unit_c.to_core()
    unit_b1.to_core()
    unit_k.cross()
    small_end()
    unit_b0.to_core()
    unit_v.to_core()
    unit_o.to_core()
    unit_k.to_core()
    sums_out.wait()
    for d in gn_swaps:
        d.wait_send()
    x_sent()
    c_sent()
    input_sent()
    block_arrived()
    input_arrived()
    units = [unit_c] + unit_b + [unit_o] + unit_a
    for u in units[1:]:
        u.step2_sent()
    for u in [unit_o] + unit_a:
        u.step1_sent()
    for u in units:
        u.end()


def run_layer(lengths, offsets, vectors, inner_bias, x, ct, wq, wk, wv, wo, w1, w2):
    rows, feat = wq.shape
    hid = w2.shape[0]
    seq = x.shape[1] * LINE
    half = feat // 2
    r_big, r_small = hid // 2 // PLANE, rows // PLANE
    f32, bf = jnp.float32, jnp.bfloat16
    dma, plain = pltpu.SemaphoreType.DMA, pltpu.SemaphoreType.REGULAR
    anywhere = pl.BlockSpec(memory_space=pl.ANY)
    here, scalars = pl.BlockSpec(memory_space=pltpu.VMEM), pl.BlockSpec(memory_space=pltpu.SMEM)
    small, bounds = (16, 384), (lengths.shape[0], 8, 128)
    made = [
        (x.shape, bf), (x.shape, bf), ((hid, feat), bf), ((rows, LINE * hid), bf),
        ((rows, feat), bf), ((rows, feat), bf), ((rows, feat), bf), ((rows, feat), bf), ((16, feat), f32),
        ((seq // 2, feat), bf), ((seq, feat), bf), ((seq, 4 * half), bf), ((feat, 3 * half), bf), ((feat, half), bf),
    ]
    held = [
        (small, bf), (bounds, jnp.int32), ((LINE,) + small, bf), (bounds, jnp.int32), ((small[0], feat), f32), ((1, 2 * hid), f32),
        ((seq, feat), bf), ((seq, feat), bf), ((feat, 4 * half), bf), ((feat, half), bf), ((feat, 2 * hid), bf),
        ((2 * hid, feat), bf), ((seq, 2 * hid), bf), ((feat, 2 * hid), bf), ((seq, feat), bf), ((seq, feat), bf),
        ((8 * r_big, feat), bf), ((4 * r_big, feat), bf), ((3 * r_big, feat), bf),
        ((4 * r_small, 4 * half), bf), ((3 * r_small, 4 * half), bf),
        ((seq, 256), bf), ((half // HEAD_DIM, seq), f32),
        ((seq // 2, feat), bf), ((seq // 2, feat), bf), ((TILE, feat), f32),
        ((1, 16, feat), f32), ((6, 16, feat), f32),
    ]
    out = pl.pallas_call(
        layer_kernel,
        out_shape=tuple(jax.ShapeDtypeStruct(shape, dtype) for shape, dtype in made),
        in_specs=[scalars] + [here] * (2 + len(vectors)) + [anywhere] * 8,
        out_specs=(anywhere,) * len(made),
        scratch_shapes=[pltpu.VMEM(shape, dtype) for shape, dtype in held]
        + [
            dma((3,)), dma((3,)), dma((4,)), dma((4,)), dma((4,)), dma((4,)),
            dma((4, 5)), dma((12, 4)), dma((12, 5)), dma((7,)), dma((2,)), dma((2,)), dma((4,)), dma((4,)), dma((5,)),
            dma((4, 3)), dma((7, 12)), dma((7, 12)), dma((2, 2)), dma((2, 2)), dma((9,)), dma((9,)), dma((6,)), dma((6,)),
            dma((8,)), plain, plain, plain, plain, plain,
        ],
        compiler_params=pltpu.CompilerParams(
            collective_id=0, has_side_effects=True, vmem_limit_bytes=VMEM_LIMIT
        ),
        name="layer",
    )(lengths, offsets, *vectors, inner_bias, x, ct, wq, wk, wv, wo, w1, w2)
    return out[:9]


def finish_kernel(
    block_ref, input_ref, w2_ref, w1_ref, q_ref, k_ref, v_ref, o_ref, small_ref,
    block_o, input_o, gain_o, shift_o, q_o, bq_o, k_o, v_o, bv_o, o_o, bo_o, gain_two_o, shift_two_o, w1_o, b1_o, w2_o, b2_o,
    held, wide, blocks, sums, ins, outs,
):
    z = lax.axis_index("chrom")
    rows, feat = q_ref.shape
    tiles = [(ref, to, pl.ds(0, rows), pl.ds(0, feat)) for ref, to in ((q_ref, q_o), (k_ref, k_o), (v_ref, v_o), (o_ref, o_o))]
    tiles += [(w1_ref, w1_o, pl.ds(0, rows), pl.ds(n * feat, feat)) for n in range(w1_ref.shape[1] // feat)]
    tiles += [(w2_ref, w2_o, pl.ds(n * rows, rows), pl.ds(0, feat)) for n in range(w2_ref.shape[0] // rows)]
    small_in = pltpu.make_async_copy(small_ref, sums, ins.at[len(tiles)])
    small_in.start()
    loads = [pltpu.make_async_copy(ref.at[at, cols], held.at[n], ins.at[n]) for n, (ref, _, at, cols) in enumerate(tiles)]
    loads += [
        pltpu.make_async_copy(ref, blocks.at[n], ins.at[len(tiles) + 1 + n]) for n, ref in enumerate((block_ref, input_ref))
    ]
    for d in loads:
        d.start()
    small_in.wait()
    spots = (gain_o, shift_o, bq_o, bv_o, bo_o, gain_two_o, shift_two_o, b2_o)
    for n, to in enumerate(spots):
        value = sums[n : n + 1, 0:rows]
        for s in range(1, LINE):
            value = jnp.where(z == s, sums[n : n + 1, s * rows : (s + 1) * rows], value)
        to[...] = value[0, :]
    value = sums[VECTORS : VECTORS + 1, :]
    for s in range(1, LINE):
        value = jnp.where(z == s, sums[VECTORS + s : VECTORS + s + 1, :], value)
    b1_o[...] = value[0, :]
    stores = []
    for n, (_, to, at, cols) in enumerate(tiles):
        loads[n].wait()
        wide[n] = held[n].astype(jnp.float32)
        stores.append(pltpu.make_async_copy(wide.at[n], to.at[at, cols], outs.at[n]))
        stores[-1].start()
    for n, to in enumerate((block_o, input_o)):
        loads[len(tiles) + n].wait()
        stores.append(pltpu.make_async_copy(blocks.at[n], to, outs.at[len(tiles) + n]))
        stores[-1].start()
    for d in stores:
        d.wait()


def finish(block_out, input_grad, w2, w1, q, k, v, o, sums):
    f32 = jnp.float32
    rows, feat = q.shape
    hid = w2.shape[0]
    tiles = 4 + w1.shape[1] // feat + hid // rows
    anywhere, here = pl.BlockSpec(memory_space=pl.ANY), pl.BlockSpec(memory_space=pltpu.VMEM)
    matrix, vector = jax.ShapeDtypeStruct((rows, feat), f32), jax.ShapeDtypeStruct((rows,), f32)
    block = jax.ShapeDtypeStruct(block_out.shape, block_out.dtype)
    made = (
        block, block, vector, vector, matrix, vector, matrix, matrix, vector, matrix, vector, vector, vector,
        jax.ShapeDtypeStruct(w1.shape, f32), jax.ShapeDtypeStruct((hid,), f32), jax.ShapeDtypeStruct(w2.shape, f32), vector,
    )
    return pl.pallas_call(
        finish_kernel,
        out_shape=made,
        in_specs=[anywhere] * 9,
        out_specs=tuple(here if len(m.shape) == 1 else anywhere for m in made),
        scratch_shapes=[
            pltpu.VMEM((tiles, rows, feat), q.dtype), pltpu.VMEM((tiles, rows, feat), f32),
            pltpu.VMEM((2,) + block_out.shape, block_out.dtype), pltpu.VMEM(sums.shape, f32),
            pltpu.SemaphoreType.DMA((tiles + 3,)), pltpu.SemaphoreType.DMA((tiles + 2,)),
        ],
        compiler_params=pltpu.CompilerParams(vmem_limit_bytes=VMEM_LIMIT),
        name="finish",
    )(block_out, input_grad, w2, w1, q, k, v, o, sums)


def paired_local(
    inputs, lengths, offsets, cotangent, norm_gain, norm_shift, query_proj, query_bias, key_proj, value_proj,
    value_bias, output_proj, output_bias, second_gain, second_shift, inner_proj, inner_bias, outer_proj, outer_bias,
):
    vectors = (norm_gain, norm_shift, query_bias, value_bias, output_bias, second_gain, second_shift, outer_bias)
    grads = run_layer(
        lengths, offsets, vectors, inner_bias, inputs, cotangent,
        query_proj, key_proj, value_proj, output_proj, inner_proj, outer_proj,
    )
    return finish(*grads)


def solution(mesh):
    paired = mesh.shape["chrom"] == 4 and mesh.shape["cells"] == 8
    placed = (
        P("cells", "chrom", None),
        P("cells"),
        P("cells", None),
        P("cells", "chrom", None),
        P("chrom"),
        P("chrom"),
        P("chrom", None),
        P("chrom"),
        P("chrom", None),
        P("chrom", None),
        P("chrom"),
        P("chrom", None),
        P("chrom"),
        P("chrom"),
        P("chrom"),
        P("chrom", None),
        P("chrom"),
        P("chrom", None),
        P("chrom"),
    )
    return jax.shard_map(
        paired_local if paired else general,
        mesh=mesh,
        in_specs=placed,
        out_specs=(
            P("cells", "chrom", None),
            P("cells", "chrom", None),
            P("chrom"),
            P("chrom"),
            P("chrom", None),
            P("chrom"),
            P("chrom", None),
            P("chrom", None),
            P("chrom"),
            P("chrom", None),
            P("chrom"),
            P("chrom"),
            P("chrom"),
            P("chrom", None),
            P("chrom"),
            P("chrom", None),
            P("chrom"),
        ),
        check_vma=False,
    )
```

```python
import functools

import jax
import jax.numpy as jnp
from jax import lax
from jax.experimental import pallas as pl
from jax.experimental.pallas import tpu as pltpu
from jax.sharding import PartitionSpec as P

HEADS = 20
HEAD_DIM = 64


eps_norm = 1e-05
group_bias = 1.0


def layer_norm(values, gain, shift):
    center = values - jnp.mean(values, axis=-1, keepdims=True)
    spread = jnp.mean(center * center, axis=-1, keepdims=True)
    return center * lax.rsqrt(spread + eps_norm) * gain + shift


def gelu_exact(values):
    return jax.nn.gelu(values, approximate=False)


def product(left, right):
    return jnp.dot(left, right, preferred_element_type=jnp.float32)


def left_product(left, right):
    return jnp.einsum("ra,rb->ab", left, right, preferred_element_type=jnp.float32)


def right_back(left, right):
    return jnp.einsum("rb,ab->ra", left, right, preferred_element_type=jnp.float32)


def column_sum(values):
    return jnp.sum(values, axis=0, dtype=jnp.float32)


def split_rows(value, outer, inner_count):
    return value.reshape(
        (outer, inner_count, value.shape[0] // (outer * inner_count)) + value.shape[1:]
    )


def general(
    inputs,
    lengths,
    offsets,
    cotangent,
    norm_gain,
    norm_shift,
    query_proj,
    query_bias,
    key_proj,
    value_proj,
    value_bias,
    output_proj,
    output_bias,
    second_gain,
    second_shift,
    inner_proj,
    inner_bias,
    outer_proj,
    outer_bias,
):
    count_chrom = lax.axis_size("chrom")
    count_cells = lax.axis_size("cells")
    block_index = lax.axis_index("chrom")
    cells_here, tokens_here, feat_width = inputs.shape
    seq_len = tokens_here * count_chrom
    row_count = cells_here * tokens_here
    inv_root = HEAD_DIM ** (-0.5)
    places = jnp.arange(seq_len, dtype=jnp.int32)
    key_live = places[None, :] < lengths[:, None]
    groups = jnp.sum((places[None, :, None] >= offsets[:, None, :]).astype(jnp.int32), axis=2)
    query_groups = lax.dynamic_slice_in_dim(groups, block_index * tokens_here, tokens_here, 1)
    query_live = lax.dynamic_slice_in_dim(key_live, block_index * tokens_here, tokens_here, 1)
    same_group = (query_groups[:, :, None] == groups[:, None, :]).astype(jnp.float32)
    mask_bias = jnp.where(key_live[:, None, :], group_bias * same_group, -jnp.inf)[:, None]
    gathered = (
        lax.all_gather(norm_gain, "chrom", axis=0, tiled=True),
        lax.all_gather(norm_shift, "chrom", axis=0, tiled=True),
        lax.all_gather(query_proj, "chrom", axis=0, tiled=True),
        lax.all_gather(query_bias, "chrom", axis=0, tiled=True),
        lax.all_gather(key_proj, "chrom", axis=0, tiled=True),
        lax.all_gather(value_proj, "chrom", axis=0, tiled=True),
        lax.all_gather(value_bias, "chrom", axis=0, tiled=True),
        lax.all_gather(output_proj, "chrom", axis=0, tiled=True),
        lax.all_gather(output_bias, "chrom", axis=0, tiled=True),
        lax.all_gather(second_gain, "chrom", axis=0, tiled=True),
        lax.all_gather(second_shift, "chrom", axis=0, tiled=True),
        lax.all_gather(inner_proj, "chrom", axis=0, tiled=True),
        lax.all_gather(inner_bias, "chrom", axis=0, tiled=True),
        lax.all_gather(outer_proj, "chrom", axis=0, tiled=True),
        lax.all_gather(outer_bias, "chrom", axis=0, tiled=True),
    )
    gain_one = gathered[0].astype(jnp.float32)
    shift_one = gathered[1].astype(jnp.float32)
    gain_two = gathered[9].astype(jnp.float32)
    shift_two = gathered[10].astype(jnp.float32)
    states = inputs.astype(jnp.float32).reshape(row_count, feat_width)
    normed_full, norm_back = jax.vjp(layer_norm, states, gain_one, shift_one)
    normed = normed_full.astype(jnp.bfloat16)
    queries = (product(normed, gathered[2]) + gathered[3].astype(jnp.float32)).astype(jnp.bfloat16)
    key_rows = product(normed, gathered[4]).astype(jnp.bfloat16)
    vals = (product(normed, gathered[5]) + gathered[6].astype(jnp.float32)).astype(jnp.bfloat16)
    keys_all, vals_all = (
        lax.all_gather(
            key_rows.reshape(cells_here, tokens_here, feat_width), "chrom", axis=1, tiled=True
        ),
        lax.all_gather(
            vals.reshape(cells_here, tokens_here, feat_width), "chrom", axis=1, tiled=True
        ),
    )
    query_heads = queries.reshape(cells_here, tokens_here, HEADS, HEAD_DIM)
    key_heads = keys_all.reshape(cells_here, seq_len, HEADS, HEAD_DIM)
    val_heads = vals_all.reshape(cells_here, seq_len, HEADS, HEAD_DIM)

    def scores_of():
        raw = (
            jnp.einsum(
                "cqhd,ckhd->chqk", query_heads, key_heads, preferred_element_type=jnp.float32
            )
            * inv_root
        )
        return raw + mask_bias

    masked = scores_of()
    row_max = jnp.max(masked, axis=-1, keepdims=True)
    exp_scores = jnp.exp(masked - row_max)
    exp_total = jnp.sum(exp_scores, axis=-1, keepdims=True)
    attn_probs = exp_scores / exp_total
    log_total = row_max + jnp.log(exp_total)
    mixed_out = jnp.einsum(
        "chqk,ckhd->cqhd",
        attn_probs.astype(jnp.bfloat16),
        val_heads,
        preferred_element_type=jnp.float32,
    )
    mixed_out = mixed_out.astype(jnp.bfloat16).reshape(row_count, feat_width)
    attended = product(mixed_out, gathered[7]) + gathered[8].astype(jnp.float32)
    middle = states + attended
    second_full, second_back = jax.vjp(layer_norm, middle, gain_two, shift_two)
    second = second_full.astype(jnp.bfloat16)
    inner_pre = product(second, gathered[11]) + gathered[12].astype(jnp.float32)
    active_full, gelu_back = jax.vjp(gelu_exact, inner_pre)
    active = active_full.astype(jnp.bfloat16)
    result = middle + product(active, gathered[13]) + gathered[14].astype(jnp.float32)
    live_rows = query_live.reshape(row_count, 1)
    block_out = (
        jnp.where(live_rows, result, 0.0)
        .astype(jnp.bfloat16)
        .reshape(cells_here, tokens_here, feat_width)
    )
    upstream = jnp.where(
        live_rows, cotangent.reshape(row_count, feat_width), jnp.zeros((), jnp.bfloat16)
    )
    outer_bias_grad = column_sum(upstream)
    outer_proj_grad = left_product(active, upstream)
    grad_active = right_back(upstream, gathered[13])
    (grad_inner_full,) = gelu_back(grad_active)
    grad_inner = grad_inner_full.astype(jnp.bfloat16)
    inner_bias_grad = column_sum(grad_inner)
    inner_proj_grad = left_product(second, grad_inner)
    grad_second = right_back(grad_inner, gathered[11])
    grad_middle_norm, second_gain_grad, second_shift_grad = second_back(grad_second)
    grad_middle = upstream.astype(jnp.float32) + grad_middle_norm
    grad_attended = grad_middle.astype(jnp.bfloat16)
    output_bias_grad = column_sum(grad_attended)
    output_proj_grad = left_product(mixed_out, grad_attended)
    grad_mixed = right_back(grad_attended, gathered[7]).astype(jnp.bfloat16)
    grad_mixed = grad_mixed.reshape(cells_here, tokens_here, HEADS, HEAD_DIM)
    attn_again = jnp.exp(scores_of() - log_total)
    grad_probs = jnp.einsum(
        "cqhd,ckhd->chqk", grad_mixed, val_heads, preferred_element_type=jnp.float32
    )
    row_dot = jnp.sum(attn_again * grad_probs, axis=-1, keepdims=True)
    grad_raw = (attn_again * (grad_probs - row_dot)).astype(jnp.bfloat16)
    grad_vals_part = jnp.einsum(
        "chqk,cqhd->ckhd",
        attn_again.astype(jnp.bfloat16),
        grad_mixed,
        preferred_element_type=jnp.float32,
    )
    grad_keys_part = (
        jnp.einsum("chqk,cqhd->ckhd", grad_raw, query_heads, preferred_element_type=jnp.float32)
        * inv_root
    )
    grad_queries = (
        jnp.einsum("chqk,ckhd->cqhd", grad_raw, key_heads, preferred_element_type=jnp.float32)
        * inv_root
    ).astype(jnp.bfloat16)
    grad_queries = grad_queries.reshape(row_count, feat_width)
    grad_keys_sum, grad_vals_sum = (
        lax.psum_scatter(
            grad_keys_part.reshape(cells_here, seq_len, feat_width).astype(jnp.bfloat16),
            "chrom",
            scatter_dimension=1,
            tiled=True,
        ).astype(jnp.float32),
        lax.psum_scatter(
            grad_vals_part.reshape(cells_here, seq_len, feat_width).astype(jnp.bfloat16),
            "chrom",
            scatter_dimension=1,
            tiled=True,
        ).astype(jnp.float32),
    )
    grad_keys = grad_keys_sum.astype(jnp.bfloat16).reshape(row_count, feat_width)
    grad_vals = grad_vals_sum.astype(jnp.bfloat16).reshape(row_count, feat_width)
    query_proj_grad = left_product(normed, grad_queries)
    query_bias_grad = column_sum(grad_queries)
    key_proj_grad = left_product(normed, grad_keys)
    value_proj_grad = left_product(normed, grad_vals)
    value_bias_grad = column_sum(grad_vals)
    grad_normed = (
        right_back(grad_queries, gathered[2])
        + right_back(grad_keys, gathered[4])
        + right_back(grad_vals, gathered[5])
    )
    grad_states_norm, norm_gain_grad, norm_shift_grad = norm_back(grad_normed)
    input_grad = (
        (grad_middle + grad_states_norm)
        .astype(jnp.bfloat16)
        .reshape(cells_here, tokens_here, feat_width)
    )
    grad_list = (
        norm_gain_grad,
        norm_shift_grad,
        query_proj_grad,
        query_bias_grad,
        key_proj_grad,
        value_proj_grad,
        value_bias_grad,
        output_proj_grad,
        output_bias_grad,
        second_gain_grad,
        second_shift_grad,
        inner_proj_grad,
        inner_bias_grad,
        outer_proj_grad,
        outer_bias_grad,
    )
    pieces = tuple((split_rows(member, count_chrom, count_cells) for member in grad_list))
    section_one = (
        lax.psum_scatter(
            pieces[0].astype(jnp.bfloat16), "cells", scatter_dimension=1, tiled=True
        ).astype(jnp.float32),
        lax.psum_scatter(
            pieces[1].astype(jnp.bfloat16), "cells", scatter_dimension=1, tiled=True
        ).astype(jnp.float32),
        lax.psum_scatter(
            pieces[2].astype(jnp.bfloat16), "cells", scatter_dimension=1, tiled=True
        ).astype(jnp.float32),
        lax.psum_scatter(
            pieces[3].astype(jnp.bfloat16), "cells", scatter_dimension=1, tiled=True
        ).astype(jnp.float32),
        lax.psum_scatter(
            pieces[4].astype(jnp.bfloat16), "cells", scatter_dimension=1, tiled=True
        ).astype(jnp.float32),
        lax.psum_scatter(
            pieces[5].astype(jnp.bfloat16), "cells", scatter_dimension=1, tiled=True
        ).astype(jnp.float32),
        lax.psum_scatter(
            pieces[6].astype(jnp.bfloat16), "cells", scatter_dimension=1, tiled=True
        ).astype(jnp.float32),
        lax.psum_scatter(
            pieces[7].astype(jnp.bfloat16), "cells", scatter_dimension=1, tiled=True
        ).astype(jnp.float32),
        lax.psum_scatter(
            pieces[8].astype(jnp.bfloat16), "cells", scatter_dimension=1, tiled=True
        ).astype(jnp.float32),
        lax.psum_scatter(
            pieces[9].astype(jnp.bfloat16), "cells", scatter_dimension=1, tiled=True
        ).astype(jnp.float32),
        lax.psum_scatter(
            pieces[10].astype(jnp.bfloat16), "cells", scatter_dimension=1, tiled=True
        ).astype(jnp.float32),
        lax.psum_scatter(
            pieces[11].astype(jnp.bfloat16), "cells", scatter_dimension=1, tiled=True
        ).astype(jnp.float32),
        lax.psum_scatter(
            pieces[12].astype(jnp.bfloat16), "cells", scatter_dimension=1, tiled=True
        ).astype(jnp.float32),
        lax.psum_scatter(
            pieces[13].astype(jnp.bfloat16), "cells", scatter_dimension=1, tiled=True
        ).astype(jnp.float32),
        lax.psum_scatter(
            pieces[14].astype(jnp.bfloat16), "cells", scatter_dimension=1, tiled=True
        ).astype(jnp.float32),
    )
    section_two = (
        lax.psum_scatter(
            section_one[0].astype(jnp.bfloat16), "chrom", scatter_dimension=0, tiled=True
        ).astype(jnp.float32),
        lax.psum_scatter(
            section_one[1].astype(jnp.bfloat16), "chrom", scatter_dimension=0, tiled=True
        ).astype(jnp.float32),
        lax.psum_scatter(
            section_one[2].astype(jnp.bfloat16), "chrom", scatter_dimension=0, tiled=True
        ).astype(jnp.float32),
        lax.psum_scatter(
            section_one[3].astype(jnp.bfloat16), "chrom", scatter_dimension=0, tiled=True
        ).astype(jnp.float32),
        lax.psum_scatter(
            section_one[4].astype(jnp.bfloat16), "chrom", scatter_dimension=0, tiled=True
        ).astype(jnp.float32),
        lax.psum_scatter(
            section_one[5].astype(jnp.bfloat16), "chrom", scatter_dimension=0, tiled=True
        ).astype(jnp.float32),
        lax.psum_scatter(
            section_one[6].astype(jnp.bfloat16), "chrom", scatter_dimension=0, tiled=True
        ).astype(jnp.float32),
        lax.psum_scatter(
            section_one[7].astype(jnp.bfloat16), "chrom", scatter_dimension=0, tiled=True
        ).astype(jnp.float32),
        lax.psum_scatter(
            section_one[8].astype(jnp.bfloat16), "chrom", scatter_dimension=0, tiled=True
        ).astype(jnp.float32),
        lax.psum_scatter(
            section_one[9].astype(jnp.bfloat16), "chrom", scatter_dimension=0, tiled=True
        ).astype(jnp.float32),
        lax.psum_scatter(
            section_one[10].astype(jnp.bfloat16), "chrom", scatter_dimension=0, tiled=True
        ).astype(jnp.float32),
        lax.psum_scatter(
            section_one[11].astype(jnp.bfloat16), "chrom", scatter_dimension=0, tiled=True
        ).astype(jnp.float32),
        lax.psum_scatter(
            section_one[12].astype(jnp.bfloat16), "chrom", scatter_dimension=0, tiled=True
        ).astype(jnp.float32),
        lax.psum_scatter(
            section_one[13].astype(jnp.bfloat16), "chrom", scatter_dimension=0, tiled=True
        ).astype(jnp.float32),
        lax.psum_scatter(
            section_one[14].astype(jnp.bfloat16), "chrom", scatter_dimension=0, tiled=True
        ).astype(jnp.float32),
    )
    rejoined = (
        lax.all_gather(section_two[0].astype(jnp.bfloat16), "cells", axis=1, tiled=True).astype(
            jnp.float32
        ),
        lax.all_gather(section_two[1].astype(jnp.bfloat16), "cells", axis=1, tiled=True).astype(
            jnp.float32
        ),
        lax.all_gather(section_two[2].astype(jnp.bfloat16), "cells", axis=1, tiled=True).astype(
            jnp.float32
        ),
        lax.all_gather(section_two[3].astype(jnp.bfloat16), "cells", axis=1, tiled=True).astype(
            jnp.float32
        ),
        lax.all_gather(section_two[4].astype(jnp.bfloat16), "cells", axis=1, tiled=True).astype(
            jnp.float32
        ),
        lax.all_gather(section_two[5].astype(jnp.bfloat16), "cells", axis=1, tiled=True).astype(
            jnp.float32
        ),
        lax.all_gather(section_two[6].astype(jnp.bfloat16), "cells", axis=1, tiled=True).astype(
            jnp.float32
        ),
        lax.all_gather(section_two[7].astype(jnp.bfloat16), "cells", axis=1, tiled=True).astype(
            jnp.float32
        ),
        lax.all_gather(section_two[8].astype(jnp.bfloat16), "cells", axis=1, tiled=True).astype(
            jnp.float32
        ),
        lax.all_gather(section_two[9].astype(jnp.bfloat16), "cells", axis=1, tiled=True).astype(
            jnp.float32
        ),
        lax.all_gather(section_two[10].astype(jnp.bfloat16), "cells", axis=1, tiled=True).astype(
            jnp.float32
        ),
        lax.all_gather(section_two[11].astype(jnp.bfloat16), "cells", axis=1, tiled=True).astype(
            jnp.float32
        ),
        lax.all_gather(section_two[12].astype(jnp.bfloat16), "cells", axis=1, tiled=True).astype(
            jnp.float32
        ),
        lax.all_gather(section_two[13].astype(jnp.bfloat16), "cells", axis=1, tiled=True).astype(
            jnp.float32
        ),
        lax.all_gather(section_two[14].astype(jnp.bfloat16), "cells", axis=1, tiled=True).astype(
            jnp.float32
        ),
    )
    final = tuple(
        (
            member.reshape(
                (member.shape[0] * member.shape[1] * member.shape[2],) + member.shape[3:]
            )
            for member in rejoined
        )
    )
    return (block_out, input_grad) + tuple(final)


PLANE = 4
LINE = 4
VMEM_LIMIT = 65000 * 1024


def rows_of(start, count):
    return pl.ds(pl.multiple_of(start, 16), count)


def cols_of(start, count):
    return pl.ds(pl.multiple_of(start, 128), count)


VECTORS = 8
TILE = 256
AHEAD = 1024
BACK = 512


def nt(left, right):
    return lax.dot_general(left, right, (((1,), (1,)), ((), ())), preferred_element_type=jnp.float32)


def nn(left, right):
    return jnp.dot(left, right, preferred_element_type=jnp.float32)


def moments(values):
    center = values - jnp.mean(values, axis=-1, keepdims=True)
    spread = jnp.mean(center * center, axis=-1, keepdims=True)
    return center, lax.rsqrt(spread + eps_norm)


def gelu_and_slope(u):
    gauss = jnp.exp(u * u * -0.5)
    t = 1.0 / (1.0 + jnp.abs(u) * (0.3275911 * 0.5 ** 0.5))
    poly = 0.5 * 1.061405429
    for factor in (-1.453152027, 1.421413741, -0.284496736, 0.254829592):
        poly = poly * t + 0.5 * factor
    tail = poly * t * gauss
    phi_sum = jnp.where(u < 0.0, tail, 1.0 - tail)
    return u * phi_sum, phi_sum + u * gauss * 0.3989422804014327


def tn(left, right):
    return lax.dot_general(left, right, (((0,), (0,)), ((), ())), preferred_element_type=jnp.float32)


def layer_kernel(
    len_ref, off_ref, v0, v1, v2, v3, v4, v5, v6, v7, b_ref, x_ref, ct_ref, wq_ref, wk_ref, wv_ref, wo_ref, w1_ref, w2_ref,
    block_o, input_o, w2_o, w1_o, q_o, k_o, v_o, o_o, small_o, x_o, normed_o, qkv_o, wa_o, wob_o,
    small_ref, rag_ref, smalls, rag, vec, bias_in, xf, up, dc, do, wb, wts, big, db, two, three, r1c, r2c, zc, r2a, za, kx, lse,
    half_in, home, acc, sums, sums_in,
    sm_s, sm_r, ex_s, ex_r, fw_s, fw_r, ln_s, un_s, un_r, loc, wo_s, wo_r, pa_s, pa_r, out_s,
    ld, us, ur, hs, hr, cs, cr, ss, sr, os, free_x, free_y, freed_x, freed_y, freed_z,
):
    f32, bf = jnp.float32, jnp.bfloat16
    i, z = lax.axis_index("cells"), lax.axis_index("chrom")
    p, c = i // 2, lax.rem(i, 2)
    px, py = lax.rem(p, 2), p // 2
    x_nb, y_nb, core_nb = i + 2 - 4 * px, i + 4 - 8 * py, i + 1 - 2 * c
    p_x, p_y = p + 1 - 2 * px, p + 2 - 4 * py
    rows = wq_ref.shape[0]
    feat = wq_ref.shape[1]
    half = feat // 2
    hid = w2_ref.shape[0]
    block = x_ref.shape[1]
    seq = block * LINE
    half_seq = seq // 2
    chunks = seq // TILE
    wide = hid // 2
    mesh_id = pl.DeviceIdType.MESH
    part_rows, hid_part = rows // PLANE, hid // 2 // PLANE

    small_ref[...] = jnp.zeros(small_ref.shape, bf)
    for n, ref in enumerate((v0, v1, v2, v3, v4, v5, v6, v7)):
        small_ref[n : n + 1, 0:rows] = ref[...][None, :]
    for n in range(hid // rows):
        small_ref[VECTORS + n : VECTORS + n + 1, 0:rows] = b_ref[n * rows : (n + 1) * rows][None, :]
    count = off_ref.shape[1]
    never = 2 ** 30
    for n in range(rag_ref.shape[0]):
        rag_ref[n] = jnp.full(rag_ref.shape[1:], never, jnp.int32)
        rag_ref[n, 1:2, 0:count] = off_ref[n : n + 1, :]
        end = rag_ref[n, 1:2, :]
        group = lax.broadcasted_iota(jnp.int32, end.shape, 1)
        rag_ref[n, 0:1, :] = jnp.where(group == 0, 0, pltpu.roll(end, 1, 1))
        rag_ref[n, 2:3, :] = jnp.full(end.shape, len_ref[n], jnp.int32)

    barrier = pltpu.get_barrier_semaphore()
    line_ids = [
        (i - c + lax.rem(c + dc, 2), lax.rem(z + dz, LINE))
        for dc in range(2)
        for dz in range(LINE)
        if dc or dz
    ]
    for who in line_ids + [(x_nb, z), (y_nb, z)]:
        pl.semaphore_signal(barrier, inc=1, device_id=who, device_id_type=pl.DeviceIdType.MESH)
    pl.semaphore_wait(barrier, len(line_ids) + 2)

    def send(src, dst, s, r, who):
        return pltpu.make_async_remote_copy(
            src_ref=src, dst_ref=dst, send_sem=s, recv_sem=r, device_id=who,
            device_id_type=pl.DeviceIdType.MESH,
        )

    small_own = pltpu.make_async_copy(small_ref, smalls.at[z], loc.at[0])
    small_out = [
        send(small_ref, smalls.at[z], sm_s.at[d], sm_r.at[d], (i, lax.rem(z + d + 1, LINE)))
        for d in range(LINE - 1)
    ]

    rag_own = pltpu.make_async_copy(rag_ref.at[lax.rem(z, 2)], rag.at[0], loc.at[6])
    rag_out = send(rag_ref.at[lax.rem(z, 2)], rag.at[1], wo_s.at[1], wo_r.at[1], (core_nb, z))

    def exchange(src, dst, which):
        stay = c == z // 2
        mine, outs = None, []
        for k in range(2):
            j = lax.rem(z + k, 2)
            to = dst.at[rows_of(z * block, block), :]
            r = ex_r.at[2 * which + k]
            outs.append(send(src.at[j], to, ex_s.at[2 * which + k], r, (i - c + z // 2, 2 * c + j)))
            if k == 0:
                mine = pltpu.make_async_copy(src.at[j], to, r)

        def start():
            pl.when(stay)(mine.start)
            pl.when(jnp.logical_not(stay))(outs[0].start)
            outs[1].start()

        def arrived():
            pl.when(stay)(mine.wait)
            pl.when(jnp.logical_not(stay))(outs[0].wait_recv)
            outs[1].wait_recv()

        def sent():
            pl.when(jnp.logical_not(stay))(outs[0].wait_send)
            outs[1].wait_send()

        return start, arrived, sent

    def forward(dst, which):
        return [
            send(
                dst.at[rows_of((2 * c + b) * block, block), :],
                dst.at[rows_of((2 * c + b) * block, block), :],
                fw_s.at[2 * which + b], fw_r.at[2 * which + b], (core_nb, z),
            )
            for b in range(2)
        ]

    x_start, x_arrived, x_sent = exchange(x_ref, xf, 0)
    c_start, c_arrived, c_sent = exchange(ct_ref, up, 1)
    x_fw, c_fw = forward(xf, 0), forward(up, 1)

    wa, wol = dc.at[:, pl.ds(0, 3 * half)], dc.at[:, pl.ds(3 * half, half)]
    lands = (wa, wol, wb, wts)
    groups = range(4)
    partner, inner = z + 1 - 2 * lax.rem(z, 2), 3 - z
    low = z < 2
    middle_chip = jnp.logical_or(z == 1, z == 2)
    slot_shard = (partner, jnp.where(low, 2, 1), jnp.where(low, 3, 0))

    def own_parts(g, row, count):
        if g == 0:
            return [
                (ref.at[rows_of(row, count), cols_of(c * half, half)], pl.ds(n * half, half))
                for n, ref in enumerate((wq_ref, wk_ref, wv_ref))
            ]
        if g == 1:
            return [(wo_ref.at[rows_of(row, count), cols_of(c * half, half)], pl.ds(0, half))]
        if g == 2:
            return [
                (w1_ref.at[rows_of(row, count), cols_of(n * hid + c * (hid // 2), hid // 2)], pl.ds(n * (hid // 2), hid // 2))
                for n in range(LINE)
            ]
        return [(w2_ref.at[rows_of(c * (hid // 2) + row, count), :], pl.ds(0, feat))]

    def shape_of(g):
        return (rows, part_rows) if g < 3 else (hid // 2, hid_part)

    def piece(g, s, at):
        shard, count = shape_of(g)
        return lands[g].at[rows_of(s * shard + at * count, count), :]

    def half_piece(g, s, at, side):
        shard, count = shape_of(g)
        width = lands[g].shape[1]
        cut = width // 256 * 128
        cols = pl.ds(cut, width - cut) if side else pl.ds(0, cut)
        return lands[g].at[rows_of(s * shard + at * count, count), cols]

    def line_send(g, s, slot, e, to):
        return send(piece(g, s, p), piece(g, s, p), ln_s.at[g, e], un_r.at[3 * g + slot, 0], (i, to))

    def first(g):
        shard, count = shape_of(g)
        for src, cols in own_parts(g, p * count, count):
            dst = lands[g].at[rows_of(z * shard + p * count, count), cols]
            send(src, dst, ln_s.at[g, 0], un_r.at[3 * g, 0], (i, partner)).start()

        @pl.when(middle_chip)
        def _():
            for src, cols in own_parts(g, p * count, count):
                dst = lands[g].at[rows_of(z * shard + p * count, count), cols]
                send(src, dst, ln_s.at[g, 1], un_r.at[3 * g + 1, 0], (i, inner)).start()

    def passing(g, slot):
        if slot == 0:
            return line_send(g, slot_shard[0], 2, 2, inner)
        return line_send(g, slot_shard[slot], slot, 2 + slot, partner)

    def spread(g, slot):
        own = piece(g, slot_shard[slot], p)
        u = 3 * g + slot
        return [
            send(own, own, un_s.at[u, 0], un_r.at[u, 1], (x_nb, z)),
            send(own, own, un_s.at[u, 1], un_r.at[u, 2], (y_nb, z)),
        ]

    def cross(g, slot):
        u = 3 * g + slot
        left = half_piece(g, slot_shard[slot], p_x, 0)
        rest = half_piece(g, slot_shard[slot], p_y, 1)
        return [
            send(left, left, un_s.at[u, 2], un_r.at[u, 3], (y_nb, z)),
            send(rest, rest, un_s.at[u, 3], un_r.at[u, 4], (x_nb, z)),
        ]

    def land(g, slot):
        line_send(g, slot_shard[slot], slot, 0, partner).wait_recv()
        pl.when(middle_chip)(passing(g, slot).start)
        for d in spread(g, slot):
            d.start()

    def turn(g, slot):
        for d in spread(g, slot):
            d.wait_recv()
        for d in cross(g, slot):
            d.start()

    def own_start(g):
        shard, _ = shape_of(g)
        for src, cols in own_parts(g, 0, shard):
            pltpu.make_async_copy(src, lands[g].at[rows_of(z * shard, shard), cols], loc.at[1 + g]).start()

    def own_wait(g):
        shard, _ = shape_of(g)
        ref = lands[g].at[rows_of(z * shard, shard), :]
        pltpu.make_async_copy(ref, ref, loc.at[1 + g]).wait()

    def whole(g):
        for slot in range(3):
            for d in cross(g, slot):
                d.wait_recv()
        own_wait(g)

    def all_sent(g):
        line_send(g, z, 0, 0, partner).wait_send()

        @pl.when(middle_chip)
        def _():
            line_send(g, z, 1, 1, inner).wait_send()
            for slot in range(3):
                passing(g, slot).wait_send()

        for slot in range(3):
            for d in spread(g, slot) + cross(g, slot):
                d.wait_send()

    kept = {}

    def keep(name, src, dst):
        kept[name] = pltpu.make_async_copy(src, dst, out_s.at[len(kept)])
        kept[name].start()

    def begin():
        small_own.start()
        rag_own.start()
        rag_out.start()
        for d in small_out:
            d.start()

    def vectors():
        small_own.wait()
        for d in small_out:
            d.wait()
        width = smalls.shape[2]
        total = jnp.zeros((smalls.shape[1], feat), f32)
        at = lax.broadcasted_iota(jnp.int32, (width, feat), 0)
        to = lax.broadcasted_iota(jnp.int32, (width, feat), 1)
        for s in range(LINE):
            place = jnp.where(jnp.logical_and(at < rows, to == at + s * rows), 1.0, 0.0).astype(bf)
            total += nn(smalls[s], place)
        vec[...] = total
        at = lax.broadcasted_iota(jnp.int32, (width, hid // 2), 0)
        to = lax.broadcasted_iota(jnp.int32, (width, hid // 2), 1)
        which = lax.broadcasted_iota(jnp.int32, (smalls.shape[1], hid // 2), 0)
        for s in range(LINE):
            line_bias = jnp.zeros((1, hid // 2), f32)
            for n in range(hid // 2 // rows):
                place = jnp.where(jnp.logical_and(at < rows, to == at + n * rows), 1.0, 0.0).astype(bf)
                picked = jnp.where(which == VECTORS + c * (hid // 2 // rows) + n, nn(smalls[s], place), 0.0)
                line_bias += jnp.sum(picked, axis=0, keepdims=True)
            bias_in[:, pl.ds(s * (hid // 2), hid // 2)] = line_bias
        rag_own.wait()
        rag_out.wait()
        bounds = jnp.where(c == z // 2, rag[0], rag[1])
        lanes = lax.broadcasted_iota(jnp.int32, (TILE, 128), 1)
        for n in range(seq // TILE):
            at = pl.ds(n * TILE, TILE)
            token = lax.broadcasted_iota(jnp.int32, (TILE, 128), 0) + n * TILE
            same = jnp.logical_and(token >= bounds[0:1, :], token < bounds[1:2, :])
            dead = jnp.where(token < bounds[2:3, :], 0.0, -1e30)
            kx[at, pl.ds(128, 128)] = jnp.where(lanes == 127, dead, jnp.where(same, 1.0, 0.0)).astype(bf)

    def query_mark(at, lane):
        same = kx[at, pl.ds(128, 128)] * jnp.array(group_bias, bf)
        return jnp.where(lane == 127, jnp.ones((), bf), same)

    def x_spread():
        x_arrived()
        for d in x_fw:
            d.start()

    def norm_rows(n, _):
        at = pl.ds(pl.multiple_of(n * 64, 64), 64)
        center, r = moments(xf[at, :].astype(f32))
        db[at, pl.ds(0, feat)] = (center * r * vec[0:1, :] + vec[1:2, :]).astype(bf)
        return _

    def norm_own():
        steps = seq // 2 // 64
        lax.fori_loop(c * steps, (c + 1) * steps, norm_rows, 0)

    def norm_other():
        steps = seq // 2 // 64
        for d in x_fw:
            d.wait_recv()
        lax.fori_loop((1 - c) * steps, (2 - c) * steps, norm_rows, 0)
        keep("normed", db.at[pl.ds(0, seq), pl.ds(0, feat)], normed_o)
        keep("x", xf.at[rows_of(c * half_seq, half_seq), :], x_o)

    def project(start, stop):
        bias_row = jnp.concatenate(
            [vec[2:3, cols_of(c * half, half)], jnp.zeros((1, half), f32), vec[3:4, cols_of(c * half, half)]], axis=1
        )
        for at in range(start, stop, TILE):
            width = min(TILE, stop - at)
            got = nn(db[pl.ds(0, seq), pl.ds(0, feat)], dc[:, pl.ds(at, width)])
            big[:, pl.ds(at, width)] = (got + bias_row[:, at : at + width]).astype(bf)
        if stop == 3 * half:
            keep("wa", wa, wa_o)

    def attend(t):
        lane = lax.broadcasted_iota(jnp.int32, (AHEAD, 128), 1)
        k2 = big[:, pl.ds(half + t * 128, 128)]
        v2t = jnp.transpose(big[:, pl.ds(2 * half + t * 128, 128)])
        kx[:, :128] = k2

        def chunk(n, _):
            at = pl.ds(pl.multiple_of(n * AHEAD, AHEAD), AHEAD)
            q2 = big[at, pl.ds(t * 128, 128)] * jnp.array(HEAD_DIM ** (-0.5), bf)
            mark = query_mark(at, lane)
            both = []
            for h in range(2):
                own = lane < HEAD_DIM if h == 0 else lane >= HEAD_DIM
                qx = jnp.concatenate([jnp.where(own, q2, jnp.zeros((), bf)), mark], axis=1)
                s = nt(kx[...], qx)
                top = jnp.max(s, axis=0, keepdims=True)
                e = jnp.exp(s - top)
                total = jnp.sum(e, axis=0, keepdims=True)
                o = nn(v2t[h * HEAD_DIM : (h + 1) * HEAD_DIM, :], e.astype(bf))
                both.append(o / total)
                lse[2 * t + h : 2 * t + h + 1, at] = top + jnp.log(total)
            big[at, pl.ds(3 * half + t * 128, 128)] = jnp.transpose(jnp.concatenate(both, axis=0)).astype(bf)
            return _

        lax.fori_loop(0, seq // AHEAD, chunk, 0)
        if t == half // 128 - 1:
            keep("qkv", big, qkv_o)

    wo_own = pltpu.make_async_copy(
        wol.at[rows_of(c * half, half), :], do.at[rows_of(c * half, half), :], loc.at[5]
    )
    wo_out = send(
        wol.at[rows_of((1 - c) * half, half), :],
        do.at[rows_of(c * half, half), :], wo_s.at[0], wo_r.at[0], (core_nb, z),
    )

    def wo_swap():
        wo_own.start()
        wo_out.start()

    def wo_ready():
        wo_own.wait()
        wo_out.wait()
        keep("wob", do, wob_o)

    part = db.at[pl.ds(0, seq), pl.ds(feat, feat)]
    part_swaps = [
        send(part.at[pl.ds(n * TILE, TILE), :], three.at[pl.ds(n * TILE, TILE), :], pa_s.at[n], pa_r.at[n], (core_nb, z))
        for n in range(chunks)
    ]

    def output_rows(n):
        at = pl.ds(n * TILE, TILE)
        for m in range(2):
            db[at, pl.ds(feat + m * half, half)] = nn(
                big[at, pl.ds(3 * half, half)], do[pl.ds(m * half, half), :]
            ).astype(bf)
        part_swaps[n].start()

    def second_rows(n, _):
        at = pl.ds(pl.multiple_of(n * 64, 64), 64)
        total = xf[at, :].astype(f32) + (
            db[at, pl.ds(feat, feat)].astype(f32) + three[at, :].astype(f32) + vec[4:5, :]
        )
        xf[at, :] = total.astype(bf)
        center, r = moments(total)
        two[at, :] = (center * r * vec[5:6, :] + vec[6:7, :]).astype(bf)
        return _

    def second_norm(n):
        if n == 0:
            kept["x"].wait()
            for d in x_fw:
                d.wait_send()
        part_swaps[n].wait()
        lax.fori_loop(n * TILE // 64, (n + 1) * TILE // 64, second_rows, 0)

    tiles = 2 * hid // TILE

    def inner_tile(n):
        if n == 0:
            for name in ("qkv", "normed"):
                kept[name].wait()
        cols = pl.ds(n * TILE, TILE)

        def tile_rows(m, _):
            at = pl.ds(pl.multiple_of(m * TILE, TILE), TILE)
            u = nn(two[at, :], wb[:, cols]) + bias_in[:, cols]
            value, slope = gelu_and_slope(u)
            big[at, cols] = value.astype(bf)
            db[at, cols] = slope.astype(bf)
            return _

        lax.fori_loop(0, chunks, tile_rows, 0, unroll=4)

    def c_spread():
        c_arrived()
        for d in c_fw:
            d.start()

    loads = {}

    def load(name, pairs):
        n = len(loads)
        copies = [pltpu.make_async_copy(src, dst, ld.at[n, m]) for m, (src, dst) in enumerate(pairs)]
        loads[name] = copies
        for d in copies:
            d.start()

    here = set()

    def loaded(*names):
        for name in names:
            for d in loads[name] if name not in here else ():
                d.wait()
            here.add(name)

    class Unit:
        def __init__(self, n, d, col, r, w, r1, r2, zl, parts):
            self.n, self.d, self.col, self.r, self.w = n, d, col, r, w
            self.r1_at, self.r2_at, self.z_at, self.parts = r1, r2, zl, parts

        def region(self, base, row, count=1):
            ref, row0, col0 = base
            return ref.at[rows_of(row0 + row * self.r, count * self.r), pl.ds(col0, self.w)]

        def own(self, s, a, b):
            if self.col is None:
                return self.region((self.d, 0, s // 2 * self.w), (s % 2 * 2 + a) * 2 + b)
            return self.region((self.d, 0, self.col), (s * 2 + a) * 2 + b)

        def r1(self, side, m, n):
            return self.region(self.r1_at, (side * 2 + m) * 2 + n)

        def r2(self, s):
            return self.region(self.r2_at, s)

        def zl(self, d):
            return self.region(self.z_at, d)

        def sems(self, e):
            return us.at[self.n, e], ur.at[self.n, e]

        def total(self, e, count):
            ref = self.region(self.r1_at, 0, count)
            return send(ref, ref, *self.sems(e), (x_nb, z))

        def step1(self, s):
            for n in range(2):
                if s < 2:
                    send(self.own(s, n, 1 - px), self.r1(0, s, n), *self.sems(0), (x_nb, z)).start()
                else:
                    send(self.own(s, 1 - py, n), self.r1(1, s - 2, n), *self.sems(1), (y_nb, z)).start()

        def step1_all(self):
            for s in (0, 2, 1, 3):
                self.step1(s)

        def add(self, to, *more):
            value = to[...].astype(f32)
            for ref in more:
                value = value + ref[...].astype(f32)
            to[...] = value.astype(bf)

        def step2(self):
            self.total(0, 4).wait_recv()
            for m in range(2):
                for n in range(2):
                    self.add(self.r1(0, m, n), self.own(m, n, px))
                send(self.r1(0, m, 1 - py), self.r2(m), *self.sems(2), (y_nb, z)).start()
            self.total(1, 4).wait_recv()
            for m in range(2):
                for n in range(2):
                    self.add(self.r1(1, m, n), self.own(2 + m, py, n))
                send(self.r1(1, m, 1 - px), self.r2(2 + m), *self.sems(3), (x_nb, z)).start()

        def line(self):
            self.total(2, 2).wait_recv()
            for m in range(2):
                self.add(self.r2(m), self.r1(0, m, py))
            self.total(3, 2).wait_recv()
            for m in range(2):
                self.add(self.r2(2 + m), self.r1(1, m, px))
            for d in range(LINE - 1):
                to = lax.rem(z + d + 1, LINE)
                send(self.r2(to), self.zl(d), *self.sems(4 + d), (i, to)).start()

        def spread(self):
            for d in range(LINE - 1):
                self.total(4 + d, 1).wait_recv()
            self.add(self.r2(z), *[self.zl(d) for d in range(LINE - 1)])
            for off, width, place in self.parts:
                ref, row0, col0 = self.r2_at
                src = ref.at[rows_of(row0 + z * self.r, self.r), pl.ds(col0 + off, width)]
                dst = place(p, 0, width)
                send(src, dst, *self.sems(7), (x_nb, z)).start()
                send(src, dst, *self.sems(8), (y_nb, z)).start()
                pltpu.make_async_copy(src, dst, os.at[self.n]).start()

        def cross(self):
            self.total(7, 1).wait_recv()
            self.total(8, 1).wait_recv()
            for off, width, place in self.parts:
                cut = width // 256 * 128
                left, rest = place(p_x, 0, cut), place(p_y, cut, width - cut)
                send(left, left, *self.sems(9), (y_nb, z)).start()
                send(rest, rest, *self.sems(10), (x_nb, z)).start()

        def crossed(self, e):
            off = 0
            for _, width, _place in self.parts:
                cut = width // 256 * 128
                off += cut if e == 9 else width - cut
            ref, row0, col0 = self.r1_at
            ref = ref.at[rows_of(row0, self.r), pl.ds(col0, off)]
            return send(ref, ref, *self.sems(e), (x_nb, z))

        def to_core(self):
            self.crossed(9).wait_recv()
            self.crossed(10).wait_recv()
            ref = self.region(self.r1_at, 0)
            pltpu.make_async_copy(ref, ref, os.at[self.n]).wait()
            for off, width, place in self.parts:
                mine = place(None, 0, width)
                send(mine, mine, *self.sems(11), (core_nb, z)).start()

        def step2_sent(self):
            self.total(2, 2).wait_send()
            self.total(3, 2).wait_send()

        def end(self):
            self.total(11, 4).wait()
            for e in range(4, 9):
                self.total(e, 1).wait_send()
            self.crossed(9).wait_send()
            self.crossed(10).wait_send()

        def step1_sent(self):
            self.total(0, 4).wait_send()
            self.total(1, 4).wait_send()

    def place_w2(at, off, width):
        first, count = (0, half) if at is None else (at * (hid // 2 // PLANE), hid // 2 // PLANE)
        return w2_o.at[rows_of(c * (hid // 2) + first, count), pl.ds(off, width)]

    def place_w1(n):
        def place(at, off, width):
            first, count = (0, rows) if at is None else (at * (rows // PLANE), rows // PLANE)
            return w1_o.at[rows_of(first, count), cols_of(n * hid + c * (hid // 2) + off, width)]

        return place

    def place_of(ref):
        def place(at, off, width):
            first, count = (0, rows) if at is None else (at * (rows // PLANE), rows // PLANE)
            return ref.at[rows_of(first, count), cols_of(c * half + off, width)]

        return place

    r_big, r_small = hid // 2 // PLANE, rows // PLANE
    unit_c = Unit(0, dc, None, r_big, feat, (r1c, 0, 0), (r2c, 0, 0), (zc, 0, 0), [(0, feat, place_w2)])
    unit_b = [
        Unit(
            1 + n, db, n * hid, r_small, hid, (wb, 0, n * hid), (wb, 8 * r_small, n * hid), (wb, 12 * r_small, n * hid),
            [(m * (hid // 2), hid // 2, place_w1(2 * n + m)) for m in range(2)],
        )
        for n in range(2)
    ]
    spots = ((0, 0), (0, half), (8 * r_small, 0), (8 * r_small, half))
    unit_o = Unit(3, do, 0, r_small, half, (r1c,) + spots[3], (r2a, 0, 0), (za, 0, 0), [(0, half, place_of(o_o))])
    unit_a = [
        Unit(
            4 + n, db, n * half, r_small, half, (r1c,) + spots[n], (r2a, 0, (1 + n) * half), (za, 0, (1 + n) * half),
            [(0, half, place_of(ref))],
        )
        for n, ref in enumerate((q_o, k_o, v_o))
    ]

    def going_home(src, dst, e):
        stay = c == z // 2
        mine, outs = None, []
        for k in range(2):
            b = lax.rem(z + k, 2)
            part = src.at[rows_of(b * block, block), :]
            to = dst.at[lax.rem(z, 2)]
            outs.append(send(part, to, hs.at[e, k], hr.at[e, k], (i - c + z // 2, 2 * c + b)))
            if k == 0:
                mine = pltpu.make_async_copy(part, to, hr.at[e, k])

        def start():
            pl.when(stay)(mine.start)
            pl.when(jnp.logical_not(stay))(outs[0].start)
            outs[1].start()

        def sent():
            pl.when(stay)(mine.wait)
            pl.when(jnp.logical_not(stay))(outs[0].wait_send)
            outs[1].wait_send()

        def arrived():
            pl.when(jnp.logical_not(stay))(outs[0].wait_recv)
            outs[1].wait_recv()

        def start_one(b):
            k = lax.rem(z + b, 2)
            part, to = src.at[pl.ds(b * block, block), :], dst.at[lax.rem(z, 2)]
            here = jnp.logical_and(stay, k == 0)
            pl.when(here)(pltpu.make_async_copy(part, to, hr.at[e, k]).start)
            away = send(part, to, hs.at[e, k], hr.at[e, k], (i - c + z // 2, 2 * c + b))
            pl.when(jnp.logical_not(here))(away.start)

        return start, sent, arrived, start_one

    block_start, block_sent, block_arrived, _ = going_home(home, block_o, 0)
    _, input_sent, input_arrived, input_one = going_home(home, input_o, 1)

    first_core = jnp.where(c == 0, 1.0, 0.0)
    zero_row = jnp.zeros((1, feat), f32)

    def mask():
        sums[0] = jnp.zeros(sums.shape[1:], f32)
        for d in c_fw:
            d.wait()

        def mask_rows(n, total):
            at = pl.ds(pl.multiple_of(n * TILE, TILE), TILE)
            gone = kx[at, 255:256].astype(f32) < 0.0
            value = jnp.where(gone, 0.0, up[at, :].astype(f32))
            up[at, :] = value.astype(bf)
            return total + jnp.sum(value, axis=0, keepdims=True)

        up_sum = lax.fori_loop(0, chunks, mask_rows, zero_row)
        sums[0, 7:8, :] = up_sum * first_core
        kept["wa"].wait()
        for g in (0, 1):
            all_sent(g)

    def outer_rows(s):
        dc[s % 2 * wide : (s % 2 + 1) * wide, s // 2 * feat : (s // 2 + 1) * feat] = tn(big[:, s * wide : (s + 1) * wide], up[...]).astype(bf)
        unit_c.step1(s)

    swaps = [
        send(half_in.at[pl.ds(n * TILE, TILE), :], half_in.at[pl.ds(n * TILE, TILE), :], cs.at[n], cr.at[n], (core_nb, z))
        for n in range(half_seq // TILE)
    ]

    def block_other():
        kept["wob"].wait()
        for n in range(half_seq // TILE):
            at = rows_of((1 - c) * half_seq + n * TILE, TILE)
            to = pl.ds(n * TILE, TILE)
            got = nn(big[at, :], wts[...]).astype(bf)
            for m in range(2):
                held = pl.ds(m * half_seq + n * TILE, TILE)
                do[held, :] = got[:, m * half : (m + 1) * half]
                send(
                    do.at[held, :], half_in.at[to, pl.ds(m * half, half)], cs.at[n], cr.at[n], (core_nb, z)
                ).start()

    def block_own():
        for n in range(half_seq // TILE):
            at = rows_of(c * half_seq + n * TILE, TILE)
            to = pl.ds(n * TILE, TILE)
            acc[...] = nn(big[at, :], wts[...])
            swaps[n].wait_recv()
            gone = kx[at, 255:256].astype(f32) < 0.0
            value = xf[at, :].astype(f32) + acc[...] + half_in[to, :].astype(f32) + vec[7:8, :]
            home[to, :] = jnp.where(gone, 0.0, value).astype(bf)

    def through_gelu():
        def tile(n, _):
            cols = pl.ds(pl.multiple_of(n * TILE, TILE), TILE)
            got = (nt(up[...], wts[cols, :]) * db[pl.ds(0, seq), cols].astype(f32)).astype(bf)
            big[:, cols] = got
            bias_in[:, cols] = jnp.sum(got.astype(f32), axis=0, keepdims=True)
            return _

        lax.fori_loop(0, 2 * hid // TILE, tile, 0)
        for s in range(LINE):
            sums[0, 8 + s : 9 + s, cols_of(c * wide, wide)] = bias_in[:, s * wide : (s + 1) * wide]

    def inner_grad(n):
        def inner_rows(m, _):
            at = pl.ds(pl.multiple_of(m * TILE, TILE), TILE)
            db[at, pl.ds(n * hid, hid)] = tn(two[:, at], big[:, pl.ds(n * hid, hid)]).astype(bf)
            return _

        lax.fori_loop(0, feat // TILE, inner_rows, 0)

    gs_swaps = [
        send(db.at[pl.ds(n * TILE, TILE), pl.ds(0, feat)], three.at[pl.ds(n * TILE, TILE), :], cs.at[2 + n], cr.at[2 + n], (core_nb, z))
        for n in range(chunks)
    ]

    def to_second(n):
        if n == 0:
            for d in swaps:
                d.wait_send()
        at = pl.ds(n * TILE, TILE)
        db[at, pl.ds(0, feat)] = nt(big[at, :], wb[...]).astype(bf)
        gs_swaps[n].start()
        if n == chunks - 1:
            all_sent(2)
            pl.semaphore_signal(freed_x, inc=1, device_id=(x_nb, z), device_id_type=mesh_id)
            pl.semaphore_signal(freed_y, inc=1, device_id=(y_nb, z), device_id_type=mesh_id)
            for d in range(1, LINE):
                pl.semaphore_signal(
                    freed_z, inc=1, device_id=(i, lax.rem(z + d, LINE)), device_id_type=mesh_id
                )

    def inner_free():
        pl.semaphore_wait(freed_x, 1)
        pl.semaphore_wait(freed_y, 1)
        pl.semaphore_wait(freed_z, LINE - 1)

    def weights_load():
        all_sent(3)
        load(
            "wa",
            [
                (wa_o.at[:, pl.ds(0, feat)], wts.at[pl.ds(0, feat), :]),
                (wa_o.at[:, pl.ds(feat, half)], wts.at[pl.ds(feat, feat), pl.ds(0, half)]),
                (wob_o, wts.at[pl.ds(feat, feat), pl.ds(half, half)]),
            ],
        )

    def qkv_load():
        load("qkv", [(qkv_o, big)])
        load("normed", [(normed_o, two)])

    def back_rows(n, carry):
        gain_sum, shift_sum, out_sum = carry
        at = pl.ds(pl.multiple_of(n * 64, 64), 64)
        g = db[at, pl.ds(0, feat)].astype(f32) + three[at, :].astype(f32)
        center, r = moments(xf[at, :].astype(f32))
        hat = center * r
        gh = g * hat
        h = g * vec[5:6, :]
        first = jnp.mean(h, axis=-1, keepdims=True)
        slant = jnp.mean(h * hat, axis=-1, keepdims=True)
        got = (up[at, :].astype(f32) + r * (h - first - hat * slant)).astype(bf)
        three[at, :] = got
        return (
            gain_sum + jnp.sum(gh, axis=0, keepdims=True),
            shift_sum + jnp.sum(g, axis=0, keepdims=True),
            out_sum + jnp.sum(got.astype(f32), axis=0, keepdims=True),
        )

    def second_back():
        carry = (zero_row, zero_row, zero_row)
        for n in range(chunks):
            gs_swaps[n].wait()
            carry = lax.fori_loop(n * TILE // 64, (n + 1) * TILE // 64, back_rows, carry)
        sums[0, 5:6, :] = carry[0] * first_core
        sums[0, 6:7, :] = carry[1] * first_core
        sums[0, 4:5, :] = carry[2] * first_core
        load("x", [(x_o, up.at[pl.ds(0, half_seq), :])])

    stage = dc.at[pl.ds(0, half), pl.ds(0, half)]
    o_swap = send(stage, do.at[rows_of(c * half, half), :], cs.at[6], cr.at[6], (core_nb, z))

    def output_grad():
        loaded("qkv")
        unit_c.step1_sent()
        dc[pl.ds(0, half), pl.ds(0, half)] = tn(
            big[:, pl.ds(3 * half, half)], three[:, cols_of((1 - c) * half, half)]
        ).astype(bf)
        o_swap.start()
        do[rows_of(c * half, half), :] = tn(big[:, pl.ds(3 * half, half)], three[:, cols_of(c * half, half)]).astype(bf)

    def mixed_grad():
        loaded("wa")
        for n in range(chunks):
            at = pl.ds(n * TILE, TILE)
            dc[at, pl.ds(3 * half, half)] = (
                nt(three[at, pl.ds(0, half)], wts[pl.ds(feat, half), pl.ds(half, half)])
                + nt(three[at, pl.ds(half, half)], wts[pl.ds(feat + half, half), pl.ds(half, half)])
            ).astype(bf)

    root = HEAD_DIM ** (-0.5)

    def attend_back(t):
        lane = lax.broadcasted_iota(jnp.int32, (BACK, 128), 1)
        k2 = big[:, pl.ds(half + t * 128, 128)]
        k2t = jnp.transpose(k2)
        kx[:, :128] = k2
        acc[...] = jnp.zeros(acc.shape, f32)

        def chunk(n, _):
            at = pl.ds(pl.multiple_of(n * BACK, BACK), BACK)
            q2 = big[at, pl.ds(t * 128, 128)] * jnp.array(root, bf)
            mark = query_mark(at, lane)
            g2 = dc[at, pl.ds(3 * half + t * 128, 128)]
            both = []
            for h in range(2):
                own = lane < HEAD_DIM if h == 0 else lane >= HEAD_DIM
                qm = jnp.where(own, q2, jnp.zeros((), bf))
                gm = jnp.where(own, g2, jnp.zeros((), bf))
                s = nt(kx[...], jnp.concatenate([qm, mark], axis=1))
                prob = jnp.exp(s - lse[2 * t + h : 2 * t + h + 1, at])
                grad = nt(big[:, pl.ds(2 * half + t * 128, 128)], gm)
                both_of = prob * grad
                dot = jnp.sum(both_of, axis=0, keepdims=True)
                ds = (both_of - prob * dot).astype(bf)
                for which, got in enumerate((nn(ds, qm), nn(prob.astype(bf), gm))):
                    for m in range(chunks):
                        acc[:, pl.ds((which * chunks + m) * 128, 128)] += got[m * TILE : (m + 1) * TILE]
                both.append(nn(k2t[h * HEAD_DIM : (h + 1) * HEAD_DIM, :], ds))
            dc[at, pl.ds(t * 128, 128)] = (jnp.transpose(jnp.concatenate(both, axis=0)) * root).astype(bf)
            return _

        lax.fori_loop(0, seq // BACK, chunk, 0)
        for which in range(2):
            for m in range(chunks):
                dc[pl.ds(m * TILE, TILE), pl.ds((1 + which) * half + t * 128, 128)] = acc[
                    :, pl.ds((which * chunks + m) * 128, 128)
                ].astype(bf)
        if t == half // 128 - 1:
            sums[0, 2:3, cols_of(c * half, half)] = jnp.sum(
                dc[pl.ds(0, seq), pl.ds(0, half)].astype(f32), axis=0, keepdims=True
            )
            sums[0, 3:4, cols_of(c * half, half)] = jnp.sum(
                dc[pl.ds(0, seq), pl.ds(2 * half, half)].astype(f32), axis=0, keepdims=True
            )

    def free_landing():
        unit_c.step2_sent()
        pl.semaphore_signal(free_x, inc=1, device_id=(x_nb, z), device_id_type=mesh_id)
        pl.semaphore_signal(free_y, inc=1, device_id=(y_nb, z), device_id_type=mesh_id)

    def landing_free():
        pl.semaphore_wait(free_x, 1)
        pl.semaphore_wait(free_y, 1)

    def query_key_grad():
        loaded("normed")
        for u in unit_b:
            u.step1_sent()

        def qk_rows(m, _):
            at = pl.ds(pl.multiple_of(m * TILE, TILE), TILE)
            db[at, pl.ds(0, feat)] = tn(two[:, at], dc[pl.ds(0, seq), pl.ds(0, feat)]).astype(bf)
            return _

        lax.fori_loop(0, feat // TILE, qk_rows, 0)

    def value_grad():
        def v_rows(m, _):
            at = pl.ds(pl.multiple_of(m * TILE, TILE), TILE)
            db[at, pl.ds(feat, half)] = tn(two[:, at], dc[pl.ds(0, seq), pl.ds(feat, half)]).astype(bf)
            return _

        lax.fori_loop(0, feat // TILE, v_rows, 0)

    def first_part(at):
        at = rows_of(at, TILE)
        return nt(dc[at, pl.ds(0, feat)], wts[pl.ds(0, feat), :]) + nt(
            dc[at, pl.ds(feat, half)], wts[pl.ds(feat, feat), pl.ds(0, half)]
        )

    gn_swaps = [
        send(
            up.at[pl.ds(half_seq + n * TILE, TILE), :], half_in.at[pl.ds(n * TILE, TILE), :], cs.at[7 + n], cr.at[7 + n],
            (core_nb, z),
        )
        for n in range(half_seq // TILE)
    ]

    def to_first(n):
        if n == 0:
            loaded("x")
        up[pl.ds(half_seq + n * TILE, TILE), :] = first_part((1 - c) * half_seq + n * TILE).astype(bf)
        gn_swaps[n].start()

    first_sums = [zero_row, zero_row]

    def first_back(n):
        if n == 0:
            block_sent()
        acc[...] = first_part(c * half_seq + n * TILE)
        gn_swaps[n].wait_recv()

        def first_rows(m, carry):
            gain_sum, shift_sum = carry
            at = pl.ds(pl.multiple_of(m * 64, 64), 64)
            here = pl.ds(pl.multiple_of(n * TILE + m * 64, 64), 64)
            g = acc[at, :] + half_in[here, :].astype(f32)
            center, r = moments(up[here, :].astype(f32))
            hat = center * r
            gh = g * hat
            h = g * vec[0:1, :]
            first = jnp.mean(h, axis=-1, keepdims=True)
            slant = jnp.mean(h * hat, axis=-1, keepdims=True)
            got = three[rows_of(c * half_seq + n * TILE + m * 64, 64), :].astype(f32) + r * (h - first - hat * slant)
            home[here, :] = got.astype(bf)
            return (
                gain_sum + jnp.sum(gh, axis=0, keepdims=True),
                shift_sum + jnp.sum(g, axis=0, keepdims=True),
            )

        first_sums[:] = lax.fori_loop(0, TILE // 64, first_rows, tuple(first_sums))
        input_one(n)
        if n == half_seq // TILE - 1:
            sums[0, 0:1, :] = first_sums[0]
            sums[0, 1:2, :] = first_sums[1]

    small_who = [(core_nb, z), (x_nb, z), (y_nb, z)]
    small = [send(sums.at[0], sums_in.at[n], ss.at[n], sr.at[n], small_who[n]) for n in range(3)] + [
        send(sums.at[0], sums_in.at[3 + d], ss.at[3 + d], sr.at[3 + d], (i, lax.rem(z + d + 1, LINE)))
        for d in range(LINE - 1)
    ]
    sums_out = pltpu.make_async_copy(sums.at[0], small_o, os.at[7])

    def small_step(n):
        if n > 0:
            small[n - 1].wait()
            sums[0] = sums[0] + sums_in[n - 1]
        for d in small[3:] if n == 3 else small[n : n + 1]:
            d.start()

    def small_end():
        for d in range(LINE - 1):
            small[3 + d].wait()
        sums[0] = sums[0] + ((sums_in[3] + sums_in[4]) + sums_in[5])
        sums_out.start()

    (unit_b0, unit_b1), (unit_q, unit_k, unit_v) = unit_b, unit_a

    begin()
    first(0)
    for g in groups:
        own_start(g)
    first(1)
    land(0, 1)
    land(0, 0)
    land(1, 0)
    first(2)
    turn(0, 1)
    land(0, 2)
    land(1, 2)
    land(1, 1)
    x_start()
    turn(0, 0)
    vectors()
    turn(0, 2)
    land(2, 0)
    land(2, 1)
    turn(1, 2)
    turn(1, 0)
    first(3)
    x_spread()
    whole(0)
    turn(1, 1)
    norm_own()
    norm_other()
    turn(2, 1)
    project(0, 512)
    turn(2, 0)
    project(512, 1024)
    project(1024, 1536)
    project(1536, 3 * half)
    whole(1)
    land(3, 0)
    wo_swap()
    land(2, 2)
    attend(0)
    wo_ready()
    land(3, 1)
    attend(1)
    attend(2)
    c_start()
    attend(3)
    attend(4)
    output_rows(0)
    output_rows(1)
    output_rows(2)
    output_rows(3)
    turn(2, 2)
    turn(3, 0)
    second_norm(0)
    second_norm(1)
    second_norm(2)
    second_norm(3)
    land(3, 2)
    turn(3, 1)
    whole(2)
    inner_tile(0)
    inner_tile(1)
    inner_tile(2)
    inner_tile(3)
    inner_tile(4)
    inner_tile(5)
    inner_tile(6)
    c_spread()
    inner_tile(7)
    inner_tile(8)
    inner_tile(9)
    turn(3, 2)
    mask()
    outer_rows(0)
    outer_rows(2)
    outer_rows(1)
    outer_rows(3)
    whole(3)
    block_other()
    block_own()
    through_gelu()
    weights_load()
    to_second(0)
    to_second(1)
    to_second(2)
    to_second(3)
    unit_c.step2()
    second_back()
    block_start()
    inner_grad(0)
    inner_free()
    unit_b0.step1_all()
    inner_grad(1)
    qkv_load()
    output_grad()
    o_swap.wait()
    mixed_grad()
    attend_back(0)
    unit_c.line()
    free_landing()
    unit_b1.step1_all()
    attend_back(1)
    attend_back(2)
    unit_b0.step2()
    landing_free()
    unit_o.step1_all()
    attend_back(3)
    unit_b1.step2()
    attend_back(4)
    query_key_grad()
    unit_q.step1_all()
    to_first(0)
    unit_b0.line()
    value_grad()
    unit_b1.line()
    unit_o.step2()
    unit_k.step1_all()
    unit_q.step2()
    unit_v.step1_all()
    to_first(1)
    unit_o.line()
    unit_q.line()
    unit_k.step2()
    unit_v.step2()
    unit_b1.spread()
    unit_o.spread()
    unit_k.line()
    unit_c.spread()
    unit_q.spread()
    unit_v.line()
    unit_o.cross()
    first_back(0)
    first_back(1)
    small_step(0)
    unit_k.spread()
    unit_q.cross()
    unit_b0.spread()
    small_step(1)
    unit_v.spread()
    unit_b1.cross()
    unit_q.to_core()
    small_step(2)
    unit_c.cross()
    unit_v.cross()
    unit_b0.cross()
    small_step(3)
    unit_c.to_core()
    unit_b1.to_core()
    unit_k.cross()
    small_end()
    unit_b0.to_core()
    unit_v.to_core()
    unit_o.to_core()
    unit_k.to_core()
    sums_out.wait()
    for d in gn_swaps:
        d.wait_send()
    x_sent()
    c_sent()
    input_sent()
    block_arrived()
    input_arrived()
    units = [unit_c] + unit_b + [unit_o] + unit_a
    for u in units[1:]:
        u.step2_sent()
    for u in [unit_o] + unit_a:
        u.step1_sent()
    for u in units:
        u.end()


def run_layer(lengths, offsets, vectors, inner_bias, x, ct, wq, wk, wv, wo, w1, w2):
    rows, feat = wq.shape
    hid = w2.shape[0]
    seq = x.shape[1] * LINE
    half = feat // 2
    r_big, r_small = hid // 2 // PLANE, rows // PLANE
    f32, bf = jnp.float32, jnp.bfloat16
    dma, plain = pltpu.SemaphoreType.DMA, pltpu.SemaphoreType.REGULAR
    anywhere = pl.BlockSpec(memory_space=pl.ANY)
    here, scalars = pl.BlockSpec(memory_space=pltpu.VMEM), pl.BlockSpec(memory_space=pltpu.SMEM)
    small, bounds = (16, 384), (lengths.shape[0], 8, 128)
    made = [
        (x.shape, bf), (x.shape, bf), ((hid, feat), bf), ((rows, LINE * hid), bf),
        ((rows, feat), bf), ((rows, feat), bf), ((rows, feat), bf), ((rows, feat), bf), ((16, feat), f32),
        ((seq // 2, feat), bf), ((seq, feat), bf), ((seq, 4 * half), bf), ((feat, 3 * half), bf), ((feat, half), bf),
    ]
    held = [
        (small, bf), (bounds, jnp.int32), ((LINE,) + small, bf), (bounds, jnp.int32), ((small[0], feat), f32), ((1, 2 * hid), f32),
        ((seq, feat), bf), ((seq, feat), bf), ((feat, 4 * half), bf), ((feat, half), bf), ((feat, 2 * hid), bf),
        ((2 * hid, feat), bf), ((seq, 2 * hid), bf), ((feat, 2 * hid), bf), ((seq, feat), bf), ((seq, feat), bf),
        ((8 * r_big, feat), bf), ((4 * r_big, feat), bf), ((3 * r_big, feat), bf),
        ((4 * r_small, 4 * half), bf), ((3 * r_small, 4 * half), bf),
        ((seq, 256), bf), ((half // HEAD_DIM, seq), f32),
        ((seq // 2, feat), bf), ((seq // 2, feat), bf), ((TILE, feat), f32),
        ((1, 16, feat), f32), ((6, 16, feat), f32),
    ]
    out = pl.pallas_call(
        layer_kernel,
        out_shape=tuple(jax.ShapeDtypeStruct(shape, dtype) for shape, dtype in made),
        in_specs=[scalars] + [here] * (2 + len(vectors)) + [anywhere] * 8,
        out_specs=(anywhere,) * len(made),
        scratch_shapes=[pltpu.VMEM(shape, dtype) for shape, dtype in held]
        + [
            dma((3,)), dma((3,)), dma((4,)), dma((4,)), dma((4,)), dma((4,)),
            dma((4, 5)), dma((12, 4)), dma((12, 5)), dma((7,)), dma((2,)), dma((2,)), dma((4,)), dma((4,)), dma((5,)),
            dma((4, 3)), dma((7, 12)), dma((7, 12)), dma((2, 2)), dma((2, 2)), dma((9,)), dma((9,)), dma((6,)), dma((6,)),
            dma((8,)), plain, plain, plain, plain, plain,
        ],
        compiler_params=pltpu.CompilerParams(
            collective_id=0, has_side_effects=True, vmem_limit_bytes=VMEM_LIMIT
        ),
        name="layer",
    )(lengths, offsets, *vectors, inner_bias, x, ct, wq, wk, wv, wo, w1, w2)
    return out[:9]


def finish_kernel(
    block_ref, input_ref, w2_ref, w1_ref, q_ref, k_ref, v_ref, o_ref, small_ref,
    block_o, input_o, gain_o, shift_o, q_o, bq_o, k_o, v_o, bv_o, o_o, bo_o, gain_two_o, shift_two_o, w1_o, b1_o, w2_o, b2_o,
    held, wide, blocks, sums, ins, outs,
):
    z = lax.axis_index("chrom")
    rows, feat = q_ref.shape
    tiles = [(ref, to, pl.ds(0, rows), pl.ds(0, feat)) for ref, to in ((q_ref, q_o), (k_ref, k_o), (v_ref, v_o), (o_ref, o_o))]
    tiles += [(w1_ref, w1_o, pl.ds(0, rows), pl.ds(n * feat, feat)) for n in range(w1_ref.shape[1] // feat)]
    tiles += [(w2_ref, w2_o, pl.ds(n * rows, rows), pl.ds(0, feat)) for n in range(w2_ref.shape[0] // rows)]
    small_in = pltpu.make_async_copy(small_ref, sums, ins.at[len(tiles)])
    small_in.start()
    loads = [pltpu.make_async_copy(ref.at[at, cols], held.at[n], ins.at[n]) for n, (ref, _, at, cols) in enumerate(tiles)]
    loads += [
        pltpu.make_async_copy(ref, blocks.at[n], ins.at[len(tiles) + 1 + n]) for n, ref in enumerate((block_ref, input_ref))
    ]
    for d in loads:
        d.start()
    small_in.wait()
    spots = (gain_o, shift_o, bq_o, bv_o, bo_o, gain_two_o, shift_two_o, b2_o)
    for n, to in enumerate(spots):
        value = sums[n : n + 1, 0:rows]
        for s in range(1, LINE):
            value = jnp.where(z == s, sums[n : n + 1, s * rows : (s + 1) * rows], value)
        to[...] = value[0, :]
    value = sums[VECTORS : VECTORS + 1, :]
    for s in range(1, LINE):
        value = jnp.where(z == s, sums[VECTORS + s : VECTORS + s + 1, :], value)
    b1_o[...] = value[0, :]
    stores = []
    for n, (_, to, at, cols) in enumerate(tiles):
        loads[n].wait()
        wide[n] = held[n].astype(jnp.float32)
        stores.append(pltpu.make_async_copy(wide.at[n], to.at[at, cols], outs.at[n]))
        stores[-1].start()
    for n, to in enumerate((block_o, input_o)):
        loads[len(tiles) + n].wait()
        stores.append(pltpu.make_async_copy(blocks.at[n], to, outs.at[len(tiles) + n]))
        stores[-1].start()
    for d in stores:
        d.wait()


def finish(block_out, input_grad, w2, w1, q, k, v, o, sums):
    f32 = jnp.float32
    rows, feat = q.shape
    hid = w2.shape[0]
    tiles = 4 + w1.shape[1] // feat + hid // rows
    anywhere, here = pl.BlockSpec(memory_space=pl.ANY), pl.BlockSpec(memory_space=pltpu.VMEM)
    matrix, vector = jax.ShapeDtypeStruct((rows, feat), f32), jax.ShapeDtypeStruct((rows,), f32)
    block = jax.ShapeDtypeStruct(block_out.shape, block_out.dtype)
    made = (
        block, block, vector, vector, matrix, vector, matrix, matrix, vector, matrix, vector, vector, vector,
        jax.ShapeDtypeStruct(w1.shape, f32), jax.ShapeDtypeStruct((hid,), f32), jax.ShapeDtypeStruct(w2.shape, f32), vector,
    )
    return pl.pallas_call(
        finish_kernel,
        out_shape=made,
        in_specs=[anywhere] * 9,
        out_specs=tuple(here if len(m.shape) == 1 else anywhere for m in made),
        scratch_shapes=[
            pltpu.VMEM((tiles, rows, feat), q.dtype), pltpu.VMEM((tiles, rows, feat), f32),
            pltpu.VMEM((2,) + block_out.shape, block_out.dtype), pltpu.VMEM(sums.shape, f32),
            pltpu.SemaphoreType.DMA((tiles + 3,)), pltpu.SemaphoreType.DMA((tiles + 2,)),
        ],
        compiler_params=pltpu.CompilerParams(vmem_limit_bytes=VMEM_LIMIT),
        name="finish",
    )(block_out, input_grad, w2, w1, q, k, v, o, sums)


def paired_local(
    inputs, lengths, offsets, cotangent, norm_gain, norm_shift, query_proj, query_bias, key_proj, value_proj,
    value_bias, output_proj, output_bias, second_gain, second_shift, inner_proj, inner_bias, outer_proj, outer_bias,
):
    vectors = (norm_gain, norm_shift, query_bias, value_bias, output_bias, second_gain, second_shift, outer_bias)
    grads = run_layer(
        lengths, offsets, vectors, inner_bias, inputs, cotangent,
        query_proj, key_proj, value_proj, output_proj, inner_proj, outer_proj,
    )
    return finish(*grads)


def solution(mesh):
    paired = mesh.shape["chrom"] == 4 and mesh.shape["cells"] == 8
    placed = (
        P("cells", "chrom", None),
        P("cells"),
        P("cells", None),
        P("cells", "chrom", None),
        P("chrom"),
        P("chrom"),
        P("chrom", None),
        P("chrom"),
        P("chrom", None),
        P("chrom", None),
        P("chrom"),
        P("chrom", None),
        P("chrom"),
        P("chrom"),
        P("chrom"),
        P("chrom", None),
        P("chrom"),
        P("chrom", None),
        P("chrom"),
    )
    return jax.shard_map(
        paired_local if paired else general,
        mesh=mesh,
        in_specs=placed,
        out_specs=(
            P("cells", "chrom", None),
            P("cells", "chrom", None),
            P("chrom"),
            P("chrom"),
            P("chrom", None),
            P("chrom"),
            P("chrom", None),
            P("chrom", None),
            P("chrom"),
            P("chrom", None),
            P("chrom"),
            P("chrom"),
            P("chrom"),
            P("chrom", None),
            P("chrom"),
            P("chrom", None),
            P("chrom"),
        ),
        check_vma=False,
    )
```
